32 devices in a mesh: grp: 4 (over x, core), reg: 8 (over z, y).
Axes of the slice: x: 2, y: 2, z: 4, core: 2. Of those that a mesh axis runs over, the one named last changes fastest.
Arguments:
- grain_pos: float32 [3, 524288], P(None, ('grp', 'reg')), may hold values from -6 to 6
- grain_vel: float32 [3, 524288], P(None, ('grp', 'reg')), may hold values from -6 to 6
- grain_vol: float32 [524288], P(('grp', 'reg')), may hold values from 0.5 to 2
- drag_coef: float32 [524288], P(('grp', 'reg')), may hold values from 0.2 to 2
- grain_count: int32 [32], P(('grp', 'reg')), may hold values from 0 to 16384, as said below
- contact_rows: int32 [8, 524288], P(None, ('grp', 'reg')), may hold values from -1 to 255, as said below
- contact_stiff: float32 [8, 524288], P(None, ('grp', 'reg')), may hold values from 0.05 to 0.5
- partner_block: int32 [4096], P(('grp', 'reg')), may hold values from 0 to 191, as said below
- halo_list: int32 [2, 131072], P(None, ('grp', 'reg')), may hold values from 0 to 16383, as said below
- grain_cell: int32 [524288], P(('grp', 'reg')), may hold values from 0 to 127
- tile_cell_block: int32 [4096], P(('grp', 'reg')), may hold values from 0 to 2047
- pressure_old: float32 [32, 128, 512], P('reg'), may hold values from -6 to 6
- pressure_source: float32 [32, 128, 512], P('reg'), may hold values from -6 to 6
- solid_old: float32 [32, 128, 512], P('reg'), may hold values from 0 to 1.5
Outputs:
- new_vel: float32 [3, 524288], P(None, ('grp', 'reg'))
The draws below stay inside these ranges and needn't reach their ends.
Inputs may be any that keep to these rules, and one draw needn't show every extreme that they name: `grain_count`: devices of the last grp index hold no grains; a device's live grains fill its first slots; some device holds 16384. `contact_rows`: for a live grain in block t, entries 0 to 127 name grains of block t and entries 128 to 255 name grains of block partner_block[t]; every named grain is live; -1 marks an empty slot. Entries of slots that are not live carry no meaning. `partner_block`: blocks below 128 are the device's own, the next 32 are those received from the lower region, the last 32 those from the upper region; a block holding live grains never names a region that does not exist. `halo_list`: every entry names a live grain of its device where the device holds grains, else 0.
All inputs are finite; a program needn't handle non-finite values.
Results may differ from the reference program's by a relative error of at most 0.0003.
Values sent between devices are 32-bit elements; how exact they have to be, the bound alone decides.
No kernel may reach another device: no remote copies, remote signals or barrier semaphores. Data moves between devices by JAX's collectives and lax.ppermute only.
A program may use at most 64 MiB of HBM per device.

```python
import math
import jax
import jax.numpy as jnp
from jax import lax

CAP = 16384
BLOCK = 128
K = 8
ITERS = 4
CY = 128
CZ = 512
SLOTS = 524288
TILES = 4096
HALO = 4096
HALOS = 131072
NX = 32
CELLS = 262144
N_GRP = 4
N_REG = 8
DEVICES = 32


def held_counts(key):
    count_key = jax.random.fold_in(key, 11)
    first_key, second_key = jax.random.split(count_key)
    device_ids = jnp.arange(DEVICES)
    drawn = jax.random.randint(first_key, (DEVICES,), CAP // 8, CAP + 1)
    fullest = jax.random.randint(second_key, (), 0, (N_GRP - 1) * N_REG)
    drawn = jnp.where(device_ids == fullest, CAP, drawn)
    return jnp.where(device_ids >= (N_GRP - 1) * N_REG, 0, drawn).astype(jnp.int32)


def partner_blocks(key):
    counts = held_counts(key)
    per_dev = CAP // BLOCK
    halo_blocks = HALO // BLOCK
    tile_ids = jnp.arange(TILES)
    device = tile_ids // per_dev
    tile_index = tile_ids % per_dev
    region = device % N_REG
    held_grains = counts[device]
    live_tiles = (held_grains + BLOCK - 1) // BLOCK
    subkeys = jax.random.split(jax.random.fold_in(key, 23), 4)
    own_pick = jax.random.randint(subkeys[0], (TILES,), 0, jnp.maximum(live_tiles, 1))
    lower_ok = region > 0
    upper_ok = region < N_REG - 1
    coin_flip = jax.random.randint(subkeys[1], (TILES,), 0, 2)
    go_upper = jnp.where(lower_ok & upper_ok, coin_flip == 1, upper_ok)
    side_pick = per_dev + jnp.where(go_upper, halo_blocks, 0) + jax.random.randint(subkeys[2], (TILES,), 0, halo_blocks)
    use_halo = jax.random.randint(subkeys[3], (TILES,), 0, 2) == 1
    chosen = jnp.where(use_halo, side_pick, own_pick)
    dead_tile = tile_index >= live_tiles
    filler = jnp.where(tile_index % 2 == 0, 0, per_dev + 2 * halo_blocks - 1)
    return jnp.where(dead_tile, filler, chosen).astype(jnp.int32)


def draw_grain_count(key, part):
    return held_counts(key)


def draw_partner_block(key, part):
    return partner_blocks(key)


def draw_contact_rows(key, part):
    counts = held_counts(key)
    blocks = partner_blocks(key)
    per_dev = CAP // BLOCK
    slot_ids = jnp.arange(SLOTS)
    device = slot_ids // CAP
    local_slot = slot_ids % CAP
    tile_index = local_slot // BLOCK
    held_grains = counts[device]
    partner = blocks[slot_ids // BLOCK]
    subkeys = jax.random.split(jax.random.fold_in(key, 37), 2)
    rows_drawn = jax.random.randint(subkeys[0], (K, SLOTS), 0, 2 * BLOCK)
    keep_slot = jax.random.randint(subkeys[1], (K, SLOTS), 0, 4) > 0
    target_block = jnp.where(rows_drawn < BLOCK, tile_index[None, :], partner[None, :])
    target_row = rows_drawn % BLOCK
    target_live = jnp.where(target_block < per_dev, target_block * BLOCK + target_row < held_grains[None, :], True)
    source_live = (local_slot < held_grains)[None, :]
    valid = keep_slot & target_live & source_live
    dead_fill = jnp.where(jnp.arange(K)[:, None] == 0, 2 * BLOCK - 1, -1)
    return jnp.where(source_live, jnp.where(valid, rows_drawn, -1), dead_fill).astype(jnp.int32)


def draw_halo_list(key, part):
    counts = held_counts(key)
    entry_ids = jnp.arange(HALOS)
    device = entry_ids // HALO
    held_grains = jnp.maximum(counts[device], 1)[None, :]
    drawn = jax.random.randint(jax.random.fold_in(key, 53), (2, HALOS), 0, held_grains)
    leading = (entry_ids % HALO == 0)[None, :] & (jnp.arange(2)[:, None] == 0)
    return jnp.where(leading, held_grains - 1, drawn).astype(jnp.int32)


def place_ends(values, key, least, largest):
    place = [jax.random.randint(jax.random.fold_in(key, axis), (), 0, length) for axis, length in enumerate(values.shape)]
    longest = values.shape.index(max(values.shape))
    beside = place[:longest] + [(place[longest] + 1) % values.shape[longest]] + place[longest + 1:]
    return values.at[tuple(place)].set(least).at[tuple(beside)].set(largest)


def steps_of(own_key, shape, cuts, low, top_value):
    def one(position, shards_of):
        steps = jax.random.uniform(jax.random.fold_in(jax.random.fold_in(own_key, 6), position), (shards_of,), jnp.float32, low / len(cuts), top_value / len(cuts))
        return jnp.repeat(jnp.exp(steps), shape[position] // shards_of).reshape((-1,) + (1,) * (len(shape) - position - 1))

    loudness = one(*cuts[0])
    for cut in cuts[1:]:
        loudness = loudness * one(*cut)
    return loudness


def scatter_about(key, dims, spread, reach, cuts=(), kind=jnp.bfloat16):
    array = spread * jax.random.normal(key, dims, jnp.float32)
    if cuts:
        array = array * steps_of(key, dims, cuts, -0.22, 0.18)
    return jnp.clip(array, -reach, reach).astype(kind)


def setup_inputs(seed: int = 0) -> dict:
    arg_keys = jax.random.split(jax.random.key(seed), 15)
    return {
        "grain_pos": scatter_about(arg_keys[0], (3, SLOTS), 1.0, 6.0, ((1, 32),), jnp.float32),
        "grain_vel": scatter_about(arg_keys[1], (3, SLOTS), 1.0, 6.0, ((1, 32),), jnp.float32),
        "grain_vol": jnp.clip(jnp.exp(math.log(2.0) - 1.3862944 * jax.random.uniform(arg_keys[2], (SLOTS,), jnp.float32) ** steps_of(arg_keys[2], (SLOTS,), ((0, 32),), -0.2, 0.2)), 0.5, 2.0),
        "drag_coef": jnp.clip(jnp.exp(math.log(2.0) - 2.3025851 * jax.random.uniform(arg_keys[3], (SLOTS,), jnp.float32) ** steps_of(arg_keys[3], (SLOTS,), ((0, 32),), -0.2, 0.2)), 0.2, 2.0),
        "grain_count": draw_grain_count(jax.random.fold_in(arg_keys[14], 71), 0),
        "contact_rows": draw_contact_rows(jax.random.fold_in(arg_keys[14], 71), 0),
        "contact_stiff": jnp.clip(jnp.exp(math.log(0.5) - 2.3025851 * jax.random.uniform(arg_keys[6], (K, SLOTS), jnp.float32) ** steps_of(arg_keys[6], (K, SLOTS), ((1, 32),), -0.2, 0.2)), 0.05, 0.5),
        "partner_block": draw_partner_block(jax.random.fold_in(arg_keys[14], 71), 0),
        "halo_list": draw_halo_list(jax.random.fold_in(arg_keys[14], 71), 0),
        "grain_cell": place_ends(jax.random.randint(arg_keys[9], (SLOTS,), 0, BLOCK), jax.random.fold_in(arg_keys[9], 1), 0, BLOCK - 1).astype(jnp.int32),
        "tile_cell_block": place_ends(jax.random.randint(arg_keys[10], (TILES,), 0, CELLS // BLOCK), jax.random.fold_in(arg_keys[10], 1), 0, (CELLS // BLOCK) - 1).astype(jnp.int32),
        "pressure_old": scatter_about(arg_keys[11], (NX, CY, CZ), 1.0, 6.0, ((0, 8),), jnp.float32),
        "pressure_source": scatter_about(arg_keys[12], (NX, CY, CZ), 1.0, 6.0, ((0, 8),), jnp.float32),
        "solid_old": jnp.clip(1.5 * jax.random.uniform(arg_keys[13], (NX, CY, CZ), jnp.float32) ** steps_of(arg_keys[13], (NX, CY, CZ), ((0, 8),), -0.2, 0.2), 0.0, 1.5),
    }


SPRING = 1.0
DAMPING = 0.5
TIME_STEP = 0.5


def neighbours(padded):
    summed = padded[2:, 1:-1, 1:-1] + padded[:-2, 1:-1, 1:-1]
    summed = summed + padded[1:-1, 2:, 1:-1] + padded[1:-1, :-2, 1:-1]
    return summed + padded[1:-1, 1:-1, 2:] + padded[1:-1, 1:-1, :-2]


def per_device(packed):
    extended, rows_dev, stiff_dev, blocks_dev = packed
    tiles_here = CAP // BLOCK
    grain_state = extended[:, :CAP]
    partner = jnp.take(extended.reshape(6, -1, BLOCK), blocks_dev, axis=1)
    paired = jnp.concatenate([grain_state.reshape(6, tiles_here, BLOCK), partner], 2)
    rows_tiled = rows_dev.reshape(K, tiles_here, BLOCK)
    stiff_tiled = stiff_dev.reshape(K, tiles_here, BLOCK)
    columns = jnp.arange(2 * BLOCK, dtype=jnp.int32)
    weights = jnp.zeros((tiles_here, BLOCK, 2 * BLOCK), jnp.float32)
    for slot_index in range(K):
        weights = weights + jnp.where(rows_tiled[slot_index][:, :, None] == columns, stiff_tiled[slot_index][:, :, None], jnp.float32(0.0))
    summed = jnp.einsum("tij,ctj->cti", weights, paired, precision=lax.Precision.HIGHEST)
    stiff_total = jnp.sum(jnp.where(rows_tiled >= 0, stiff_tiled, jnp.float32(0.0)), 0)
    own_rows = paired[:, :, :BLOCK]
    spring = SPRING * (stiff_total * own_rows[:3] - summed[:3])
    damper = DAMPING * (summed[3:] - stiff_total * own_rows[3:])
    return (spring + damper).reshape(3, CAP)


def reference(grain_pos, grain_vel, grain_vol, drag_coef, grain_count, contact_rows, contact_stiff, partner_block, halo_list, grain_cell, tile_cell_block, pressure_old, pressure_source, solid_old):
    live_mask = (jnp.arange(CAP, dtype=jnp.int32)[None, :] < grain_count[:, None]).astype(jnp.float32).reshape(SLOTS)
    grain_state = jnp.concatenate([grain_pos, grain_vel], 0).reshape(6, N_GRP, N_REG, CAP)
    halo_rows = halo_list.reshape(2, N_GRP, N_REG, HALO).astype(jnp.int32)
    downward = jnp.take_along_axis(grain_state, halo_rows[0][None], axis=3)
    upward = jnp.take_along_axis(grain_state, halo_rows[1][None], axis=3)
    from_lower = jnp.pad(upward, ((0, 0), (0, 0), (1, 0), (0, 0)))[:, :, :-1]
    from_upper = jnp.pad(downward, ((0, 0), (0, 0), (0, 1), (0, 0)))[:, :, 1:]
    extended = jnp.concatenate([grain_state, from_lower, from_upper], 3)
    extended = jnp.transpose(extended, (1, 2, 0, 3)).reshape(DEVICES, 6, CAP + 2 * HALO)
    rows_all = jnp.transpose(contact_rows.reshape(K, DEVICES, CAP), (1, 0, 2))
    stiff_all = jnp.transpose(contact_stiff.reshape(K, DEVICES, CAP), (1, 0, 2))
    blocks_all = partner_block.reshape(DEVICES, CAP // BLOCK)
    contact = lax.map(per_device, (extended, rows_all, stiff_all, blocks_all))
    contact = jnp.transpose(contact, (1, 0, 2)).reshape(3, SLOTS)
    slot_ids = jnp.arange(SLOTS, dtype=jnp.int32)
    device_ids = slot_ids // CAP
    block_of_slot = jnp.take(tile_cell_block, slot_ids // BLOCK).astype(jnp.int32)
    global_cell = ((device_ids % N_REG) * CELLS + block_of_slot * BLOCK + grain_cell).astype(jnp.int32)
    solid_now = jax.ops.segment_sum(grain_vol * live_mask, global_cell, num_segments=NX * CY * CZ).reshape(NX, CY, CZ)
    drag_sum = jax.ops.segment_sum(drag_coef * live_mask, global_cell, num_segments=NX * CY * CZ).reshape(NX, CY, CZ)
    porous = 1.0 / (1.0 + solid_now)
    diagonal = 6.0 * porous + drag_sum + 1.0
    driving = pressure_source + solid_now - solid_old
    pressure = pressure_old
    for sweep_index in range(ITERS):
        pressure = (driving + porous * neighbours(jnp.pad(pressure, 1))) / diagonal
    weight = 1.0 / (porous + drag_sum)
    padded = jnp.pad(pressure, 1)
    grad_x = 0.5 * (padded[2:, 1:-1, 1:-1] - padded[:-2, 1:-1, 1:-1])
    grad_y = 0.5 * (padded[1:-1, 2:, 1:-1] - padded[1:-1, :-2, 1:-1])
    grad_z = 0.5 * (padded[1:-1, 1:-1, 2:] - padded[1:-1, 1:-1, :-2])
    fields = jnp.stack([grad_x, grad_y, grad_z, weight]).reshape(4, -1)
    at_grain = jnp.take(fields, global_cell, axis=1)
    gradient = at_grain[:3]
    fluid_vel = -gradient * at_grain[3]
    force = contact - grain_vol * gradient + drag_coef * (fluid_vel - grain_vel)
    return (grain_vel + TIME_STEP * force / grain_vol) * live_mask
```

```python
import functools

import jax
import jax.numpy as jnp
from jax import lax
from jax.experimental import pallas as pl
from jax.experimental.pallas import tpu as pltpu
from jax.sharding import PartitionSpec as P

BLOCK = 128
SUB = 8
CORES = 2
SPRING = 1.0
DAMPING = 0.5
TIME_STEP = 0.5

VMEM = pl.BlockSpec(memory_space=pltpu.VMEM)
SMEM = pl.BlockSpec(memory_space=pltpu.SMEM)
F32 = jnp.float32
BF16 = jnp.bfloat16


def iota(shape, dim):
    return lax.broadcasted_iota(jnp.int32, shape, dim)


def shaped(*dims):
    return jax.ShapeDtypeStruct(dims, F32)


def call(kernel, outs, specs, args, scratch=(), flops=0, size=0):
    return pl.pallas_call(
        kernel,
        out_shape=outs,
        in_specs=specs,
        out_specs=jax.tree.map(lambda _: VMEM, outs),
        scratch_shapes=list(scratch),
        compiler_params=pltpu.CompilerParams(vmem_limit_bytes=40 * 1024 * 1024),
        cost_estimate=pl.CostEstimate(flops=flops, bytes_accessed=size, transcendentals=0),
    )(*args)


def lanes_of(source, index):
    return jnp.take_along_axis(source, index, axis=1, mode="promise_in_bounds")


def thirds(value):
    high = value.astype(BF16)
    rest = value - high.astype(F32)
    middle = rest.astype(BF16)
    low = (rest - middle.astype(F32)).astype(BF16)
    return high, middle, low


def deposit_kernel(count, cell, vol, drag, ids, out):
    tiles = cell.shape[0]
    sub = iota((SUB, BLOCK), 0)
    rows_c = iota((BLOCK, BLOCK), 0)
    even = sub % 2 == 0
    low_pair = sub % 4 < 2

    def step(group, carry):
        first = pl.multiple_of(group * SUB, SUB)
        slot = (first + sub) * BLOCK + iota((SUB, BLOCK), 1)
        live = slot < count[0]
        cells = cell[pl.ds(first, SUB), :]
        parts = thirds(jnp.where(live, vol[pl.ds(first, SUB), :], 0.0)) + thirds(
            jnp.where(live, drag[pl.ds(first, SUB), :], 0.0)
        )
        parts = [part.astype(F32) for part in parts]
        left = jnp.concatenate([jnp.where(even, part, 0.0) for part in parts], 0)
        right = jnp.concatenate([jnp.where(even, 0.0, part) for part in parts], 0)
        loads = jnp.concatenate([left, right], 1).astype(BF16)
        sums = [jnp.zeros((SUB, BLOCK), F32), jnp.zeros((SUB, BLOCK), F32)]
        for quad in range(SUB // 4):
            hot = [
                jnp.where(
                    rows_c == jnp.broadcast_to(cells[t : t + 1, :], (BLOCK, BLOCK)), 1.0, 0.0
                ).astype(BF16)
                for t in range(4 * quad, 4 * quad + 4)
            ]
            picked = jnp.concatenate(
                [jnp.concatenate(hot[:2], 1), jnp.concatenate(hot[2:], 1)], 0
            )
            placed = lax.dot_general(
                loads, picked, (((1,), (1,)), ((), ())), preferred_element_type=F32
            )
            for field in range(2):
                base = field * 3 * SUB
                total = placed[base : base + SUB] + placed[base + SUB : base + 2 * SUB]
                total = total + placed[base + 2 * SUB : base + 3 * SUB]
                chosen = jnp.where(low_pair, total[:, :BLOCK], total[:, BLOCK:])
                sums[field] = jnp.where(sub // 4 == quad, chosen, sums[field])
        out[pl.ds(first, SUB), :BLOCK] = sums[0]
        out[pl.ds(first, SUB), BLOCK:] = sums[1]
        return carry

    lax.fori_loop(0, tiles // SUB, step, 0, unroll=2)
    out[tiles : tiles + SUB, :BLOCK] = jnp.broadcast_to(ids[...].astype(F32), (SUB, BLOCK))
    out[tiles : tiles + SUB, BLOCK:] = jnp.zeros((SUB, BLOCK), F32)


def halo_kernel(pos, vel, lists, state, down, up, index):
    tiles = pos.shape[1] // BLOCK
    rows = lists.shape[1] // BLOCK
    for tile in range(tiles):
        lanes = slice(tile * BLOCK, (tile + 1) * BLOCK)
        mixed = SPRING * pos[:, lanes] - DAMPING * vel[:, lanes]
        for axis in range(3):
            state[axis * tiles + tile : axis * tiles + tile + 1, :] = mixed[axis : axis + 1]
    for side in range(2):
        for row in range(rows):
            index[side * rows + row : side * rows + row + 1, :] = lists[
                side : side + 1, row * BLOCK : (row + 1) * BLOCK
            ]
    groups = 2 * rows // SUB
    named = [index[g * SUB : (g + 1) * SUB, :] for g in range(groups)]
    block = [lax.shift_right_logical(value, 7) for value in named]
    lane = [value & (BLOCK - 1) for value in named]

    def step(source, sums):
        new = []
        spread = [
            jnp.broadcast_to(state[pl.ds(axis * tiles + source, 1), :], (SUB, BLOCK))
            for axis in range(3)
        ]
        for g in range(groups):
            here = block[g] == source
            for axis in range(3):
                new.append(
                    jnp.where(here, lanes_of(spread[axis], lane[g]), sums[3 * g + axis])
                )
        return tuple(new)

    zero = jnp.zeros((SUB, BLOCK), F32)
    sums = lax.fori_loop(0, tiles, step, (zero,) * (3 * groups), unroll=2)
    for side, out in enumerate((down, up)):
        for axis in range(3):
            for g in range(groups // 2):
                first = axis * rows + g * SUB
                out[first : first + SUB, :] = sums[3 * (side * groups // 2 + g) + axis]


def contact_kernel(partner, state, lower, upper, named, stiff, out, extended):
    tiles = state.shape[0] // 3
    rows = lower.shape[0] // 3
    blocks = tiles + 2 * rows
    for axis in range(3):
        extended[axis * blocks : axis * blocks + tiles, :] = state[
            axis * tiles : (axis + 1) * tiles, :
        ]
        for place, side in enumerate((lower, upper)):
            first = axis * blocks + tiles + place * rows
            extended[first : first + rows, :] = side[axis * rows : (axis + 1) * rows, :]

    def step(tile, carry):
        lanes = pl.ds(pl.multiple_of(tile * BLOCK, BLOCK), BLOCK)
        entry = named[:, lanes]
        weight = jnp.where(entry >= 0, stiff[:, lanes], 0.0)
        own = entry < BLOCK
        lane = entry & (BLOCK - 1)
        other = partner[tile]
        for axis in range(3):
            mine = jnp.broadcast_to(extended[pl.ds(axis * blocks + tile, 1), :], entry.shape)
            theirs = jnp.broadcast_to(extended[pl.ds(axis * blocks + other, 1), :], entry.shape)
            met = jnp.where(own, lanes_of(mine, lane), lanes_of(theirs, lane))
            pull = jnp.sum(weight * (mine - met), axis=0, keepdims=True)
            out[pl.ds(axis * tiles + tile, 1), :] = pull
        return carry

    lax.fori_loop(0, tiles, step, 0, unroll=4)


def shifted(plane):
    height, width = plane.shape
    row = iota(plane.shape, 0)
    column = iota(plane.shape, 1)
    above = jnp.where(row == 0, 0.0, pltpu.roll(plane, 1, 0))
    below = jnp.where(row == height - 1, 0.0, pltpu.roll(plane, height - 1, 0))
    left = jnp.where(column == 0, 0.0, pltpu.roll(plane, 1, 1))
    right = jnp.where(column == width - 1, 0.0, pltpu.roll(plane, width - 1, 1))
    return above, below, left, right


def sweep(plane_at, constant, factor, new, low, high):
    count = new.shape[0]
    for x in range(count):
        above, below, left, right = shifted(plane_at(x))
        near = plane_at(x - 1) + plane_at(x + 1) + above + below + left + right
        value = constant[x] + factor[x] * near
        new[x] = value
        if x == 0:
            low[...] = value
        if x == count - 1:
            high[...] = value


def first_kernel(
    start, mine, second, third, pressure, source, solid_before, before, after,
    constant, factor, new, low, high, weight,
):
    tiles = mine.shape[0] - SUB
    planes, height, width = new.shape
    full = pressure.shape[1]
    zones = width // BLOCK
    first = pl.multiple_of(start[0], SUB)
    parts = [thirds(group[:tiles, :]) for group in (mine, second, third)]
    loads = [jnp.concatenate([part[i] for part in parts], 0) for i in range(3)]
    ids = jnp.concatenate([group[tiles : tiles + 1, :BLOCK] for group in (mine, second, third)], 1)
    ids = ids.astype(jnp.int32)

    def gathered(wanted):
        hot = jnp.where(wanted == jnp.broadcast_to(ids, wanted.shape), 1.0, 0.0).astype(BF16)
        total = jnp.dot(hot, loads[2], preferred_element_type=F32)
        total = total + jnp.dot(hot, loads[1], preferred_element_type=F32)
        total = total + jnp.dot(hot, loads[0], preferred_element_type=F32)
        return total[:, :BLOCK], total[:, BLOCK:]

    row = iota((height, 3 * tiles), 0) * zones
    for x in range(planes):
        for zone in range(zones):
            lanes = slice(zone * BLOCK, (zone + 1) * BLOCK)
            solid, drag = gathered(row + ((x * full + first) * zones + zone))
            porous = 1.0 / (1.0 + solid)
            inverse = 1.0 / (6.0 * porous + drag + 1.0)
            driving = source[x, pl.ds(first, height), lanes] + solid
            driving = driving - solid_before[x, pl.ds(first, height), lanes]
            constant[x, :, lanes] = driving * inverse
            factor[x, :, lanes] = porous * inverse

    def plane_at(x):
        if x < 0:
            return before[...]
        if x == planes:
            return after[...]
        return pressure[x, pl.ds(first, height), :]

    sweep(plane_at, constant, factor, new, low, high)
    own = jnp.transpose(jnp.broadcast_to(ids[:, :tiles], (tiles, tiles)).astype(F32))
    own = own.astype(jnp.int32)
    solid, drag = gathered(jnp.concatenate([own] * 3, 1))
    weight[...] = 1.0 / (1.0 / (1.0 + solid) + drag)


def sweep_kernel(old, before, after, constant, factor, new, low, high):
    planes = new.shape[0]

    def plane_at(x):
        if x < 0:
            return before[...]
        if x == planes:
            return after[...]
        return old[x]

    sweep(plane_at, constant, factor, new, low, high)


def pick_rows(place, ids, fields, out, height, full, width, own_rows):
    first, owner = place[0], place[1]
    zones = width // BLOCK

    def step(tile, carry):
        block = ids[tile]
        zone = block % zones
        line = block // zones
        x, y = line // full, line % full
        here = y // own_rows == owner
        inside = jnp.where(here, y - first, 0)
        row = fields[pl.ds((x * zones + zone) * height + inside, 1), :]
        out[pl.ds(tile, 1), :] = jnp.where(here, row, 0.0)
        return carry

    lax.fori_loop(0, out.shape[0], step, 0, unroll=8)


def cross_kernel(full, own_rows, place, ids_a, ids_b, ids_c, pressure, out_a, out_b, out_c, fields):
    planes, height, width = pressure.shape
    zones = width // BLOCK
    for x in range(planes):
        above, below, left, right = shifted(pressure[x])
        grad_y = 0.5 * (below - above)
        grad_z = 0.5 * (right - left)
        for zone in range(zones):
            rows = slice((x * zones + zone) * height, (x * zones + zone + 1) * height)
            lanes = slice(zone * BLOCK, (zone + 1) * BLOCK)
            fields[rows, :BLOCK] = grad_y[:, lanes]
            fields[rows, BLOCK:] = grad_z[:, lanes]
    for ids, out in ((ids_a, out_a), (ids_b, out_b), (ids_c, out_c)):
        pick_rows(place, ids, fields, out, height, full, width, own_rows)


def along_kernel(
    full, own_rows, place, ids_a, ids_b, ids_c, pressure, before, after, out_a, out_b, out_c, fields
):
    planes, height, width = pressure.shape
    zones = width // BLOCK
    for x in range(planes):
        behind = before[...] if x == 0 else pressure[x - 1]
        ahead = after[...] if x == planes - 1 else pressure[x + 1]
        grad_x = 0.5 * (ahead - behind)
        for zone in range(zones):
            rows = slice((x * zones + zone) * height, (x * zones + zone + 1) * height)
            fields[rows, :] = grad_x[:, zone * BLOCK : (zone + 1) * BLOCK]
    for ids, out in ((ids_a, out_a), (ids_b, out_b), (ids_c, out_c)):
        pick_rows(place, ids, fields, out, height, full, width, own_rows)


def final_kernel(
    count, along_a, along_b, along_c, cross_a, cross_b, cross_c, weight, contact, vel, vol, drag,
    cell, out,
):
    tiles = cell.shape[0]
    cells = cell[...]
    cross = cross_a[...] + cross_b[...] + cross_c[...]
    fields = [along_a[...] + along_b[...] + along_c[...], cross[:, :BLOCK], cross[:, BLOCK:]]
    heft = lanes_of(weight[...], cells)
    slot = iota(cells.shape, 0) * BLOCK + iota(cells.shape, 1)
    live = slot < count[0]
    volume = vol[...]
    push = TIME_STEP / volume
    for axis in range(3):
        gradient = lanes_of(fields[axis], cells)
        own = jnp.concatenate(
            [vel[axis : axis + 1, t * BLOCK : (t + 1) * BLOCK] for t in range(tiles)], 0
        )
        fluid = -gradient * heft
        force = contact[axis * tiles : (axis + 1) * tiles, :] - volume * gradient
        force = force + drag[...] * (fluid - own)
        new = jnp.where(live, own + force * push, 0.0)
        for t in range(tiles):
            out[axis : axis + 1, t * BLOCK : (t + 1) * BLOCK] = new[t : t + 1, :]


def on_device(
    grain_pos,
    grain_vel,
    grain_vol,
    drag_coef,
    grain_count,
    contact_rows,
    contact_stiff,
    partner_block,
    halo_list,
    grain_cell,
    tile_cell_block,
    pressure_old,
    pressure_source,
    solid_old,
):
    groups, regions = lax.axis_size("grp"), lax.axis_size("reg")
    holding = groups - 1
    halves = groups // CORES
    slots = grain_pos.shape[1]
    tiles = slots // BLOCK
    planes, full, width = pressure_old.shape
    own_rows = full // halves
    height = min(full, own_rows + SUB * min(2, halves - 1))
    group = lax.axis_index("grp")
    half = group // CORES
    first = jnp.clip(half * own_rows - SUB, 0, full - height).astype(jnp.int32)
    start = first.reshape(1)
    owner = jnp.where(group % CORES == 0, half, -1).astype(jnp.int32)
    place = jnp.stack([first, owner])

    def send(value, pairs):
        return lax.ppermute(value, ("grp", "reg"), [(a[0] * regions + a[1], b[0] * regions + b[1]) for a, b in pairs])

    def along_reg(value, step, members):
        pairs = [
            ((g, r), (g, r + step)) for g in members for r in range(regions) if 0 <= r + step < regions
        ]
        return send(value, pairs)

    def along_grp(value, step, members):
        pairs = [((g, r), ((g + step) % holding, r)) for g in members for r in range(regions)]
        return send(value, pairs)

    owners = range(0, groups, CORES)
    holders = range(holding)

    count = grain_count
    cell = grain_cell.reshape(tiles, BLOCK)
    vol = grain_vol.reshape(tiles, BLOCK)
    drag = drag_coef.reshape(tiles, BLOCK)
    ids = tile_cell_block.reshape(1, tiles)
    field_bytes = 4 * planes * height * width

    mine = call(
        deposit_kernel, shaped(tiles + SUB, 2 * BLOCK), [SMEM] + [VMEM] * 4,
        (count, cell, vol, drag, ids), flops=2 * 32 * 48 * 65536, size=5 * 4 * slots,
    )
    second = along_grp(mine, 1, holders)
    third = along_grp(mine, 2, holders)
    ids_b = second[tiles, :BLOCK].astype(jnp.int32)
    ids_c = third[tiles, :BLOCK].astype(jnp.int32)

    def edge(x):
        return lax.dynamic_slice(pressure_old, (x, first, 0), (1, height, width))[0]

    before = along_reg(edge(planes - 1), 1, owners)
    after = along_reg(edge(0), -1, owners)

    rows = halo_list.shape[1] // BLOCK
    state, down, up = call(
        halo_kernel, (shaped(3 * tiles, BLOCK), shaped(3 * rows, BLOCK), shaped(3 * rows, BLOCK)),
        [VMEM] * 3, (grain_pos, grain_vel, halo_list),
        [pltpu.VMEM((2 * rows, BLOCK), jnp.int32)], flops=8 * 3 * 16384 * 128, size=4 * 4 * 3 * slots,
    )
    lower = along_reg(up, 1, holders)
    upper = along_reg(down, -1, holders)

    field = shaped(planes, height, width)
    plane = shaped(height, width)
    constant, factor, pressure, low, high, weight = call(
        first_kernel, (field, field, field, plane, plane, shaped(tiles, BLOCK)),
        [SMEM] + [VMEM] * 8,
        (start, mine, second, third, pressure_old, pressure_source, solid_old, before, after),
        flops=planes * height * 4 * 384 * 256 * 6, size=9 * field_bytes,
    )
    for _ in range(3):
        before = along_reg(high, 1, owners)
        after = along_reg(low, -1, owners)
        pressure, low, high = call(
            sweep_kernel, (field, plane, plane), [VMEM] * 5,
            (pressure, before, after, constant, factor),
            flops=8 * field_bytes // 4, size=5 * field_bytes,
        )
    before = along_reg(high, 1, owners)
    after = along_reg(low, -1, owners)

    contact = call(
        contact_kernel, shaped(3 * tiles, BLOCK), [SMEM] + [VMEM] * 5,
        (partner_block, state, lower, upper, contact_rows, contact_stiff),
        [pltpu.VMEM((3 * (tiles + 2 * rows), BLOCK), F32)],
        flops=60 * 8 * slots, size=4 * 20 * slots,
    )
    pair = shaped(tiles, 2 * BLOCK)
    cross_a, cross_b, cross_c = call(
        functools.partial(cross_kernel, full, own_rows), (pair, pair, pair), [SMEM] * 4 + [VMEM],
        (place, tile_cell_block, ids_b, ids_c, pressure),
        [pltpu.VMEM((planes * height * width // BLOCK, 2 * BLOCK), F32)],
        flops=4 * field_bytes, size=3 * field_bytes,
    )
    cross_b = along_grp(cross_b, -1, owners)
    cross_c = along_grp(cross_c, -2, owners)
    single = shaped(tiles, BLOCK)
    along_a, along_b, along_c = call(
        functools.partial(along_kernel, full, own_rows), (single,) * 3, [SMEM] * 4 + [VMEM] * 3,
        (place, tile_cell_block, ids_b, ids_c, pressure, before, after),
        [pltpu.VMEM((planes * height * width // BLOCK, BLOCK), F32)],
        flops=field_bytes, size=2 * field_bytes,
    )
    along_b = along_grp(along_b, -1, owners)
    along_c = along_grp(along_c, -2, owners)
    return call(
        final_kernel, shaped(3, slots), [SMEM] + [VMEM] * 12,
        (
            count, along_a, along_b, along_c, cross_a, cross_b, cross_c, weight, contact, grain_vel,
            vol, drag, cell,
        ),
        flops=60 * slots, size=4 * 20 * slots,
    )


def solution(mesh):
    in_specs = (
        P(None, ("grp", "reg")),
        P(None, ("grp", "reg")),
        P(("grp", "reg")),
        P(("grp", "reg")),
        P(("grp", "reg")),
        P(None, ("grp", "reg")),
        P(None, ("grp", "reg")),
        P(("grp", "reg")),
        P(None, ("grp", "reg")),
        P(("grp", "reg")),
        P(("grp", "reg")),
        P("reg", None, None),
        P("reg", None, None),
        P("reg", None, None),
    )
    out_specs = P(None, ("grp", "reg"))
    return jax.shard_map(
        on_device, mesh=mesh, in_specs=in_specs, out_specs=out_specs, check_vma=False
    )
```

```python
import functools

import jax
import jax.numpy as jnp
from jax import lax
from jax.experimental import pallas as pl
from jax.experimental.pallas import tpu as pltpu
from jax.sharding import PartitionSpec as P

BLOCK = 128
SUB = 8
CORES = 2
ITERS = 4
SPRING = 1.0
DAMPING = 0.5
TIME_STEP = 0.5

VMEM = pl.BlockSpec(memory_space=pltpu.VMEM)
SMEM = pl.BlockSpec(memory_space=pltpu.SMEM)
F32 = jnp.float32
BF16 = jnp.bfloat16


def iota(shape, dim):
    return lax.broadcasted_iota(jnp.int32, shape, dim)


def shaped(*dims):
    return jax.ShapeDtypeStruct(dims, F32)


def call(kernel, outs, specs, args, scratch=(), flops=0, size=0):
    return pl.pallas_call(
        kernel,
        out_shape=outs,
        in_specs=specs,
        out_specs=jax.tree.map(lambda _: VMEM, outs),
        scratch_shapes=list(scratch),
        compiler_params=pltpu.CompilerParams(vmem_limit_bytes=40 * 1024 * 1024),
        cost_estimate=pl.CostEstimate(flops=flops, bytes_accessed=size, transcendentals=0),
    )(*args)


def lanes_of(source, index):
    return jnp.take_along_axis(source, index, axis=1, mode="promise_in_bounds")


def thirds(value):
    high = value.astype(BF16)
    rest = value - high.astype(F32)
    middle = rest.astype(BF16)
    low = (rest - middle.astype(F32)).astype(BF16)
    return high, middle, low


def deposit_kernel(count, cell, vol, drag, ids, out):
    tiles = cell.shape[0]
    sub = iota((SUB, BLOCK), 0)
    rows_c = iota((BLOCK, BLOCK), 0)
    even = sub % 2 == 0
    low_pair = sub % 4 < 2

    def step(group, carry):
        first = pl.multiple_of(group * SUB, SUB)
        slot = (first + sub) * BLOCK + iota((SUB, BLOCK), 1)
        live = slot < count[0]
        cells = cell[pl.ds(first, SUB), :]
        parts = thirds(jnp.where(live, vol[pl.ds(first, SUB), :], 0.0)) + thirds(
            jnp.where(live, drag[pl.ds(first, SUB), :], 0.0)
        )
        parts = [part.astype(F32) for part in parts]
        left = jnp.concatenate([jnp.where(even, part, 0.0) for part in parts], 0)
        right = jnp.concatenate([jnp.where(even, 0.0, part) for part in parts], 0)
        loads = jnp.concatenate([left, right], 1).astype(BF16)
        sums = [jnp.zeros((SUB, BLOCK), F32), jnp.zeros((SUB, BLOCK), F32)]
        for quad in range(SUB // 4):
            hot = [
                jnp.where(
                    rows_c == jnp.broadcast_to(cells[t : t + 1, :], (BLOCK, BLOCK)), 1.0, 0.0
                ).astype(BF16)
                for t in range(4 * quad, 4 * quad + 4)
            ]
            picked = jnp.concatenate(
                [jnp.concatenate(hot[:2], 1), jnp.concatenate(hot[2:], 1)], 0
            )
            placed = lax.dot_general(
                loads, picked, (((1,), (1,)), ((), ())), preferred_element_type=F32
            )
            for field in range(2):
                base = field * 3 * SUB
                total = placed[base : base + SUB] + placed[base + SUB : base + 2 * SUB]
                total = total + placed[base + 2 * SUB : base + 3 * SUB]
                chosen = jnp.where(low_pair, total[:, :BLOCK], total[:, BLOCK:])
                sums[field] = jnp.where(sub // 4 == quad, chosen, sums[field])
        out[pl.ds(first, SUB), :BLOCK] = sums[0]
        out[pl.ds(first, SUB), BLOCK:] = sums[1]
        return carry

    lax.fori_loop(0, tiles // SUB, step, 0, unroll=2)
    out[tiles : tiles + SUB, :BLOCK] = jnp.broadcast_to(ids[...].astype(F32), (SUB, BLOCK))
    out[tiles : tiles + SUB, BLOCK:] = jnp.zeros((SUB, BLOCK), F32)


def halo_kernel(pos, vel, lists, state, down, up, index):
    tiles = pos.shape[1] // BLOCK
    rows = lists.shape[1] // BLOCK
    for tile in range(tiles):
        lanes = slice(tile * BLOCK, (tile + 1) * BLOCK)
        mixed = SPRING * pos[:, lanes] - DAMPING * vel[:, lanes]
        for axis in range(3):
            state[axis * tiles + tile : axis * tiles + tile + 1, :] = mixed[axis : axis + 1]
    for side in range(2):
        for row in range(rows):
            index[side * rows + row : side * rows + row + 1, :] = lists[
                side : side + 1, row * BLOCK : (row + 1) * BLOCK
            ]
    groups = 2 * rows // SUB
    named = [index[g * SUB : (g + 1) * SUB, :] for g in range(groups)]
    block = [lax.shift_right_logical(value, 7) for value in named]
    lane = [value & (BLOCK - 1) for value in named]

    def step(source, sums):
        new = []
        spread = [
            jnp.broadcast_to(state[pl.ds(axis * tiles + source, 1), :], (SUB, BLOCK))
            for axis in range(3)
        ]
        for g in range(groups):
            here = block[g] == source
            for axis in range(3):
                new.append(
                    jnp.where(here, lanes_of(spread[axis], lane[g]), sums[3 * g + axis])
                )
        return tuple(new)

    zero = jnp.zeros((SUB, BLOCK), F32)
    sums = lax.fori_loop(0, tiles, step, (zero,) * (3 * groups), unroll=2)
    for side, out in enumerate((down, up)):
        for axis in range(3):
            for g in range(groups // 2):
                first = axis * rows + g * SUB
                out[first : first + SUB, :] = sums[3 * (side * groups // 2 + g) + axis]


def contact_kernel(partner, state, lower, upper, named, stiff, out, extended):
    tiles = state.shape[0] // 3
    rows = lower.shape[0] // 3
    blocks = tiles + 2 * rows
    for axis in range(3):
        extended[axis * blocks : axis * blocks + tiles, :] = state[
            axis * tiles : (axis + 1) * tiles, :
        ]
        for place, side in enumerate((lower, upper)):
            first = axis * blocks + tiles + place * rows
            extended[first : first + rows, :] = side[axis * rows : (axis + 1) * rows, :]

    def step(tile, carry):
        lanes = pl.ds(pl.multiple_of(tile * BLOCK, BLOCK), BLOCK)
        entry = named[:, lanes]
        weight = jnp.where(entry >= 0, stiff[:, lanes], 0.0)
        own = entry < BLOCK
        lane = entry & (BLOCK - 1)
        other = partner[tile]
        for axis in range(3):
            mine = jnp.broadcast_to(extended[pl.ds(axis * blocks + tile, 1), :], entry.shape)
            theirs = jnp.broadcast_to(extended[pl.ds(axis * blocks + other, 1), :], entry.shape)
            met = jnp.where(own, lanes_of(mine, lane), lanes_of(theirs, lane))
            pull = jnp.sum(weight * (mine - met), axis=0, keepdims=True)
            out[pl.ds(axis * tiles + tile, 1), :] = pull
        return carry

    lax.fori_loop(0, tiles, step, 0, unroll=4)


def shifted(plane):
    height, width = plane.shape
    row = iota(plane.shape, 0)
    column = iota(plane.shape, 1)
    above = jnp.where(row == 0, 0.0, pltpu.roll(plane, 1, 0))
    below = jnp.where(row == height - 1, 0.0, pltpu.roll(plane, height - 1, 0))
    left = jnp.where(column == 0, 0.0, pltpu.roll(plane, 1, 1))
    right = jnp.where(column == width - 1, 0.0, pltpu.roll(plane, width - 1, 1))
    return above, below, left, right


def placed(groups, tiles):
    parts = [thirds(group[:tiles, :]) for group in groups]
    loads = [jnp.concatenate([part[i] for part in parts], 0) for i in range(3)]
    ids = jnp.concatenate([group[tiles : tiles + 1, :BLOCK] for group in groups], 1)
    ids = ids.astype(jnp.int32)

    def gathered(wanted):
        hot = jnp.where(wanted == jnp.broadcast_to(ids, wanted.shape), 1.0, 0.0).astype(BF16)
        total = jnp.dot(hot, loads[2], preferred_element_type=F32)
        total = total + jnp.dot(hot, loads[1], preferred_element_type=F32)
        total = total + jnp.dot(hot, loads[0], preferred_element_type=F32)
        return total[:, :BLOCK], total[:, BLOCK:]

    return ids, gathered


def coefficients(gathered, tiles, first, full, driven, constant, factor, base, present):
    planes, height, width = driven.shape
    zones = width // BLOCK
    shape = (zones * height, 3 * tiles)
    line = iota(shape, 0)
    block = (line % height) * zones + line // height + first * zones

    def plane(x, carry):
        solid, drag = gathered(block + x * (full * zones))
        porous = 1.0 / (1.0 + solid)
        inverse = 1.0 / (6.0 * porous + drag + 1.0)
        if present is not None:
            inverse = jnp.where(present, inverse, 0.0)
        scale = porous * inverse
        for zone in range(zones):
            lanes = slice(zone * BLOCK, (zone + 1) * BLOCK)
            rows = slice(zone * height, (zone + 1) * height)
            driving = driven[x, :, lanes] + solid[rows]
            constant[base + x, :, lanes] = driving * inverse[rows]
            factor[base + x, :, lanes] = scale[rows]
        return carry

    lax.fori_loop(0, planes, plane, 0)


def own_kernel(full, place, mine, second, third, driven, constant, factor, weight, joined):
    stride = mine.shape[0]
    tiles = stride - SUB
    groups = (mine, second, third)
    for index, group in enumerate(groups):
        joined[index * stride : (index + 1) * stride, :] = group[...]
    ids, gathered = placed(groups, tiles)
    coefficients(gathered, tiles, place[0], full, driven, constant, factor, 0, None)
    own = jnp.transpose(jnp.broadcast_to(ids[:, :tiles], (tiles, tiles)).astype(F32))
    solid, drag = gathered(jnp.concatenate([own.astype(jnp.int32)] * 3, 1))
    weight[...] = 1.0 / (1.0 / (1.0 + solid) + drag)


def solve_kernel(
    full, sweeps, place, rows_at, joined_lower, joined_upper, driven_near, driven_far, pressure,
    near, far, beyond, own_constant, own_factor, out_a, out_b, out_c,
    driven, constant, factor, old, new, fields,
):
    planes, height, width = pressure.shape
    zones = width // BLOCK
    stride = joined_lower.shape[0] // 3
    tiles = stride - SUB
    odd, lower, upper = place[1] == 1, place[2] == 1, place[3] == 1
    rim = sweeps + 1

    @pl.when(odd)
    def _():
        driven[:planes] = driven_near[...]
        driven[planes:] = driven_far[...]
        old[0] = beyond[...]
        old[1 : 1 + planes] = near[...]
        old[rim + planes : rim + 2 * planes + 1] = far[...]

    @pl.when(jnp.logical_not(odd))
    def _():
        driven[:planes] = driven_far[...]
        driven[planes:] = driven_near[...]
        old[: 1 + planes] = far[...]
        old[rim + planes : rim + 2 * planes] = near[...]
        old[rim + 2 * planes] = beyond[...]

    old[rim : rim + planes] = pressure[...]
    constant[planes : 2 * planes] = own_constant[...]
    factor[planes : 2 * planes] = own_factor[...]
    for index, (joined, present) in enumerate(((joined_lower, lower), (joined_upper, upper))):
        groups = [joined.at[i * stride : (i + 1) * stride] for i in range(3)]
        _, gathered = placed(groups, tiles)
        coefficients(
            gathered, tiles, place[0], full, driven.at[index * planes : (index + 1) * planes],
            constant, factor, 2 * index * planes, present,
        )

    def sweep(source, target, depth):
        def plane(x, carry):
            centre = source[x]
            above, below, left, right = shifted(centre)
            around = source[x - 1] + source[x + 1] + above + below + left + right
            target[x] = constant[x - 1] + factor[x - 1] * around
            return carry

        lax.fori_loop(depth, 3 * planes + 2 - depth, plane, 0)

    for index in range(sweeps):
        source, target = (old, new) if index % 2 == 0 else (new, old)
        sweep(source, target, index + 1)
    last = old if sweeps % 2 == 0 else new

    def gradient(x, carry):
        centre = last[rim + x]
        above, below, left, right = shifted(centre)
        grads = (last[rim + x + 1] - last[rim + x - 1], below - above, right - left)
        for zone in range(zones):
            first = pl.multiple_of((x * zones + zone) * height, SUB)
            for axis, grad in enumerate(grads):
                fields[pl.ds(first, height), axis * BLOCK : (axis + 1) * BLOCK] = (
                    0.5 * grad[:, zone * BLOCK : (zone + 1) * BLOCK]
                )
        return carry

    lax.fori_loop(0, planes, gradient, 0)
    none = planes * zones * height
    fields[none : none + SUB, :] = jnp.zeros((SUB, 3 * BLOCK), F32)

    def pick(tile, carry):
        for index, out in enumerate((out_a, out_b, out_c)):
            out[pl.ds(tile, 1), :] = fields[pl.ds(rows_at[index * tiles + tile], 1), :]
        return carry

    lax.fori_loop(0, tiles, pick, 0, unroll=8)


def final_kernel(
    count, grads_a, grads_b, grads_c, weight, contact, vel, vol, drag, cell, out,
):
    tiles = cell.shape[0]
    cells = cell[...]
    heft = lanes_of(weight[...], cells)
    slot = iota(cells.shape, 0) * BLOCK + iota(cells.shape, 1)
    live = slot < count[0]
    volume = vol[...]
    push = TIME_STEP / volume
    for axis in range(3):
        lanes = slice(axis * BLOCK, (axis + 1) * BLOCK)
        gradient = lanes_of(grads_a[:, lanes] + grads_b[:, lanes] + grads_c[:, lanes], cells)
        own = jnp.concatenate(
            [vel[axis : axis + 1, t * BLOCK : (t + 1) * BLOCK] for t in range(tiles)], 0
        )
        fluid = -gradient * heft
        force = contact[axis * tiles : (axis + 1) * tiles, :] - volume * gradient
        force = force + drag[...] * (fluid - own)
        new = jnp.where(live, own + force * push, 0.0)
        for t in range(tiles):
            out[axis : axis + 1, t * BLOCK : (t + 1) * BLOCK] = new[t : t + 1, :]


def on_device(
    grain_pos,
    grain_vel,
    grain_vol,
    drag_coef,
    grain_count,
    contact_rows,
    contact_stiff,
    partner_block,
    halo_list,
    grain_cell,
    tile_cell_block,
    pressure_old,
    pressure_source,
    solid_old,
):
    groups, regions = lax.axis_size("grp"), lax.axis_size("reg")
    holding = groups - 1
    halves = groups // CORES
    slots = grain_pos.shape[1]
    tiles = slots // BLOCK
    planes, full, width = pressure_old.shape
    zones = width // BLOCK
    own_rows = full // halves
    height = min(full, own_rows + SUB * min(2, halves - 1))
    group, region = lax.axis_index("grp"), lax.axis_index("reg")
    half = group // CORES
    first = jnp.clip(half * own_rows - SUB, 0, full - height)
    odd = region % 2 == 1
    place = jnp.stack([first, odd, region > 0, region < regions - 1]).astype(jnp.int32)
    owners = range(0, groups, CORES)
    holders = range(holding)

    def send(value, pairs):
        flat = [(a[0] * regions + a[1], b[0] * regions + b[1]) for a, b in pairs]
        return lax.ppermute(value, ("grp", "reg"), flat)

    def along_reg(value, members, goes):
        pairs = [
            ((g, r), (g, r + goes[r % 2]))
            for g in members
            for r in range(regions)
            if 0 <= r + goes[r % 2] < regions
        ]
        return send(value, pairs)

    def along_grp(value, step, members):
        pairs = [((g, r), ((g + step) % holding, r)) for g in members for r in range(regions)]
        return send(value, pairs)

    count = grain_count
    cell = grain_cell.reshape(tiles, BLOCK)
    vol = grain_vol.reshape(tiles, BLOCK)
    drag = drag_coef.reshape(tiles, BLOCK)
    ids = tile_cell_block.reshape(1, tiles)
    field_bytes = 4 * planes * height * width

    mine = call(
        deposit_kernel, shaped(tiles + SUB, 2 * BLOCK), [SMEM] + [VMEM] * 4,
        (count, cell, vol, drag, ids), flops=2 * 32 * 48 * 65536, size=5 * 4 * slots,
    )
    second = along_grp(mine, 1, holders)
    third = along_grp(mine, 2, holders)

    def window(whole):
        return lax.dynamic_slice(whole, (0, first, 0), (planes, height, width))

    driven = window(pressure_source) - window(solid_old)
    pressure = window(pressure_old)
    driven_near = along_reg(driven, owners, (1, -1))
    near = along_reg(pressure, owners, (1, -1))
    ends = jnp.where(odd, pressure[planes - 1], pressure[0])
    beyond = along_reg(ends, owners, (-2, 2))
    driven_far = along_reg(driven_near, owners, (2, -2))
    inner = jnp.where(odd, pressure[:1], pressure[planes - 1 :])
    far = along_reg(
        jnp.where(
            odd, jnp.concatenate([near, inner], 0), jnp.concatenate([inner, near], 0)
        ),
        owners, (2, -2),
    )

    field = shaped(planes, height, width)
    constant, factor, weight, joined = call(
        functools.partial(own_kernel, full),
        (field, field, shaped(tiles, BLOCK), shaped(3 * (tiles + SUB), 2 * BLOCK)),
        [SMEM] + [VMEM] * 4, (place, mine, second, third, driven),
        flops=planes * height * 4 * 384 * 256 * 6, size=9 * field_bytes,
    )
    joined_lower = along_reg(joined, owners, (1, 1))
    joined_upper = along_reg(joined, owners, (-1, -1))

    rows = halo_list.shape[1] // BLOCK
    state, down, up = call(
        halo_kernel, (shaped(3 * tiles, BLOCK), shaped(3 * rows, BLOCK), shaped(3 * rows, BLOCK)),
        [VMEM] * 3, (grain_pos, grain_vel, halo_list),
        [pltpu.VMEM((2 * rows, BLOCK), jnp.int32)], flops=8 * 3 * 16384 * 128, size=4 * 4 * 3 * slots,
    )
    lower = along_reg(up, holders, (1, 1))
    upper = along_reg(down, holders, (-1, -1))

    blocks = jnp.concatenate(
        [tile_cell_block, second[tiles, :BLOCK].astype(jnp.int32), third[tiles, :BLOCK].astype(jnp.int32)]
    )
    line, zone = blocks // zones, blocks % zones
    x, y = line // full, line % full
    held = (y // own_rows == half) & (group % CORES == 0)
    rows_at = jnp.where(held, (x * zones + zone) * height + y - first, planes * zones * height)

    grads = shaped(tiles, 3 * BLOCK)
    window_of = lambda count: pltpu.VMEM((count, height, width), F32)
    grads_a, grads_b, grads_c = call(
        functools.partial(solve_kernel, full, ITERS), (grads,) * 3, [SMEM] * 2 + [VMEM] * 10,
        (
            place, rows_at, joined_lower, joined_upper, driven_near, driven_far, pressure, near, far,
            beyond, constant, factor,
        ),
        [
            window_of(2 * planes), window_of(3 * planes), window_of(3 * planes),
            window_of(3 * planes + 2), window_of(3 * planes + 2),
            pltpu.VMEM((planes * zones * height + SUB, 3 * BLOCK), F32),
        ],
        flops=2 * planes * height * 4 * 384 * 256 * 6, size=20 * field_bytes,
    )
    grads_b = along_grp(grads_b, -1, owners)
    grads_c = along_grp(grads_c, -2, owners)

    contact = call(
        contact_kernel, shaped(3 * tiles, BLOCK), [SMEM] + [VMEM] * 5,
        (partner_block, state, lower, upper, contact_rows, contact_stiff),
        [pltpu.VMEM((3 * (tiles + 2 * rows), BLOCK), F32)],
        flops=60 * 8 * slots, size=4 * 20 * slots,
    )
    return call(
        final_kernel, shaped(3, slots), [SMEM] + [VMEM] * 9,
        (count, grads_a, grads_b, grads_c, weight, contact, grain_vel, vol, drag, cell),
        flops=60 * slots, size=4 * 20 * slots,
    )


def solution(mesh):
    in_specs = (
        P(None, ("grp", "reg")),
        P(None, ("grp", "reg")),
        P(("grp", "reg")),
        P(("grp", "reg")),
        P(("grp", "reg")),
        P(None, ("grp", "reg")),
        P(None, ("grp", "reg")),
        P(("grp", "reg")),
        P(None, ("grp", "reg")),
        P(("grp", "reg")),
        P(("grp", "reg")),
        P("reg", None, None),
        P("reg", None, None),
        P("reg", None, None),
    )
    out_specs = P(None, ("grp", "reg"))
    return jax.shard_map(
        on_device, mesh=mesh, in_specs=in_specs, out_specs=out_specs, check_vma=False
    )
```

```python
import functools

import jax
import jax.numpy as jnp
from jax import lax
from jax.experimental import pallas as pl
from jax.experimental.pallas import tpu as pltpu
from jax.sharding import PartitionSpec as P

BLOCK = 128
SUB = 8
CORES = 2
ITERS = 4
SPRING = 1.0
DAMPING = 0.5
TIME_STEP = 0.5

VMEM = pl.BlockSpec(memory_space=pltpu.VMEM)
SMEM = pl.BlockSpec(memory_space=pltpu.SMEM)
ANY = pl.BlockSpec(memory_space=pl.ANY)
F32 = jnp.float32
BF16 = jnp.bfloat16


def iota(shape, dim):
    return lax.broadcasted_iota(jnp.int32, shape, dim)


def shaped(*dims):
    return jax.ShapeDtypeStruct(dims, F32)


def call(kernel, outs, specs, args, scratch=(), flops=0, size=0):
    return pl.pallas_call(
        kernel,
        out_shape=outs,
        in_specs=specs,
        out_specs=jax.tree.map(lambda _: VMEM, outs),
        scratch_shapes=list(scratch),
        compiler_params=pltpu.CompilerParams(vmem_limit_bytes=40 * 1024 * 1024),
        cost_estimate=pl.CostEstimate(flops=flops, bytes_accessed=size, transcendentals=0),
    )(*args)


def lanes_of(source, index):
    return jnp.take_along_axis(source, index, axis=1, mode="promise_in_bounds")


def halves_of(value):
    high = value.astype(BF16)
    return high, (value - high.astype(F32)).astype(BF16)


def entry_kernel(
    count, place, cell, vol, drag, ids, pressure_old, source, solid_before,
    out, pressure, driven, ends, solid, sems,
):
    tiles = cell.shape[0]
    planes, height, _ = pressure.shape
    rows = pl.ds(pl.multiple_of(place[0], SUB), height)
    copies = [
        pltpu.make_async_copy(whole.at[:, rows, :], part, sems.at[index])
        for index, (whole, part) in enumerate(
            ((pressure_old, pressure), (source, driven), (solid_before, solid))
        )
    ]
    for copy in copies:
        copy.start()
    sub = iota((SUB, BLOCK), 0)
    rows_c = iota((BLOCK, BLOCK), 0)
    even = sub % 2 == 0
    low_pair = sub % 4 < 2

    def step(group, carry):
        first = pl.multiple_of(group * SUB, SUB)
        slot = (first + sub) * BLOCK + iota((SUB, BLOCK), 1)
        live = slot < count[0]
        cells = cell[pl.ds(first, SUB), :]
        parts = halves_of(jnp.where(live, vol[pl.ds(first, SUB), :], 0.0)) + halves_of(
            jnp.where(live, drag[pl.ds(first, SUB), :], 0.0)
        )
        parts = [part.astype(F32) for part in parts]
        left = jnp.concatenate([jnp.where(even, part, 0.0) for part in parts], 0)
        right = jnp.concatenate([jnp.where(even, 0.0, part) for part in parts], 0)
        loads = jnp.concatenate([left, right], 1).astype(BF16)
        sums = [jnp.zeros((SUB, BLOCK), F32), jnp.zeros((SUB, BLOCK), F32)]
        for quad in range(SUB // 4):
            hot = [
                jnp.where(
                    rows_c == jnp.broadcast_to(cells[t : t + 1, :], (BLOCK, BLOCK)), 1.0, 0.0
                ).astype(BF16)
                for t in range(4 * quad, 4 * quad + 4)
            ]
            picked = jnp.concatenate(
                [jnp.concatenate(hot[:2], 1), jnp.concatenate(hot[2:], 1)], 0
            )
            placed = lax.dot_general(
                loads, picked, (((1,), (1,)), ((), ())), preferred_element_type=F32
            )
            for field in range(2):
                base = field * 2 * SUB
                total = placed[base : base + SUB] + placed[base + SUB : base + 2 * SUB]
                chosen = jnp.where(low_pair, total[:, :BLOCK], total[:, BLOCK:])
                sums[field] = jnp.where(sub // 4 == quad, chosen, sums[field])
        out[pl.ds(first, SUB), :BLOCK] = sums[0]
        out[pl.ds(first, SUB), BLOCK:] = sums[1]
        return carry

    lax.fori_loop(0, tiles // SUB, step, 0, unroll=2)
    out[tiles : tiles + SUB, :BLOCK] = jnp.broadcast_to(ids[...].astype(F32), (SUB, BLOCK))
    out[tiles : tiles + SUB, BLOCK:] = jnp.zeros((SUB, BLOCK), F32)
    for copy in copies:
        copy.wait()
    driven[...] = driven[...] - solid[...]

    @pl.when(place[1] == 1)
    def _():
        ends[...] = pressure[planes - 1]

    @pl.when(place[1] != 1)
    def _():
        ends[...] = pressure[0]


def halo_kernel(pos, vel, lists, state, down, up):
    tiles = pos.shape[1] // BLOCK
    rows = lists.shape[1] // BLOCK
    for tile in range(tiles):
        lanes = slice(tile * BLOCK, (tile + 1) * BLOCK)
        mixed = SPRING * pos[:, lanes] - DAMPING * vel[:, lanes]
        for axis in range(3):
            state[axis * tiles + tile : axis * tiles + tile + 1, :] = mixed[axis : axis + 1]
    turned = [
        jnp.concatenate(halves_of(jnp.transpose(state[axis * tiles : (axis + 1) * tiles, :])), 1)
        for axis in range(3)
    ]
    turned = jnp.concatenate(turned, 0)
    span = 2 * BLOCK
    row = iota((BLOCK, span), 0)

    for side, out in enumerate((down, up)):

        def step(part, carry):
            named = lists[side : side + 1, pl.ds(pl.multiple_of(part * span, span), span)]
            block = lax.shift_right_logical(named, 7)
            lane = named & (BLOCK - 1)
            hot = jnp.where(row == jnp.broadcast_to(block, row.shape), 1.0, 0.0).astype(BF16)
            found = jnp.dot(
                turned, jnp.concatenate([hot, hot], 0), preferred_element_type=F32
            )
            here = row == jnp.broadcast_to(lane, row.shape)
            for axis in range(3):
                value = jnp.where(here, found[axis * BLOCK : (axis + 1) * BLOCK], 0.0)
                value = jnp.sum(value, axis=0, keepdims=True)
                for half in range(2):
                    out[pl.ds(axis * rows + 2 * part + half, 1), :] = value[
                        :, half * BLOCK : (half + 1) * BLOCK
                    ]
            return carry

        lax.fori_loop(0, rows // 2, step, 0, unroll=2)


def contact_kernel(partner, state, lower, upper, named, stiff, out, extended):
    tiles = state.shape[0] // 3
    rows = lower.shape[0] // 3
    blocks = tiles + 2 * rows
    for axis in range(3):
        extended[axis * blocks : axis * blocks + tiles, :] = state[
            axis * tiles : (axis + 1) * tiles, :
        ]
        for place, side in enumerate((lower, upper)):
            first = axis * blocks + tiles + place * rows
            extended[first : first + rows, :] = side[axis * rows : (axis + 1) * rows, :]

    def step(tile, carry):
        lanes = pl.ds(pl.multiple_of(tile * BLOCK, BLOCK), BLOCK)
        entry = named[:, lanes]
        weight = jnp.where(entry >= 0, stiff[:, lanes], 0.0)
        own = entry < BLOCK
        lane = entry & (BLOCK - 1)
        other = partner[tile]
        for axis in range(3):
            mine = jnp.broadcast_to(extended[pl.ds(axis * blocks + tile, 1), :], entry.shape)
            theirs = jnp.broadcast_to(extended[pl.ds(axis * blocks + other, 1), :], entry.shape)
            met = jnp.where(own, lanes_of(mine, lane), lanes_of(theirs, lane))
            pull = jnp.sum(weight * (mine - met), axis=0, keepdims=True)
            out[pl.ds(axis * tiles + tile, 1), :] = pull
        return carry

    lax.fori_loop(0, tiles, step, 0, unroll=4)


def shifted(plane):
    height, width = plane.shape
    row = iota(plane.shape, 0)
    column = iota(plane.shape, 1)
    above = jnp.where(row == 0, 0.0, pltpu.roll(plane, 1, 0))
    below = jnp.where(row == height - 1, 0.0, pltpu.roll(plane, height - 1, 0))
    left = jnp.where(column == 0, 0.0, pltpu.roll(plane, 1, 1))
    right = jnp.where(column == width - 1, 0.0, pltpu.roll(plane, width - 1, 1))
    return above, below, left, right


def placed(groups, tiles):
    parts = [halves_of(group[:tiles, :]) for group in groups]
    loads = jnp.concatenate([part[i] for i in range(2) for part in parts], 0)
    ids = jnp.concatenate([group[tiles : tiles + 1, :BLOCK] for group in groups], 1)
    ids = ids.astype(jnp.int32)

    def gathered(wanted):
        hot = jnp.where(wanted == jnp.broadcast_to(ids, wanted.shape), 1.0, 0.0).astype(BF16)
        total = jnp.dot(
            jnp.concatenate([hot, hot], 1), loads, preferred_element_type=F32
        )
        return total[:, :BLOCK], total[:, BLOCK:]

    return ids, gathered


def coefficients(gathered, tiles, first, full, driven, constant, factor, base, present):
    planes, height, width = driven.shape
    zones = width // BLOCK
    shape = (zones * height, 3 * tiles)
    line = iota(shape, 0)
    block = (line % height) * zones + line // height + first * zones

    def plane(x, carry):
        solid, drag = gathered(block + x * (full * zones))
        porous = 1.0 / (1.0 + solid)
        inverse = 1.0 / (6.0 * porous + drag + 1.0)
        if present is not None:
            inverse = jnp.where(present, inverse, 0.0)
        scale = porous * inverse
        for zone in range(zones):
            lanes = slice(zone * BLOCK, (zone + 1) * BLOCK)
            rows = slice(zone * height, (zone + 1) * height)
            driving = driven[x, :, lanes] + solid[rows]
            constant[base + x, :, lanes] = driving * inverse[rows]
            factor[base + x, :, lanes] = scale[rows]
        return carry

    lax.fori_loop(0, planes, plane, 0)


def own_kernel(full, own_rows, place, mine, second, third, driven, constant, factor, weight, rows_at):
    stride = mine.shape[0]
    tiles = stride - SUB
    planes, height, width = driven.shape
    zones = width // BLOCK
    ids, gathered = placed((mine, second, third), tiles)
    coefficients(gathered, tiles, place[0], full, driven, constant, factor, 0, None)
    turned = [
        jnp.transpose(
            jnp.broadcast_to(ids[:, i * tiles : (i + 1) * tiles], (BLOCK, tiles)).astype(F32)
        ).astype(jnp.int32)
        for i in range(3)
    ]
    solid, drag = gathered(jnp.concatenate([turned[0]] * 3, 1))
    weight[...] = 1.0 / (1.0 / (1.0 + solid) + drag)
    for i, block in enumerate(turned):
        line, zone = block // zones, block % zones
        x, y = line // full, line % full
        row = (x * zones + zone) * height + y - place[0]
        rows_at[i * tiles : (i + 1) * tiles, :] = jnp.where(y // own_rows == place[4], row, -1)


def solve_kernel(
    full, sweeps, place, rows_at, joined_lower, joined_upper, driven_near, driven_far, pressure,
    near, far, beyond, own_constant, own_factor, out_a, out_b, out_c,
    driven, constant, factor, old, new, fields, sems,
):
    planes, height, width = pressure.shape
    zones = width // BLOCK
    stride = joined_lower.shape[0] // 3
    tiles = stride - SUB
    odd, lower, upper = place[1] == 1, place[2] == 1, place[3] == 1
    rim = sweeps + 1

    def copies(moves, base):
        return [
            pltpu.make_async_copy(source, target, sems.at[base + index])
            for index, (source, target) in enumerate(moves)
        ]

    always = copies(
        (
            (pressure, old.at[rim : rim + planes]),
            (own_constant, constant.at[planes : 2 * planes]),
            (own_factor, factor.at[planes : 2 * planes]),
        ),
        0,
    )
    of_odd = (
        (driven_near, driven.at[:planes]),
        (driven_far, driven.at[planes:]),
        (beyond, old.at[0]),
        (near, old.at[1 : 1 + planes]),
        (far, old.at[rim + planes : rim + 2 * planes + 1]),
    )
    of_even = (
        (driven_far, driven.at[:planes]),
        (driven_near, driven.at[planes:]),
        (beyond, old.at[rim + 2 * planes]),
        (near, old.at[rim + planes : rim + 2 * planes]),
        (far, old.at[: 1 + planes]),
    )

    def each(act, chosen):
        @pl.when(odd)
        def _():
            for copy in copies(of_odd[chosen], len(always) + (chosen.start or 0)):
                act(copy)

        @pl.when(jnp.logical_not(odd))
        def _():
            for copy in copies(of_even[chosen], len(always) + (chosen.start or 0)):
                act(copy)

    each(lambda copy: copy.start(), slice(None))
    for copy in always:
        copy.start()
    each(lambda copy: copy.wait(), slice(0, 2))
    for index, (joined, present) in enumerate(((joined_lower, lower), (joined_upper, upper))):
        groups = [joined.at[i * stride : (i + 1) * stride] for i in range(3)]
        _, gathered = placed(groups, tiles)
        coefficients(
            gathered, tiles, place[0], full, driven.at[index * planes : (index + 1) * planes],
            constant, factor, 2 * index * planes, present,
        )
    each(lambda copy: copy.wait(), slice(2, 5))
    for copy in always:
        copy.wait()

    def sweep(source, target, depth):
        def plane(x, carry):
            centre = source[x]
            above, below, left, right = shifted(centre)
            around = source[x - 1] + source[x + 1] + above + below + left + right
            target[x] = constant[x - 1] + factor[x - 1] * around
            return carry

        lax.fori_loop(depth, 3 * planes + 2 - depth, plane, 0)

    for index in range(sweeps):
        source, target = (old, new) if index % 2 == 0 else (new, old)
        sweep(source, target, index + 1)
    last = old if sweeps % 2 == 0 else new

    def gradient(x, carry):
        centre = last[rim + x]
        above, below, left, right = shifted(centre)
        grads = (last[rim + x + 1] - last[rim + x - 1], below - above, right - left)
        for zone in range(zones):
            first = pl.multiple_of((x * zones + zone) * height, SUB)
            for axis, grad in enumerate(grads):
                fields[pl.ds(first, height), axis * BLOCK : (axis + 1) * BLOCK] = (
                    0.5 * grad[:, zone * BLOCK : (zone + 1) * BLOCK]
                )
        return carry

    lax.fori_loop(0, planes, gradient, 0)
    span = 3 * BLOCK
    wanted = jnp.concatenate([rows_at[...]] * 3, 1)
    column = iota(wanted.shape, 1)
    total = jnp.zeros((3 * tiles, span), F32)
    for part in range(planes * zones * height // span):
        hot = jnp.where(wanted == column + part * span, 1.0, 0.0).astype(BF16)
        for piece in halves_of(fields[part * span : (part + 1) * span, :]):
            total = total + jnp.dot(hot, piece, preferred_element_type=F32)
    for index, out in enumerate((out_a, out_b, out_c)):
        out[...] = total[index * tiles : (index + 1) * tiles]


def final_kernel(
    count, grads_a, grads_b, grads_c, weight, contact, vel, vol, drag, cell, out,
):
    tiles = cell.shape[0]
    cells = cell[...]
    heft = lanes_of(weight[...], cells)
    slot = iota(cells.shape, 0) * BLOCK + iota(cells.shape, 1)
    live = slot < count[0]
    volume = vol[...]
    push = TIME_STEP / volume
    for axis in range(3):
        lanes = slice(axis * BLOCK, (axis + 1) * BLOCK)
        gradient = lanes_of(grads_a[:, lanes] + grads_b[:, lanes] + grads_c[:, lanes], cells)
        own = jnp.concatenate(
            [vel[axis : axis + 1, t * BLOCK : (t + 1) * BLOCK] for t in range(tiles)], 0
        )
        fluid = -gradient * heft
        force = contact[axis * tiles : (axis + 1) * tiles, :] - volume * gradient
        force = force + drag[...] * (fluid - own)
        new = jnp.where(live, own + force * push, 0.0)
        for t in range(tiles):
            out[axis : axis + 1, t * BLOCK : (t + 1) * BLOCK] = new[t : t + 1, :]


def on_device(
    grain_pos,
    grain_vel,
    grain_vol,
    drag_coef,
    grain_count,
    contact_rows,
    contact_stiff,
    partner_block,
    halo_list,
    grain_cell,
    tile_cell_block,
    pressure_old,
    pressure_source,
    solid_old,
):
    groups, regions = lax.axis_size("grp"), lax.axis_size("reg")
    holding = groups - 1
    halves = groups // CORES
    slots = grain_pos.shape[1]
    tiles = slots // BLOCK
    planes, full, width = pressure_old.shape
    zones = width // BLOCK
    own_rows = full // halves
    height = min(full, own_rows + SUB * min(2, halves - 1))
    group, region = lax.axis_index("grp"), lax.axis_index("reg")
    half = group // CORES
    first = jnp.clip(half * own_rows - SUB, 0, full - height)
    odd = region % 2 == 1
    place = jnp.stack(
        [first, odd, region > 0, region < regions - 1, jnp.where(group % CORES == 0, half, -1)]
    ).astype(jnp.int32)
    owners = range(0, groups, CORES)
    holders = range(holding)

    def send(value, pairs):
        flat = [(a[0] * regions + a[1], b[0] * regions + b[1]) for a, b in pairs]
        return lax.ppermute(value, ("grp", "reg"), flat)

    def along_reg(value, members, goes):
        pairs = [
            ((g, r), (g, r + goes[r % 2]))
            for g in members
            for r in range(regions)
            if 0 <= r + goes[r % 2] < regions
        ]
        return send(value, pairs)

    def along_grp(value, step, members):
        pairs = [((g, r), ((g + step) % holding, r)) for g in members for r in range(regions)]
        return send(value, pairs)

    count = grain_count
    cell = grain_cell.reshape(tiles, BLOCK)
    vol = grain_vol.reshape(tiles, BLOCK)
    drag = drag_coef.reshape(tiles, BLOCK)
    ids = tile_cell_block.reshape(1, tiles)
    field_bytes = 4 * planes * height * width

    field = shaped(planes, height, width)
    mine, pressure, driven, ends = call(
        entry_kernel, (shaped(tiles + SUB, 2 * BLOCK), field, field, shaped(height, width)),
        [SMEM] * 2 + [VMEM] * 4 + [ANY] * 3,
        (count, place, cell, vol, drag, ids, pressure_old, pressure_source, solid_old),
        [pltpu.VMEM((planes, height, width), F32), pltpu.SemaphoreType.DMA((3,))],
        flops=2 * 32 * 48 * 65536, size=5 * 4 * slots,
    )
    second = along_grp(mine, 1, holders)
    third = along_grp(mine, 2, holders)
    near = along_reg(pressure, owners, (1, -1))
    driven_near = along_reg(driven, owners, (1, -1))
    beyond = along_reg(ends, owners, (-2, 2))
    joined = jnp.concatenate([mine, second, third], 0)
    joined_lower = along_reg(joined, owners, (1, 1))
    joined_upper = along_reg(joined, owners, (-1, -1))
    driven_far = along_reg(driven_near, owners, (2, -2))
    inner = jnp.where(odd, pressure[:1], pressure[planes - 1 :])
    far = along_reg(
        jnp.where(
            odd, jnp.concatenate([near, inner], 0), jnp.concatenate([inner, near], 0)
        ),
        owners, (2, -2),
    )

    constant, factor, weight, rows_at = call(
        functools.partial(own_kernel, full, own_rows),
        (
            field, field, shaped(tiles, BLOCK),
            jax.ShapeDtypeStruct((3 * tiles, BLOCK), jnp.int32),
        ),
        [SMEM] + [VMEM] * 4, (place, mine, second, third, driven),
        flops=planes * height * 4 * 384 * 256 * 6, size=9 * field_bytes,
    )

    rows = halo_list.shape[1] // BLOCK
    state, down, up = call(
        halo_kernel, (shaped(3 * tiles, BLOCK), shaped(3 * rows, BLOCK), shaped(3 * rows, BLOCK)),
        [VMEM] * 3, (grain_pos, grain_vel, halo_list), flops=8 * 3 * 16384 * 128, size=4 * 4 * 3 * slots,
    )
    lower = along_reg(up, holders, (1, 1))
    upper = along_reg(down, holders, (-1, -1))

    grads = shaped(tiles, 3 * BLOCK)
    window_of = lambda count: pltpu.VMEM((count, height, width), F32)
    grads_a, grads_b, grads_c = call(
        functools.partial(solve_kernel, full, ITERS), (grads,) * 3, [SMEM] + [VMEM] * 3 + [ANY] * 8,
        (
            place, rows_at, joined_lower, joined_upper, driven_near, driven_far, pressure, near, far,
            beyond, constant, factor,
        ),
        [
            window_of(2 * planes), window_of(3 * planes), window_of(3 * planes),
            window_of(3 * planes + 2), window_of(3 * planes + 2),
            pltpu.VMEM((planes * zones * height, 3 * BLOCK), F32),
            pltpu.SemaphoreType.DMA((8,)),
        ],
        flops=2 * planes * height * 4 * 384 * 256 * 6, size=20 * field_bytes,
    )
    grads_b = along_grp(grads_b, -1, owners)
    grads_c = along_grp(grads_c, -2, owners)

    contact = call(
        contact_kernel, shaped(3 * tiles, BLOCK), [SMEM] + [VMEM] * 5,
        (partner_block, state, lower, upper, contact_rows, contact_stiff),
        [pltpu.VMEM((3 * (tiles + 2 * rows), BLOCK), F32)],
        flops=60 * 8 * slots, size=4 * 20 * slots,
    )
    return call(
        final_kernel, shaped(3, slots), [SMEM] + [VMEM] * 9,
        (count, grads_a, grads_b, grads_c, weight, contact, grain_vel, vol, drag, cell),
        flops=60 * slots, size=4 * 20 * slots,
    )


def solution(mesh):
    in_specs = (
        P(None, ("grp", "reg")),
        P(None, ("grp", "reg")),
        P(("grp", "reg")),
        P(("grp", "reg")),
        P(("grp", "reg")),
        P(None, ("grp", "reg")),
        P(None, ("grp", "reg")),
        P(("grp", "reg")),
        P(None, ("grp", "reg")),
        P(("grp", "reg")),
        P(("grp", "reg")),
        P("reg", None, None),
        P("reg", None, None),
        P("reg", None, None),
    )
    out_specs = P(None, ("grp", "reg"))
    return jax.shard_map(
        on_device, mesh=mesh, in_specs=in_specs, out_specs=out_specs, check_vma=False
    )
```

```python
import functools

import jax
import jax.numpy as jnp
from jax import lax
from jax.experimental import pallas as pl
from jax.experimental.pallas import tpu as pltpu
from jax.sharding import PartitionSpec as P

BLOCK = 128
SUB = 8
CORES = 2
ITERS = 4
SPRING = 1.0
DAMPING = 0.5
TIME_STEP = 0.5

VMEM = pl.BlockSpec(memory_space=pltpu.VMEM)
SMEM = pl.BlockSpec(memory_space=pltpu.SMEM)
ANY = pl.BlockSpec(memory_space=pl.ANY)
HBM = pl.BlockSpec(memory_space=pltpu.HBM)
F32 = jnp.float32
BF16 = jnp.bfloat16


def iota(shape, dim):
    return lax.broadcasted_iota(jnp.int32, shape, dim)


def shaped(*dims):
    return jax.ShapeDtypeStruct(dims, F32)


def call(kernel, outs, specs, args, scratch=(), flops=0, size=0, limit=40_000_000):
    return pl.pallas_call(
        kernel,
        out_shape=outs,
        in_specs=specs,
        out_specs=jax.tree.map(lambda _: VMEM, outs),
        scratch_shapes=list(scratch),
        compiler_params=pltpu.CompilerParams(vmem_limit_bytes=limit),
        cost_estimate=pl.CostEstimate(flops=flops, bytes_accessed=size, transcendentals=0),
    )(*args)


def lanes_of(source, index):
    return jnp.take_along_axis(source, index, axis=1, mode="promise_in_bounds")


def halves_of(value):
    high = value.astype(BF16)
    return high, (value - high.astype(F32)).astype(BF16)


def entry_kernel(
    count, place, cell_at, vol_at, drag_at, ids, pressure_old, source, solid_before,
    out, pressure, driven, ends, solid, cell, vol, drag, sems,
):
    tiles = cell.shape[0]
    planes, height, _ = pressure.shape
    rows = pl.ds(pl.multiple_of(place[0], SUB), height)
    moves = [(cell_at, cell), (vol_at, vol), (drag_at, drag)] + [
        (whole.at[:, rows, :], part)
        for whole, part in ((pressure_old, pressure), (source, driven), (solid_before, solid))
    ]
    copies = [
        pltpu.make_async_copy(whole, part, sems.at[index])
        for index, (whole, part) in enumerate(moves)
    ]
    for copy in copies:
        copy.start()
    for copy in copies[:3]:
        copy.wait()
    sub = iota((SUB, BLOCK), 0)
    rows_c = iota((BLOCK, BLOCK), 0)
    even = sub % 2 == 0
    low_pair = sub % 4 < 2

    def step(group, carry):
        first = pl.multiple_of(group * SUB, SUB)
        slot = (first + sub) * BLOCK + iota((SUB, BLOCK), 1)
        live = slot < count[0]
        cells = cell[pl.ds(first, SUB), :]
        parts = halves_of(jnp.where(live, vol[pl.ds(first, SUB), :], 0.0)) + halves_of(
            jnp.where(live, drag[pl.ds(first, SUB), :], 0.0)
        )
        parts = [part.astype(F32) for part in parts]
        left = jnp.concatenate([jnp.where(even, part, 0.0) for part in parts], 0)
        right = jnp.concatenate([jnp.where(even, 0.0, part) for part in parts], 0)
        loads = jnp.concatenate([left, right], 1).astype(BF16)
        sums = [jnp.zeros((SUB, BLOCK), F32), jnp.zeros((SUB, BLOCK), F32)]
        for quad in range(SUB // 4):
            hot = [
                jnp.where(
                    rows_c == jnp.broadcast_to(cells[t : t + 1, :], (BLOCK, BLOCK)), 1.0, 0.0
                ).astype(BF16)
                for t in range(4 * quad, 4 * quad + 4)
            ]
            picked = jnp.concatenate(
                [jnp.concatenate(hot[:2], 1), jnp.concatenate(hot[2:], 1)], 0
            )
            placed = lax.dot_general(
                loads, picked, (((1,), (1,)), ((), ())), preferred_element_type=F32
            )
            for field in range(2):
                base = field * 2 * SUB
                total = placed[base : base + SUB] + placed[base + SUB : base + 2 * SUB]
                chosen = jnp.where(low_pair, total[:, :BLOCK], total[:, BLOCK:])
                sums[field] = jnp.where(sub // 4 == quad, chosen, sums[field])
        out[pl.ds(first, SUB), :BLOCK] = sums[0]
        out[pl.ds(first, SUB), BLOCK:] = sums[1]
        return carry

    lax.fori_loop(0, tiles // SUB, step, 0, unroll=2)
    out[tiles : tiles + SUB, :BLOCK] = jnp.broadcast_to(ids[...].astype(F32), (SUB, BLOCK))
    out[tiles : tiles + SUB, BLOCK:] = jnp.zeros((SUB, BLOCK), F32)
    for copy in copies[3:]:
        copy.wait()
    driven[...] = driven[...] - solid[...]

    @pl.when(place[1] == 1)
    def _():
        ends[...] = pressure[planes - 1]

    @pl.when(place[1] != 1)
    def _():
        ends[...] = pressure[0]


def halo_kernel(pos, vel, lists, state, down, up):
    tiles = pos.shape[1] // BLOCK
    rows = lists.shape[1] // BLOCK
    for tile in range(tiles):
        lanes = slice(tile * BLOCK, (tile + 1) * BLOCK)
        mixed = SPRING * pos[:, lanes] - DAMPING * vel[:, lanes]
        for axis in range(3):
            state[axis * tiles + tile : axis * tiles + tile + 1, :] = mixed[axis : axis + 1]
    turned = [
        jnp.concatenate(halves_of(jnp.transpose(state[axis * tiles : (axis + 1) * tiles, :])), 1)
        for axis in range(3)
    ]
    turned = jnp.concatenate(turned, 0)
    span = 2 * BLOCK
    row = iota((BLOCK, span), 0)

    for side, out in enumerate((down, up)):

        def step(part, carry):
            named = lists[side : side + 1, pl.ds(pl.multiple_of(part * span, span), span)]
            block = lax.shift_right_logical(named, 7)
            lane = named & (BLOCK - 1)
            hot = jnp.where(row == jnp.broadcast_to(block, row.shape), 1.0, 0.0).astype(BF16)
            found = jnp.dot(
                turned, jnp.concatenate([hot, hot], 0), preferred_element_type=F32
            )
            here = row == jnp.broadcast_to(lane, row.shape)
            for axis in range(3):
                value = jnp.where(here, found[axis * BLOCK : (axis + 1) * BLOCK], 0.0)
                value = jnp.sum(value, axis=0, keepdims=True)
                for half in range(2):
                    out[pl.ds(axis * rows + 2 * part + half, 1), :] = value[
                        :, half * BLOCK : (half + 1) * BLOCK
                    ]
            return carry

        lax.fori_loop(0, rows // 2, step, 0, unroll=2)


def contact_kernel(partner, state, lower, upper, named, stiff, _, out, extended):
    tiles = state.shape[0] // 3
    rows = lower.shape[0] // 3
    blocks = tiles + 2 * rows
    for axis in range(3):
        extended[axis * blocks : axis * blocks + tiles, :] = state[
            axis * tiles : (axis + 1) * tiles, :
        ]
        for place, side in enumerate((lower, upper)):
            first = axis * blocks + tiles + place * rows
            extended[first : first + rows, :] = side[axis * rows : (axis + 1) * rows, :]

    def step(tile, carry):
        lanes = pl.ds(pl.multiple_of(tile * BLOCK, BLOCK), BLOCK)
        entry = named[:, lanes]
        weight = jnp.where(entry >= 0, stiff[:, lanes], 0.0)
        own = entry < BLOCK
        lane = entry & (BLOCK - 1)
        other = partner[tile]
        for axis in range(3):
            mine = jnp.broadcast_to(extended[pl.ds(axis * blocks + tile, 1), :], entry.shape)
            theirs = jnp.broadcast_to(extended[pl.ds(axis * blocks + other, 1), :], entry.shape)
            met = jnp.where(own, lanes_of(mine, lane), lanes_of(theirs, lane))
            pull = jnp.sum(weight * (mine - met), axis=0, keepdims=True)
            out[pl.ds(axis * tiles + tile, 1), :] = pull
        return carry

    lax.fori_loop(0, tiles, step, 0, unroll=4)


def shifted(plane):
    height, width = plane.shape
    row = iota(plane.shape, 0)
    column = iota(plane.shape, 1)
    above = jnp.where(row == 0, 0.0, pltpu.roll(plane, 1, 0))
    below = jnp.where(row == height - 1, 0.0, pltpu.roll(plane, height - 1, 0))
    left = jnp.where(column == 0, 0.0, pltpu.roll(plane, 1, 1))
    right = jnp.where(column == width - 1, 0.0, pltpu.roll(plane, width - 1, 1))
    return above, below, left, right


def placed(groups, tiles):
    parts = [halves_of(group[:tiles, :]) for group in groups]
    loads = jnp.concatenate([part[i] for i in range(2) for part in parts], 0)
    ids = jnp.concatenate([group[tiles : tiles + 1, :BLOCK] for group in groups], 1)
    ids = ids.astype(jnp.int32)

    def gathered(wanted):
        hot = jnp.where(wanted == jnp.broadcast_to(ids, wanted.shape), 1.0, 0.0).astype(BF16)
        total = jnp.dot(
            jnp.concatenate([hot, hot], 1), loads, preferred_element_type=F32
        )
        return total[:, :BLOCK], total[:, BLOCK:]

    return ids, gathered


def coefficients(gathered, tiles, first, full, driven, constant, factor, base, present):
    planes, height, width = driven.shape
    zones = width // BLOCK
    shape = (zones * height, 3 * tiles)
    line = iota(shape, 0)
    block = (line % height) * zones + line // height + first * zones

    def plane(x, carry):
        solid, drag = gathered(block + x * (full * zones))
        porous = 1.0 / (1.0 + solid)
        inverse = 1.0 / (6.0 * porous + drag + 1.0)
        if present is not None:
            inverse = jnp.where(present, inverse, 0.0)
        scale = porous * inverse
        for zone in range(zones):
            lanes = slice(zone * BLOCK, (zone + 1) * BLOCK)
            rows = slice(zone * height, (zone + 1) * height)
            driving = driven[x, :, lanes] + solid[rows]
            constant[base + x, :, lanes] = driving * inverse[rows]
            factor[base + x, :, lanes] = scale[rows]
        return carry

    lax.fori_loop(0, planes, plane, 0)


def own_kernel(
    full, own_rows, place, mine, second, third, driven, _, constant, factor, weight, rows_at
):
    stride = mine.shape[0]
    tiles = stride - SUB
    planes, height, width = driven.shape
    zones = width // BLOCK
    ids, gathered = placed((mine, second, third), tiles)
    coefficients(gathered, tiles, place[0], full, driven, constant, factor, 0, None)
    turned = [
        jnp.transpose(
            jnp.broadcast_to(ids[:, i * tiles : (i + 1) * tiles], (BLOCK, tiles)).astype(F32)
        ).astype(jnp.int32)
        for i in range(3)
    ]
    solid, drag = gathered(jnp.concatenate([turned[0]] * 3, 1))
    weight[...] = 1.0 / (1.0 / (1.0 + solid) + drag)
    for i, block in enumerate(turned):
        line, zone = block // zones, block % zones
        x, y = line // full, line % full
        row = (x * zones + zone) * height + y - place[0]
        rows_at[i * tiles : (i + 1) * tiles, :] = jnp.where(y // own_rows == place[4], row, -1)


def solve_kernel(
    full, sweeps, place, rows_at, joined_near, joined_far, driven_near, driven_far, pressure,
    near, far, beyond, own_constant, own_factor, _lower, _upper, out_a, out_b, out_c,
    constant, factor, old, new, fields,
):
    planes, height, width = pressure.shape
    zones = width // BLOCK
    stride = joined_near.shape[0] // 3
    tiles = stride - SUB
    odd, lower, upper = place[1] == 1, place[2] == 1, place[3] == 1
    rim = sweeps + 1
    for joined, driven, below, present in (
        (joined_near, driven_near, odd, jnp.where(odd, place[2], place[3])),
        (joined_far, driven_far, jnp.logical_not(odd), jnp.where(odd, place[3], place[2])),
    ):
        groups = [joined.at[i * stride : (i + 1) * stride] for i in range(3)]
        _, gathered = placed(groups, tiles)
        coefficients(
            gathered, tiles, place[0], full, driven, constant, factor,
            jnp.where(below, 0, planes), present == 1,
        )
    old[pl.ds(jnp.where(odd, 1, rim + planes), planes)] = near[...]
    old[pl.ds(jnp.where(odd, rim + planes, 0), planes + 1)] = far[...]
    old[pl.ds(jnp.where(odd, 0, rim + 2 * planes), 1)] = beyond[...][None]
    old[rim : rim + planes] = pressure[...]

    def sweep(source, target, depth):
        def over(constants, factors, shift):
            def plane(x, carry):
                centre = source[x]
                above, below, left, right = shifted(centre)
                around = source[x - 1] + source[x + 1] + above + below + left + right
                target[x] = constants[x - shift] + factors[x - shift] * around
                return carry

            return plane

        lax.fori_loop(depth, rim, over(constant, factor, 1), 0)
        lax.fori_loop(rim, rim + planes, over(own_constant, own_factor, rim), 0)
        lax.fori_loop(
            rim + planes, 3 * planes + 2 - depth, over(constant, factor, 1 + planes), 0
        )

    for index in range(sweeps):
        source, target = (old, new) if index % 2 == 0 else (new, old)
        sweep(source, target, index + 1)
    last = old if sweeps % 2 == 0 else new

    def gradient(x, carry):
        centre = last[rim + x]
        above, below, left, right = shifted(centre)
        grads = (last[rim + x + 1] - last[rim + x - 1], below - above, right - left)
        for zone in range(zones):
            first = pl.multiple_of((x * zones + zone) * height, SUB)
            for axis, grad in enumerate(grads):
                fields[pl.ds(first, height), axis * BLOCK : (axis + 1) * BLOCK] = (
                    0.5 * grad[:, zone * BLOCK : (zone + 1) * BLOCK]
                )
        return carry

    lax.fori_loop(0, planes, gradient, 0)
    span = 3 * BLOCK
    wanted = jnp.concatenate([rows_at[...]] * 3, 1)
    column = iota(wanted.shape, 1)
    total = jnp.zeros((3 * tiles, span), F32)
    for part in range(planes * zones * height // span):
        hot = jnp.where(wanted == column + part * span, 1.0, 0.0).astype(BF16)
        for piece in halves_of(fields[part * span : (part + 1) * span, :]):
            total = total + jnp.dot(hot, piece, preferred_element_type=F32)
    for index, out in enumerate((out_a, out_b, out_c)):
        out[...] = total[index * tiles : (index + 1) * tiles]


def final_kernel(
    count, grads_a, grads_b, grads_c, weight, contact, vel, vol, drag, cell, out,
):
    tiles = cell.shape[0]
    cells = cell[...]
    heft = lanes_of(weight[...], cells)
    slot = iota(cells.shape, 0) * BLOCK + iota(cells.shape, 1)
    live = slot < count[0]
    volume = vol[...]
    push = TIME_STEP / volume
    for axis in range(3):
        lanes = slice(axis * BLOCK, (axis + 1) * BLOCK)
        gradient = lanes_of(grads_a[:, lanes] + grads_b[:, lanes] + grads_c[:, lanes], cells)
        own = jnp.concatenate(
            [vel[axis : axis + 1, t * BLOCK : (t + 1) * BLOCK] for t in range(tiles)], 0
        )
        fluid = -gradient * heft
        force = contact[axis * tiles : (axis + 1) * tiles, :] - volume * gradient
        force = force + drag[...] * (fluid - own)
        new = jnp.where(live, own + force * push, 0.0)
        for t in range(tiles):
            out[axis : axis + 1, t * BLOCK : (t + 1) * BLOCK] = new[t : t + 1, :]


def on_device(
    grain_pos,
    grain_vel,
    grain_vol,
    drag_coef,
    grain_count,
    contact_rows,
    contact_stiff,
    partner_block,
    halo_list,
    grain_cell,
    tile_cell_block,
    pressure_old,
    pressure_source,
    solid_old,
):
    groups, regions = lax.axis_size("grp"), lax.axis_size("reg")
    holding = groups - 1
    halves = groups // CORES
    slots = grain_pos.shape[1]
    tiles = slots // BLOCK
    planes, full, width = pressure_old.shape
    zones = width // BLOCK
    own_rows = full // halves
    height = min(full, own_rows + SUB * min(2, halves - 1))
    group, region = lax.axis_index("grp"), lax.axis_index("reg")
    half = group // CORES
    first = jnp.clip(half * own_rows - SUB, 0, full - height)
    odd = region % 2 == 1
    place = jnp.stack(
        [first, odd, region > 0, region < regions - 1, jnp.where(group % CORES == 0, half, -1)]
    ).astype(jnp.int32)
    owners = range(0, groups, CORES)
    holders = range(holding)

    def send(value, pairs):
        flat = [(a[0] * regions + a[1], b[0] * regions + b[1]) for a, b in pairs]
        return lax.ppermute(value, ("grp", "reg"), flat)

    def along_reg(value, members, goes):
        pairs = [
            ((g, r), (g, r + goes[r % 2]))
            for g in members
            for r in range(regions)
            if 0 <= r + goes[r % 2] < regions
        ]
        return send(value, pairs)

    def along_grp(value, step, members):
        pairs = [((g, r), ((g + step) % holding, r)) for g in members for r in range(regions)]
        return send(value, pairs)

    count = grain_count
    cell = grain_cell.reshape(tiles, BLOCK)
    vol = grain_vol.reshape(tiles, BLOCK)
    drag = drag_coef.reshape(tiles, BLOCK)
    ids = tile_cell_block.reshape(1, tiles)
    field_bytes = 4 * planes * height * width

    field = shaped(planes, height, width)
    mine, pressure, driven, ends = call(
        entry_kernel, (shaped(tiles + SUB, 2 * BLOCK), field, field, shaped(height, width)),
        [SMEM] * 2 + [HBM] * 3 + [VMEM] + [HBM] * 3,
        (count, place, cell, vol, drag, ids, pressure_old, pressure_source, solid_old),
        [
            pltpu.VMEM((planes, height, width), F32), pltpu.VMEM((tiles, BLOCK), jnp.int32),
            pltpu.VMEM((tiles, BLOCK), F32), pltpu.VMEM((tiles, BLOCK), F32),
            pltpu.SemaphoreType.DMA((6,)),
        ],
        flops=2 * 32 * 48 * 65536, size=5 * 4 * slots, limit=61_500_000,
    )
    second = along_grp(mine, 1, holders)
    third = along_grp(mine, 2, holders)
    near = along_reg(pressure, owners, (1, -1))
    driven_near = along_reg(driven, owners, (1, -1))
    beyond = along_reg(ends, owners, (-2, 2))
    joined = jnp.concatenate([mine, second, third], 0)
    joined_near = along_reg(joined, owners, (1, -1))
    joined_far = along_reg(joined, owners, (-1, 1))
    driven_far = along_reg(driven_near, owners, (2, -2))
    inner = jnp.where(odd, pressure[:1], pressure[planes - 1 :])
    far = along_reg(
        jnp.where(
            odd, jnp.concatenate([near, inner], 0), jnp.concatenate([inner, near], 0)
        ),
        owners, (2, -2),
    )

    rows = halo_list.shape[1] // BLOCK
    state, down, up = call(
        halo_kernel, (shaped(3 * tiles, BLOCK), shaped(3 * rows, BLOCK), shaped(3 * rows, BLOCK)),
        [VMEM] * 3, (grain_pos, grain_vel, halo_list), flops=8 * 3 * 16384 * 128, size=4 * 4 * 3 * slots,
    )
    lower = along_reg(up, holders, (1, 1))
    upper = along_reg(down, holders, (-1, -1))

    constant, factor, weight, rows_at = call(
        functools.partial(own_kernel, full, own_rows),
        (
            field, field, shaped(tiles, BLOCK),
            jax.ShapeDtypeStruct((3 * tiles, BLOCK), jnp.int32),
        ),
        [SMEM] + [VMEM] * 4 + [ANY], (place, mine, second, third, driven, state),
        flops=planes * height * 4 * 384 * 256 * 6, size=9 * field_bytes,
    )

    grads = shaped(tiles, 3 * BLOCK)
    window_of = lambda count: pltpu.VMEM((count, height, width), F32)
    grads_a, grads_b, grads_c = call(
        functools.partial(solve_kernel, full, ITERS), (grads,) * 3, [SMEM] + [VMEM] * 11 + [ANY] * 2,
        (
            place, rows_at, joined_near, joined_far, driven_near, driven_far, pressure, near, far,
            beyond, constant, factor, lower, upper,
        ),
        [
            window_of(2 * planes), window_of(2 * planes),
            window_of(3 * planes + 2), window_of(3 * planes + 2),
            pltpu.VMEM((planes * zones * height, 3 * BLOCK), F32),
        ],
        flops=2 * planes * height * 4 * 384 * 256 * 6, size=20 * field_bytes,
    )
    grads_b = along_grp(grads_b, -1, owners)
    grads_c = along_grp(grads_c, -2, owners)

    contact = call(
        contact_kernel, shaped(3 * tiles, BLOCK), [SMEM] + [VMEM] * 5 + [ANY],
        (partner_block, state, lower, upper, contact_rows, contact_stiff, grads_a),
        [pltpu.VMEM((3 * (tiles + 2 * rows), BLOCK), F32)],
        flops=60 * 8 * slots, size=4 * 20 * slots,
    )
    return call(
        final_kernel, shaped(3, slots), [SMEM] + [VMEM] * 9,
        (count, grads_a, grads_b, grads_c, weight, contact, grain_vel, vol, drag, cell),
        flops=60 * slots, size=4 * 20 * slots,
    )


def solution(mesh):
    in_specs = (
        P(None, ("grp", "reg")),
        P(None, ("grp", "reg")),
        P(("grp", "reg")),
        P(("grp", "reg")),
        P(("grp", "reg")),
        P(None, ("grp", "reg")),
        P(None, ("grp", "reg")),
        P(("grp", "reg")),
        P(None, ("grp", "reg")),
        P(("grp", "reg")),
        P(("grp", "reg")),
        P("reg", None, None),
        P("reg", None, None),
        P("reg", None, None),
    )
    out_specs = P(None, ("grp", "reg"))
    return jax.shard_map(
        on_device, mesh=mesh, in_specs=in_specs, out_specs=out_specs, check_vma=False
    )
```

```python
import functools

import jax
import jax.numpy as jnp
from jax import lax
from jax.experimental import pallas as pl
from jax.experimental.pallas import tpu as pltpu
from jax.sharding import PartitionSpec as P

BLOCK = 128
SUB = 8
CORES = 2
ITERS = 4
SPRING = 1.0
DAMPING = 0.5
TIME_STEP = 0.5

VMEM = pl.BlockSpec(memory_space=pltpu.VMEM)
SMEM = pl.BlockSpec(memory_space=pltpu.SMEM)
ANY = pl.BlockSpec(memory_space=pl.ANY)
HBM = pl.BlockSpec(memory_space=pltpu.HBM)
F32 = jnp.float32
BF16 = jnp.bfloat16


def iota(shape, dim):
    return lax.broadcasted_iota(jnp.int32, shape, dim)


def shaped(*dims):
    return jax.ShapeDtypeStruct(dims, F32)


def call(kernel, outs, specs, args, scratch=(), flops=0, size=0, limit=40_000_000):
    return pl.pallas_call(
        kernel,
        out_shape=outs,
        in_specs=specs,
        out_specs=jax.tree.map(lambda _: VMEM, outs),
        scratch_shapes=list(scratch),
        compiler_params=pltpu.CompilerParams(vmem_limit_bytes=limit),
        cost_estimate=pl.CostEstimate(flops=flops, bytes_accessed=size, transcendentals=0),
    )(*args)


def lanes_of(source, index):
    return jnp.take_along_axis(source, index, axis=1, mode="promise_in_bounds")


def halves_of(value):
    high = value.astype(BF16)
    return high, (value - high.astype(F32)).astype(BF16)


def entry_kernel(
    count, place, cell_at, vol_at, drag_at, ids, pressure_old, source, solid_before,
    out, pressure, driven, ends, solid, cell, vol, drag, sems,
):
    tiles = cell.shape[0]
    planes, height, _ = pressure.shape
    rows = pl.ds(pl.multiple_of(place[0], SUB), height)
    moves = [(cell_at, cell), (vol_at, vol), (drag_at, drag)] + [
        (whole.at[:, rows, :], part)
        for whole, part in ((pressure_old, pressure), (source, driven), (solid_before, solid))
    ]
    copies = [
        pltpu.make_async_copy(whole, part, sems.at[index])
        for index, (whole, part) in enumerate(moves)
    ]
    for copy in copies:
        copy.start()
    for copy in copies[:3]:
        copy.wait()
    sub = iota((SUB, BLOCK), 0)
    rows_c = iota((BLOCK, BLOCK), 0)
    even = sub % 2 == 0
    low_pair = sub % 4 < 2

    def step(group, carry):
        first = pl.multiple_of(group * SUB, SUB)
        slot = (first + sub) * BLOCK + iota((SUB, BLOCK), 1)
        live = slot < count[0]
        cells = cell[pl.ds(first, SUB), :]
        parts = halves_of(jnp.where(live, vol[pl.ds(first, SUB), :], 0.0)) + halves_of(
            jnp.where(live, drag[pl.ds(first, SUB), :], 0.0)
        )
        parts = [part.astype(F32) for part in parts]
        left = jnp.concatenate([jnp.where(even, part, 0.0) for part in parts], 0)
        right = jnp.concatenate([jnp.where(even, 0.0, part) for part in parts], 0)
        loads = jnp.concatenate([left, right], 1).astype(BF16)
        sums = [jnp.zeros((SUB, BLOCK), F32), jnp.zeros((SUB, BLOCK), F32)]
        for quad in range(SUB // 4):
            hot = [
                jnp.where(
                    rows_c == jnp.broadcast_to(cells[t : t + 1, :], (BLOCK, BLOCK)), 1.0, 0.0
                ).astype(BF16)
                for t in range(4 * quad, 4 * quad + 4)
            ]
            picked = jnp.concatenate(
                [jnp.concatenate(hot[:2], 1), jnp.concatenate(hot[2:], 1)], 0
            )
            placed = lax.dot_general(
                loads, picked, (((1,), (1,)), ((), ())), preferred_element_type=F32
            )
            for field in range(2):
                base = field * 2 * SUB
                total = placed[base : base + SUB] + placed[base + SUB : base + 2 * SUB]
                chosen = jnp.where(low_pair, total[:, :BLOCK], total[:, BLOCK:])
                sums[field] = jnp.where(sub // 4 == quad, chosen, sums[field])
        out[pl.ds(first, SUB), :BLOCK] = sums[0]
        out[pl.ds(first, SUB), BLOCK:] = sums[1]
        return carry

    lax.fori_loop(0, tiles // SUB, step, 0, unroll=2)
    out[tiles : tiles + SUB, :BLOCK] = jnp.broadcast_to(ids[...].astype(F32), (SUB, BLOCK))
    out[tiles : tiles + SUB, BLOCK:] = jnp.zeros((SUB, BLOCK), F32)
    for copy in copies[3:]:
        copy.wait()
    driven[...] = driven[...] - solid[...]

    @pl.when(place[1] == 1)
    def _():
        ends[...] = pressure[planes - 1]

    @pl.when(place[1] != 1)
    def _():
        ends[...] = pressure[0]


def halo_kernel(pos, vel, lists, state, down, up):
    tiles = pos.shape[1] // BLOCK
    rows = lists.shape[1] // BLOCK
    for tile in range(tiles):
        lanes = slice(tile * BLOCK, (tile + 1) * BLOCK)
        mixed = SPRING * pos[:, lanes] - DAMPING * vel[:, lanes]
        for axis in range(3):
            state[axis * tiles + tile : axis * tiles + tile + 1, :] = mixed[axis : axis + 1]
    turned = [
        jnp.concatenate(halves_of(jnp.transpose(state[axis * tiles : (axis + 1) * tiles, :])), 1)
        for axis in range(3)
    ]
    turned = jnp.concatenate(turned, 0)
    span = 2 * BLOCK
    row = iota((BLOCK, span), 0)

    for side, out in enumerate((down, up)):

        def step(part, carry):
            named = lists[side : side + 1, pl.ds(pl.multiple_of(part * span, span), span)]
            block = lax.shift_right_logical(named, 7)
            lane = named & (BLOCK - 1)
            hot = jnp.where(row == jnp.broadcast_to(block, row.shape), 1.0, 0.0).astype(BF16)
            found = jnp.dot(
                turned, jnp.concatenate([hot, hot], 0), preferred_element_type=F32
            )
            here = row == jnp.broadcast_to(lane, row.shape)
            for axis in range(3):
                value = jnp.where(here, found[axis * BLOCK : (axis + 1) * BLOCK], 0.0)
                value = jnp.sum(value, axis=0, keepdims=True)
                for half in range(2):
                    out[pl.ds(axis * rows + 2 * part + half, 1), :] = value[
                        :, half * BLOCK : (half + 1) * BLOCK
                    ]
            return carry

        lax.fori_loop(0, rows // 2, step, 0, unroll=2)


def contact_kernel(partner, state, lower, upper, named, stiff, _, out, extended):
    tiles = state.shape[0] // 3
    rows = lower.shape[0] // 3
    blocks = tiles + 2 * rows
    for axis in range(3):
        extended[axis * blocks : axis * blocks + tiles, :] = state[
            axis * tiles : (axis + 1) * tiles, :
        ]
        for place, side in enumerate((lower, upper)):
            first = axis * blocks + tiles + place * rows
            extended[first : first + rows, :] = side[axis * rows : (axis + 1) * rows, :]

    def step(tile, carry):
        lanes = pl.ds(pl.multiple_of(tile * BLOCK, BLOCK), BLOCK)
        entry = named[:, lanes]
        weight = jnp.where(entry >= 0, stiff[:, lanes], 0.0)
        own = entry < BLOCK
        lane = entry & (BLOCK - 1)
        other = partner[tile]
        for axis in range(3):
            mine = jnp.broadcast_to(extended[pl.ds(axis * blocks + tile, 1), :], entry.shape)
            theirs = jnp.broadcast_to(extended[pl.ds(axis * blocks + other, 1), :], entry.shape)
            met = jnp.where(own, lanes_of(mine, lane), lanes_of(theirs, lane))
            pull = jnp.sum(weight * (mine - met), axis=0, keepdims=True)
            out[pl.ds(axis * tiles + tile, 1), :] = pull
        return carry

    lax.fori_loop(0, tiles, step, 0, unroll=4)


def shifted(plane):
    height, width = plane.shape
    row = iota(plane.shape, 0)
    column = iota(plane.shape, 1)
    above = jnp.where(row == 0, 0.0, pltpu.roll(plane, 1, 0))
    below = jnp.where(row == height - 1, 0.0, pltpu.roll(plane, height - 1, 0))
    left = jnp.where(column == 0, 0.0, pltpu.roll(plane, 1, 1))
    right = jnp.where(column == width - 1, 0.0, pltpu.roll(plane, width - 1, 1))
    return above, below, left, right


def inverse_of(value):
    near = pl.reciprocal(value, approx=True)
    return near * (2.0 - value * near)


def placed(joined, tiles):
    stride = tiles + SUB
    groups = [joined.at[i * stride : (i + 1) * stride] for i in range(joined.shape[0] // stride)]
    parts = [halves_of(group[:tiles, :]) for group in groups]
    loads = jnp.concatenate([part[i] for i in range(2) for part in parts], 0)
    ids = jnp.concatenate([group[tiles : tiles + 1, :BLOCK] for group in groups], 1)
    ids = ids.astype(jnp.int32)

    def gathered(wanted):
        hot = jnp.where(wanted == jnp.broadcast_to(ids, wanted.shape), 1.0, 0.0).astype(BF16)
        total = jnp.dot(
            jnp.concatenate([hot, hot], 1), loads, preferred_element_type=F32
        )
        return total[:, :BLOCK], total[:, BLOCK:]

    return ids, gathered


def coefficients(gathered, tiles, first, full, driven, constant, factor, base, present):
    planes, height, width = driven.shape
    zones = width // BLOCK
    shape = (zones * height, 3 * tiles)
    line = iota(shape, 0)
    block = (line % height) * zones + line // height + first * zones

    def plane(x, carry):
        solid, drag = gathered(block + x * (full * zones))
        voids = 1.0 + solid
        scale = inverse_of(6.0 + (drag + 1.0) * voids)
        if present is not None:
            scale = jnp.where(present, scale, 0.0)
        inverse = voids * scale
        for zone in range(zones):
            lanes = slice(zone * BLOCK, (zone + 1) * BLOCK)
            rows = slice(zone * height, (zone + 1) * height)
            driving = driven[x, :, lanes] + solid[rows]
            constant[base + x, :, lanes] = driving * inverse[rows]
            factor[base + x, :, lanes] = scale[rows]
        return carry

    lax.fori_loop(0, planes, plane, 0)


def own_kernel(
    full, own_rows, place, joined, driven, _, constant, factor, weight, rows_at
):
    tiles = weight.shape[0]
    planes, height, width = driven.shape
    zones = width // BLOCK
    ids, gathered = placed(joined, tiles)
    coefficients(gathered, tiles, place[0], full, driven, constant, factor, 0, None)
    turned = [
        jnp.transpose(
            jnp.broadcast_to(ids[:, i * tiles : (i + 1) * tiles], (BLOCK, tiles)).astype(F32)
        ).astype(jnp.int32)
        for i in range(3)
    ]

    def before(places):
        index = lax.rem(place[5] + 3 - places, 3)
        return jnp.where(index == 0, turned[0], jnp.where(index == 1, turned[1], turned[2]))

    solid, drag = gathered(jnp.concatenate([before(0)] * 3, 1))
    weight[...] = 1.0 / (1.0 / (1.0 + solid) + drag)
    for i in range(3):
        block = before(i)
        line, zone = block // zones, block % zones
        x, y = line // full, line % full
        row = (x * zones + zone) * height + y - place[0]
        rows_at[i * tiles : (i + 1) * tiles, :] = jnp.where(y // own_rows == place[4], row, -1)


def solve_kernel(
    full, sweeps, place, rows_at, joined_near, joined_far, driven_near, driven_far, pressure,
    near, far, beyond, own_constant, own_factor, out_a, out_b, out_c,
    constant, factor, old, new, fields,
):
    planes, height, width = pressure.shape
    zones = width // BLOCK
    stride = joined_near.shape[0] // 3
    tiles = stride - SUB
    odd, lower, upper = place[1] == 1, place[2] == 1, place[3] == 1
    rim = sweeps + 1
    for joined, driven, below, present in (
        (joined_near, driven_near, odd, jnp.where(odd, place[2], place[3])),
        (joined_far, driven_far, jnp.logical_not(odd), jnp.where(odd, place[3], place[2])),
    ):
        _, gathered = placed(joined, tiles)
        coefficients(
            gathered, tiles, place[0], full, driven, constant, factor,
            jnp.where(below, 0, planes), present == 1,
        )
    old[pl.ds(jnp.where(odd, 1, rim + planes), planes)] = near[...]
    old[pl.ds(jnp.where(odd, rim + planes, 0), planes + 1)] = far[...]
    old[pl.ds(jnp.where(odd, 0, rim + 2 * planes), 1)] = beyond[...][None]
    old[rim : rim + planes] = pressure[...]

    def sweep(source, target, depth):
        def over(constants, factors, shift):
            def plane(x, carry):
                centre = source[x]
                above, below, left, right = shifted(centre)
                around = source[x - 1] + source[x + 1] + above + below + left + right
                target[x] = constants[x - shift] + factors[x - shift] * around
                return carry

            return plane

        lax.fori_loop(depth, rim, over(constant, factor, 1), 0)
        lax.fori_loop(rim, rim + planes, over(own_constant, own_factor, rim), 0)
        lax.fori_loop(
            rim + planes, 3 * planes + 2 - depth, over(constant, factor, 1 + planes), 0
        )

    for index in range(sweeps):
        source, target = (old, new) if index % 2 == 0 else (new, old)
        sweep(source, target, index + 1)
    last = old if sweeps % 2 == 0 else new

    def gradient(x, carry):
        centre = last[rim + x]
        above, below, left, right = shifted(centre)
        grads = (last[rim + x + 1] - last[rim + x - 1], below - above, right - left)
        for zone in range(zones):
            first = pl.multiple_of((x * zones + zone) * height, SUB)
            for axis, grad in enumerate(grads):
                fields[pl.ds(first, height), axis * BLOCK : (axis + 1) * BLOCK] = (
                    0.5 * grad[:, zone * BLOCK : (zone + 1) * BLOCK]
                )
        return carry

    lax.fori_loop(0, planes, gradient, 0)
    span = 3 * BLOCK
    wanted = jnp.concatenate([rows_at[...]] * 3, 1)
    column = iota(wanted.shape, 1)
    total = jnp.zeros((3 * tiles, span), F32)
    for part in range(planes * zones * height // span):
        hot = jnp.where(wanted == column + part * span, 1.0, 0.0).astype(BF16)
        for piece in halves_of(fields[part * span : (part + 1) * span, :]):
            total = total + jnp.dot(hot, piece, preferred_element_type=F32)
    for index, out in enumerate((out_a, out_b, out_c)):
        out[...] = total[index * tiles : (index + 1) * tiles]


def final_kernel(
    count, grads_a, grads_b, grads_c, weight, contact, vel, vol, drag, cell, out,
):
    tiles = cell.shape[0]
    cells = cell[...]
    heft = lanes_of(weight[...], cells)
    slot = iota(cells.shape, 0) * BLOCK + iota(cells.shape, 1)
    live = slot < count[0]
    volume = vol[...]
    push = TIME_STEP / volume
    for axis in range(3):
        lanes = slice(axis * BLOCK, (axis + 1) * BLOCK)
        gradient = lanes_of(grads_a[:, lanes] + grads_b[:, lanes] + grads_c[:, lanes], cells)
        own = jnp.concatenate(
            [vel[axis : axis + 1, t * BLOCK : (t + 1) * BLOCK] for t in range(tiles)], 0
        )
        fluid = -gradient * heft
        force = contact[axis * tiles : (axis + 1) * tiles, :] - volume * gradient
        force = force + drag[...] * (fluid - own)
        new = jnp.where(live, own + force * push, 0.0)
        for t in range(tiles):
            out[axis : axis + 1, t * BLOCK : (t + 1) * BLOCK] = new[t : t + 1, :]


def on_device(
    grain_pos,
    grain_vel,
    grain_vol,
    drag_coef,
    grain_count,
    contact_rows,
    contact_stiff,
    partner_block,
    halo_list,
    grain_cell,
    tile_cell_block,
    pressure_old,
    pressure_source,
    solid_old,
):
    groups, regions = lax.axis_size("grp"), lax.axis_size("reg")
    holding = groups - 1
    halves = groups // CORES
    slots = grain_pos.shape[1]
    tiles = slots // BLOCK
    planes, full, width = pressure_old.shape
    zones = width // BLOCK
    own_rows = full // halves
    height = min(full, own_rows + SUB * min(2, halves - 1))
    group, region = lax.axis_index("grp"), lax.axis_index("reg")
    half = group // CORES
    first = jnp.clip(half * own_rows - SUB, 0, full - height)
    odd = region % 2 == 1
    place = jnp.stack(
        [first, odd, region > 0, region < regions - 1, jnp.where(group % CORES == 0, half, -1), group]
    ).astype(jnp.int32)
    owners = range(0, groups, CORES)
    holders = range(holding)

    def send(value, pairs):
        flat = [(a[0] * regions + a[1], b[0] * regions + b[1]) for a, b in pairs]
        return lax.ppermute(value, ("grp", "reg"), flat)

    def along_reg(value, members, goes):
        pairs = [
            ((g, r), (g, r + goes[r % 2]))
            for g in members
            for r in range(regions)
            if 0 <= r + goes[r % 2] < regions
        ]
        return send(value, pairs)

    def along_grp(value, step, members):
        pairs = [((g, r), ((g + step) % holding, r)) for g in members for r in range(regions)]
        return send(value, pairs)

    count = grain_count
    cell = grain_cell.reshape(tiles, BLOCK)
    vol = grain_vol.reshape(tiles, BLOCK)
    drag = drag_coef.reshape(tiles, BLOCK)
    ids = tile_cell_block.reshape(1, tiles)
    field_bytes = 4 * planes * height * width

    field = shaped(planes, height, width)
    mine, pressure, driven, ends = call(
        entry_kernel, (shaped(tiles + SUB, 2 * BLOCK), field, field, shaped(height, width)),
        [SMEM] * 2 + [HBM] * 3 + [VMEM] + [HBM] * 3,
        (count, place, cell, vol, drag, ids, pressure_old, pressure_source, solid_old),
        [
            pltpu.VMEM((planes, height, width), F32), pltpu.VMEM((tiles, BLOCK), jnp.int32),
            pltpu.VMEM((tiles, BLOCK), F32), pltpu.VMEM((tiles, BLOCK), F32),
            pltpu.SemaphoreType.DMA((6,)),
        ],
        flops=2 * 32 * 48 * 65536, size=5 * 4 * slots, limit=61_500_000,
    )
    gathered = lax.all_gather(mine, "grp")
    joined = gathered[:holding].reshape(holding * (tiles + SUB), 2 * BLOCK)
    near = along_reg(pressure, owners, (1, -1))
    driven_near = along_reg(driven, owners, (1, -1))
    beyond = along_reg(ends, owners, (-2, 2))
    joined_near = along_reg(joined, owners, (1, -1))
    joined_far = along_reg(joined, owners, (-1, 1))
    driven_far = along_reg(driven_near, owners, (2, -2))
    inner = jnp.where(odd, pressure[:1], pressure[planes - 1 :])
    far = along_reg(
        jnp.where(
            odd, jnp.concatenate([near, inner], 0), jnp.concatenate([inner, near], 0)
        ),
        owners, (2, -2),
    )

    rows = halo_list.shape[1] // BLOCK
    state, down, up = call(
        halo_kernel, (shaped(3 * tiles, BLOCK), shaped(3 * rows, BLOCK), shaped(3 * rows, BLOCK)),
        [VMEM] * 3, (grain_pos, grain_vel, halo_list), flops=8 * 3 * 16384 * 128, size=4 * 4 * 3 * slots,
    )
    lower = along_reg(up, holders, (1, 1))
    upper = along_reg(down, holders, (-1, -1))

    constant, factor, weight, rows_at = call(
        functools.partial(own_kernel, full, own_rows),
        (
            field, field, shaped(tiles, BLOCK),
            jax.ShapeDtypeStruct((3 * tiles, BLOCK), jnp.int32),
        ),
        [SMEM] + [VMEM] * 2 + [ANY], (place, joined, driven, state),
        flops=planes * height * 4 * 384 * 256 * 6, size=9 * field_bytes,
    )

    grads = shaped(tiles, 3 * BLOCK)
    window_of = lambda count: pltpu.VMEM((count, height, width), F32)
    grads_a, grads_b, grads_c = call(
        functools.partial(solve_kernel, full, ITERS), (grads,) * 3, [SMEM] + [VMEM] * 11,
        (
            place, rows_at, joined_near, joined_far, driven_near, driven_far, pressure, near, far,
            beyond, constant, factor,
        ),
        [
            window_of(2 * planes), window_of(2 * planes),
            window_of(3 * planes + 2), window_of(3 * planes + 2),
            pltpu.VMEM((planes * zones * height, 3 * BLOCK), F32),
        ],
        flops=2 * planes * height * 4 * 384 * 256 * 6, size=20 * field_bytes,
    )
    grads_b = along_grp(grads_b, -1, owners)
    grads_c = along_grp(grads_c, -2, owners)

    contact = call(
        contact_kernel, shaped(3 * tiles, BLOCK), [SMEM] + [VMEM] * 5 + [ANY],
        (partner_block, state, lower, upper, contact_rows, contact_stiff, grads_a),
        [pltpu.VMEM((3 * (tiles + 2 * rows), BLOCK), F32)],
        flops=60 * 8 * slots, size=4 * 20 * slots,
    )
    return call(
        final_kernel, shaped(3, slots), [SMEM] + [VMEM] * 9,
        (count, grads_a, grads_b, grads_c, weight, contact, grain_vel, vol, drag, cell),
        flops=60 * slots, size=4 * 20 * slots,
    )


def solution(mesh):
    in_specs = (
        P(None, ("grp", "reg")),
        P(None, ("grp", "reg")),
        P(("grp", "reg")),
        P(("grp", "reg")),
        P(("grp", "reg")),
        P(None, ("grp", "reg")),
        P(None, ("grp", "reg")),
        P(("grp", "reg")),
        P(None, ("grp", "reg")),
        P(("grp", "reg")),
        P(("grp", "reg")),
        P("reg", None, None),
        P("reg", None, None),
        P("reg", None, None),
    )
    out_specs = P(None, ("grp", "reg"))
    return jax.shard_map(
        on_device, mesh=mesh, in_specs=in_specs, out_specs=out_specs, check_vma=False
    )
```

```python
import functools

import jax
import jax.numpy as jnp
from jax import lax
from jax.experimental import pallas as pl
from jax.experimental.pallas import tpu as pltpu
from jax.sharding import PartitionSpec as P

BLOCK = 128
SUB = 8
CORES = 2
ITERS = 4
SPRING = 1.0
DAMPING = 0.5
TIME_STEP = 0.5

VMEM = pl.BlockSpec(memory_space=pltpu.VMEM)
SMEM = pl.BlockSpec(memory_space=pltpu.SMEM)
ANY = pl.BlockSpec(memory_space=pl.ANY)
HBM = pl.BlockSpec(memory_space=pltpu.HBM)
F32 = jnp.float32
BF16 = jnp.bfloat16


def iota(shape, dim):
    return lax.broadcasted_iota(jnp.int32, shape, dim)


def shaped(*dims):
    return jax.ShapeDtypeStruct(dims, F32)


def call(kernel, outs, specs, args, scratch=(), flops=0, size=0, limit=40_000_000):
    return pl.pallas_call(
        kernel,
        out_shape=outs,
        in_specs=specs,
        out_specs=jax.tree.map(lambda _: VMEM, outs),
        scratch_shapes=list(scratch),
        compiler_params=pltpu.CompilerParams(vmem_limit_bytes=limit),
        cost_estimate=pl.CostEstimate(flops=flops, bytes_accessed=size, transcendentals=0),
    )(*args)


def lanes_of(source, index):
    return jnp.take_along_axis(source, index, axis=1, mode="promise_in_bounds")


def halves_of(value):
    high = value.astype(BF16)
    return high, (value - high.astype(F32)).astype(BF16)


def window_kernel(place, pressure_old, source, solid_before, window, ends, inner, solid, sems):
    planes, height, _ = solid.shape
    rows = pl.ds(pl.multiple_of(place[0], SUB), height)
    moves = ((pressure_old, window.at[:planes]), (source, window.at[planes:]), (solid_before, solid))
    copies = [
        pltpu.make_async_copy(whole.at[:, rows, :], part, sems.at[index])
        for index, (whole, part) in enumerate(moves)
    ]
    for copy in copies:
        copy.start()
    for copy in copies:
        copy.wait()
    window[planes:] = window[planes:] - solid[...]
    odd = place[1]
    ends[...] = window[odd * (planes - 1)]
    inner[...] = window[(1 - odd) * (planes - 1)]


def forward_kernel(near, inner, _joined, _beyond, out):
    count = near.shape[0]
    out[:count] = near[...]
    out[count] = inner[...]


def deposit_kernel(count, cell, vol, drag, ids, _, out):
    tiles = cell.shape[0]
    sub = iota((SUB, BLOCK), 0)
    rows_c = iota((BLOCK, BLOCK), 0)
    even = sub % 2 == 0
    low_pair = sub % 4 < 2

    def step(group, carry):
        first = pl.multiple_of(group * SUB, SUB)
        slot = (first + sub) * BLOCK + iota((SUB, BLOCK), 1)
        live = slot < count[0]
        cells = cell[pl.ds(first, SUB), :]
        parts = halves_of(jnp.where(live, vol[pl.ds(first, SUB), :], 0.0)) + halves_of(
            jnp.where(live, drag[pl.ds(first, SUB), :], 0.0)
        )
        parts = [part.astype(F32) for part in parts]
        left = jnp.concatenate([jnp.where(even, part, 0.0) for part in parts], 0)
        right = jnp.concatenate([jnp.where(even, 0.0, part) for part in parts], 0)
        loads = jnp.concatenate([left, right], 1).astype(BF16)
        sums = [jnp.zeros((SUB, BLOCK), F32), jnp.zeros((SUB, BLOCK), F32)]
        for quad in range(SUB // 4):
            hot = [
                jnp.where(
                    rows_c == jnp.broadcast_to(cells[t : t + 1, :], (BLOCK, BLOCK)), 1.0, 0.0
                ).astype(BF16)
                for t in range(4 * quad, 4 * quad + 4)
            ]
            picked = jnp.concatenate(
                [jnp.concatenate(hot[:2], 1), jnp.concatenate(hot[2:], 1)], 0
            )
            placed = lax.dot_general(
                loads, picked, (((1,), (1,)), ((), ())), preferred_element_type=F32
            )
            for field in range(2):
                base = field * 2 * SUB
                total = placed[base : base + SUB] + placed[base + SUB : base + 2 * SUB]
                chosen = jnp.where(low_pair, total[:, :BLOCK], total[:, BLOCK:])
                sums[field] = jnp.where(sub // 4 == quad, chosen, sums[field])
        out[pl.ds(first, SUB), :BLOCK] = sums[0]
        out[pl.ds(first, SUB), BLOCK:] = sums[1]
        return carry

    lax.fori_loop(0, tiles // SUB, step, 0, unroll=4)
    out[tiles : tiles + SUB, :BLOCK] = jnp.broadcast_to(ids[...].astype(F32), (SUB, BLOCK))
    out[tiles : tiles + SUB, BLOCK:] = jnp.zeros((SUB, BLOCK), F32)


def halo_kernel(pos, vel, lists, state, down, up):
    tiles = pos.shape[1] // BLOCK
    rows = lists.shape[1] // BLOCK
    for tile in range(tiles):
        lanes = slice(tile * BLOCK, (tile + 1) * BLOCK)
        mixed = SPRING * pos[:, lanes] - DAMPING * vel[:, lanes]
        for axis in range(3):
            state[axis * tiles + tile : axis * tiles + tile + 1, :] = mixed[axis : axis + 1]
    turned = [
        jnp.concatenate(halves_of(jnp.transpose(state[axis * tiles : (axis + 1) * tiles, :])), 1)
        for axis in range(3)
    ]
    turned = jnp.concatenate(turned, 0)
    span = 2 * BLOCK
    row = iota((BLOCK, span), 0)

    for side, out in enumerate((down, up)):

        def step(part, carry):
            named = lists[side : side + 1, pl.ds(pl.multiple_of(part * span, span), span)]
            block = lax.shift_right_logical(named, 7)
            lane = named & (BLOCK - 1)
            hot = jnp.where(row == jnp.broadcast_to(block, row.shape), 1.0, 0.0).astype(BF16)
            found = jnp.dot(
                turned, jnp.concatenate([hot, hot], 0), preferred_element_type=F32
            )
            here = row == jnp.broadcast_to(lane, row.shape)
            for axis in range(3):
                value = jnp.where(here, found[axis * BLOCK : (axis + 1) * BLOCK], 0.0)
                value = jnp.sum(value, axis=0, keepdims=True)
                for half in range(2):
                    out[pl.ds(axis * rows + 2 * part + half, 1), :] = value[
                        :, half * BLOCK : (half + 1) * BLOCK
                    ]
            return carry

        lax.fori_loop(0, rows // 2, step, 0, unroll=4)


def contact_kernel(partner, state, lower, upper, named, stiff, _, out, extended):
    tiles = state.shape[0] // 3
    rows = lower.shape[0] // 3
    blocks = tiles + 2 * rows
    for axis in range(3):
        extended[axis * blocks : axis * blocks + tiles, :] = state[
            axis * tiles : (axis + 1) * tiles, :
        ]
        for place, side in enumerate((lower, upper)):
            first = axis * blocks + tiles + place * rows
            extended[first : first + rows, :] = side[axis * rows : (axis + 1) * rows, :]

    def step(tile, carry):
        lanes = pl.ds(pl.multiple_of(tile * BLOCK, BLOCK), BLOCK)
        entry = named[:, lanes]
        weight = jnp.where(entry >= 0, stiff[:, lanes], 0.0)
        own = entry < BLOCK
        lane = entry & (BLOCK - 1)
        other = partner[tile]
        for axis in range(3):
            mine = jnp.broadcast_to(extended[pl.ds(axis * blocks + tile, 1), :], entry.shape)
            theirs = jnp.broadcast_to(extended[pl.ds(axis * blocks + other, 1), :], entry.shape)
            met = jnp.where(own, lanes_of(mine, lane), lanes_of(theirs, lane))
            pull = jnp.sum(weight * (mine - met), axis=0, keepdims=True)
            out[pl.ds(axis * tiles + tile, 1), :] = pull
        return carry

    lax.fori_loop(0, tiles, step, 0, unroll=4)


def shifted(plane):
    height, width = plane.shape
    row = iota(plane.shape, 0)
    column = iota(plane.shape, 1)
    above = jnp.where(row == 0, 0.0, pltpu.roll(plane, 1, 0))
    below = jnp.where(row == height - 1, 0.0, pltpu.roll(plane, height - 1, 0))
    left = jnp.where(column == 0, 0.0, pltpu.roll(plane, 1, 1))
    right = jnp.where(column == width - 1, 0.0, pltpu.roll(plane, width - 1, 1))
    return above, below, left, right


def inverse_of(value):
    near = pl.reciprocal(value, approx=True)
    return near * (2.0 - value * near)


def placed(joined, tiles):
    stride = tiles + SUB
    groups = [joined.at[i * stride : (i + 1) * stride] for i in range(joined.shape[0] // stride)]
    parts = [halves_of(group[:tiles, :]) for group in groups]
    loads = jnp.concatenate([part[i] for i in range(2) for part in parts], 0)
    ids = jnp.concatenate([group[tiles : tiles + 1, :BLOCK] for group in groups], 1)
    ids = ids.astype(jnp.int32)

    def gathered(wanted):
        hot = jnp.where(wanted == jnp.broadcast_to(ids, wanted.shape), 1.0, 0.0).astype(BF16)
        total = jnp.dot(
            jnp.concatenate([hot, hot], 1), loads, preferred_element_type=F32
        )
        return total[:, :BLOCK], total[:, BLOCK:]

    return ids, gathered


def coefficients(gathered, tiles, first, full, driven, planes, constant, factor, base, present):
    _, height, width = driven.shape
    zones = width // BLOCK
    shape = (zones * height, 3 * tiles)
    line = iota(shape, 0)
    block = (line % height) * zones + line // height + first * zones

    for x in range(planes):
        solid, drag = gathered(block + x * (full * zones))
        voids = 1.0 + solid
        scale = inverse_of(6.0 + (drag + 1.0) * voids)
        if present is not None:
            scale = jnp.where(present, scale, 0.0)
        inverse = voids * scale
        for zone in range(zones):
            lanes = slice(zone * BLOCK, (zone + 1) * BLOCK)
            rows = slice(zone * height, (zone + 1) * height)
            driving = driven[planes + x, :, lanes] + solid[rows]
            constant[base + x, :, lanes] = driving * inverse[rows]
            factor[base + x, :, lanes] = scale[rows]


def own_kernel(full, own_rows, place, joined, window, _, constant, factor, weight, rows_at):
    tiles = weight.shape[0]
    planes, height, width = constant.shape
    zones = width // BLOCK
    ids, gathered = placed(joined, tiles)
    coefficients(gathered, tiles, place[0], full, window, planes, constant, factor, 0, None)
    turned = [
        jnp.transpose(
            jnp.broadcast_to(ids[:, i * tiles : (i + 1) * tiles], (BLOCK, tiles)).astype(F32)
        ).astype(jnp.int32)
        for i in range(3)
    ]

    def before(places):
        index = lax.rem(place[5] + 3 - places, 3)
        return jnp.where(index == 0, turned[0], jnp.where(index == 1, turned[1], turned[2]))

    solid, drag = gathered(jnp.concatenate([before(0)] * 3, 1))
    weight[...] = 1.0 / (1.0 / (1.0 + solid) + drag)
    for i in range(3):
        block = before(i)
        line, zone = block // zones, block % zones
        x, y = line // full, line % full
        row = (x * zones + zone) * height + y - place[0]
        rows_at[i * tiles : (i + 1) * tiles, :] = jnp.where(y // own_rows == place[4], row, -1)


def solve_kernel(
    full, sweeps, place, rows_at, joined_near, joined_far, window, near, far, beyond,
    own_constant, own_factor, _lower, _upper, out_a, out_b, out_c,
    constant, factor, old, new, fields,
):
    planes, height, width = own_constant.shape
    zones = width // BLOCK
    tiles = joined_near.shape[0] // 3 - SUB
    odd = place[1] == 1
    rim = sweeps + 1
    for joined, driven, below, present in (
        (joined_near, near, odd, jnp.where(odd, place[2], place[3])),
        (joined_far, far, jnp.logical_not(odd), jnp.where(odd, place[3], place[2])),
    ):
        _, gathered = placed(joined, tiles)
        coefficients(
            gathered, tiles, place[0], full, driven, planes, constant, factor,
            jnp.where(below, 0, planes), present == 1,
        )
    old[pl.ds(jnp.where(odd, 1, rim + planes), planes)] = near[:planes]
    old[pl.ds(jnp.where(odd, rim + planes, 1), planes)] = far[:planes]
    old[pl.ds(jnp.where(odd, rim + 2 * planes, 0), 1)] = far[2 * planes :]
    old[pl.ds(jnp.where(odd, 0, rim + 2 * planes), 1)] = beyond[...][None]
    old[rim : rim + planes] = window[:planes]

    def sweep(source, target, depth):
        def over(constants, factors, shift):
            def plane(x, carry):
                centre = source[x]
                above, below, left, right = shifted(centre)
                around = source[x - 1] + source[x + 1] + above + below + left + right
                target[x] = constants[x - shift] + factors[x - shift] * around
                return carry

            return plane

        lax.fori_loop(depth, rim, over(constant, factor, 1), 0, unroll=2)
        lax.fori_loop(rim, rim + planes, over(own_constant, own_factor, rim), 0, unroll=2)
        lax.fori_loop(
            rim + planes, 3 * planes + 2 - depth, over(constant, factor, 1 + planes), 0, unroll=2
        )

    for index in range(sweeps):
        source, target = (old, new) if index % 2 == 0 else (new, old)
        sweep(source, target, index + 1)
    last = old if sweeps % 2 == 0 else new

    def gradient(x, carry):
        centre = last[rim + x]
        above, below, left, right = shifted(centre)
        grads = (last[rim + x + 1] - last[rim + x - 1], below - above, right - left)
        for zone in range(zones):
            first = pl.multiple_of((x * zones + zone) * height, SUB)
            for axis, grad in enumerate(grads):
                fields[pl.ds(first, height), axis * BLOCK : (axis + 1) * BLOCK] = (
                    0.5 * grad[:, zone * BLOCK : (zone + 1) * BLOCK]
                )
        return carry

    lax.fori_loop(0, planes, gradient, 0, unroll=2)
    wanted = jnp.concatenate([rows_at[...]] * (planes * zones * height // BLOCK), 1)
    hot = jnp.where(wanted == iota(wanted.shape, 1), 1.0, 0.0).astype(BF16)
    pieces = jnp.concatenate(halves_of(fields[...]), 1)
    total = jnp.dot(hot, pieces, preferred_element_type=F32)
    total = total[:, : 3 * BLOCK] + total[:, 3 * BLOCK :]
    for index, out in enumerate((out_a, out_b, out_c)):
        out[...] = total[index * tiles : (index + 1) * tiles]


def final_kernel(
    count, grads_a, grads_b, grads_c, weight, contact, vel, vol, drag, cell, out,
):
    tiles = cell.shape[0]
    cells = cell[...]
    heft = lanes_of(weight[...], cells)
    slot = iota(cells.shape, 0) * BLOCK + iota(cells.shape, 1)
    live = slot < count[0]
    volume = vol[...]
    push = TIME_STEP / volume
    for axis in range(3):
        lanes = slice(axis * BLOCK, (axis + 1) * BLOCK)
        gradient = lanes_of(grads_a[:, lanes] + grads_b[:, lanes] + grads_c[:, lanes], cells)
        own = jnp.concatenate(
            [vel[axis : axis + 1, t * BLOCK : (t + 1) * BLOCK] for t in range(tiles)], 0
        )
        fluid = -gradient * heft
        force = contact[axis * tiles : (axis + 1) * tiles, :] - volume * gradient
        force = force + drag[...] * (fluid - own)
        new = jnp.where(live, own + force * push, 0.0)
        for t in range(tiles):
            out[axis : axis + 1, t * BLOCK : (t + 1) * BLOCK] = new[t : t + 1, :]


def on_device(
    grain_pos,
    grain_vel,
    grain_vol,
    drag_coef,
    grain_count,
    contact_rows,
    contact_stiff,
    partner_block,
    halo_list,
    grain_cell,
    tile_cell_block,
    pressure_old,
    pressure_source,
    solid_old,
):
    groups, regions = lax.axis_size("grp"), lax.axis_size("reg")
    holding = groups - 1
    halves = groups // CORES
    slots = grain_pos.shape[1]
    tiles = slots // BLOCK
    planes, full, width = pressure_old.shape
    zones = width // BLOCK
    own_rows = full // halves
    height = min(full, own_rows + SUB * min(2, halves - 1))
    group, region = lax.axis_index("grp"), lax.axis_index("reg")
    half = group // CORES
    first = jnp.clip(half * own_rows - SUB, 0, full - height)
    odd = region % 2 == 1
    place = jnp.stack(
        [first, odd, region > 0, region < regions - 1, jnp.where(group % CORES == 0, half, -1), group]
    ).astype(jnp.int32)
    owners = range(0, groups, CORES)
    holders = range(holding)

    def send(value, pairs):
        flat = [(a[0] * regions + a[1], b[0] * regions + b[1]) for a, b in pairs]
        return lax.ppermute(value, ("grp", "reg"), flat)

    def along_reg(value, members, goes):
        pairs = [
            ((g, r), (g, r + goes[r % 2]))
            for g in members
            for r in range(regions)
            if 0 <= r + goes[r % 2] < regions
        ]
        return send(value, pairs)

    def along_grp(value, step, members):
        pairs = [((g, r), ((g + step) % holding, r)) for g in members for r in range(regions)]
        return send(value, pairs)

    count = grain_count
    cell = grain_cell.reshape(tiles, BLOCK)
    vol = grain_vol.reshape(tiles, BLOCK)
    drag = drag_coef.reshape(tiles, BLOCK)
    ids = tile_cell_block.reshape(1, tiles)
    field_bytes = 4 * planes * height * width

    field = shaped(planes, height, width)
    plane = shaped(height, width)
    window, ends, inner = call(
        window_kernel, (shaped(2 * planes, height, width), plane, plane), [SMEM] + [HBM] * 3,
        (place, pressure_old, pressure_source, solid_old),
        [pltpu.VMEM((planes, height, width), F32), pltpu.SemaphoreType.DMA((3,))],
        flops=field_bytes, size=6 * field_bytes, limit=61_500_000,
    )
    near = along_reg(window, owners, (1, -1))
    mine = call(
        deposit_kernel, shaped(tiles + SUB, 2 * BLOCK), [SMEM] + [VMEM] * 4 + [ANY],
        (count, cell, vol, drag, ids, ends), flops=2 * 32 * 48 * 65536, size=5 * 4 * slots,
    )
    joined = lax.all_gather(mine, "grp")
    joined = joined[:holding].reshape(holding * (tiles + SUB), 2 * BLOCK)
    joined_near = along_reg(joined, owners, (1, -1))
    joined_far = along_reg(joined, owners, (-1, 1))
    beyond = along_reg(ends, owners, (-2, 2))
    far = along_reg(
        call(
            forward_kernel, shaped(2 * planes + 1, height, width), [VMEM] * 2 + [ANY] * 2,
            (near, inner, joined, beyond),
            size=5 * field_bytes,
        ),
        owners, (2, -2),
    )

    rows = halo_list.shape[1] // BLOCK
    state, down, up = call(
        halo_kernel, (shaped(3 * tiles, BLOCK), shaped(3 * rows, BLOCK), shaped(3 * rows, BLOCK)),
        [VMEM] * 3, (grain_pos, grain_vel, halo_list), flops=8 * 3 * 16384 * 128, size=4 * 4 * 3 * slots,
    )
    lower = along_reg(up, holders, (1, 1))
    upper = along_reg(down, holders, (-1, -1))

    constant, factor, weight, rows_at = call(
        functools.partial(own_kernel, full, own_rows),
        (
            field, field, shaped(tiles, BLOCK),
            jax.ShapeDtypeStruct((3 * tiles, BLOCK), jnp.int32),
        ),
        [SMEM] + [VMEM] * 2 + [ANY], (place, joined, window, state),
        flops=planes * height * 4 * 384 * 256 * 6, size=9 * field_bytes,
    )

    grads = shaped(tiles, 3 * BLOCK)
    window_of = lambda count: pltpu.VMEM((count, height, width), F32)
    grads_a, grads_b, grads_c = call(
        functools.partial(solve_kernel, full, ITERS), (grads,) * 3,
        [SMEM] + [VMEM] * 9 + [ANY] * 2,
        (
            place, rows_at, joined_near, joined_far, window, near, far, beyond, constant, factor,
            lower, upper,
        ),
        [
            window_of(2 * planes), window_of(2 * planes),
            window_of(3 * planes + 2), window_of(3 * planes + 2),
            pltpu.VMEM((planes * zones * height, 3 * BLOCK), F32),
        ],
        flops=2 * planes * height * 4 * 384 * 256 * 6, size=20 * field_bytes,
    )
    grads_b = along_grp(grads_b, -1, owners)
    grads_c = along_grp(grads_c, -2, owners)

    contact = call(
        contact_kernel, shaped(3 * tiles, BLOCK), [SMEM] + [VMEM] * 5 + [ANY],
        (partner_block, state, lower, upper, contact_rows, contact_stiff, grads_a),
        [pltpu.VMEM((3 * (tiles + 2 * rows), BLOCK), F32)],
        flops=60 * 8 * slots, size=4 * 20 * slots,
    )
    return call(
        final_kernel, shaped(3, slots), [SMEM] + [VMEM] * 9,
        (count, grads_a, grads_b, grads_c, weight, contact, grain_vel, vol, drag, cell),
        flops=60 * slots, size=4 * 20 * slots,
    )


def solution(mesh):
    in_specs = (
        P(None, ("grp", "reg")),
        P(None, ("grp", "reg")),
        P(("grp", "reg")),
        P(("grp", "reg")),
        P(("grp", "reg")),
        P(None, ("grp", "reg")),
        P(None, ("grp", "reg")),
        P(("grp", "reg")),
        P(None, ("grp", "reg")),
        P(("grp", "reg")),
        P(("grp", "reg")),
        P("reg", None, None),
        P("reg", None, None),
        P("reg", None, None),
    )
    out_specs = P(None, ("grp", "reg"))
    return jax.shard_map(
        on_device, mesh=mesh, in_specs=in_specs, out_specs=out_specs, check_vma=False
    )
```

```python
import functools

import jax
import jax.numpy as jnp
from jax import lax
from jax.experimental import pallas as pl
from jax.experimental.pallas import tpu as pltpu
from jax.sharding import PartitionSpec as P

BLOCK = 128
SUB = 8
CORES = 2
ITERS = 4
SPRING = 1.0
DAMPING = 0.5
TIME_STEP = 0.5

VMEM = pl.BlockSpec(memory_space=pltpu.VMEM)
SMEM = pl.BlockSpec(memory_space=pltpu.SMEM)
ANY = pl.BlockSpec(memory_space=pl.ANY)
HBM = pl.BlockSpec(memory_space=pltpu.HBM)
F32 = jnp.float32
BF16 = jnp.bfloat16


def iota(shape, dim):
    return lax.broadcasted_iota(jnp.int32, shape, dim)


def shaped(*dims):
    return jax.ShapeDtypeStruct(dims, F32)


def call(kernel, outs, specs, args, scratch=(), flops=0, size=0, limit=40_000_000):
    return pl.pallas_call(
        kernel,
        out_shape=outs,
        in_specs=specs,
        out_specs=jax.tree.map(lambda _: VMEM, outs),
        scratch_shapes=list(scratch),
        compiler_params=pltpu.CompilerParams(vmem_limit_bytes=limit),
        cost_estimate=pl.CostEstimate(flops=flops, bytes_accessed=size, transcendentals=0),
    )(*args)


class Place:
    def __init__(self, full, height):
        groups, regions = lax.axis_size("grp"), lax.axis_size("reg")
        self.group, region = lax.axis_index("grp"), lax.axis_index("reg")
        self.half = self.group // CORES
        self.own_rows = full // (groups // CORES)
        first = jnp.clip(self.half * self.own_rows - SUB, 0, full - height)
        self.first = pl.multiple_of(first, SUB)
        self.sweeps = self.group % CORES == 0
        self.parity = region % 2
        self.odd = self.parity == 1
        self.lower, self.upper = region > 0, region < regions - 1


def lanes_of(source, index):
    return jnp.take_along_axis(source, index, axis=1, mode="promise_in_bounds")


def halves_of(value):
    high = value.astype(BF16)
    return high, (value - high.astype(F32)).astype(BF16)


def window_kernel(pressure_old, source, solid_before, window, ends, inner, dummy, solid, sems):
    planes, height, _ = solid.shape
    place = Place(pressure_old.shape[1], height)
    rows = pl.ds(place.first, height)
    copies = []
    for x in range(planes):
        for whole, part in (
            (pressure_old, window.at[x]), (source, window.at[planes + x]), (solid_before, solid.at[x])
        ):
            copies.append(
                pltpu.make_async_copy(whole.at[x, rows, :], part, sems.at[len(copies)])
            )
    for copy in copies:
        copy.start()
    dummy[...] = jnp.zeros(dummy.shape, F32)
    for copy in copies:
        copy.wait()
    window[planes:] = window[planes:] - solid[...]
    ends[...] = window[place.parity * (planes - 1)]
    inner[...] = window[(1 - place.parity) * (planes - 1)]


def forward_kernel(near, inner, _joined, _beyond, out):
    count = near.shape[0]
    out[:count] = near[...]
    out[count] = inner[...]


def deposit_kernel(count, cell, vol, drag, ids, _, out):
    tiles = cell.shape[0]
    sub = iota((SUB, BLOCK), 0)
    rows_c = iota((BLOCK, BLOCK), 0)
    even = sub % 2 == 0
    low_pair = sub % 4 < 2

    def step(group, carry):
        first = pl.multiple_of(group * SUB, SUB)
        slot = (first + sub) * BLOCK + iota((SUB, BLOCK), 1)
        live = slot < count[0]
        cells = cell[pl.ds(first, SUB), :]
        parts = halves_of(jnp.where(live, vol[pl.ds(first, SUB), :], 0.0)) + halves_of(
            jnp.where(live, drag[pl.ds(first, SUB), :], 0.0)
        )
        parts = [part.astype(F32) for part in parts]
        left = jnp.concatenate([jnp.where(even, part, 0.0) for part in parts], 0)
        right = jnp.concatenate([jnp.where(even, 0.0, part) for part in parts], 0)
        loads = jnp.concatenate([left, right], 1).astype(BF16)
        sums = [jnp.zeros((SUB, BLOCK), F32), jnp.zeros((SUB, BLOCK), F32)]
        for quad in range(SUB // 4):
            hot = [
                jnp.where(
                    rows_c == jnp.broadcast_to(cells[t : t + 1, :], (BLOCK, BLOCK)), 1.0, 0.0
                ).astype(BF16)
                for t in range(4 * quad, 4 * quad + 4)
            ]
            picked = jnp.concatenate(
                [jnp.concatenate(hot[:2], 1), jnp.concatenate(hot[2:], 1)], 0
            )
            placed = lax.dot_general(
                loads, picked, (((1,), (1,)), ((), ())), preferred_element_type=F32
            )
            for field in range(2):
                base = field * 2 * SUB
                total = placed[base : base + SUB] + placed[base + SUB : base + 2 * SUB]
                chosen = jnp.where(low_pair, total[:, :BLOCK], total[:, BLOCK:])
                sums[field] = jnp.where(sub // 4 == quad, chosen, sums[field])
        out[pl.ds(first, SUB), :BLOCK] = sums[0]
        out[pl.ds(first, SUB), BLOCK:] = sums[1]
        return carry

    lax.fori_loop(0, tiles // SUB, step, 0, unroll=4)
    out[tiles : tiles + SUB, :BLOCK] = jnp.broadcast_to(ids[...].astype(F32), (SUB, BLOCK))
    out[tiles : tiles + SUB, BLOCK:] = jnp.zeros((SUB, BLOCK), F32)


def halo_kernel(pos, vel, lists, _, state, near, far, dummy):
    dummy[...] = jnp.zeros(dummy.shape, F32)
    tiles = pos.shape[1] // BLOCK
    rows = lists.shape[1] // BLOCK
    for tile in range(tiles):
        lanes = slice(tile * BLOCK, (tile + 1) * BLOCK)
        mixed = SPRING * pos[:, lanes] - DAMPING * vel[:, lanes]
        for axis in range(3):
            state[axis * tiles + tile : axis * tiles + tile + 1, :] = mixed[axis : axis + 1]
    turned = [
        jnp.concatenate(halves_of(jnp.transpose(state[axis * tiles : (axis + 1) * tiles, :])), 1)
        for axis in range(3)
    ]
    turned = jnp.concatenate(turned, 0)
    span = 2 * BLOCK
    row = iota((BLOCK, span), 0)

    odd = lax.axis_index("reg") % 2
    for away, out in enumerate((near, far)):
        side = 1 - odd if away == 0 else odd

        def step(part, carry):
            named = lists[:, pl.ds(pl.multiple_of(part * span, span), span)]
            named = jnp.where(side == 0, named[:1], named[1:])
            block = lax.shift_right_logical(named, 7)
            lane = named & (BLOCK - 1)
            hot = jnp.where(row == jnp.broadcast_to(block, row.shape), 1.0, 0.0).astype(BF16)
            found = jnp.dot(
                turned, jnp.concatenate([hot, hot], 0), preferred_element_type=F32
            )
            here = row == jnp.broadcast_to(lane, row.shape)
            for axis in range(3):
                value = jnp.where(here, found[axis * BLOCK : (axis + 1) * BLOCK], 0.0)
                value = jnp.sum(value, axis=0, keepdims=True)
                for half in range(2):
                    out[pl.ds(axis * rows + 2 * part + half, 1), :] = value[
                        :, half * BLOCK : (half + 1) * BLOCK
                    ]
            return carry

        lax.fori_loop(0, rows // 2, step, 0, unroll=4)


def message_kernel(joined, halo_near, halo_far, near, far):
    half = halo_near.shape[0] // 2
    rows = near.shape[0] - half
    for halo, out in ((halo_near, near), (halo_far, far)):
        out[:rows, :] = joined[:rows, :]
        out[rows:, :BLOCK] = halo[:half, :]
        out[rows:, BLOCK:] = halo[half:, :]


def contact_kernel(
    partner, state, message_near, message_far, halo_near, halo_far, named, stiff, _, out, extended
):
    tiles = state.shape[0] // 3
    rows = halo_near.shape[0] // 3
    blocks = tiles + 2 * rows
    base = message_near.shape[0] - 3 * rows // 2
    odd = lax.axis_index("reg") % 2
    sweeps = lax.axis_index("grp") % CORES == 0
    for axis in range(3):
        extended[axis * blocks : axis * blocks + tiles, :] = state[
            axis * tiles : (axis + 1) * tiles, :
        ]
    for message, halo, upper in (
        (message_near, halo_near, 1 - odd), (message_far, halo_far, odd)
    ):
        carried = jnp.concatenate([message[base:, :BLOCK], message[base:, BLOCK:]], 0)
        carried = jnp.where(sweeps, carried, halo[...])
        for axis in range(3):
            first = pl.multiple_of(axis * blocks + tiles + upper * rows, SUB)
            extended[pl.ds(first, rows), :] = carried[axis * rows : (axis + 1) * rows]

    def step(tile, carry):
        lanes = pl.ds(pl.multiple_of(tile * BLOCK, BLOCK), BLOCK)
        entry = named[:, lanes]
        weight = jnp.where(entry >= 0, stiff[:, lanes], 0.0)
        own = entry < BLOCK
        lane = entry & (BLOCK - 1)
        other = partner[tile]
        for axis in range(3):
            mine = jnp.broadcast_to(extended[pl.ds(axis * blocks + tile, 1), :], entry.shape)
            theirs = jnp.broadcast_to(extended[pl.ds(axis * blocks + other, 1), :], entry.shape)
            met = jnp.where(own, lanes_of(mine, lane), lanes_of(theirs, lane))
            pull = jnp.sum(weight * (mine - met), axis=0, keepdims=True)
            out[pl.ds(axis * tiles + tile, 1), :] = pull
        return carry

    lax.fori_loop(0, tiles, step, 0, unroll=4)


def shifted(plane):
    height, width = plane.shape
    row = iota((SUB, width), 0)
    column = iota((height, BLOCK), 1)
    above, below = pltpu.roll(plane, 1, 0), pltpu.roll(plane, height - 1, 0)
    left, right = pltpu.roll(plane, 1, 1), pltpu.roll(plane, width - 1, 1)
    above = jnp.concatenate([jnp.where(row == 0, 0.0, above[:SUB]), above[SUB:]], 0)
    below = jnp.concatenate([below[:-SUB], jnp.where(row == SUB - 1, 0.0, below[-SUB:])], 0)
    left = jnp.concatenate([jnp.where(column == 0, 0.0, left[:, :BLOCK]), left[:, BLOCK:]], 1)
    right = jnp.concatenate(
        [right[:, :-BLOCK], jnp.where(column == BLOCK - 1, 0.0, right[:, -BLOCK:])], 1
    )
    return above, below, left, right


def inverse_of(value):
    near = pl.reciprocal(value, approx=True)
    return near * (2.0 - value * near)


def placed(joined, tiles):
    stride = tiles + SUB
    groups = [joined.at[i * stride : (i + 1) * stride] for i in range(3)]
    parts = [halves_of(group[:tiles, :]) for group in groups]
    loads = jnp.concatenate([part[i] for i in range(2) for part in parts], 0)
    ids = jnp.concatenate([group[tiles : tiles + 1, :BLOCK] for group in groups], 1)
    ids = ids.astype(jnp.int32)

    def gathered(wanted):
        hot = jnp.where(wanted == jnp.broadcast_to(ids, wanted.shape), 1.0, 0.0).astype(BF16)
        total = jnp.dot(
            jnp.concatenate([hot, hot], 1), loads, preferred_element_type=F32
        )
        return total[:, :BLOCK], total[:, BLOCK:]

    return ids, gathered


def coefficients(gathered, tiles, first, full, driven, planes, constant, factor, base, present):
    _, height, width = driven.shape
    zones = width // BLOCK
    shape = (zones * height, 3 * tiles)
    line = iota(shape, 0)
    block = (line % height) * zones + line // height + first * zones

    for x in range(planes):
        solid, drag = gathered(block + x * (full * zones))
        voids = 1.0 + solid
        scale = inverse_of(6.0 + (drag + 1.0) * voids)
        if present is not None:
            scale = jnp.where(present, scale, 0.0)
        inverse = voids * scale
        for zone in range(zones):
            lanes = slice(zone * BLOCK, (zone + 1) * BLOCK)
            rows = slice(zone * height, (zone + 1) * height)
            driving = driven[planes + x, :, lanes] + solid[rows]
            constant[base + x, :, lanes] = driving * inverse[rows]
            factor[base + x, :, lanes] = scale[rows]


def own_kernel(full, joined, window, _, constant, factor, weight, rows_at):
    tiles = weight.shape[0]
    planes, height, width = constant.shape
    place = Place(full, height)
    zones = width // BLOCK
    ids, gathered = placed(joined, tiles)
    coefficients(gathered, tiles, place.first, full, window, planes, constant, factor, 0, None)
    turned = [
        jnp.transpose(
            jnp.broadcast_to(ids[:, i * tiles : (i + 1) * tiles], (BLOCK, tiles)).astype(F32)
        ).astype(jnp.int32)
        for i in range(3)
    ]

    def before(places):
        index = lax.rem(place.group + 3 - places, 3)
        return jnp.where(index == 0, turned[0], jnp.where(index == 1, turned[1], turned[2]))

    solid, drag = gathered(jnp.concatenate([before(0)] * 3, 1))
    weight[...] = 1.0 / (1.0 / (1.0 + solid) + drag)
    for i in range(3):
        block = before(i)
        line, zone = block // zones, block % zones
        x, y = line // full, line % full
        row = (x * zones + zone) * height + y - place.first
        held = y // place.own_rows == jnp.where(place.sweeps, place.half, -1)
        rows_at[i * tiles : (i + 1) * tiles, :] = jnp.where(held, row, -1)


def solve_kernel(
    full, sweeps, rows_at, joined_near, joined_far, window, near, far, beyond,
    own_constant, own_factor, _near, _far, out_a, out_b, out_c,
    constant, factor, old, new, fields,
):
    planes, height, width = own_constant.shape
    zones = width // BLOCK
    tiles = out_a.shape[0]
    place = Place(full, height)
    odd = place.odd
    rim = sweeps + 1
    for joined, driven, below, present in (
        (joined_near, near, odd, jnp.where(odd, place.lower, place.upper)),
        (joined_far, far, jnp.logical_not(odd), jnp.where(odd, place.upper, place.lower)),
    ):
        _, gathered = placed(joined, tiles)
        coefficients(
            gathered, tiles, place.first, full, driven, planes, constant, factor,
            jnp.where(below, 0, planes), present,
        )
    old[pl.ds(jnp.where(odd, 1, rim + planes), planes)] = near[:planes]
    old[pl.ds(jnp.where(odd, rim + planes, 1), planes)] = far[:planes]
    old[pl.ds(jnp.where(odd, rim + 2 * planes, 0), 1)] = far[2 * planes :]
    old[pl.ds(jnp.where(odd, 0, rim + 2 * planes), 1)] = beyond[...][None]
    old[rim : rim + planes] = window[:planes]

    def sweep(source, target, depth):
        def over(constants, factors, shift):
            def plane(x, carry):
                centre = source[x]
                above, below, left, right = shifted(centre)
                around = source[x - 1] + source[x + 1] + above + below + left + right
                target[x] = constants[x - shift] + factors[x - shift] * around
                return carry

            return plane

        lax.fori_loop(depth, rim, over(constant, factor, 1), 0, unroll=2)
        lax.fori_loop(rim, rim + planes, over(own_constant, own_factor, rim), 0, unroll=2)
        lax.fori_loop(
            rim + planes, 3 * planes + 2 - depth, over(constant, factor, 1 + planes), 0, unroll=2
        )

    for index in range(sweeps):
        source, target = (old, new) if index % 2 == 0 else (new, old)
        sweep(source, target, index + 1)
    last = old if sweeps % 2 == 0 else new

    def gradient(x, carry):
        centre = last[rim + x]
        above, below, left, right = shifted(centre)
        grads = (last[rim + x + 1] - last[rim + x - 1], below - above, right - left)
        for zone in range(zones):
            first = pl.multiple_of((x * zones + zone) * height, SUB)
            for axis, grad in enumerate(grads):
                fields[pl.ds(first, height), axis * BLOCK : (axis + 1) * BLOCK] = (
                    0.5 * grad[:, zone * BLOCK : (zone + 1) * BLOCK]
                )
        return carry

    lax.fori_loop(0, planes, gradient, 0, unroll=2)
    wanted = jnp.concatenate([rows_at[...]] * (planes * zones * height // BLOCK), 1)
    hot = jnp.where(wanted == iota(wanted.shape, 1), 1.0, 0.0).astype(BF16)
    pieces = jnp.concatenate(halves_of(fields[...]), 1)
    total = jnp.dot(hot, pieces, preferred_element_type=F32)
    total = total[:, : 3 * BLOCK] + total[:, 3 * BLOCK :]
    for index, out in enumerate((out_a, out_b, out_c)):
        out[...] = total[index * tiles : (index + 1) * tiles]


def final_kernel(
    count, grads_a, grads_b, grads_c, weight, contact, vel, vol, drag, cell, out,
):
    tiles = cell.shape[0]
    cells = cell[...]
    heft = lanes_of(weight[...], cells)
    slot = iota(cells.shape, 0) * BLOCK + iota(cells.shape, 1)
    live = slot < count[0]
    volume = vol[...]
    push = TIME_STEP / volume
    for axis in range(3):
        lanes = slice(axis * BLOCK, (axis + 1) * BLOCK)
        gradient = lanes_of(grads_a[:, lanes] + grads_b[:, lanes] + grads_c[:, lanes], cells)
        own = jnp.concatenate(
            [vel[axis : axis + 1, t * BLOCK : (t + 1) * BLOCK] for t in range(tiles)], 0
        )
        fluid = -gradient * heft
        force = contact[axis * tiles : (axis + 1) * tiles, :] - volume * gradient
        force = force + drag[...] * (fluid - own)
        new = jnp.where(live, own + force * push, 0.0)
        for t in range(tiles):
            out[axis : axis + 1, t * BLOCK : (t + 1) * BLOCK] = new[t : t + 1, :]


def on_device(
    grain_pos,
    grain_vel,
    grain_vol,
    drag_coef,
    grain_count,
    contact_rows,
    contact_stiff,
    partner_block,
    halo_list,
    grain_cell,
    tile_cell_block,
    pressure_old,
    pressure_source,
    solid_old,
):
    groups, regions = lax.axis_size("grp"), lax.axis_size("reg")
    holding = groups - 1
    halves = groups // CORES
    slots = grain_pos.shape[1]
    tiles = slots // BLOCK
    planes, full, width = pressure_old.shape
    zones = width // BLOCK
    own_rows = full // halves
    height = min(full, own_rows + SUB * min(2, halves - 1))
    owners = range(0, groups, CORES)
    holders = range(holding)

    def send(value, pairs):
        flat = [(a[0] * regions + a[1], b[0] * regions + b[1]) for a, b in pairs]
        return lax.ppermute(value, ("grp", "reg"), flat)

    def along_reg(value, members, goes):
        pairs = [
            ((g, r), (g, r + goes[r % 2]))
            for g in members
            for r in range(regions)
            if 0 <= r + goes[r % 2] < regions
        ]
        return send(value, pairs)

    def along_grp(value, step, members):
        pairs = [((g, r), ((g + step) % holding, r)) for g in members for r in range(regions)]
        return send(value, pairs)

    count = grain_count
    cell = grain_cell.reshape(tiles, BLOCK)
    vol = grain_vol.reshape(tiles, BLOCK)
    drag = drag_coef.reshape(tiles, BLOCK)
    ids = tile_cell_block.reshape(1, tiles)
    field_bytes = 4 * planes * height * width

    field = shaped(planes, height, width)
    plane = shaped(height, width)
    window, ends, inner, dummy = call(
        window_kernel, (shaped(2 * planes, height, width), plane, plane, shaped(SUB, BLOCK)),
        [HBM] * 3, (pressure_old, pressure_source, solid_old),
        [pltpu.VMEM((planes, height, width), F32), pltpu.SemaphoreType.DMA((3 * planes,))],
        flops=field_bytes, size=6 * field_bytes, limit=61_500_000,
    )
    near = along_reg(window, owners, (1, -1))
    rows = halo_list.shape[1] // BLOCK
    halo = shaped(3 * rows, BLOCK)
    state, halo_near, halo_far, after_halo = call(
        halo_kernel, (shaped(3 * tiles, BLOCK), halo, halo, shaped(SUB, BLOCK)),
        [VMEM] * 4, (grain_pos, grain_vel, halo_list, dummy), flops=8 * 3 * 16384 * 128,
        size=4 * 4 * 3 * slots,
    )
    mine = call(
        deposit_kernel, shaped(tiles + SUB, 2 * BLOCK), [SMEM] + [VMEM] * 5,
        (count, cell, vol, drag, ids, after_halo), flops=2 * 32 * 48 * 65536, size=5 * 4 * slots,
    )
    joined = lax.all_gather(mine, "grp")
    joined = joined.reshape(groups * (tiles + SUB), 2 * BLOCK)
    message = shaped(holding * (tiles + SUB) + 3 * rows // 2, 2 * BLOCK)
    message_near, message_far = call(
        message_kernel, (message,) * 2, [VMEM] * 3, (joined, halo_near, halo_far),
        size=8 * 2 * BLOCK * 500,
    )
    message_near = along_reg(message_near, owners, (1, -1))
    message_far = along_reg(message_far, owners, (-1, 1))
    beyond = along_reg(ends, owners, (-2, 2))
    far = along_reg(
        call(
            forward_kernel, shaped(2 * planes + 1, height, width), [VMEM] * 2 + [ANY] * 2,
            (near, inner, joined, beyond),
            size=5 * field_bytes,
        ),
        owners, (2, -2),
    )

    others = [g for g in holders if g not in owners]
    halo_near = along_reg(halo_near, others, (1, -1))
    halo_far = along_reg(halo_far, others, (-1, 1))
    constant, factor, weight, rows_at = call(
        functools.partial(own_kernel, full),
        (
            field, field, shaped(tiles, BLOCK),
            jax.ShapeDtypeStruct((3 * tiles, BLOCK), jnp.int32),
        ),
        [VMEM] * 3, (joined, window, dummy),
        flops=planes * height * 4 * 384 * 256 * 6, size=9 * field_bytes,
    )

    grads = shaped(tiles, 3 * BLOCK)
    window_of = lambda count: pltpu.VMEM((count, height, width), F32)
    grads_a, grads_b, grads_c = call(
        functools.partial(solve_kernel, full, ITERS), (grads,) * 3,
        [VMEM] * 9 + [ANY] * 2,
        (
            rows_at, message_near, message_far, window, near, far, beyond, constant, factor,
            halo_near, halo_far,
        ),
        [
            window_of(2 * planes), window_of(2 * planes),
            window_of(3 * planes + 2), window_of(3 * planes + 2),
            pltpu.VMEM((planes * zones * height, 3 * BLOCK), F32),
        ],
        flops=2 * planes * height * 4 * 384 * 256 * 6, size=20 * field_bytes,
    )
    grads_b = along_grp(grads_b, -1, owners)
    grads_c = along_grp(grads_c, -2, owners)

    contact = call(
        contact_kernel, shaped(3 * tiles, BLOCK), [SMEM] + [VMEM] * 7 + [ANY],
        (
            partner_block, state, message_near, message_far, halo_near, halo_far, contact_rows,
            contact_stiff, grads_a,
        ),
        [pltpu.VMEM((3 * (tiles + 2 * rows), BLOCK), F32)],
        flops=60 * 8 * slots, size=4 * 20 * slots,
    )
    return call(
        final_kernel, shaped(3, slots), [SMEM] + [VMEM] * 9,
        (count, grads_a, grads_b, grads_c, weight, contact, grain_vel, vol, drag, cell),
        flops=60 * slots, size=4 * 20 * slots,
    )


def solution(mesh):
    in_specs = (
        P(None, ("grp", "reg")),
        P(None, ("grp", "reg")),
        P(("grp", "reg")),
        P(("grp", "reg")),
        P(("grp", "reg")),
        P(None, ("grp", "reg")),
        P(None, ("grp", "reg")),
        P(("grp", "reg")),
        P(None, ("grp", "reg")),
        P(("grp", "reg")),
        P(("grp", "reg")),
        P("reg", None, None),
        P("reg", None, None),
        P("reg", None, None),
    )
    out_specs = P(None, ("grp", "reg"))
    return jax.shard_map(
        on_device, mesh=mesh, in_specs=in_specs, out_specs=out_specs, check_vma=False
    )
```

```python
import functools

import jax
import jax.numpy as jnp
from jax import lax
from jax.experimental import pallas as pl
from jax.experimental.pallas import tpu as pltpu
from jax.sharding import PartitionSpec as P

BLOCK = 128
SUB = 8
CORES = 2
ITERS = 4
SPRING = 1.0
DAMPING = 0.5
TIME_STEP = 0.5

VMEM = pl.BlockSpec(memory_space=pltpu.VMEM)
SMEM = pl.BlockSpec(memory_space=pltpu.SMEM)
ANY = pl.BlockSpec(memory_space=pl.ANY)
HBM = pl.BlockSpec(memory_space=pltpu.HBM)
F32 = jnp.float32
BF16 = jnp.bfloat16


def iota(shape, dim):
    return lax.broadcasted_iota(jnp.int32, shape, dim)


def shaped(*dims):
    return jax.ShapeDtypeStruct(dims, F32)


def call(kernel, outs, specs, args, scratch=(), flops=0, size=0, limit=40_000_000):
    return pl.pallas_call(
        kernel,
        out_shape=outs,
        in_specs=specs,
        out_specs=jax.tree.map(lambda _: VMEM, outs),
        scratch_shapes=list(scratch),
        compiler_params=pltpu.CompilerParams(vmem_limit_bytes=limit),
        cost_estimate=pl.CostEstimate(flops=flops, bytes_accessed=size, transcendentals=0),
    )(*args)


class Place:
    def __init__(self, full, height):
        groups, regions = lax.axis_size("grp"), lax.axis_size("reg")
        self.group, region = lax.axis_index("grp"), lax.axis_index("reg")
        self.half = self.group // CORES
        self.own_rows = full // (groups // CORES)
        first = jnp.clip(self.half * self.own_rows - SUB, 0, full - height)
        self.first = pl.multiple_of(first, SUB)
        self.sweeps = self.group % CORES == 0
        self.parity = region % 2
        self.odd = self.parity == 1
        self.lower, self.upper = region > 0, region < regions - 1


def lanes_of(source, index):
    return jnp.take_along_axis(source, index, axis=1, mode="promise_in_bounds")


def halves_of(value):
    high = value.astype(BF16)
    return high, (value - high.astype(F32)).astype(BF16)


def window_kernel(pressure_old, source, solid_before, window, inner, dummy, solid, sems):
    planes, height, _ = solid.shape
    place = Place(pressure_old.shape[1], height)
    rows = pl.ds(place.first, height)
    copies = []
    for x in range(planes):
        for whole, part in (
            (pressure_old, window.at[x]), (source, window.at[planes + x]), (solid_before, solid.at[x])
        ):
            copies.append(
                pltpu.make_async_copy(whole.at[x, rows, :], part, sems.at[len(copies)])
            )
    for copy in copies:
        copy.start()
    dummy[...] = jnp.zeros(dummy.shape, F32)
    for copy in copies:
        copy.wait()
    window[planes:] = window[planes:] - solid[...]
    inner[...] = window[(1 - place.parity) * (planes - 1)]


def forward_kernel(near, inner, _halo, _second, _third, out, dummy):
    dummy[...] = jnp.zeros(dummy.shape, F32)
    count = near.shape[0]
    out[:count] = near[...]
    out[count] = inner[...]


def deposit_kernel(count, cell, vol, drag, ids, _, out, dummy):
    dummy[...] = jnp.zeros(dummy.shape, F32)
    tiles = cell.shape[0]
    sub = iota((SUB, BLOCK), 0)
    rows_c = iota((BLOCK, BLOCK), 0)
    even = sub % 2 == 0
    low_pair = sub % 4 < 2

    def step(group, carry):
        first = pl.multiple_of(group * SUB, SUB)
        slot = (first + sub) * BLOCK + iota((SUB, BLOCK), 1)
        live = slot < count[0]
        cells = cell[pl.ds(first, SUB), :]
        parts = halves_of(jnp.where(live, vol[pl.ds(first, SUB), :], 0.0)) + halves_of(
            jnp.where(live, drag[pl.ds(first, SUB), :], 0.0)
        )
        parts = [part.astype(F32) for part in parts]
        left = jnp.concatenate([jnp.where(even, part, 0.0) for part in parts], 0)
        right = jnp.concatenate([jnp.where(even, 0.0, part) for part in parts], 0)
        loads = jnp.concatenate([left, right], 1).astype(BF16)
        sums = [jnp.zeros((SUB, BLOCK), F32), jnp.zeros((SUB, BLOCK), F32)]
        for quad in range(SUB // 4):
            hot = [
                jnp.where(
                    rows_c == jnp.broadcast_to(cells[t : t + 1, :], (BLOCK, BLOCK)), 1.0, 0.0
                ).astype(BF16)
                for t in range(4 * quad, 4 * quad + 4)
            ]
            picked = jnp.concatenate(
                [jnp.concatenate(hot[:2], 1), jnp.concatenate(hot[2:], 1)], 0
            )
            placed = lax.dot_general(
                loads, picked, (((1,), (1,)), ((), ())), preferred_element_type=F32
            )
            for field in range(2):
                base = field * 2 * SUB
                total = placed[base : base + SUB] + placed[base + SUB : base + 2 * SUB]
                chosen = jnp.where(low_pair, total[:, :BLOCK], total[:, BLOCK:])
                sums[field] = jnp.where(sub // 4 == quad, chosen, sums[field])
        out[pl.ds(first, SUB), :BLOCK] = sums[0]
        out[pl.ds(first, SUB), BLOCK:] = sums[1]
        return carry

    lax.fori_loop(0, tiles // SUB, step, 0, unroll=4)
    out[tiles : tiles + SUB, :BLOCK] = jnp.broadcast_to(ids[...].astype(F32), (SUB, BLOCK))
    out[tiles : tiles + SUB, BLOCK:] = jnp.zeros((SUB, BLOCK), F32)


def halo_kernel(pos, vel, lists, _, state, near, far, dummy):
    dummy[...] = jnp.zeros(dummy.shape, F32)
    tiles = pos.shape[1] // BLOCK
    rows = lists.shape[1] // BLOCK
    for tile in range(tiles):
        lanes = slice(tile * BLOCK, (tile + 1) * BLOCK)
        mixed = SPRING * pos[:, lanes] - DAMPING * vel[:, lanes]
        for axis in range(3):
            state[axis * tiles + tile : axis * tiles + tile + 1, :] = mixed[axis : axis + 1]
    turned = [
        jnp.concatenate(halves_of(jnp.transpose(state[axis * tiles : (axis + 1) * tiles, :])), 1)
        for axis in range(3)
    ]
    turned = jnp.concatenate(turned, 0)
    span = 2 * BLOCK
    row = iota((BLOCK, span), 0)

    odd = lax.axis_index("reg") % 2
    for away, out in enumerate((near, far)):
        side = 1 - odd if away == 0 else odd

        def step(part, carry):
            named = lists[:, pl.ds(pl.multiple_of(part * span, span), span)]
            named = jnp.where(side == 0, named[:1], named[1:])
            block = lax.shift_right_logical(named, 7)
            lane = named & (BLOCK - 1)
            hot = jnp.where(row == jnp.broadcast_to(block, row.shape), 1.0, 0.0).astype(BF16)
            found = jnp.dot(
                turned, jnp.concatenate([hot, hot], 0), preferred_element_type=F32
            )
            here = row == jnp.broadcast_to(lane, row.shape)
            for axis in range(3):
                value = jnp.where(here, found[axis * BLOCK : (axis + 1) * BLOCK], 0.0)
                value = jnp.sum(value, axis=0, keepdims=True)
                for half in range(2):
                    out[pl.ds(axis * rows + 2 * part + half, 1), :] = value[
                        :, half * BLOCK : (half + 1) * BLOCK
                    ]
            return carry

        lax.fori_loop(0, rows // 2, step, 0, unroll=4)


def message_kernel(mine, second, third, halo_near, halo_far, _, near, far, dummy):
    dummy[...] = jnp.zeros(dummy.shape, F32)
    stride = mine.shape[0]
    half = halo_near.shape[0] // 2
    rows = near.shape[0] - half
    for halo, out in ((halo_near, near), (halo_far, far)):
        for index, group in enumerate((mine, second, third)):
            out[index * stride : (index + 1) * stride, :] = group[...]
        out[rows:, :BLOCK] = halo[:half, :]
        out[rows:, BLOCK:] = halo[half:, :]


def contact_kernel(
    partner, state, message_near, message_far, halo_near, halo_far, named, stiff, _, out, extended
):
    tiles = state.shape[0] // 3
    rows = halo_near.shape[0] // 3
    blocks = tiles + 2 * rows
    base = message_near.shape[0] - 3 * rows // 2
    odd = lax.axis_index("reg") % 2
    sweeps = lax.axis_index("grp") % CORES == 0
    for axis in range(3):
        extended[axis * blocks : axis * blocks + tiles, :] = state[
            axis * tiles : (axis + 1) * tiles, :
        ]
    for message, halo, upper in (
        (message_near, halo_near, 1 - odd), (message_far, halo_far, odd)
    ):
        carried = jnp.concatenate([message[base:, :BLOCK], message[base:, BLOCK:]], 0)
        carried = jnp.where(sweeps, carried, halo[...])
        for axis in range(3):
            first = pl.multiple_of(axis * blocks + tiles + upper * rows, SUB)
            extended[pl.ds(first, rows), :] = carried[axis * rows : (axis + 1) * rows]

    def step(tile, carry):
        lanes = pl.ds(pl.multiple_of(tile * BLOCK, BLOCK), BLOCK)
        entry = named[:, lanes]
        weight = jnp.where(entry >= 0, stiff[:, lanes], 0.0)
        own = entry < BLOCK
        lane = entry & (BLOCK - 1)
        other = partner[tile]
        for axis in range(3):
            mine = jnp.broadcast_to(extended[pl.ds(axis * blocks + tile, 1), :], entry.shape)
            theirs = jnp.broadcast_to(extended[pl.ds(axis * blocks + other, 1), :], entry.shape)
            met = jnp.where(own, lanes_of(mine, lane), lanes_of(theirs, lane))
            pull = jnp.sum(weight * (mine - met), axis=0, keepdims=True)
            out[pl.ds(axis * tiles + tile, 1), :] = pull
        return carry

    lax.fori_loop(0, tiles, step, 0, unroll=4)


def shifted(plane):
    height, width = plane.shape
    row = iota((SUB, width), 0)
    column = iota((height, BLOCK), 1)
    above, below = pltpu.roll(plane, 1, 0), pltpu.roll(plane, height - 1, 0)
    left, right = pltpu.roll(plane, 1, 1), pltpu.roll(plane, width - 1, 1)
    above = jnp.concatenate([jnp.where(row == 0, 0.0, above[:SUB]), above[SUB:]], 0)
    below = jnp.concatenate([below[:-SUB], jnp.where(row == SUB - 1, 0.0, below[-SUB:])], 0)
    left = jnp.concatenate([jnp.where(column == 0, 0.0, left[:, :BLOCK]), left[:, BLOCK:]], 1)
    right = jnp.concatenate(
        [right[:, :-BLOCK], jnp.where(column == BLOCK - 1, 0.0, right[:, -BLOCK:])], 1
    )
    return above, below, left, right


def inverse_of(value):
    near = pl.reciprocal(value, approx=True)
    return near * (2.0 - value * near)


def placed(groups, tiles):
    parts = [halves_of(group[:tiles, :]) for group in groups]
    loads = jnp.concatenate([part[i] for i in range(2) for part in parts], 0)
    ids = jnp.concatenate([group[tiles : tiles + 1, :BLOCK] for group in groups], 1)
    ids = ids.astype(jnp.int32)

    def gathered(wanted):
        hot = jnp.where(wanted == jnp.broadcast_to(ids, wanted.shape), 1.0, 0.0).astype(BF16)
        total = jnp.dot(
            jnp.concatenate([hot, hot], 1), loads, preferred_element_type=F32
        )
        return total[:, :BLOCK], total[:, BLOCK:]

    return ids, gathered


def coefficients(gathered, tiles, first, full, driven, planes, constant, factor, base, present):
    _, height, width = driven.shape
    zones = width // BLOCK
    shape = (zones * height, 3 * tiles)
    line = iota(shape, 0)
    block = (line % height) * zones + line // height + first * zones

    for x in range(planes):
        solid, drag = gathered(block + x * (full * zones))
        voids = 1.0 + solid
        scale = inverse_of(6.0 + (drag + 1.0) * voids)
        if present is not None:
            scale = jnp.where(present, scale, 0.0)
        inverse = voids * scale
        for zone in range(zones):
            lanes = slice(zone * BLOCK, (zone + 1) * BLOCK)
            rows = slice(zone * height, (zone + 1) * height)
            driving = driven[planes + x, :, lanes] + solid[rows]
            constant[base + x, :, lanes] = driving * inverse[rows]
            factor[base + x, :, lanes] = scale[rows]


def own_kernel(
    full, mine, second, third, window, _message, _near, _far, constant, factor, weight, rows_at, ends
):
    tiles = weight.shape[0]
    planes, height, width = constant.shape
    place = Place(full, height)
    zones = width // BLOCK
    ends[...] = window[place.parity * (planes - 1)]
    ids, gathered = placed((mine, second, third), tiles)
    coefficients(gathered, tiles, place.first, full, window, planes, constant, factor, 0, None)
    turned = [
        jnp.transpose(
            jnp.broadcast_to(ids[:, i * tiles : (i + 1) * tiles], (BLOCK, tiles)).astype(F32)
        ).astype(jnp.int32)
        for i in range(3)
    ]
    solid, drag = gathered(jnp.concatenate([turned[0]] * 3, 1))
    weight[...] = 1.0 / (1.0 / (1.0 + solid) + drag)
    for i in range(3):
        block = turned[i]
        line, zone = block // zones, block % zones
        x, y = line // full, line % full
        row = (x * zones + zone) * height + y - place.first
        held = y // place.own_rows == jnp.where(place.sweeps, place.half, -1)
        rows_at[i * tiles : (i + 1) * tiles, :] = jnp.where(held, row, -1)


def solve_kernel(
    full, sweeps, rows_at, joined_near, joined_far, window, near, far, beyond,
    own_constant, own_factor, out_a, out_b, out_c,
    constant, factor, old, new, fields,
):
    planes, height, width = own_constant.shape
    zones = width // BLOCK
    tiles = out_a.shape[0]
    place = Place(full, height)
    odd = place.odd
    rim = sweeps + 1
    for joined, driven, below, present in (
        (joined_near, near, odd, jnp.where(odd, place.lower, place.upper)),
        (joined_far, far, jnp.logical_not(odd), jnp.where(odd, place.upper, place.lower)),
    ):
        stride = tiles + SUB
        groups = [joined.at[i * stride : (i + 1) * stride] for i in range(3)]
        _, gathered = placed(groups, tiles)
        coefficients(
            gathered, tiles, place.first, full, driven, planes, constant, factor,
            jnp.where(below, 0, planes), present,
        )
    old[pl.ds(jnp.where(odd, 1, rim + planes), planes)] = near[:planes]
    old[pl.ds(jnp.where(odd, rim + planes, 1), planes)] = far[:planes]
    old[pl.ds(jnp.where(odd, rim + 2 * planes, 0), 1)] = far[2 * planes :]
    old[pl.ds(jnp.where(odd, 0, rim + 2 * planes), 1)] = beyond[...][None]
    old[rim : rim + planes] = window[:planes]

    def sweep(source, target, depth):
        def over(constants, factors, shift):
            def plane(x, carry):
                centre = source[x]
                above, below, left, right = shifted(centre)
                around = source[x - 1] + source[x + 1] + above + below + left + right
                target[x] = constants[x - shift] + factors[x - shift] * around
                return carry

            return plane

        lax.fori_loop(depth, rim, over(constant, factor, 1), 0, unroll=2)
        lax.fori_loop(rim, rim + planes, over(own_constant, own_factor, rim), 0, unroll=2)
        lax.fori_loop(
            rim + planes, 3 * planes + 2 - depth, over(constant, factor, 1 + planes), 0, unroll=2
        )

    for index in range(sweeps):
        source, target = (old, new) if index % 2 == 0 else (new, old)
        sweep(source, target, index + 1)
    last = old if sweeps % 2 == 0 else new

    def gradient(x, carry):
        centre = last[rim + x]
        above, below, left, right = shifted(centre)
        grads = (last[rim + x + 1] - last[rim + x - 1], below - above, right - left)
        for zone in range(zones):
            first = pl.multiple_of((x * zones + zone) * height, SUB)
            for axis, grad in enumerate(grads):
                fields[pl.ds(first, height), axis * BLOCK : (axis + 1) * BLOCK] = (
                    0.5 * grad[:, zone * BLOCK : (zone + 1) * BLOCK]
                )
        return carry

    lax.fori_loop(0, planes, gradient, 0, unroll=2)
    wanted = jnp.concatenate([rows_at[...]] * (planes * zones * height // BLOCK), 1)
    hot = jnp.where(wanted == iota(wanted.shape, 1), 1.0, 0.0).astype(BF16)
    pieces = jnp.concatenate(halves_of(fields[...]), 1)
    total = jnp.dot(hot, pieces, preferred_element_type=F32)
    total = total[:, : 3 * BLOCK] + total[:, 3 * BLOCK :]
    for index, out in enumerate((out_a, out_b, out_c)):
        out[...] = total[index * tiles : (index + 1) * tiles]


def final_kernel(
    count, grads_a, grads_b, grads_c, weight, contact, vel, vol, drag, cell, out,
):
    tiles = cell.shape[0]
    cells = cell[...]
    heft = lanes_of(weight[...], cells)
    slot = iota(cells.shape, 0) * BLOCK + iota(cells.shape, 1)
    live = slot < count[0]
    volume = vol[...]
    push = TIME_STEP / volume
    for axis in range(3):
        lanes = slice(axis * BLOCK, (axis + 1) * BLOCK)
        gradient = lanes_of(grads_a[:, lanes] + grads_b[:, lanes] + grads_c[:, lanes], cells)
        own = jnp.concatenate(
            [vel[axis : axis + 1, t * BLOCK : (t + 1) * BLOCK] for t in range(tiles)], 0
        )
        fluid = -gradient * heft
        force = contact[axis * tiles : (axis + 1) * tiles, :] - volume * gradient
        force = force + drag[...] * (fluid - own)
        new = jnp.where(live, own + force * push, 0.0)
        for t in range(tiles):
            out[axis : axis + 1, t * BLOCK : (t + 1) * BLOCK] = new[t : t + 1, :]


def on_device(
    grain_pos,
    grain_vel,
    grain_vol,
    drag_coef,
    grain_count,
    contact_rows,
    contact_stiff,
    partner_block,
    halo_list,
    grain_cell,
    tile_cell_block,
    pressure_old,
    pressure_source,
    solid_old,
):
    groups, regions = lax.axis_size("grp"), lax.axis_size("reg")
    holding = groups - 1
    halves = groups // CORES
    slots = grain_pos.shape[1]
    tiles = slots // BLOCK
    planes, full, width = pressure_old.shape
    zones = width // BLOCK
    own_rows = full // halves
    height = min(full, own_rows + SUB * min(2, halves - 1))
    owners = range(0, groups, CORES)
    holders = range(holding)

    def send(value, pairs):
        flat = [(a[0] * regions + a[1], b[0] * regions + b[1]) for a, b in pairs]
        return lax.ppermute(value, ("grp", "reg"), flat)

    def along_reg(value, members, goes):
        pairs = [
            ((g, r), (g, r + goes[r % 2]))
            for g in members
            for r in range(regions)
            if 0 <= r + goes[r % 2] < regions
        ]
        return send(value, pairs)

    def along_grp(value, step, members):
        pairs = [((g, r), ((g + step) % holding, r)) for g in members for r in range(regions)]
        return send(value, pairs)

    count = grain_count
    cell = grain_cell.reshape(tiles, BLOCK)
    vol = grain_vol.reshape(tiles, BLOCK)
    drag = drag_coef.reshape(tiles, BLOCK)
    ids = tile_cell_block.reshape(1, tiles)
    field_bytes = 4 * planes * height * width

    field = shaped(planes, height, width)
    plane = shaped(height, width)
    small = shaped(SUB, BLOCK)
    window, inner, after_window = call(
        window_kernel, (shaped(2 * planes, height, width), plane, small),
        [HBM] * 3, (pressure_old, pressure_source, solid_old),
        [pltpu.VMEM((planes, height, width), F32), pltpu.SemaphoreType.DMA((3 * planes,))],
        flops=field_bytes, size=6 * field_bytes, limit=61_500_000,
    )
    near = along_reg(window, owners, (1, -1))
    mine, after_deposit = call(
        deposit_kernel, (shaped(tiles + SUB, 2 * BLOCK), small), [SMEM] + [VMEM] * 5,
        (count, cell, vol, drag, ids, after_window), flops=2 * 32 * 48 * 65536, size=5 * 4 * slots,
    )
    second = along_grp(mine, 1, holders)
    third = along_grp(mine, 2, holders)
    rows = halo_list.shape[1] // BLOCK
    halo = shaped(3 * rows, BLOCK)
    state, halo_near, halo_far, after_halo = call(
        halo_kernel, (shaped(3 * tiles, BLOCK), halo, halo, small),
        [VMEM] * 4, (grain_pos, grain_vel, halo_list, after_deposit), flops=2 * 3 * 8 * BLOCK * BLOCK * slots // 4,
        size=4 * 4 * 3 * slots,
    )
    far, after_forward = call(
        forward_kernel, (shaped(2 * planes + 1, height, width), small), [VMEM] * 5,
        (near, inner, after_halo, second, third), size=5 * field_bytes,
    )
    far = along_reg(far, owners, (2, -2))
    message = shaped(holding * (tiles + SUB) + 3 * rows // 2, 2 * BLOCK)
    message_near, message_far, after_message = call(
        message_kernel, (message, message, small), [VMEM] * 6,
        (mine, second, third, halo_near, halo_far, after_forward), size=8 * 2 * BLOCK * 500,
    )
    message_near = along_reg(message_near, owners, (1, -1))
    message_far = along_reg(message_far, owners, (-1, 1))
    others = [g for g in holders if g not in owners]
    halo_near = along_reg(halo_near, others, (1, -1))
    halo_far = along_reg(halo_far, others, (-1, 1))
    constant, factor, weight, rows_at, ends = call(
        functools.partial(own_kernel, full),
        (
            field, field, shaped(tiles, BLOCK),
            jax.ShapeDtypeStruct((3 * tiles, BLOCK), jnp.int32), plane,
        ),
        [VMEM] * 7, (mine, second, third, window, after_message, halo_near, halo_far),
        flops=planes * height * 4 * 384 * 256 * 6, size=9 * field_bytes,
    )
    beyond = along_reg(ends, owners, (-2, 2))

    grads = shaped(tiles, 3 * BLOCK)
    window_of = lambda count: pltpu.VMEM((count, height, width), F32)
    grads_a, grads_b, grads_c = call(
        functools.partial(solve_kernel, full, ITERS), (grads,) * 3,
        [VMEM] * 9,
        (rows_at, message_near, message_far, window, near, far, beyond, constant, factor),
        [
            window_of(2 * planes), window_of(2 * planes),
            window_of(3 * planes + 2), window_of(3 * planes + 2),
            pltpu.VMEM((planes * zones * height, 3 * BLOCK), F32),
        ],
        flops=2 * planes * height * 4 * 384 * 256 * 6, size=20 * field_bytes,
    )
    grads_b = along_grp(grads_b, -1, owners)
    grads_c = along_grp(grads_c, -2, owners)

    contact = call(
        contact_kernel, shaped(3 * tiles, BLOCK), [SMEM] + [VMEM] * 7 + [ANY],
        (
            partner_block, state, message_near, message_far, halo_near, halo_far, contact_rows,
            contact_stiff, grads_a,
        ),
        [pltpu.VMEM((3 * (tiles + 2 * rows), BLOCK), F32)],
        flops=60 * 8 * slots, size=4 * 20 * slots,
    )
    return call(
        final_kernel, shaped(3, slots), [SMEM] + [VMEM] * 9,
        (count, grads_a, grads_b, grads_c, weight, contact, grain_vel, vol, drag, cell),
        flops=60 * slots, size=4 * 20 * slots,
    )


def solution(mesh):
    in_specs = (
        P(None, ("grp", "reg")),
        P(None, ("grp", "reg")),
        P(("grp", "reg")),
        P(("grp", "reg")),
        P(("grp", "reg")),
        P(None, ("grp", "reg")),
        P(None, ("grp", "reg")),
        P(("grp", "reg")),
        P(None, ("grp", "reg")),
        P(("grp", "reg")),
        P(("grp", "reg")),
        P("reg", None, None),
        P("reg", None, None),
        P("reg", None, None),
    )
    out_specs = P(None, ("grp", "reg"))
    return jax.shard_map(
        on_device, mesh=mesh, in_specs=in_specs, out_specs=out_specs, check_vma=False
    )
```

```python
import functools

import jax
import jax.numpy as jnp
from jax import lax
from jax.experimental import pallas as pl
from jax.experimental.pallas import tpu as pltpu
from jax.sharding import PartitionSpec as P

BLOCK = 128
SUB = 8
CORES = 2
ITERS = 4
SPRING = 1.0
DAMPING = 0.5
TIME_STEP = 0.5

VMEM = pl.BlockSpec(memory_space=pltpu.VMEM)
SMEM = pl.BlockSpec(memory_space=pltpu.SMEM)
ANY = pl.BlockSpec(memory_space=pl.ANY)
HBM = pl.BlockSpec(memory_space=pltpu.HBM)
F32 = jnp.float32
BF16 = jnp.bfloat16


def iota(shape, dim):
    return lax.broadcasted_iota(jnp.int32, shape, dim)


def shaped(*dims):
    return jax.ShapeDtypeStruct(dims, F32)


def call(kernel, outs, specs, args, scratch=(), flops=0, size=0, limit=40_000_000, place=VMEM):
    return pl.pallas_call(
        kernel,
        out_shape=outs,
        in_specs=specs,
        out_specs=jax.tree.map(lambda _: place, outs),
        scratch_shapes=list(scratch),
        compiler_params=pltpu.CompilerParams(vmem_limit_bytes=limit),
        cost_estimate=pl.CostEstimate(flops=flops, bytes_accessed=size, transcendentals=0),
    )(*args)


class Place:
    def __init__(self, full, height):
        groups, regions = lax.axis_size("grp"), lax.axis_size("reg")
        self.group, region = lax.axis_index("grp"), lax.axis_index("reg")
        self.half = self.group // CORES
        self.own_rows = full // (groups // CORES)
        first = jnp.clip(self.half * self.own_rows - SUB, 0, full - height)
        self.first = pl.multiple_of(first, SUB)
        self.sweeps = self.group % CORES == 0
        self.parity = region % 2
        self.odd = self.parity == 1
        self.lower, self.upper = region > 0, region < regions - 1


def lanes_of(source, index):
    return jnp.take_along_axis(source, index, axis=1, mode="promise_in_bounds")


def halves_of(value):
    high = value.astype(BF16)
    return high, (value - high.astype(F32)).astype(BF16)


def window_kernel(pressure_old, source, solid_before, window, inner, driven, solid, sems):
    planes, height, _ = solid.shape
    place = Place(pressure_old.shape[1], height)
    rows = pl.ds(place.first, height)
    end = (1 - place.parity) * (planes - 1)
    copy = lambda whole, part, index: pltpu.make_async_copy(whole, part, sems.at[index])
    fetched = [
        (
            copy(source.at[x, rows, :], driven.at[x], 2 * x),
            copy(solid_before.at[x, rows, :], solid.at[x], 2 * x + 1),
        )
        for x in range(planes)
    ]
    straight = [
        copy(pressure_old.at[x, rows, :], window.at[x], 2 * planes + x) for x in range(planes)
    ] + [copy(pressure_old.at[end, rows, :], inner, 3 * planes)]
    for pair in fetched:
        for one in pair:
            one.start()
    for one in straight:
        one.start()
    stored = [
        copy(driven.at[x], window.at[planes + x], 3 * planes + 1 + x) for x in range(planes)
    ]
    for x, pair in enumerate(fetched):
        for one in pair:
            one.wait()
        driven[x] = driven[x] - solid[x]
        stored[x].start()
    for one in straight + stored:
        one.wait()


def forward_kernel(near, inner, _halo, _second, _third, out, dummy):
    dummy[...] = jnp.zeros(dummy.shape, F32)
    count = near.shape[0]
    out[:count] = near[...]
    out[count] = inner[...]


def deposit_kernel(count, cell, vol, drag, ids, out, dummy):
    dummy[...] = jnp.zeros(dummy.shape, F32)
    tiles = cell.shape[0]
    sub = iota((SUB, BLOCK), 0)
    rows_c = iota((BLOCK, BLOCK), 0)
    even = sub % 2 == 0
    low_pair = sub % 4 < 2

    def step(group, carry):
        first = pl.multiple_of(group * SUB, SUB)
        slot = (first + sub) * BLOCK + iota((SUB, BLOCK), 1)
        live = slot < count[0]
        cells = cell[pl.ds(first, SUB), :]
        parts = halves_of(jnp.where(live, vol[pl.ds(first, SUB), :], 0.0)) + halves_of(
            jnp.where(live, drag[pl.ds(first, SUB), :], 0.0)
        )
        parts = [part.astype(F32) for part in parts]
        left = jnp.concatenate([jnp.where(even, part, 0.0) for part in parts], 0)
        right = jnp.concatenate([jnp.where(even, 0.0, part) for part in parts], 0)
        loads = jnp.concatenate([left, right], 1).astype(BF16)
        sums = [jnp.zeros((SUB, BLOCK), F32), jnp.zeros((SUB, BLOCK), F32)]
        for quad in range(SUB // 4):
            hot = [
                jnp.where(
                    rows_c == jnp.broadcast_to(cells[t : t + 1, :], (BLOCK, BLOCK)), 1.0, 0.0
                ).astype(BF16)
                for t in range(4 * quad, 4 * quad + 4)
            ]
            picked = jnp.concatenate(
                [jnp.concatenate(hot[:2], 1), jnp.concatenate(hot[2:], 1)], 0
            )
            placed = lax.dot_general(
                loads, picked, (((1,), (1,)), ((), ())), preferred_element_type=F32
            )
            for field in range(2):
                base = field * 2 * SUB
                total = placed[base : base + SUB] + placed[base + SUB : base + 2 * SUB]
                chosen = jnp.where(low_pair, total[:, :BLOCK], total[:, BLOCK:])
                sums[field] = jnp.where(sub // 4 == quad, chosen, sums[field])
        out[pl.ds(first, SUB), :BLOCK] = sums[0]
        out[pl.ds(first, SUB), BLOCK:] = sums[1]
        return carry

    lax.fori_loop(0, tiles // SUB, step, 0, unroll=4)
    out[tiles : tiles + SUB, :BLOCK] = jnp.broadcast_to(ids[...].astype(F32), (SUB, BLOCK))
    out[tiles : tiles + SUB, BLOCK:] = jnp.zeros((SUB, BLOCK), F32)


def halo_kernel(pos, vel, lists, _, state, near, far, dummy):
    dummy[...] = jnp.zeros(dummy.shape, F32)
    tiles = pos.shape[1] // BLOCK
    rows = lists.shape[1] // BLOCK
    for tile in range(tiles):
        lanes = slice(tile * BLOCK, (tile + 1) * BLOCK)
        mixed = SPRING * pos[:, lanes] - DAMPING * vel[:, lanes]
        for axis in range(3):
            state[axis * tiles + tile : axis * tiles + tile + 1, :] = mixed[axis : axis + 1]
    turned = [
        jnp.concatenate(halves_of(jnp.transpose(state[axis * tiles : (axis + 1) * tiles, :])), 1)
        for axis in range(3)
    ]
    turned = jnp.concatenate(turned, 0)
    span = 2 * BLOCK
    row = iota((BLOCK, span), 0)

    odd = lax.axis_index("reg") % 2
    for away, out in enumerate((near, far)):
        side = 1 - odd if away == 0 else odd

        def step(part, carry):
            named = lists[:, pl.ds(pl.multiple_of(part * span, span), span)]
            named = jnp.where(side == 0, named[:1], named[1:])
            block = lax.shift_right_logical(named, 7)
            lane = named & (BLOCK - 1)
            hot = jnp.where(row == jnp.broadcast_to(block, row.shape), 1.0, 0.0).astype(BF16)
            found = jnp.dot(
                turned, jnp.concatenate([hot, hot], 0), preferred_element_type=F32
            )
            here = row == jnp.broadcast_to(lane, row.shape)
            for axis in range(3):
                value = jnp.where(here, found[axis * BLOCK : (axis + 1) * BLOCK], 0.0)
                value = jnp.sum(value, axis=0, keepdims=True)
                for half in range(2):
                    out[pl.ds(axis * rows + 2 * part + half, 1), :] = value[
                        :, half * BLOCK : (half + 1) * BLOCK
                    ]
            return carry

        lax.fori_loop(0, rows // 2, step, 0, unroll=8)


def message_kernel(mine, second, third, halo_near, halo_far, _, near, far, dummy):
    dummy[...] = jnp.zeros(dummy.shape, F32)
    stride = mine.shape[0]
    half = halo_near.shape[0] // 2
    rows = near.shape[0] - half
    for halo, out in ((halo_near, near), (halo_far, far)):
        for index, group in enumerate((mine, second, third)):
            out[index * stride : (index + 1) * stride, :] = group[...]
        out[rows:, :BLOCK] = halo[:half, :]
        out[rows:, BLOCK:] = halo[half:, :]


def contact_kernel(
    partner, state, message_near, message_far, halo_near, halo_far, named, stiff, _, out, extended
):
    tiles = state.shape[0] // 3
    rows = halo_near.shape[0] // 3
    blocks = tiles + 2 * rows
    base = message_near.shape[0] - 3 * rows // 2
    odd = lax.axis_index("reg") % 2
    sweeps = lax.axis_index("grp") % CORES == 0
    for axis in range(3):
        extended[axis * blocks : axis * blocks + tiles, :] = state[
            axis * tiles : (axis + 1) * tiles, :
        ]
    for message, halo, upper in (
        (message_near, halo_near, 1 - odd), (message_far, halo_far, odd)
    ):
        carried = jnp.concatenate([message[base:, :BLOCK], message[base:, BLOCK:]], 0)
        carried = jnp.where(sweeps, carried, halo[...])
        for axis in range(3):
            first = pl.multiple_of(axis * blocks + tiles + upper * rows, SUB)
            extended[pl.ds(first, rows), :] = carried[axis * rows : (axis + 1) * rows]

    def step(tile, carry):
        lanes = pl.ds(pl.multiple_of(tile * BLOCK, BLOCK), BLOCK)
        entry = named[:, lanes]
        weight = jnp.where(entry >= 0, stiff[:, lanes], 0.0)
        own = entry < BLOCK
        lane = entry & (BLOCK - 1)
        other = partner[tile]
        for axis in range(3):
            mine = jnp.broadcast_to(extended[pl.ds(axis * blocks + tile, 1), :], entry.shape)
            theirs = jnp.broadcast_to(extended[pl.ds(axis * blocks + other, 1), :], entry.shape)
            met = jnp.where(own, lanes_of(mine, lane), lanes_of(theirs, lane))
            pull = jnp.sum(weight * (mine - met), axis=0, keepdims=True)
            out[pl.ds(axis * tiles + tile, 1), :] = pull
        return carry

    lax.fori_loop(0, tiles, step, 0, unroll=4)


def shifted(plane):
    height, width = plane.shape
    row = iota((SUB, width), 0)
    column = iota((height, BLOCK), 1)
    above, below = pltpu.roll(plane, 1, 0), pltpu.roll(plane, height - 1, 0)
    left, right = pltpu.roll(plane, 1, 1), pltpu.roll(plane, width - 1, 1)
    above = jnp.concatenate([jnp.where(row == 0, 0.0, above[:SUB]), above[SUB:]], 0)
    below = jnp.concatenate([below[:-SUB], jnp.where(row == SUB - 1, 0.0, below[-SUB:])], 0)
    left = jnp.concatenate([jnp.where(column == 0, 0.0, left[:, :BLOCK]), left[:, BLOCK:]], 1)
    right = jnp.concatenate(
        [right[:, :-BLOCK], jnp.where(column == BLOCK - 1, 0.0, right[:, -BLOCK:])], 1
    )
    return above, below, left, right


def inverse_of(value):
    near = pl.reciprocal(value, approx=True)
    return near * (2.0 - value * near)


def placed(groups, tiles):
    parts = [halves_of(group[:tiles, :]) for group in groups]
    loads = jnp.concatenate([part[i] for i in range(2) for part in parts], 0)
    ids = jnp.concatenate([group[tiles : tiles + 1, :BLOCK] for group in groups], 1)
    ids = ids.astype(jnp.int32)

    def gathered(wanted):
        hot = jnp.where(wanted == jnp.broadcast_to(ids, wanted.shape), 1.0, 0.0).astype(BF16)
        total = jnp.dot(
            jnp.concatenate([hot, hot], 1), loads, preferred_element_type=F32
        )
        return total[:, :BLOCK], total[:, BLOCK:]

    return ids, gathered


def coefficients(gathered, tiles, first, full, driven, planes, constant, factor, base, present):
    _, height, width = driven.shape
    zones = width // BLOCK
    shape = (zones * height, 3 * tiles)
    line = iota(shape, 0)
    block = (line % height) * zones + line // height + first * zones

    for x in range(planes):
        solid, drag = gathered(block + x * (full * zones))
        voids = 1.0 + solid
        scale = inverse_of(6.0 + (drag + 1.0) * voids)
        if present is not None:
            scale = jnp.where(present, scale, 0.0)
        inverse = voids * scale
        for zone in range(zones):
            lanes = slice(zone * BLOCK, (zone + 1) * BLOCK)
            rows = slice(zone * height, (zone + 1) * height)
            driving = driven[planes + x, :, lanes] + solid[rows]
            constant[base + x, :, lanes] = driving * inverse[rows]
            factor[base + x, :, lanes] = scale[rows]


def own_kernel(
    full, mine, second, third, window, _message, _near, _far, constant, factor, weight, rows_at, ends
):
    tiles = weight.shape[0]
    planes, height, width = constant.shape
    place = Place(full, height)
    zones = width // BLOCK
    ends[...] = window[place.parity * (planes - 1)]
    ids, gathered = placed((mine, second, third), tiles)
    coefficients(gathered, tiles, place.first, full, window, planes, constant, factor, 0, None)
    turned = [
        jnp.transpose(
            jnp.broadcast_to(ids[:, i * tiles : (i + 1) * tiles], (BLOCK, tiles)).astype(F32)
        ).astype(jnp.int32)
        for i in range(3)
    ]
    solid, drag = gathered(jnp.concatenate([turned[0]] * 3, 1))
    weight[...] = 1.0 / (1.0 / (1.0 + solid) + drag)
    for i in range(3):
        block = turned[i]
        line, zone = block // zones, block % zones
        x, y = line // full, line % full
        row = (x * zones + zone) * height + y - place.first
        held = y // place.own_rows == jnp.where(place.sweeps, place.half, -1)
        rows_at[i * tiles : (i + 1) * tiles, :] = jnp.where(held, row, -1)


def solve_kernel(
    full, sweeps, rows_at, joined_near, joined_far, window, near, far, beyond,
    own_constant, own_factor, out_a, out_b, out_c,
    constant, factor, old, new, fields,
):
    planes, height, width = own_constant.shape
    zones = width // BLOCK
    tiles = out_a.shape[0]
    place = Place(full, height)
    odd = place.odd
    rim = sweeps + 1
    for joined, driven, below, present in (
        (joined_near, near, odd, jnp.where(odd, place.lower, place.upper)),
        (joined_far, far, jnp.logical_not(odd), jnp.where(odd, place.upper, place.lower)),
    ):
        stride = tiles + SUB
        groups = [joined.at[i * stride : (i + 1) * stride] for i in range(3)]
        _, gathered = placed(groups, tiles)
        coefficients(
            gathered, tiles, place.first, full, driven, planes, constant, factor,
            jnp.where(below, 0, planes), present,
        )
    old[pl.ds(jnp.where(odd, 1, rim + planes), planes)] = near[:planes]
    old[pl.ds(jnp.where(odd, rim + planes, 1), planes)] = far[:planes]
    old[pl.ds(jnp.where(odd, rim + 2 * planes, 0), 1)] = far[2 * planes :]
    old[pl.ds(jnp.where(odd, 0, rim + 2 * planes), 1)] = beyond[...][None]
    old[rim : rim + planes] = window[:planes]

    def sweep(source, target, depth):
        def over(constants, factors, shift):
            def plane(x, carry):
                centre = source[x]
                above, below, left, right = shifted(centre)
                around = source[x - 1] + source[x + 1] + above + below + left + right
                target[x] = constants[x - shift] + factors[x - shift] * around
                return carry

            return plane

        lax.fori_loop(depth, rim, over(constant, factor, 1), 0, unroll=4)
        lax.fori_loop(rim, rim + planes, over(own_constant, own_factor, rim), 0, unroll=4)
        lax.fori_loop(
            rim + planes, 3 * planes + 2 - depth, over(constant, factor, 1 + planes), 0, unroll=4
        )

    for index in range(sweeps):
        source, target = (old, new) if index % 2 == 0 else (new, old)
        sweep(source, target, index + 1)
    last = old if sweeps % 2 == 0 else new

    def gradient(x, carry):
        centre = last[rim + x]
        above, below, left, right = shifted(centre)
        grads = (last[rim + x + 1] - last[rim + x - 1], below - above, right - left)
        for zone in range(zones):
            first = pl.multiple_of((x * zones + zone) * height, SUB)
            for axis, grad in enumerate(grads):
                fields[pl.ds(first, height), axis * BLOCK : (axis + 1) * BLOCK] = (
                    0.5 * grad[:, zone * BLOCK : (zone + 1) * BLOCK]
                )
        return carry

    lax.fori_loop(0, planes, gradient, 0, unroll=4)
    wanted = jnp.concatenate([rows_at[...]] * (planes * zones * height // BLOCK), 1)
    hot = jnp.where(wanted == iota(wanted.shape, 1), 1.0, 0.0).astype(BF16)
    pieces = jnp.concatenate(halves_of(fields[...]), 1)
    total = jnp.dot(hot, pieces, preferred_element_type=F32)
    total = total[:, : 3 * BLOCK] + total[:, 3 * BLOCK :]
    for index, out in enumerate((out_a, out_b, out_c)):
        out[...] = total[index * tiles : (index + 1) * tiles]


def final_kernel(
    count, grads_a, grads_b, grads_c, weight, contact, vel, vol, drag, cell, out,
):
    tiles = cell.shape[0]
    cells = cell[...]
    heft = lanes_of(weight[...], cells)
    slot = iota(cells.shape, 0) * BLOCK + iota(cells.shape, 1)
    live = slot < count[0]
    volume = vol[...]
    push = TIME_STEP / volume
    for axis in range(3):
        lanes = slice(axis * BLOCK, (axis + 1) * BLOCK)
        gradient = lanes_of(grads_a[:, lanes] + grads_b[:, lanes] + grads_c[:, lanes], cells)
        own = jnp.concatenate(
            [vel[axis : axis + 1, t * BLOCK : (t + 1) * BLOCK] for t in range(tiles)], 0
        )
        fluid = -gradient * heft
        force = contact[axis * tiles : (axis + 1) * tiles, :] - volume * gradient
        force = force + drag[...] * (fluid - own)
        new = jnp.where(live, own + force * push, 0.0)
        for t in range(tiles):
            out[axis : axis + 1, t * BLOCK : (t + 1) * BLOCK] = new[t : t + 1, :]


def on_device(
    grain_pos,
    grain_vel,
    grain_vol,
    drag_coef,
    grain_count,
    contact_rows,
    contact_stiff,
    partner_block,
    halo_list,
    grain_cell,
    tile_cell_block,
    pressure_old,
    pressure_source,
    solid_old,
):
    groups, regions = lax.axis_size("grp"), lax.axis_size("reg")
    holding = groups - 1
    halves = groups // CORES
    slots = grain_pos.shape[1]
    tiles = slots // BLOCK
    planes, full, width = pressure_old.shape
    zones = width // BLOCK
    own_rows = full // halves
    height = min(full, own_rows + SUB * min(2, halves - 1))
    owners = range(0, groups, CORES)
    holders = range(holding)

    def send(value, pairs):
        flat = [(a[0] * regions + a[1], b[0] * regions + b[1]) for a, b in pairs]
        return lax.ppermute(value, ("grp", "reg"), flat)

    def along_reg(value, members, goes):
        pairs = [
            ((g, r), (g, r + goes[r % 2]))
            for g in members
            for r in range(regions)
            if 0 <= r + goes[r % 2] < regions
        ]
        return send(value, pairs)

    def along_grp(value, step, members):
        pairs = [((g, r), ((g + step) % holding, r)) for g in members for r in range(regions)]
        return send(value, pairs)

    count = grain_count
    cell = grain_cell.reshape(tiles, BLOCK)
    vol = grain_vol.reshape(tiles, BLOCK)
    drag = drag_coef.reshape(tiles, BLOCK)
    ids = tile_cell_block.reshape(1, tiles)
    field_bytes = 4 * planes * height * width

    field = shaped(planes, height, width)
    plane = shaped(height, width)
    small = shaped(SUB, BLOCK)
    window, inner = call(
        window_kernel, (shaped(2 * planes, height, width), plane),
        [HBM] * 3, (pressure_old, pressure_source, solid_old),
        [pltpu.VMEM((planes, height, width), F32)] * 2
        + [pltpu.SemaphoreType.DMA((4 * planes + 1,))],
        flops=field_bytes, size=6 * field_bytes, limit=61_950_000, place=HBM,
    )
    near = along_reg(window, owners, (1, -1))
    mine, after_deposit = call(
        deposit_kernel, (shaped(tiles + SUB, 2 * BLOCK), small), [SMEM] + [VMEM] * 4,
        (count, cell, vol, drag, ids), flops=2 * 32 * 48 * 65536, size=5 * 4 * slots,
    )
    second = along_grp(mine, 1, holders)
    third = along_grp(mine, 2, holders)
    rows = halo_list.shape[1] // BLOCK
    halo = shaped(3 * rows, BLOCK)
    state, halo_near, halo_far, after_halo = call(
        halo_kernel, (shaped(3 * tiles, BLOCK), halo, halo, small),
        [VMEM] * 4, (grain_pos, grain_vel, halo_list, after_deposit), flops=2 * 3 * 8 * BLOCK * BLOCK * slots // 4,
        size=4 * 4 * 3 * slots,
    )
    far, after_forward = call(
        forward_kernel, (shaped(2 * planes + 1, height, width), small), [VMEM] * 5,
        (near, inner, after_halo, second, third), size=5 * field_bytes,
    )
    far = along_reg(far, owners, (2, -2))
    message = shaped(holding * (tiles + SUB) + 3 * rows // 2, 2 * BLOCK)
    message_near, message_far, after_message = call(
        message_kernel, (message, message, small), [VMEM] * 6,
        (mine, second, third, halo_near, halo_far, after_forward), size=8 * 2 * BLOCK * 500,
    )
    message_near = along_reg(message_near, owners, (1, -1))
    message_far = along_reg(message_far, owners, (-1, 1))
    others = [g for g in holders if g not in owners]
    halo_near = along_reg(halo_near, others, (1, -1))
    halo_far = along_reg(halo_far, others, (-1, 1))
    constant, factor, weight, rows_at, ends = call(
        functools.partial(own_kernel, full),
        (
            field, field, shaped(tiles, BLOCK),
            jax.ShapeDtypeStruct((3 * tiles, BLOCK), jnp.int32), plane,
        ),
        [VMEM] * 7, (mine, second, third, window, after_message, halo_near, halo_far),
        flops=planes * height * 4 * 384 * 256 * 6, size=9 * field_bytes,
    )
    beyond = along_reg(ends, owners, (-2, 2))

    grads = shaped(tiles, 3 * BLOCK)
    window_of = lambda count: pltpu.VMEM((count, height, width), F32)
    grads_a, grads_b, grads_c = call(
        functools.partial(solve_kernel, full, ITERS), (grads,) * 3,
        [VMEM] * 9,
        (rows_at, message_near, message_far, window, near, far, beyond, constant, factor),
        [
            window_of(2 * planes), window_of(2 * planes),
            window_of(3 * planes + 2), window_of(3 * planes + 2),
            pltpu.VMEM((planes * zones * height, 3 * BLOCK), F32),
        ],
        flops=2 * planes * height * 4 * 384 * 256 * 6, size=20 * field_bytes,
    )
    grads_b = along_grp(grads_b, -1, owners)
    grads_c = along_grp(grads_c, -2, owners)

    contact = call(
        contact_kernel, shaped(3 * tiles, BLOCK), [SMEM] + [VMEM] * 7 + [ANY],
        (
            partner_block, state, message_near, message_far, halo_near, halo_far, contact_rows,
            contact_stiff, grads_a,
        ),
        [pltpu.VMEM((3 * (tiles + 2 * rows), BLOCK), F32)],
        flops=60 * 8 * slots, size=4 * 20 * slots,
    )
    return call(
        final_kernel, shaped(3, slots), [SMEM] + [VMEM] * 9,
        (count, grads_a, grads_b, grads_c, weight, contact, grain_vel, vol, drag, cell),
        flops=60 * slots, size=4 * 20 * slots,
    )


def solution(mesh):
    in_specs = (
        P(None, ("grp", "reg")),
        P(None, ("grp", "reg")),
        P(("grp", "reg")),
        P(("grp", "reg")),
        P(("grp", "reg")),
        P(None, ("grp", "reg")),
        P(None, ("grp", "reg")),
        P(("grp", "reg")),
        P(None, ("grp", "reg")),
        P(("grp", "reg")),
        P(("grp", "reg")),
        P("reg", None, None),
        P("reg", None, None),
        P("reg", None, None),
    )
    out_specs = P(None, ("grp", "reg"))
    return jax.shard_map(
        on_device, mesh=mesh, in_specs=in_specs, out_specs=out_specs, check_vma=False
    )
```

```python
import functools

import jax
import jax.numpy as jnp
from jax import lax
from jax.experimental import pallas as pl
from jax.experimental.pallas import tpu as pltpu
from jax.sharding import PartitionSpec as P

BLOCK = 128
SUB = 8
CORES = 2
ITERS = 4
SPRING = 1.0
DAMPING = 0.5
TIME_STEP = 0.5

VMEM = pl.BlockSpec(memory_space=pltpu.VMEM)
SMEM = pl.BlockSpec(memory_space=pltpu.SMEM)
ANY = pl.BlockSpec(memory_space=pl.ANY)
HBM = pl.BlockSpec(memory_space=pltpu.HBM)
F32 = jnp.float32
BF16 = jnp.bfloat16


def iota(shape, dim):
    return lax.broadcasted_iota(jnp.int32, shape, dim)


def shaped(*dims):
    return jax.ShapeDtypeStruct(dims, F32)


def call(kernel, outs, specs, args, scratch=(), flops=0, size=0, limit=40_000_000, place=VMEM):
    return pl.pallas_call(
        kernel,
        out_shape=outs,
        in_specs=specs,
        out_specs=jax.tree.map(lambda _: place, outs),
        scratch_shapes=list(scratch),
        compiler_params=pltpu.CompilerParams(vmem_limit_bytes=limit),
        cost_estimate=pl.CostEstimate(flops=flops, bytes_accessed=size, transcendentals=0),
    )(*args)


class Place:
    def __init__(self, full, height):
        groups, regions = lax.axis_size("grp"), lax.axis_size("reg")
        self.group, region = lax.axis_index("grp"), lax.axis_index("reg")
        self.half = self.group // CORES
        self.own_rows = full // (groups // CORES)
        first = jnp.clip(self.half * self.own_rows - SUB, 0, full - height)
        self.first = pl.multiple_of(first, SUB)
        self.sweeps = self.group % CORES == 0
        self.parity = region % 2
        self.odd = self.parity == 1
        self.lower, self.upper = region > 0, region < regions - 1


def lanes_of(source, index):
    return jnp.take_along_axis(source, index, axis=1, mode="promise_in_bounds")


def halves_of(value):
    high = value.astype(BF16)
    return high, (value - high.astype(F32)).astype(BF16)


def window_kernel(pressure_old, source, solid_before, window, inner, pressure, driven, solid, sems):
    planes, height, _ = solid.shape
    place = Place(pressure_old.shape[1], height)
    rows = pl.ds(place.first, height)
    used = []

    def copy(whole, part):
        used.append(None)
        return pltpu.make_async_copy(whole, part, sems.at[len(used) - 1])

    fetched = [
        [copy(whole.at[x, rows, :], part.at[x]) for x in range(planes)]
        for whole, part in ((pressure_old, pressure), (source, driven), (solid_before, solid))
    ]
    stored = [copy(pressure.at[x], window.at[x]) for x in range(planes)]
    stored += [copy(driven.at[x], window.at[planes + x]) for x in range(planes)]
    stored.append(copy(pressure.at[(1 - place.parity) * (planes - 1)], inner))
    for x in range(planes):
        for part in fetched:
            part[x].start()
    for x in range(planes):
        fetched[0][x].wait()
        stored[x].start()
        fetched[1][x].wait()
        fetched[2][x].wait()
        driven[x] = driven[x] - solid[x]
        stored[planes + x].start()
    stored[2 * planes].start()
    for one in stored:
        one.wait()


def forward_kernel(near, inner, _halo, _second, _third, out, dummy):
    dummy[...] = jnp.zeros(dummy.shape, F32)
    count = near.shape[0]
    out[:count] = near[...]
    out[count] = inner[...]


def deposit_kernel(count, cell, vol, drag, ids, out, dummy):
    dummy[...] = jnp.zeros(dummy.shape, F32)
    tiles = cell.shape[0]
    sub = iota((SUB, BLOCK), 0)
    rows_c = iota((BLOCK, BLOCK), 0)
    even = sub % 2 == 0
    low_pair = sub % 4 < 2

    def step(group, carry):
        first = pl.multiple_of(group * SUB, SUB)
        slot = (first + sub) * BLOCK + iota((SUB, BLOCK), 1)
        live = slot < count[0]
        cells = cell[pl.ds(first, SUB), :]
        parts = halves_of(jnp.where(live, vol[pl.ds(first, SUB), :], 0.0)) + halves_of(
            jnp.where(live, drag[pl.ds(first, SUB), :], 0.0)
        )
        parts = [part.astype(F32) for part in parts]
        left = jnp.concatenate([jnp.where(even, part, 0.0) for part in parts], 0)
        right = jnp.concatenate([jnp.where(even, 0.0, part) for part in parts], 0)
        loads = jnp.concatenate([left, right], 1).astype(BF16)
        sums = [jnp.zeros((SUB, BLOCK), F32), jnp.zeros((SUB, BLOCK), F32)]
        for quad in range(SUB // 4):
            hot = [
                jnp.where(
                    rows_c == jnp.broadcast_to(cells[t : t + 1, :], (BLOCK, BLOCK)), 1.0, 0.0
                ).astype(BF16)
                for t in range(4 * quad, 4 * quad + 4)
            ]
            picked = jnp.concatenate(
                [jnp.concatenate(hot[:2], 1), jnp.concatenate(hot[2:], 1)], 0
            )
            placed = lax.dot_general(
                loads, picked, (((1,), (1,)), ((), ())), preferred_element_type=F32
            )
            for field in range(2):
                base = field * 2 * SUB
                total = placed[base : base + SUB] + placed[base + SUB : base + 2 * SUB]
                chosen = jnp.where(low_pair, total[:, :BLOCK], total[:, BLOCK:])
                sums[field] = jnp.where(sub // 4 == quad, chosen, sums[field])
        out[pl.ds(first, SUB), :BLOCK] = sums[0]
        out[pl.ds(first, SUB), BLOCK:] = sums[1]
        return carry

    lax.fori_loop(0, tiles // SUB, step, 0, unroll=4)
    out[tiles : tiles + SUB, :BLOCK] = jnp.broadcast_to(ids[...].astype(F32), (SUB, BLOCK))
    out[tiles : tiles + SUB, BLOCK:] = jnp.zeros((SUB, BLOCK), F32)


def halo_kernel(pos, vel, lists, _, state, near, far, dummy):
    dummy[...] = jnp.zeros(dummy.shape, F32)
    tiles = pos.shape[1] // BLOCK
    rows = lists.shape[1] // BLOCK
    for tile in range(tiles):
        lanes = slice(tile * BLOCK, (tile + 1) * BLOCK)
        mixed = SPRING * pos[:, lanes] - DAMPING * vel[:, lanes]
        for axis in range(3):
            state[axis * tiles + tile : axis * tiles + tile + 1, :] = mixed[axis : axis + 1]
    turned = [
        jnp.concatenate(halves_of(jnp.transpose(state[axis * tiles : (axis + 1) * tiles, :])), 1)
        for axis in range(3)
    ]
    turned = jnp.concatenate(turned, 0)
    span = 2 * BLOCK
    row = iota((BLOCK, span), 0)

    odd = lax.axis_index("reg") % 2
    for away, out in enumerate((near, far)):
        side = 1 - odd if away == 0 else odd

        def step(part, carry):
            named = lists[:, pl.ds(pl.multiple_of(part * span, span), span)]
            named = jnp.where(side == 0, named[:1], named[1:])
            block = lax.shift_right_logical(named, 7)
            lane = named & (BLOCK - 1)
            hot = jnp.where(row == jnp.broadcast_to(block, row.shape), 1.0, 0.0).astype(BF16)
            found = jnp.dot(
                turned, jnp.concatenate([hot, hot], 0), preferred_element_type=F32
            )
            here = row == jnp.broadcast_to(lane, row.shape)
            for axis in range(3):
                value = jnp.where(here, found[axis * BLOCK : (axis + 1) * BLOCK], 0.0)
                value = jnp.sum(value, axis=0, keepdims=True)
                for half in range(2):
                    out[pl.ds(axis * rows + 2 * part + half, 1), :] = value[
                        :, half * BLOCK : (half + 1) * BLOCK
                    ]
            return carry

        lax.fori_loop(0, rows // 2, step, 0, unroll=8)


def message_kernel(mine, second, third, halo_near, halo_far, _, near, far, dummy):
    dummy[...] = jnp.zeros(dummy.shape, F32)
    stride = mine.shape[0]
    half = halo_near.shape[0] // 2
    rows = near.shape[0] - half
    for halo, out in ((halo_near, near), (halo_far, far)):
        for index, group in enumerate((mine, second, third)):
            out[index * stride : (index + 1) * stride, :] = group[...]
        out[rows:, :BLOCK] = halo[:half, :]
        out[rows:, BLOCK:] = halo[half:, :]


def contact_kernel(
    partner, state, message_near, message_far, halo_near, halo_far, named, stiff, _, out, extended
):
    tiles = state.shape[0] // 3
    rows = halo_near.shape[0] // 3
    blocks = tiles + 2 * rows
    base = message_near.shape[0] - 3 * rows // 2
    odd = lax.axis_index("reg") % 2
    sweeps = lax.axis_index("grp") % CORES == 0
    for axis in range(3):
        extended[axis * blocks : axis * blocks + tiles, :] = state[
            axis * tiles : (axis + 1) * tiles, :
        ]
    for message, halo, upper in (
        (message_near, halo_near, 1 - odd), (message_far, halo_far, odd)
    ):
        carried = jnp.concatenate([message[base:, :BLOCK], message[base:, BLOCK:]], 0)
        carried = jnp.where(sweeps, carried, halo[...])
        for axis in range(3):
            first = pl.multiple_of(axis * blocks + tiles + upper * rows, SUB)
            extended[pl.ds(first, rows), :] = carried[axis * rows : (axis + 1) * rows]

    def step(tile, carry):
        lanes = pl.ds(pl.multiple_of(tile * BLOCK, BLOCK), BLOCK)
        entry = named[:, lanes]
        weight = jnp.where(entry >= 0, stiff[:, lanes], 0.0)
        own = entry < BLOCK
        lane = entry & (BLOCK - 1)
        other = partner[tile]
        for axis in range(3):
            mine = jnp.broadcast_to(extended[pl.ds(axis * blocks + tile, 1), :], entry.shape)
            theirs = jnp.broadcast_to(extended[pl.ds(axis * blocks + other, 1), :], entry.shape)
            met = jnp.where(own, lanes_of(mine, lane), lanes_of(theirs, lane))
            pull = jnp.sum(weight * (mine - met), axis=0, keepdims=True)
            out[pl.ds(axis * tiles + tile, 1), :] = pull
        return carry

    lax.fori_loop(0, tiles, step, 0, unroll=4)


def shifted(plane):
    height, width = plane.shape
    row = iota((SUB, width), 0)
    column = iota((height, BLOCK), 1)
    above, below = pltpu.roll(plane, 1, 0), pltpu.roll(plane, height - 1, 0)
    left, right = pltpu.roll(plane, 1, 1), pltpu.roll(plane, width - 1, 1)
    above = jnp.concatenate([jnp.where(row == 0, 0.0, above[:SUB]), above[SUB:]], 0)
    below = jnp.concatenate([below[:-SUB], jnp.where(row == SUB - 1, 0.0, below[-SUB:])], 0)
    left = jnp.concatenate([jnp.where(column == 0, 0.0, left[:, :BLOCK]), left[:, BLOCK:]], 1)
    right = jnp.concatenate(
        [right[:, :-BLOCK], jnp.where(column == BLOCK - 1, 0.0, right[:, -BLOCK:])], 1
    )
    return above, below, left, right


def inverse_of(value):
    near = pl.reciprocal(value, approx=True)
    return near * (2.0 - value * near)


def placed(groups, tiles):
    parts = [halves_of(group[:tiles, :]) for group in groups]
    loads = jnp.concatenate([part[i] for i in range(2) for part in parts], 0)
    ids = jnp.concatenate([group[tiles : tiles + 1, :BLOCK] for group in groups], 1)
    ids = ids.astype(jnp.int32)

    def gathered(wanted):
        hot = jnp.where(wanted == jnp.broadcast_to(ids, wanted.shape), 1.0, 0.0).astype(BF16)
        total = jnp.dot(
            jnp.concatenate([hot, hot], 1), loads, preferred_element_type=F32
        )
        return total[:, :BLOCK], total[:, BLOCK:]

    return ids, gathered


def coefficients(gathered, tiles, first, full, driven, planes, constant, factor, base, present):
    _, height, width = driven.shape
    zones = width // BLOCK
    shape = (zones * height, 3 * tiles)
    line = iota(shape, 0)
    block = (line % height) * zones + line // height + first * zones

    for x in range(planes):
        solid, drag = gathered(block + x * (full * zones))
        voids = 1.0 + solid
        scale = inverse_of(6.0 + (drag + 1.0) * voids)
        if present is not None:
            scale = jnp.where(present, scale, 0.0)
        inverse = voids * scale
        for zone in range(zones):
            lanes = slice(zone * BLOCK, (zone + 1) * BLOCK)
            rows = slice(zone * height, (zone + 1) * height)
            driving = driven[planes + x, :, lanes] + solid[rows]
            constant[base + x, :, lanes] = driving * inverse[rows]
            factor[base + x, :, lanes] = scale[rows]


def own_kernel(
    full, mine, second, third, window, _message, _near, _far, constant, factor, weight, picks, ends
):
    tiles = weight.shape[0]
    planes, height, width = constant.shape
    place = Place(full, height)
    zones = width // BLOCK
    ends[...] = window[place.parity * (planes - 1)]
    ids, gathered = placed((mine, second, third), tiles)
    coefficients(gathered, tiles, place.first, full, window, planes, constant, factor, 0, None)
    turned = [
        jnp.transpose(
            jnp.broadcast_to(ids[:, i * tiles : (i + 1) * tiles], (BLOCK, tiles)).astype(F32)
        ).astype(jnp.int32)
        for i in range(3)
    ]
    solid, drag = gathered(jnp.concatenate([turned[0]] * 3, 1))
    weight[...] = 1.0 / (1.0 / (1.0 + solid) + drag)
    for i in range(3):
        block = turned[i]
        line, zone = block // zones, block % zones
        x, y = line // full, line % full
        row = (x * zones + zone) * height + y - place.first
        held = y // place.own_rows == jnp.where(place.sweeps, place.half, -1)
        row = jnp.concatenate([jnp.where(held, row, -1)] * (picks.shape[1] // BLOCK), 1)
        hot = jnp.where(row == iota(row.shape, 1), 1.0, 0.0).astype(BF16)
        picks[i * tiles : (i + 1) * tiles, :] = hot


def solve_kernel(
    full, sweeps, picks, joined_near, joined_far, window, near, far, beyond,
    own_constant, own_factor, out_a, out_b, out_c,
    constant, factor, old, new, fields,
):
    planes, height, width = own_constant.shape
    zones = width // BLOCK
    tiles = out_a.shape[0]
    place = Place(full, height)
    odd = place.odd
    rim = sweeps + 1
    for joined, driven, below, present in (
        (joined_near, near, odd, jnp.where(odd, place.lower, place.upper)),
        (joined_far, far, jnp.logical_not(odd), jnp.where(odd, place.upper, place.lower)),
    ):
        stride = tiles + SUB
        groups = [joined.at[i * stride : (i + 1) * stride] for i in range(3)]
        _, gathered = placed(groups, tiles)
        coefficients(
            gathered, tiles, place.first, full, driven, planes, constant, factor,
            jnp.where(below, 0, planes), present,
        )
    old[pl.ds(jnp.where(odd, 1, rim + planes), planes)] = near[:planes]
    old[pl.ds(jnp.where(odd, rim + planes, 1), planes)] = far[:planes]
    old[pl.ds(jnp.where(odd, rim + 2 * planes, 0), 1)] = far[2 * planes :]
    old[pl.ds(jnp.where(odd, 0, rim + 2 * planes), 1)] = beyond[...][None]
    old[rim : rim + planes] = window[:planes]

    def sweep(source, target, depth):
        def over(constants, factors, shift):
            def plane(x, carry):
                centre = source[x]
                above, below, left, right = shifted(centre)
                around = source[x - 1] + source[x + 1] + above + below + left + right
                target[x] = constants[x - shift] + factors[x - shift] * around
                return carry

            return plane

        lax.fori_loop(depth, rim, over(constant, factor, 1), 0, unroll=4)
        lax.fori_loop(rim, rim + planes, over(own_constant, own_factor, rim), 0, unroll=4)
        lax.fori_loop(
            rim + planes, 3 * planes + 2 - depth, over(constant, factor, 1 + planes), 0, unroll=4
        )

    for index in range(sweeps):
        source, target = (old, new) if index % 2 == 0 else (new, old)
        sweep(source, target, index + 1)
    last = old if sweeps % 2 == 0 else new

    def gradient(x, carry):
        centre = last[rim + x]
        above, below, left, right = shifted(centre)
        grads = (last[rim + x + 1] - last[rim + x - 1], below - above, right - left)
        for zone in range(zones):
            first = pl.multiple_of((x * zones + zone) * height, SUB)
            for axis, grad in enumerate(grads):
                fields[pl.ds(first, height), axis * BLOCK : (axis + 1) * BLOCK] = (
                    0.5 * grad[:, zone * BLOCK : (zone + 1) * BLOCK]
                )
        return carry

    lax.fori_loop(0, planes, gradient, 0, unroll=4)
    pieces = jnp.concatenate(halves_of(fields[...]), 1)
    total = jnp.dot(picks[...], pieces, preferred_element_type=F32)
    total = total[:, : 3 * BLOCK] + total[:, 3 * BLOCK :]
    for index, out in enumerate((out_a, out_b, out_c)):
        out[...] = total[index * tiles : (index + 1) * tiles]


def final_kernel(
    count, grads_a, grads_b, grads_c, weight, contact, vel, vol, drag, cell, out,
):
    tiles = cell.shape[0]
    cells = cell[...]
    heft = lanes_of(weight[...], cells)
    slot = iota(cells.shape, 0) * BLOCK + iota(cells.shape, 1)
    live = slot < count[0]
    volume = vol[...]
    push = TIME_STEP / volume
    for axis in range(3):
        lanes = slice(axis * BLOCK, (axis + 1) * BLOCK)
        gradient = lanes_of(grads_a[:, lanes] + grads_b[:, lanes] + grads_c[:, lanes], cells)
        own = jnp.concatenate(
            [vel[axis : axis + 1, t * BLOCK : (t + 1) * BLOCK] for t in range(tiles)], 0
        )
        fluid = -gradient * heft
        force = contact[axis * tiles : (axis + 1) * tiles, :] - volume * gradient
        force = force + drag[...] * (fluid - own)
        new = jnp.where(live, own + force * push, 0.0)
        for t in range(tiles):
            out[axis : axis + 1, t * BLOCK : (t + 1) * BLOCK] = new[t : t + 1, :]


def on_device(
    grain_pos,
    grain_vel,
    grain_vol,
    drag_coef,
    grain_count,
    contact_rows,
    contact_stiff,
    partner_block,
    halo_list,
    grain_cell,
    tile_cell_block,
    pressure_old,
    pressure_source,
    solid_old,
):
    groups, regions = lax.axis_size("grp"), lax.axis_size("reg")
    holding = groups - 1
    halves = groups // CORES
    slots = grain_pos.shape[1]
    tiles = slots // BLOCK
    planes, full, width = pressure_old.shape
    zones = width // BLOCK
    own_rows = full // halves
    height = min(full, own_rows + SUB * min(2, halves - 1))
    owners = range(0, groups, CORES)
    holders = range(holding)

    def send(value, pairs):
        flat = [(a[0] * regions + a[1], b[0] * regions + b[1]) for a, b in pairs]
        return lax.ppermute(value, ("grp", "reg"), flat)

    def along_reg(value, members, goes):
        pairs = [
            ((g, r), (g, r + goes[r % 2]))
            for g in members
            for r in range(regions)
            if 0 <= r + goes[r % 2] < regions
        ]
        return send(value, pairs)

    def along_grp(value, step, members):
        pairs = [((g, r), ((g + step) % holding, r)) for g in members for r in range(regions)]
        return send(value, pairs)

    count = grain_count
    cell = grain_cell.reshape(tiles, BLOCK)
    vol = grain_vol.reshape(tiles, BLOCK)
    drag = drag_coef.reshape(tiles, BLOCK)
    ids = tile_cell_block.reshape(1, tiles)
    field_bytes = 4 * planes * height * width

    field = shaped(planes, height, width)
    plane = shaped(height, width)
    small = shaped(SUB, BLOCK)
    window, inner = call(
        window_kernel, (shaped(2 * planes, height, width), plane),
        [HBM] * 3, (pressure_old, pressure_source, solid_old),
        [pltpu.VMEM((planes, height, width), F32)] * 3
        + [pltpu.SemaphoreType.DMA((5 * planes + 1,))],
        flops=field_bytes, size=6 * field_bytes, limit=61_950_000, place=HBM,
    )
    near = along_reg(window, owners, (1, -1))
    mine, after_deposit = call(
        deposit_kernel, (shaped(tiles + SUB, 2 * BLOCK), small), [SMEM] + [VMEM] * 4,
        (count, cell, vol, drag, ids), flops=2 * 32 * 48 * 65536, size=5 * 4 * slots,
    )
    second = along_grp(mine, 1, holders)
    third = along_grp(mine, 2, holders)
    rows = halo_list.shape[1] // BLOCK
    halo = shaped(3 * rows, BLOCK)
    state, halo_near, halo_far, after_halo = call(
        halo_kernel, (shaped(3 * tiles, BLOCK), halo, halo, small),
        [VMEM] * 4, (grain_pos, grain_vel, halo_list, after_deposit), flops=2 * 3 * 8 * BLOCK * BLOCK * slots // 4,
        size=4 * 4 * 3 * slots,
    )
    far, after_forward = call(
        forward_kernel, (shaped(2 * planes + 1, height, width), small), [VMEM] * 5,
        (near, inner, after_halo, second, third), size=5 * field_bytes,
    )
    far = along_reg(far, owners, (2, -2))
    message = shaped(holding * (tiles + SUB) + 3 * rows // 2, 2 * BLOCK)
    message_near, message_far, after_message = call(
        message_kernel, (message, message, small), [VMEM] * 6,
        (mine, second, third, halo_near, halo_far, after_forward), size=8 * 2 * BLOCK * 500,
    )
    message_near = along_reg(message_near, owners, (1, -1))
    message_far = along_reg(message_far, owners, (-1, 1))
    others = [g for g in holders if g not in owners]
    halo_near = along_reg(halo_near, others, (1, -1))
    halo_far = along_reg(halo_far, others, (-1, 1))
    constant, factor, weight, picks, ends = call(
        functools.partial(own_kernel, full),
        (
            field, field, shaped(tiles, BLOCK),
            jax.ShapeDtypeStruct((3 * tiles, planes * zones * height), BF16), plane,
        ),
        [VMEM] * 7, (mine, second, third, window, after_message, halo_near, halo_far),
        flops=planes * height * 4 * 384 * 256 * 6, size=9 * field_bytes,
    )
    beyond = along_reg(ends, owners, (-2, 2))

    grads = shaped(tiles, 3 * BLOCK)
    window_of = lambda count: pltpu.VMEM((count, height, width), F32)
    grads_a, grads_b, grads_c = call(
        functools.partial(solve_kernel, full, ITERS), (grads,) * 3,
        [VMEM] * 9,
        (picks, message_near, message_far, window, near, far, beyond, constant, factor),
        [
            window_of(2 * planes), window_of(2 * planes),
            window_of(3 * planes + 2), window_of(3 * planes + 2),
            pltpu.VMEM((planes * zones * height, 3 * BLOCK), F32),
        ],
        flops=2 * planes * height * 4 * 384 * 256 * 6, size=20 * field_bytes,
    )
    grads_b = along_grp(grads_b, -1, owners)
    grads_c = along_grp(grads_c, -2, owners)

    contact = call(
        contact_kernel, shaped(3 * tiles, BLOCK), [SMEM] + [VMEM] * 7 + [ANY],
        (
            partner_block, state, message_near, message_far, halo_near, halo_far, contact_rows,
            contact_stiff, grads_a,
        ),
        [pltpu.VMEM((3 * (tiles + 2 * rows), BLOCK), F32)],
        flops=60 * 8 * slots, size=4 * 20 * slots,
    )
    return call(
        final_kernel, shaped(3, slots), [SMEM] + [VMEM] * 9,
        (count, grads_a, grads_b, grads_c, weight, contact, grain_vel, vol, drag, cell),
        flops=60 * slots, size=4 * 20 * slots,
    )


def solution(mesh):
    in_specs = (
        P(None, ("grp", "reg")),
        P(None, ("grp", "reg")),
        P(("grp", "reg")),
        P(("grp", "reg")),
        P(("grp", "reg")),
        P(None, ("grp", "reg")),
        P(None, ("grp", "reg")),
        P(("grp", "reg")),
        P(None, ("grp", "reg")),
        P(("grp", "reg")),
        P(("grp", "reg")),
        P("reg", None, None),
        P("reg", None, None),
        P("reg", None, None),
    )
    out_specs = P(None, ("grp", "reg"))
    return jax.shard_map(
        on_device, mesh=mesh, in_specs=in_specs, out_specs=out_specs, check_vma=False
    )
```

```python
import functools

import jax
import jax.numpy as jnp
from jax import lax
from jax.experimental import pallas as pl
from jax.experimental.pallas import tpu as pltpu
from jax.sharding import PartitionSpec as P

BLOCK = 128
SUB = 8
CORES = 2
ITERS = 4
SPRING = 1.0
DAMPING = 0.5
TIME_STEP = 0.5

VMEM = pl.BlockSpec(memory_space=pltpu.VMEM)
SMEM = pl.BlockSpec(memory_space=pltpu.SMEM)
ANY = pl.BlockSpec(memory_space=pl.ANY)
HBM = pl.BlockSpec(memory_space=pltpu.HBM)
F32 = jnp.float32
BF16 = jnp.bfloat16


def iota(shape, dim):
    return lax.broadcasted_iota(jnp.int32, shape, dim)


def shaped(*dims):
    return jax.ShapeDtypeStruct(dims, F32)


def call(kernel, outs, specs, args, scratch=(), flops=0, size=0, limit=40_000_000, place=VMEM):
    return pl.pallas_call(
        kernel,
        out_shape=outs,
        in_specs=specs,
        out_specs=jax.tree.map(lambda _: place, outs),
        scratch_shapes=list(scratch),
        compiler_params=pltpu.CompilerParams(vmem_limit_bytes=limit),
        cost_estimate=pl.CostEstimate(flops=flops, bytes_accessed=size, transcendentals=0),
    )(*args)


class Place:
    def __init__(self, full, height):
        groups, regions = lax.axis_size("grp"), lax.axis_size("reg")
        self.group, region = lax.axis_index("grp"), lax.axis_index("reg")
        self.half = self.group // CORES
        self.own_rows = full // (groups // CORES)
        first = jnp.clip(self.half * self.own_rows - SUB, 0, full - height)
        self.first = pl.multiple_of(first, SUB)
        self.sweeps = self.group % CORES == 0
        self.parity = region % 2
        self.odd, self.even = self.parity == 1, self.parity == 0
        self.lower, self.upper = region > 0, region < regions - 1


def lanes_of(source, index):
    return jnp.take_along_axis(source, index, axis=1, mode="promise_in_bounds")


def halves_of(value):
    high = value.astype(BF16)
    return high, (value - high.astype(F32)).astype(BF16)


def window_kernel(pressure_old, source, solid_before, window, inner, pressure, driven, solid, sems):
    planes, height, _ = solid.shape
    place = Place(pressure_old.shape[1], height)
    rows = pl.ds(place.first, height)
    used = []

    def copy(whole, part):
        used.append(None)
        return pltpu.make_async_copy(whole, part, sems.at[len(used) - 1])

    fetched = [
        [copy(whole.at[x, rows, :], part.at[x]) for x in range(planes)]
        for whole, part in ((pressure_old, pressure), (source, driven), (solid_before, solid))
    ]
    stored = [copy(pressure.at[x], window.at[x]) for x in range(planes)]
    stored += [copy(driven.at[x], window.at[planes + x]) for x in range(planes)]
    stored.append(copy(pressure.at[(1 - place.parity) * (planes - 1)], inner))
    for x in range(planes):
        for part in fetched:
            part[x].start()
    for x in range(planes):
        fetched[0][x].wait()
        stored[x].start()
        fetched[1][x].wait()
        fetched[2][x].wait()
        driven[x] = driven[x] - solid[x]
        stored[planes + x].start()
    stored[2 * planes].start()
    for one in stored:
        one.wait()


def forward_kernel(near, inner, _halo, _second, _third, _near, _far, out, dummy):
    dummy[...] = jnp.zeros(dummy.shape, F32)
    count = near.shape[0]
    out[:count] = near[...]
    out[count] = inner[...]


def deposit_kernel(count, cell, vol, drag, ids, out, dummy):
    dummy[...] = jnp.zeros(dummy.shape, F32)
    tiles = cell.shape[0]
    sub = iota((SUB, BLOCK), 0)
    rows_c = iota((BLOCK, BLOCK), 0)
    even = sub % 2 == 0
    low_pair = sub % 4 < 2

    def step(group, carry):
        first = pl.multiple_of(group * SUB, SUB)
        slot = (first + sub) * BLOCK + iota((SUB, BLOCK), 1)
        live = slot < count[0]
        cells = cell[pl.ds(first, SUB), :]
        parts = halves_of(jnp.where(live, vol[pl.ds(first, SUB), :], 0.0)) + halves_of(
            jnp.where(live, drag[pl.ds(first, SUB), :], 0.0)
        )
        parts = [part.astype(F32) for part in parts]
        left = jnp.concatenate([jnp.where(even, part, 0.0) for part in parts], 0)
        right = jnp.concatenate([jnp.where(even, 0.0, part) for part in parts], 0)
        loads = jnp.concatenate([left, right], 1).astype(BF16)
        sums = [jnp.zeros((SUB, BLOCK), F32), jnp.zeros((SUB, BLOCK), F32)]
        for quad in range(SUB // 4):
            hot = [
                jnp.where(
                    rows_c == jnp.broadcast_to(cells[t : t + 1, :], (BLOCK, BLOCK)), 1.0, 0.0
                ).astype(BF16)
                for t in range(4 * quad, 4 * quad + 4)
            ]
            picked = jnp.concatenate(
                [jnp.concatenate(hot[:2], 1), jnp.concatenate(hot[2:], 1)], 0
            )
            placed = lax.dot_general(
                loads, picked, (((1,), (1,)), ((), ())), preferred_element_type=F32
            )
            for field in range(2):
                base = field * 2 * SUB
                total = placed[base : base + SUB] + placed[base + SUB : base + 2 * SUB]
                chosen = jnp.where(low_pair, total[:, :BLOCK], total[:, BLOCK:])
                sums[field] = jnp.where(sub // 4 == quad, chosen, sums[field])
        out[pl.ds(first, SUB), :BLOCK] = sums[0]
        out[pl.ds(first, SUB), BLOCK:] = sums[1]
        return carry

    lax.fori_loop(0, tiles // SUB, step, 0, unroll=4)
    out[tiles : tiles + SUB, :BLOCK] = jnp.broadcast_to(ids[...].astype(F32), (SUB, BLOCK))
    out[tiles : tiles + SUB, BLOCK:] = jnp.zeros((SUB, BLOCK), F32)


def halo_kernel(pos, vel, lists, _, state, near, far, dummy):
    dummy[...] = jnp.zeros(dummy.shape, F32)
    tiles = pos.shape[1] // BLOCK
    rows = lists.shape[1] // BLOCK
    for tile in range(tiles):
        lanes = slice(tile * BLOCK, (tile + 1) * BLOCK)
        mixed = SPRING * pos[:, lanes] - DAMPING * vel[:, lanes]
        for axis in range(3):
            state[axis * tiles + tile : axis * tiles + tile + 1, :] = mixed[axis : axis + 1]
    turned = [
        jnp.concatenate(halves_of(jnp.transpose(state[axis * tiles : (axis + 1) * tiles, :])), 1)
        for axis in range(3)
    ]
    turned = jnp.concatenate(turned, 0)
    span = 2 * BLOCK
    row = iota((BLOCK, span), 0)

    odd = lax.axis_index("reg") % 2
    for away, out in enumerate((near, far)):
        side = 1 - odd if away == 0 else odd

        def step(part, carry):
            named = lists[:, pl.ds(pl.multiple_of(part * span, span), span)]
            named = jnp.where(side == 0, named[:1], named[1:])
            block = lax.shift_right_logical(named, 7)
            lane = named & (BLOCK - 1)
            hot = jnp.where(row == jnp.broadcast_to(block, row.shape), 1.0, 0.0).astype(BF16)
            found = jnp.dot(
                turned, jnp.concatenate([hot, hot], 0), preferred_element_type=F32
            )
            here = row == jnp.broadcast_to(lane, row.shape)
            for axis in range(3):
                value = jnp.where(here, found[axis * BLOCK : (axis + 1) * BLOCK], 0.0)
                value = jnp.sum(value, axis=0, keepdims=True)
                for half in range(2):
                    out[pl.ds(axis * rows + 2 * part + half, 1), :] = value[
                        :, half * BLOCK : (half + 1) * BLOCK
                    ]
            return carry

        lax.fori_loop(0, rows // 2, step, 0, unroll=8)


def message_kernel(mine, second, third, halo_near, halo_far, window, _, near, far, ends, dummy):
    dummy[...] = jnp.zeros(dummy.shape, F32)
    ends[...] = window[(lax.axis_index("reg") % 2) * (window.shape[0] // 2 - 1)]
    stride = mine.shape[0]
    half = halo_near.shape[0] // 2
    rows = near.shape[0] - half
    for halo, out in ((halo_near, near), (halo_far, far)):
        for index, group in enumerate((mine, second, third)):
            out[index * stride : (index + 1) * stride, :] = group[...]
        out[rows:, :BLOCK] = halo[:half, :]
        out[rows:, BLOCK:] = halo[half:, :]


def contact_kernel(
    partner, state, message_near, message_far, halo_near, halo_far, named, stiff, _, out, extended
):
    tiles = state.shape[0] // 3
    rows = halo_near.shape[0] // 3
    blocks = tiles + 2 * rows
    base = message_near.shape[0] - 3 * rows // 2
    odd = lax.axis_index("reg") % 2
    sweeps = lax.axis_index("grp") % CORES == 0
    for axis in range(3):
        extended[axis * blocks : axis * blocks + tiles, :] = state[
            axis * tiles : (axis + 1) * tiles, :
        ]
    for message, halo, upper in (
        (message_near, halo_near, 1 - odd), (message_far, halo_far, odd)
    ):
        carried = jnp.concatenate([message[base:, :BLOCK], message[base:, BLOCK:]], 0)
        carried = jnp.where(sweeps, carried, halo[...])
        for axis in range(3):
            first = pl.multiple_of(axis * blocks + tiles + upper * rows, SUB)
            extended[pl.ds(first, rows), :] = carried[axis * rows : (axis + 1) * rows]

    def step(tile, carry):
        lanes = pl.ds(pl.multiple_of(tile * BLOCK, BLOCK), BLOCK)
        entry = named[:, lanes]
        weight = jnp.where(entry >= 0, stiff[:, lanes], 0.0)
        own = entry < BLOCK
        lane = entry & (BLOCK - 1)
        other = partner[tile]
        for axis in range(3):
            mine = jnp.broadcast_to(extended[pl.ds(axis * blocks + tile, 1), :], entry.shape)
            theirs = jnp.broadcast_to(extended[pl.ds(axis * blocks + other, 1), :], entry.shape)
            met = jnp.where(own, lanes_of(mine, lane), lanes_of(theirs, lane))
            pull = jnp.sum(weight * (mine - met), axis=0, keepdims=True)
            out[pl.ds(axis * tiles + tile, 1), :] = pull
        return carry

    lax.fori_loop(0, tiles, step, 0, unroll=4)


def shifted(plane):
    height, width = plane.shape
    row = iota((SUB, width), 0)
    column = iota((height, BLOCK), 1)
    above, below = pltpu.roll(plane, 1, 0), pltpu.roll(plane, height - 1, 0)
    left, right = pltpu.roll(plane, 1, 1), pltpu.roll(plane, width - 1, 1)
    above = jnp.concatenate([jnp.where(row == 0, 0.0, above[:SUB]), above[SUB:]], 0)
    below = jnp.concatenate([below[:-SUB], jnp.where(row == SUB - 1, 0.0, below[-SUB:])], 0)
    left = jnp.concatenate([jnp.where(column == 0, 0.0, left[:, :BLOCK]), left[:, BLOCK:]], 1)
    right = jnp.concatenate(
        [right[:, :-BLOCK], jnp.where(column == BLOCK - 1, 0.0, right[:, -BLOCK:])], 1
    )
    return above, below, left, right


def inverse_of(value):
    near = pl.reciprocal(value, approx=True)
    return near * (2.0 - value * near)


def placed(groups, tiles):
    parts = [halves_of(group[:tiles, :]) for group in groups]
    loads = jnp.concatenate([part[i] for i in range(2) for part in parts], 0)
    ids = jnp.concatenate([group[tiles : tiles + 1, :BLOCK] for group in groups], 1)
    ids = ids.astype(jnp.int32)

    def gathered(wanted):
        hot = jnp.where(wanted == jnp.broadcast_to(ids, wanted.shape), 1.0, 0.0).astype(BF16)
        total = jnp.dot(
            jnp.concatenate([hot, hot], 1), loads, preferred_element_type=F32
        )
        return total[:, :BLOCK], total[:, BLOCK:]

    return ids, gathered


def coefficients(gathered, tiles, first, full, driven, planes, constant, factor, turned, present):
    _, height, width = driven.shape
    zones = width // BLOCK
    shape = (zones * height, 3 * tiles)
    line = iota(shape, 0)
    block = (line % height) * zones + line // height + first * zones

    for x in range(planes):
        solid, drag = gathered(block + x * (full * zones))
        at = x if turned is None else jnp.where(turned, planes - 1 - x, x)
        voids = 1.0 + solid
        scale = inverse_of(6.0 + (drag + 1.0) * voids)
        if present is not None:
            scale = jnp.where(present, scale, 0.0)
        inverse = voids * scale
        for zone in range(zones):
            lanes = slice(zone * BLOCK, (zone + 1) * BLOCK)
            rows = slice(zone * height, (zone + 1) * height)
            driving = driven[x, :, lanes] + solid[rows]
            constant[at, :, lanes] = driving * inverse[rows]
            factor[at, :, lanes] = scale[rows]


def own_kernel(
    full, mine, second, third, window, _message, constant, factor, weight, picks
):
    tiles = weight.shape[0]
    planes, height, width = constant.shape
    place = Place(full, height)
    zones = width // BLOCK
    ids, gathered = placed((mine, second, third), tiles)
    coefficients(gathered, tiles, place.first, full, window.at[planes:], planes, constant, factor, place.even, None)
    turned = [
        jnp.transpose(
            jnp.broadcast_to(ids[:, i * tiles : (i + 1) * tiles], (BLOCK, tiles)).astype(F32)
        ).astype(jnp.int32)
        for i in range(3)
    ]
    solid, drag = gathered(jnp.concatenate([turned[0]] * 3, 1))
    weight[...] = 1.0 / (1.0 / (1.0 + solid) + drag)
    for i in range(3):
        block = turned[i]
        line, zone = block // zones, block % zones
        x, y = line // full, line % full
        row = (x * zones + zone) * height + y - place.first
        held = y // place.own_rows == jnp.where(place.sweeps, place.half, -1)
        row = jnp.concatenate([jnp.where(held, row, -1)] * (picks.shape[1] // BLOCK), 1)
        hot = jnp.where(row == iota(row.shape, 1), 1.0, 0.0).astype(BF16)
        picks[i * tiles : (i + 1) * tiles, :] = hot


def sweep(source, target, coefficient, start, stop):
    def plane(at, carry):
        above, below, left, right = shifted(source[at])
        around = source[at - 1] + source[at + 1] + above + below + left + right
        constant, factor = coefficient(at)
        target[at] = constant + factor * around
        return carry

    lax.fori_loop(start, stop, plane, 0, unroll=4)


def deposits_of(message, tiles):
    stride = tiles + SUB
    return placed([message.at[i * stride : (i + 1) * stride] for i in range(3)], tiles)[1]


def near_kernel(
    full, tiles, message, pressure, near, beyond, own_constant, own_factor, kept_even, kept_odd,
    constant, factor, old, new,
):
    planes, height, width = own_constant.shape
    place = Place(full, height)
    rim = planes + 1
    coefficients(
        deposits_of(message, tiles), tiles, place.first, full, near.at[planes:], planes,
        constant, factor, place.even, jnp.where(place.odd, place.lower, place.upper),
    )
    old[0] = beyond[...]
    for x in range(planes):
        at = jnp.where(place.even, planes - 1 - x, x)
        old[1 + x] = near[at]
        old[rim + x] = pressure[at]
    buffers = (old, new)
    for index in range(planes):
        source, target = buffers[index % 2], buffers[(index + 1) % 2]
        sweep(source, target, lambda at: (constant[at - 1], factor[at - 1]), 1 + index, rim)
        sweep(
            source, target, lambda at: (own_constant[at - rim], own_factor[at - rim]),
            rim, 2 * planes - index,
        )
    kept_even[...] = old[planes : 2 * planes]
    kept_odd[...] = new[planes : 2 * planes]


def far_kernel(
    full, tiles, picks, message, pressure, far, own_constant, own_factor, kept_even, kept_odd,
    out_a, out_b, out_c, constant, factor, old, new, fields,
):
    planes, height, width = own_constant.shape
    zones = width // BLOCK
    place = Place(full, height)
    rim = planes + 1
    coefficients(
        deposits_of(message, tiles), tiles, place.first, full, far.at[planes : 2 * planes], planes,
        constant, factor, place.even, jnp.where(place.odd, place.upper, place.lower),
    )
    old[planes : 2 * planes] = kept_even[...]
    new[planes : 2 * planes] = kept_odd[...]
    old[2 * planes] = pressure[jnp.where(place.even, 0, planes - 1)]
    for x in range(planes):
        at = jnp.where(place.even, planes - 1 - x, x)
        old[rim + planes + x] = far[at]
    old[rim + 2 * planes] = far[2 * planes]
    buffers = (old, new)
    edge = rim + planes
    for index in range(planes):
        source, target = buffers[index % 2], buffers[(index + 1) % 2]
        sweep(
            source, target, lambda at: (own_constant[at - rim], own_factor[at - rim]),
            2 * planes - index, edge,
        )
        sweep(
            source, target, lambda at: (constant[at - edge], factor[at - edge]),
            edge, edge + planes - index,
        )
    last = buffers[planes % 2]
    way = jnp.where(place.even, -0.5, 0.5)

    def gradient(x, carry):
        at = rim + x
        above, below, left, right = shifted(last[at])
        grads = (way * (last[at + 1] - last[at - 1]), 0.5 * (below - above), 0.5 * (right - left))
        line = jnp.where(place.even, planes - 1 - x, x) * zones
        for zone in range(zones):
            first = pl.multiple_of((line + zone) * height, SUB)
            for axis, grad in enumerate(grads):
                fields[pl.ds(first, height), axis * BLOCK : (axis + 1) * BLOCK] = (
                    grad[:, zone * BLOCK : (zone + 1) * BLOCK]
                )
        return carry

    lax.fori_loop(0, planes, gradient, 0, unroll=4)
    pieces = jnp.concatenate(halves_of(fields[...]), 1)
    total = jnp.dot(picks[...], pieces, preferred_element_type=F32)
    total = total[:, : 3 * BLOCK] + total[:, 3 * BLOCK :]
    for index, out in enumerate((out_a, out_b, out_c)):
        out[...] = total[index * tiles : (index + 1) * tiles]


def final_kernel(
    count, grads_a, grads_b, grads_c, weight, contact, vel, vol, drag, cell, out,
):
    tiles = cell.shape[0]
    cells = cell[...]
    heft = lanes_of(weight[...], cells)
    slot = iota(cells.shape, 0) * BLOCK + iota(cells.shape, 1)
    live = slot < count[0]
    volume = vol[...]
    push = TIME_STEP / volume
    for axis in range(3):
        lanes = slice(axis * BLOCK, (axis + 1) * BLOCK)
        gradient = lanes_of(grads_a[:, lanes] + grads_b[:, lanes] + grads_c[:, lanes], cells)
        own = jnp.concatenate(
            [vel[axis : axis + 1, t * BLOCK : (t + 1) * BLOCK] for t in range(tiles)], 0
        )
        fluid = -gradient * heft
        force = contact[axis * tiles : (axis + 1) * tiles, :] - volume * gradient
        force = force + drag[...] * (fluid - own)
        new = jnp.where(live, own + force * push, 0.0)
        for t in range(tiles):
            out[axis : axis + 1, t * BLOCK : (t + 1) * BLOCK] = new[t : t + 1, :]


def on_device(
    grain_pos,
    grain_vel,
    grain_vol,
    drag_coef,
    grain_count,
    contact_rows,
    contact_stiff,
    partner_block,
    halo_list,
    grain_cell,
    tile_cell_block,
    pressure_old,
    pressure_source,
    solid_old,
):
    groups, regions = lax.axis_size("grp"), lax.axis_size("reg")
    holding = groups - 1
    halves = groups // CORES
    slots = grain_pos.shape[1]
    tiles = slots // BLOCK
    planes, full, width = pressure_old.shape
    assert planes == ITERS
    own_rows = full // halves
    height = min(full, own_rows + SUB * min(2, halves - 1))
    owners = range(0, groups, CORES)
    holders = range(holding)

    def send(value, pairs):
        flat = [(a[0] * regions + a[1], b[0] * regions + b[1]) for a, b in pairs]
        return lax.ppermute(value, ("grp", "reg"), flat)

    def along_reg(value, members, goes):
        pairs = [
            ((g, r), (g, r + goes[r % 2]))
            for g in members
            for r in range(regions)
            if 0 <= r + goes[r % 2] < regions
        ]
        return send(value, pairs)

    def along_grp(value, step, members):
        pairs = [((g, r), ((g + step) % holding, r)) for g in members for r in range(regions)]
        return send(value, pairs)

    count = grain_count
    cell = grain_cell.reshape(tiles, BLOCK)
    vol = grain_vol.reshape(tiles, BLOCK)
    drag = drag_coef.reshape(tiles, BLOCK)
    ids = tile_cell_block.reshape(1, tiles)
    field_bytes = 4 * planes * height * width

    field = shaped(planes, height, width)
    plane = shaped(height, width)
    small = shaped(SUB, BLOCK)
    window, inner = call(
        window_kernel, (shaped(2 * planes, height, width), plane),
        [HBM] * 3, (pressure_old, pressure_source, solid_old),
        [pltpu.VMEM((planes, height, width), F32)] * 3
        + [pltpu.SemaphoreType.DMA((5 * planes + 1,))],
        flops=field_bytes, size=6 * field_bytes, limit=61_950_000, place=HBM,
    )
    near = along_reg(window, owners, (1, -1))
    mine, after_deposit = call(
        deposit_kernel, (shaped(tiles + SUB, 2 * BLOCK), small), [SMEM] + [VMEM] * 4,
        (count, cell, vol, drag, ids), flops=2 * 32 * 48 * 65536, size=5 * 4 * slots,
    )
    second = along_grp(mine, 1, holders)
    third = along_grp(mine, 2, holders)
    rows = halo_list.shape[1] // BLOCK
    halo = shaped(3 * rows, BLOCK)
    state, halo_near, halo_far, after_halo = call(
        halo_kernel, (shaped(3 * tiles, BLOCK), halo, halo, small),
        [VMEM] * 4, (grain_pos, grain_vel, halo_list, after_deposit), flops=2 * 3 * 8 * BLOCK * BLOCK * slots // 4,
        size=4 * 4 * 3 * slots,
    )
    others = [g for g in holders if g not in owners]
    came_near = along_reg(halo_near, others, (1, -1))
    came_far = along_reg(halo_far, others, (-1, 1))
    far, after_forward = call(
        forward_kernel, (shaped(2 * planes + 1, height, width), small), [VMEM] * 7,
        (near, inner, after_halo, second, third, came_near, came_far), size=5 * field_bytes,
    )
    far = along_reg(far, owners, (2, -2))
    message = shaped(holding * (tiles + SUB) + 3 * rows // 2, 2 * BLOCK)
    message_near, message_far, ends, after_message = call(
        message_kernel, (message, message, plane, small), [VMEM] * 7,
        (mine, second, third, halo_near, halo_far, window, after_forward), size=8 * 2 * BLOCK * 500,
    )
    message_near = along_reg(message_near, owners, (1, -1))
    message_far = along_reg(message_far, owners, (-1, 1))
    beyond = along_reg(ends, owners, (-2, 2))
    constant, factor, weight, picks = call(
        functools.partial(own_kernel, full),
        (
            field, field, shaped(tiles, BLOCK),
            jax.ShapeDtypeStruct((3 * tiles, planes * height * width // BLOCK), BF16),
        ),
        [VMEM] * 5, (mine, second, third, window, after_message),
        flops=planes * height * 4 * 384 * 256 * 6, size=9 * field_bytes,
    )
    window_of = lambda count: pltpu.VMEM((count, height, width), F32)
    kept_even, kept_odd = call(
        functools.partial(near_kernel, full, tiles), (field, field), [VMEM] * 6,
        (message_near, window, near, beyond, constant, factor),
        [window_of(planes)] * 2 + [window_of(2 * planes + 1)] * 2,
        flops=planes * height * 4 * 384 * 256 * 6, size=9 * field_bytes,
    )
    grads = shaped(tiles, 3 * BLOCK)
    grads_a, grads_b, grads_c = call(
        functools.partial(far_kernel, full, tiles), (grads,) * 3, [VMEM] * 8,
        (picks, message_far, window, far, constant, factor, kept_even, kept_odd),
        [window_of(planes)] * 2
        + [window_of(3 * planes + 2)] * 2
        + [pltpu.VMEM((planes * height * width // BLOCK, 3 * BLOCK), F32)],
        flops=planes * height * 4 * 384 * 256 * 6, size=9 * field_bytes,
    )
    grads_b = along_grp(grads_b, -1, owners)
    grads_c = along_grp(grads_c, -2, owners)

    contact = call(
        contact_kernel, shaped(3 * tiles, BLOCK), [SMEM] + [VMEM] * 7 + [ANY],
        (
            partner_block, state, message_near, message_far, came_near, came_far, contact_rows,
            contact_stiff, grads_a,
        ),
        [pltpu.VMEM((3 * (tiles + 2 * rows), BLOCK), F32)],
        flops=60 * 8 * slots, size=4 * 20 * slots,
    )
    return call(
        final_kernel, shaped(3, slots), [SMEM] + [VMEM] * 9,
        (count, grads_a, grads_b, grads_c, weight, contact, grain_vel, vol, drag, cell),
        flops=60 * slots, size=4 * 20 * slots,
    )


def solution(mesh):
    in_specs = (
        P(None, ("grp", "reg")),
        P(None, ("grp", "reg")),
        P(("grp", "reg")),
        P(("grp", "reg")),
        P(("grp", "reg")),
        P(None, ("grp", "reg")),
        P(None, ("grp", "reg")),
        P(("grp", "reg")),
        P(None, ("grp", "reg")),
        P(("grp", "reg")),
        P(("grp", "reg")),
        P("reg", None, None),
        P("reg", None, None),
        P("reg", None, None),
    )
    out_specs = P(None, ("grp", "reg"))
    return jax.shard_map(
        on_device, mesh=mesh, in_specs=in_specs, out_specs=out_specs, check_vma=False
    )
```

```python
import functools

import jax
import jax.numpy as jnp
from jax import lax
from jax.experimental import pallas as pl
from jax.experimental.pallas import tpu as pltpu
from jax.sharding import PartitionSpec as P

BLOCK = 128
SUB = 8
CORES = 2
ITERS = 4
SPRING = 1.0
DAMPING = 0.5
TIME_STEP = 0.5

VMEM = pl.BlockSpec(memory_space=pltpu.VMEM)
SMEM = pl.BlockSpec(memory_space=pltpu.SMEM)
ANY = pl.BlockSpec(memory_space=pl.ANY)
HBM = pl.BlockSpec(memory_space=pltpu.HBM)
F32 = jnp.float32
BF16 = jnp.bfloat16


def iota(shape, dim):
    return lax.broadcasted_iota(jnp.int32, shape, dim)


def shaped(*dims):
    return jax.ShapeDtypeStruct(dims, F32)


def call(kernel, outs, specs, args, scratch=(), flops=0, size=0, limit=40_000_000, place=VMEM):
    return pl.pallas_call(
        kernel,
        out_shape=outs,
        in_specs=specs,
        out_specs=jax.tree.map(lambda _: place, outs),
        scratch_shapes=list(scratch),
        compiler_params=pltpu.CompilerParams(vmem_limit_bytes=limit),
        cost_estimate=pl.CostEstimate(flops=flops, bytes_accessed=size, transcendentals=0),
    )(*args)


class Place:
    def __init__(self, full, height):
        groups, regions = lax.axis_size("grp"), lax.axis_size("reg")
        self.group, region = lax.axis_index("grp"), lax.axis_index("reg")
        self.half = self.group // CORES
        self.own_rows = full // (groups // CORES)
        first = jnp.clip(self.half * self.own_rows - SUB, 0, full - height)
        self.first = pl.multiple_of(first, SUB)
        self.sweeps = self.group % CORES == 0
        self.parity = region % 2
        self.odd, self.even = self.parity == 1, self.parity == 0
        self.lower, self.upper = region > 0, region < regions - 1


def lanes_of(source, index):
    return jnp.take_along_axis(source, index, axis=1, mode="promise_in_bounds")


def halves_of(value):
    high = value.astype(BF16)
    return high, (value - high.astype(F32)).astype(BF16)


def window_kernel(pressure_old, source, solid_before, window, inner, pressure, driven, solid, sems):
    planes, height, _ = solid.shape
    place = Place(pressure_old.shape[1], height)
    rows = pl.ds(place.first, height)
    used = []

    def copy(whole, part):
        used.append(None)
        return pltpu.make_async_copy(whole, part, sems.at[len(used) - 1])

    fetched = [
        [copy(whole.at[x, rows, :], part.at[x]) for x in range(planes)]
        for whole, part in ((pressure_old, pressure), (source, driven), (solid_before, solid))
    ]
    stored = [copy(pressure.at[x], window.at[x]) for x in range(planes)]
    stored += [copy(driven.at[x], window.at[planes + x]) for x in range(planes)]
    stored.append(copy(pressure.at[(1 - place.parity) * (planes - 1)], inner))
    for x in range(planes):
        for part in fetched:
            part[x].start()
    for x in range(planes):
        fetched[0][x].wait()
        stored[x].start()
        fetched[1][x].wait()
        fetched[2][x].wait()
        driven[x] = driven[x] - solid[x]
        stored[planes + x].start()
    stored[2 * planes].start()
    for one in stored:
        one.wait()


def forward_kernel(near, inner, _halo, _second, _third, _near, _far, out, dummy):
    dummy[...] = jnp.zeros(dummy.shape, F32)
    count = near.shape[0]
    out[:count] = near[...]
    out[count] = inner[...]


def deposit_kernel(count, cell, vol, drag, ids, out, dummy):
    dummy[...] = jnp.zeros(dummy.shape, F32)
    tiles = cell.shape[0]
    sub = iota((SUB, BLOCK), 0)
    rows_c = iota((BLOCK, BLOCK), 0)
    even = sub % 2 == 0
    low_pair = sub % 4 < 2

    def step(group, carry):
        first = pl.multiple_of(group * SUB, SUB)
        slot = (first + sub) * BLOCK + iota((SUB, BLOCK), 1)
        live = slot < count[0]
        cells = cell[pl.ds(first, SUB), :]
        parts = halves_of(jnp.where(live, vol[pl.ds(first, SUB), :], 0.0)) + halves_of(
            jnp.where(live, drag[pl.ds(first, SUB), :], 0.0)
        )
        parts = [part.astype(F32) for part in parts]
        left = jnp.concatenate([jnp.where(even, part, 0.0) for part in parts], 0)
        right = jnp.concatenate([jnp.where(even, 0.0, part) for part in parts], 0)
        loads = jnp.concatenate([left, right], 1).astype(BF16)
        sums = [jnp.zeros((SUB, BLOCK), F32), jnp.zeros((SUB, BLOCK), F32)]
        for quad in range(SUB // 4):
            hot = [
                jnp.where(
                    rows_c == jnp.broadcast_to(cells[t : t + 1, :], (BLOCK, BLOCK)), 1.0, 0.0
                ).astype(BF16)
                for t in range(4 * quad, 4 * quad + 4)
            ]
            picked = jnp.concatenate(
                [jnp.concatenate(hot[:2], 1), jnp.concatenate(hot[2:], 1)], 0
            )
            placed = lax.dot_general(
                loads, picked, (((1,), (1,)), ((), ())), preferred_element_type=F32
            )
            for field in range(2):
                base = field * 2 * SUB
                total = placed[base : base + SUB] + placed[base + SUB : base + 2 * SUB]
                chosen = jnp.where(low_pair, total[:, :BLOCK], total[:, BLOCK:])
                sums[field] = jnp.where(sub // 4 == quad, chosen, sums[field])
        out[pl.ds(first, SUB), :BLOCK] = sums[0]
        out[pl.ds(first, SUB), BLOCK:] = sums[1]
        return carry

    lax.fori_loop(0, tiles // SUB, step, 0, unroll=4)
    out[tiles : tiles + SUB, :BLOCK] = jnp.broadcast_to(ids[...].astype(F32), (SUB, BLOCK))
    out[tiles : tiles + SUB, BLOCK:] = jnp.zeros((SUB, BLOCK), F32)


def halo_kernel(pos, vel, lists, _, state, near, far, dummy):
    dummy[...] = jnp.zeros(dummy.shape, F32)
    tiles = pos.shape[1] // BLOCK
    rows = lists.shape[1] // BLOCK
    for tile in range(tiles):
        lanes = slice(tile * BLOCK, (tile + 1) * BLOCK)
        mixed = SPRING * pos[:, lanes] - DAMPING * vel[:, lanes]
        for axis in range(3):
            state[axis * tiles + tile : axis * tiles + tile + 1, :] = mixed[axis : axis + 1]
    turned = [
        jnp.concatenate(halves_of(jnp.transpose(state[axis * tiles : (axis + 1) * tiles, :])), 1)
        for axis in range(3)
    ]
    turned = jnp.concatenate(turned, 0)
    span = 2 * BLOCK
    row = iota((BLOCK, span), 0)

    odd = lax.axis_index("reg") % 2
    for away, out in enumerate((near, far)):
        side = 1 - odd if away == 0 else odd

        def step(part, carry):
            named = lists[:, pl.ds(pl.multiple_of(part * span, span), span)]
            named = jnp.where(side == 0, named[:1], named[1:])
            block = lax.shift_right_logical(named, 7)
            lane = named & (BLOCK - 1)
            hot = jnp.where(row == jnp.broadcast_to(block, row.shape), 1.0, 0.0).astype(BF16)
            found = jnp.dot(
                turned, jnp.concatenate([hot, hot], 0), preferred_element_type=F32
            )
            here = row == jnp.broadcast_to(lane, row.shape)
            for axis in range(3):
                value = jnp.where(here, found[axis * BLOCK : (axis + 1) * BLOCK], 0.0)
                value = jnp.sum(value, axis=0, keepdims=True)
                for half in range(2):
                    out[pl.ds(axis * rows + 2 * part + half, 1), :] = value[
                        :, half * BLOCK : (half + 1) * BLOCK
                    ]
            return carry

        lax.fori_loop(0, rows // 2, step, 0, unroll=8)


def message_kernel(mine, second, third, halo_near, halo_far, window, _, near, far, ends, dummy):
    dummy[...] = jnp.zeros(dummy.shape, F32)
    ends[...] = window[(lax.axis_index("reg") % 2) * (window.shape[0] // 2 - 1)]
    stride = mine.shape[0]
    half = halo_near.shape[0] // 2
    rows = near.shape[0] - half
    for halo, out in ((halo_near, near), (halo_far, far)):
        for index, group in enumerate((mine, second, third)):
            out[index * stride : (index + 1) * stride, :] = group[...]
        out[rows:, :BLOCK] = halo[:half, :]
        out[rows:, BLOCK:] = halo[half:, :]


def contact_kernel(
    partner, state, message_near, message_far, halo_near, halo_far, named, stiff, _, out, extended
):
    tiles = state.shape[0] // 3
    rows = halo_near.shape[0] // 3
    blocks = tiles + 2 * rows
    base = message_near.shape[0] - 3 * rows // 2
    odd = lax.axis_index("reg") % 2
    sweeps = lax.axis_index("grp") % CORES == 0
    for axis in range(3):
        extended[axis * blocks : axis * blocks + tiles, :] = state[
            axis * tiles : (axis + 1) * tiles, :
        ]
    for message, halo, upper in (
        (message_near, halo_near, 1 - odd), (message_far, halo_far, odd)
    ):
        carried = jnp.concatenate([message[base:, :BLOCK], message[base:, BLOCK:]], 0)
        carried = jnp.where(sweeps, carried, halo[...])
        for axis in range(3):
            first = pl.multiple_of(axis * blocks + tiles + upper * rows, SUB)
            extended[pl.ds(first, rows), :] = carried[axis * rows : (axis + 1) * rows]

    def step(tile, carry):
        lanes = pl.ds(pl.multiple_of(tile * BLOCK, BLOCK), BLOCK)
        entry = named[:, lanes]
        weight = jnp.where(entry >= 0, stiff[:, lanes], 0.0)
        own = entry < BLOCK
        lane = entry & (BLOCK - 1)
        other = partner[tile]
        for axis in range(3):
            mine = jnp.broadcast_to(extended[pl.ds(axis * blocks + tile, 1), :], entry.shape)
            theirs = jnp.broadcast_to(extended[pl.ds(axis * blocks + other, 1), :], entry.shape)
            met = jnp.where(own, lanes_of(mine, lane), lanes_of(theirs, lane))
            pull = jnp.sum(weight * (mine - met), axis=0, keepdims=True)
            out[pl.ds(axis * tiles + tile, 1), :] = pull
        return carry

    lax.fori_loop(0, tiles, step, 0, unroll=4)


def shifted(plane):
    height, width = plane.shape
    row = iota((SUB, width), 0)
    column = iota((height, BLOCK), 1)
    above, below = pltpu.roll(plane, 1, 0), pltpu.roll(plane, height - 1, 0)
    left, right = pltpu.roll(plane, 1, 1), pltpu.roll(plane, width - 1, 1)
    above = jnp.concatenate([jnp.where(row == 0, 0.0, above[:SUB]), above[SUB:]], 0)
    below = jnp.concatenate([below[:-SUB], jnp.where(row == SUB - 1, 0.0, below[-SUB:])], 0)
    left = jnp.concatenate([jnp.where(column == 0, 0.0, left[:, :BLOCK]), left[:, BLOCK:]], 1)
    right = jnp.concatenate(
        [right[:, :-BLOCK], jnp.where(column == BLOCK - 1, 0.0, right[:, -BLOCK:])], 1
    )
    return above, below, left, right


def inverse_of(value):
    near = pl.reciprocal(value, approx=True)
    return near * (2.0 - value * near)


def placed(groups, tiles):
    parts = [halves_of(group[:tiles, :]) for group in groups]
    loads = jnp.concatenate([part[i] for i in range(2) for part in parts], 0)
    ids = jnp.concatenate([group[tiles : tiles + 1, :BLOCK] for group in groups], 1)
    ids = ids.astype(jnp.int32)

    def gathered(wanted):
        hot = jnp.where(wanted == jnp.broadcast_to(ids, wanted.shape), 1.0, 0.0).astype(BF16)
        total = jnp.dot(
            jnp.concatenate([hot, hot], 1), loads, preferred_element_type=F32
        )
        return total[:, :BLOCK], total[:, BLOCK:]

    return ids, gathered


def coefficients(gathered, tiles, first, full, driven, planes, constant, factor, turned, present):
    _, height, width = driven.shape
    zones = width // BLOCK
    shape = (zones * height, 3 * tiles)
    line = iota(shape, 0)
    block = (line % height) * zones + line // height + first * zones

    for x in range(planes):
        solid, drag = gathered(block + x * (full * zones))
        at = x if turned is None else jnp.where(turned, planes - 1 - x, x)
        voids = 1.0 + solid
        scale = inverse_of(6.0 + (drag + 1.0) * voids)
        if present is not None:
            scale = jnp.where(present, scale, 0.0)
        inverse = voids * scale
        for zone in range(zones):
            lanes = slice(zone * BLOCK, (zone + 1) * BLOCK)
            rows = slice(zone * height, (zone + 1) * height)
            driving = driven[x, :, lanes] + solid[rows]
            constant[at, :, lanes] = driving * inverse[rows]
            factor[at, :, lanes] = scale[rows]


def own_kernel(
    full, mine, second, third, window, _message, constant, factor, weight, picks
):
    tiles = weight.shape[0]
    planes, height, width = constant.shape
    place = Place(full, height)
    zones = width // BLOCK
    ids, gathered = placed((mine, second, third), tiles)
    coefficients(gathered, tiles, place.first, full, window.at[planes:], planes, constant, factor, place.even, None)
    turned = [
        jnp.transpose(
            jnp.broadcast_to(ids[:, i * tiles : (i + 1) * tiles], (BLOCK, tiles)).astype(F32)
        ).astype(jnp.int32)
        for i in range(3)
    ]
    solid, drag = gathered(jnp.concatenate([turned[0]] * 3, 1))
    weight[...] = 1.0 / (1.0 / (1.0 + solid) + drag)
    for i in range(3):
        block = turned[i]
        line, zone = block // zones, block % zones
        x, y = line // full, line % full
        row = (x * zones + zone) * height + y - place.first
        held = y // place.own_rows == jnp.where(place.sweeps, place.half, -1)
        row = jnp.concatenate([jnp.where(held, row, -1)] * (picks.shape[1] // BLOCK), 1)
        hot = jnp.where(row == iota(row.shape, 1), 1.0, 0.0).astype(BF16)
        picks[i * tiles : (i + 1) * tiles, :] = hot


def sweep(source, target, coefficient, start, stop):
    def plane(at, carry):
        above, below, left, right = shifted(source[at])
        around = source[at - 1] + source[at + 1] + above + below + left + right
        constant, factor = coefficient(at)
        target[at] = constant + factor * around
        return carry

    lax.fori_loop(start, stop, plane, 0, unroll=4)


def deposits_of(message, tiles):
    stride = tiles + SUB
    return placed([message.at[i * stride : (i + 1) * stride] for i in range(3)], tiles)[1]


def near_kernel(
    full, tiles, message, pressure, near, beyond, own_constant, own_factor, kept_even, kept_odd,
    constant, factor, old, new,
):
    planes, height, width = own_constant.shape
    place = Place(full, height)
    rim = planes + 1
    coefficients(
        deposits_of(message, tiles), tiles, place.first, full, near.at[planes:], planes,
        constant, factor, place.even, jnp.where(place.odd, place.lower, place.upper),
    )
    old[0] = beyond[...]
    for x in range(planes):
        at = jnp.where(place.even, planes - 1 - x, x)
        old[1 + x] = near[at]
        old[rim + x] = pressure[at]
    buffers = (old, new)
    for index in range(planes):
        source, target = buffers[index % 2], buffers[(index + 1) % 2]
        sweep(source, target, lambda at: (constant[at - 1], factor[at - 1]), 1 + index, rim)
        sweep(
            source, target, lambda at: (own_constant[at - rim], own_factor[at - rim]),
            rim, 2 * planes - index,
        )
    kept_even[...] = old[planes : 2 * planes]
    kept_odd[...] = new[planes : 2 * planes]


def far_kernel(
    full, tiles, picks, message, pressure, far, own_constant, own_factor, kept_even, kept_odd,
    out_a, out_b, out_c, constant, factor, old, new, fields,
):
    planes, height, width = own_constant.shape
    zones = width // BLOCK
    place = Place(full, height)
    rim = planes + 1
    coefficients(
        deposits_of(message, tiles), tiles, place.first, full, far.at[planes : 2 * planes], planes,
        constant, factor, place.even, jnp.where(place.odd, place.upper, place.lower),
    )
    old[planes : 2 * planes] = kept_even[...]
    new[planes : 2 * planes] = kept_odd[...]
    old[2 * planes] = pressure[jnp.where(place.even, 0, planes - 1)]
    for x in range(planes):
        at = jnp.where(place.even, planes - 1 - x, x)
        old[rim + planes + x] = far[at]
    old[rim + 2 * planes] = far[2 * planes]
    buffers = (old, new)
    edge = rim + planes
    for index in range(planes):
        source, target = buffers[index % 2], buffers[(index + 1) % 2]
        sweep(
            source, target, lambda at: (own_constant[at - rim], own_factor[at - rim]),
            2 * planes - index, edge,
        )
        sweep(
            source, target, lambda at: (constant[at - edge], factor[at - edge]),
            edge, edge + planes - index,
        )
    last = buffers[planes % 2]
    way = jnp.where(place.even, -0.5, 0.5)

    def gradient(x, carry):
        at = rim + x
        above, below, left, right = shifted(last[at])
        grads = (way * (last[at + 1] - last[at - 1]), 0.5 * (below - above), 0.5 * (right - left))
        line = jnp.where(place.even, planes - 1 - x, x) * zones
        for zone in range(zones):
            first = pl.multiple_of((line + zone) * height, SUB)
            for axis, grad in enumerate(grads):
                fields[pl.ds(first, height), axis * BLOCK : (axis + 1) * BLOCK] = (
                    grad[:, zone * BLOCK : (zone + 1) * BLOCK]
                )
        return carry

    lax.fori_loop(0, planes, gradient, 0, unroll=4)
    pieces = jnp.concatenate(halves_of(fields[...]), 1)
    total = jnp.dot(picks[...], pieces, preferred_element_type=F32)
    total = total[:, : 3 * BLOCK] + total[:, 3 * BLOCK :]
    for index, out in enumerate((out_a, out_b, out_c)):
        out[...] = total[index * tiles : (index + 1) * tiles]


def final_kernel(
    count, grads_a, grads_b, grads_c, weight, contact, vel, vol, drag, cell, out,
):
    tiles = cell.shape[0]
    cells = cell[...]
    heft = lanes_of(weight[...], cells)
    slot = iota(cells.shape, 0) * BLOCK + iota(cells.shape, 1)
    live = slot < count[0]
    volume = vol[...]
    push = TIME_STEP / volume
    for axis in range(3):
        lanes = slice(axis * BLOCK, (axis + 1) * BLOCK)
        gradient = lanes_of(grads_a[:, lanes] + grads_b[:, lanes] + grads_c[:, lanes], cells)
        own = jnp.concatenate(
            [vel[axis : axis + 1, t * BLOCK : (t + 1) * BLOCK] for t in range(tiles)], 0
        )
        fluid = -gradient * heft
        force = contact[axis * tiles : (axis + 1) * tiles, :] - volume * gradient
        force = force + drag[...] * (fluid - own)
        new = jnp.where(live, own + force * push, 0.0)
        for t in range(tiles):
            out[axis : axis + 1, t * BLOCK : (t + 1) * BLOCK] = new[t : t + 1, :]


def on_device(
    grain_pos,
    grain_vel,
    grain_vol,
    drag_coef,
    grain_count,
    contact_rows,
    contact_stiff,
    partner_block,
    halo_list,
    grain_cell,
    tile_cell_block,
    pressure_old,
    pressure_source,
    solid_old,
):
    groups, regions = lax.axis_size("grp"), lax.axis_size("reg")
    holding = groups - 1
    halves = groups // CORES
    slots = grain_pos.shape[1]
    tiles = slots // BLOCK
    planes, full, width = pressure_old.shape
    assert planes == ITERS
    own_rows = full // halves
    height = min(full, own_rows + SUB * min(2, halves - 1))
    owners = range(0, groups, CORES)
    holders = range(holding)

    def send(value, pairs):
        flat = [(a[0] * regions + a[1], b[0] * regions + b[1]) for a, b in pairs]
        return lax.ppermute(value, ("grp", "reg"), flat)

    def along_reg(value, members, goes, core=0):
        pairs = [
            ((g + core, r), (g, r + goes[r % 2]))
            for g in members
            for r in range(regions)
            if 0 <= r + goes[r % 2] < regions
        ]
        return send(value, pairs)

    def along_grp(value, step, members):
        pairs = [((g, r), ((g + step) % holding, r)) for g in members for r in range(regions)]
        return send(value, pairs)

    count = grain_count
    cell = grain_cell.reshape(tiles, BLOCK)
    vol = grain_vol.reshape(tiles, BLOCK)
    drag = drag_coef.reshape(tiles, BLOCK)
    ids = tile_cell_block.reshape(1, tiles)
    field_bytes = 4 * planes * height * width

    field = shaped(planes, height, width)
    plane = shaped(height, width)
    small = shaped(SUB, BLOCK)
    window, inner = call(
        window_kernel, (shaped(2 * planes, height, width), plane),
        [HBM] * 3, (pressure_old, pressure_source, solid_old),
        [pltpu.VMEM((planes, height, width), F32)] * 3
        + [pltpu.SemaphoreType.DMA((5 * planes + 1,))],
        flops=field_bytes, size=6 * field_bytes, limit=61_950_000, place=HBM,
    )
    near = along_reg(window, owners, (1, -1), core=1)
    mine, after_deposit = call(
        deposit_kernel, (shaped(tiles + SUB, 2 * BLOCK), small), [SMEM] + [VMEM] * 4,
        (count, cell, vol, drag, ids), flops=2 * 32 * 48 * 65536, size=5 * 4 * slots,
    )
    second = along_grp(mine, 1, holders)
    third = along_grp(mine, 2, holders)
    rows = halo_list.shape[1] // BLOCK
    halo = shaped(3 * rows, BLOCK)
    state, halo_near, halo_far, after_halo = call(
        halo_kernel, (shaped(3 * tiles, BLOCK), halo, halo, small),
        [VMEM] * 4, (grain_pos, grain_vel, halo_list, after_deposit), flops=2 * 3 * 8 * BLOCK * BLOCK * slots // 4,
        size=4 * 4 * 3 * slots,
    )
    others = [g for g in holders if g not in owners]
    came_near = along_reg(halo_near, others, (1, -1))
    came_far = along_reg(halo_far, others, (-1, 1))
    far, after_forward = call(
        forward_kernel, (shaped(2 * planes + 1, height, width), small), [VMEM] * 7,
        (near, inner, after_halo, second, third, came_near, came_far), size=5 * field_bytes,
    )
    far = along_reg(far, owners, (2, -2))
    message = shaped(holding * (tiles + SUB) + 3 * rows // 2, 2 * BLOCK)
    message_near, message_far, ends, after_message = call(
        message_kernel, (message, message, plane, small), [VMEM] * 7,
        (mine, second, third, halo_near, halo_far, window, after_forward), size=8 * 2 * BLOCK * 500,
    )
    message_near = along_reg(message_near, owners, (1, -1))
    message_far = along_reg(message_far, owners, (-1, 1))
    beyond = along_reg(ends, owners, (-2, 2), core=1)
    constant, factor, weight, picks = call(
        functools.partial(own_kernel, full),
        (
            field, field, shaped(tiles, BLOCK),
            jax.ShapeDtypeStruct((3 * tiles, planes * height * width // BLOCK), BF16),
        ),
        [VMEM] * 5, (mine, second, third, window, after_message),
        flops=planes * height * 4 * 384 * 256 * 6, size=9 * field_bytes,
    )
    window_of = lambda count: pltpu.VMEM((count, height, width), F32)
    kept_even, kept_odd = call(
        functools.partial(near_kernel, full, tiles), (field, field), [VMEM] * 6,
        (message_near, window, near, beyond, constant, factor),
        [window_of(planes)] * 2 + [window_of(2 * planes + 1)] * 2,
        flops=planes * height * 4 * 384 * 256 * 6, size=9 * field_bytes,
    )
    grads = shaped(tiles, 3 * BLOCK)
    grads_a, grads_b, grads_c = call(
        functools.partial(far_kernel, full, tiles), (grads,) * 3, [VMEM] * 8,
        (picks, message_far, window, far, constant, factor, kept_even, kept_odd),
        [window_of(planes)] * 2
        + [window_of(3 * planes + 2)] * 2
        + [pltpu.VMEM((planes * height * width // BLOCK, 3 * BLOCK), F32)],
        flops=planes * height * 4 * 384 * 256 * 6, size=9 * field_bytes,
    )
    grads_b = along_grp(grads_b, -1, owners)
    grads_c = along_grp(grads_c, -2, owners)

    contact = call(
        contact_kernel, shaped(3 * tiles, BLOCK), [SMEM] + [VMEM] * 7 + [ANY],
        (
            partner_block, state, message_near, message_far, came_near, came_far, contact_rows,
            contact_stiff, grads_a,
        ),
        [pltpu.VMEM((3 * (tiles + 2 * rows), BLOCK), F32)],
        flops=60 * 8 * slots, size=4 * 20 * slots,
    )
    return call(
        final_kernel, shaped(3, slots), [SMEM] + [VMEM] * 9,
        (count, grads_a, grads_b, grads_c, weight, contact, grain_vel, vol, drag, cell),
        flops=60 * slots, size=4 * 20 * slots,
    )


def solution(mesh):
    in_specs = (
        P(None, ("grp", "reg")),
        P(None, ("grp", "reg")),
        P(("grp", "reg")),
        P(("grp", "reg")),
        P(("grp", "reg")),
        P(None, ("grp", "reg")),
        P(None, ("grp", "reg")),
        P(("grp", "reg")),
        P(None, ("grp", "reg")),
        P(("grp", "reg")),
        P(("grp", "reg")),
        P("reg", None, None),
        P("reg", None, None),
        P("reg", None, None),
    )
    out_specs = P(None, ("grp", "reg"))
    return jax.shard_map(
        on_device, mesh=mesh, in_specs=in_specs, out_specs=out_specs, check_vma=False
    )
```

```python
import functools

import jax
import jax.numpy as jnp
from jax import lax
from jax.experimental import pallas as pl
from jax.experimental.pallas import tpu as pltpu
from jax.sharding import PartitionSpec as P

BLOCK = 128
SUB = 8
CORES = 2
ITERS = 4
HEAD = 1
SPRING = 1.0
DAMPING = 0.5
TIME_STEP = 0.5

VMEM = pl.BlockSpec(memory_space=pltpu.VMEM)
SMEM = pl.BlockSpec(memory_space=pltpu.SMEM)
ANY = pl.BlockSpec(memory_space=pl.ANY)
HBM = pl.BlockSpec(memory_space=pltpu.HBM)
F32 = jnp.float32
BF16 = jnp.bfloat16


def iota(shape, dim):
    return lax.broadcasted_iota(jnp.int32, shape, dim)


def shaped(*dims):
    return jax.ShapeDtypeStruct(dims, F32)


def call(kernel, outs, specs, args, scratch=(), flops=0, size=0, limit=40_000_000, place=VMEM):
    return pl.pallas_call(
        kernel,
        out_shape=outs,
        in_specs=specs,
        out_specs=jax.tree.map(lambda _: place, outs),
        scratch_shapes=list(scratch),
        compiler_params=pltpu.CompilerParams(vmem_limit_bytes=limit),
        cost_estimate=pl.CostEstimate(flops=flops, bytes_accessed=size, transcendentals=0),
    )(*args)


class Place:
    def __init__(self, full, height):
        groups, regions = lax.axis_size("grp"), lax.axis_size("reg")
        self.group, region = lax.axis_index("grp"), lax.axis_index("reg")
        self.half = self.group // CORES
        self.own_rows = full // (groups // CORES)
        first = jnp.clip(self.half * self.own_rows - SUB, 0, full - height)
        self.first = pl.multiple_of(first, SUB)
        self.sweeps = self.group % CORES == 0
        self.parity = region % 2
        self.odd, self.even = self.parity == 1, self.parity == 0
        self.lower, self.upper = region > 0, region < regions - 1


def lanes_of(source, index):
    return jnp.take_along_axis(source, index, axis=1, mode="promise_in_bounds")


def halves_of(value):
    high = value.astype(BF16)
    return high, (value - high.astype(F32)).astype(BF16)


def window_kernel(
    pressure_old, source, solid_before, early, late, ends, inner, pressure, driven, solid, sems
):
    planes, height, _ = solid.shape
    place = Place(pressure_old.shape[1], height)
    rows = pl.ds(place.first, height)
    used = []

    def copy(whole, part):
        used.append(None)
        return pltpu.make_async_copy(whole, part, sems.at[len(used) - 1])

    fetched = [
        [copy(whole.at[x, rows, :], part.at[x]) for x in range(planes)]
        for whole, part in ((pressure_old, pressure), (source, driven), (solid_before, solid))
    ]
    stored = [copy(pressure.at[x], early.at[x]) for x in range(planes)]
    for x in range(planes):
        stored.append(copy(driven.at[x], early.at[planes + x] if x < HEAD else late.at[x - HEAD]))
    sides = (
        copy(pressure.at[place.parity * (planes - 1)], ends),
        copy(pressure.at[(1 - place.parity) * (planes - 1)], inner),
    )
    for x in range(planes):
        for part in fetched:
            part[x].start()
    for x in range(planes):
        fetched[0][x].wait()
        stored[x].start()
        fetched[1][x].wait()
        fetched[2][x].wait()
        driven[x] = driven[x] - solid[x]
        stored[planes + x].start()
    for one in sides:
        one.start()
    for one in stored:
        one.wait()
    for one in sides:
        one.wait()


def forward_kernel(near, inner, _halo, _second, _third, _near, _far, out, dummy):
    dummy[...] = jnp.zeros(dummy.shape, F32)
    count = near.shape[0]
    out[:count] = near[...]
    out[count] = inner[...]


def deposit_kernel(count, cell, vol, drag, ids, out, dummy):
    dummy[...] = jnp.zeros(dummy.shape, F32)
    tiles = cell.shape[0]
    sub = iota((SUB, BLOCK), 0)
    rows_c = iota((BLOCK, BLOCK), 0)
    even = sub % 2 == 0
    low_pair = sub % 4 < 2

    def step(group, carry):
        first = pl.multiple_of(group * SUB, SUB)
        slot = (first + sub) * BLOCK + iota((SUB, BLOCK), 1)
        live = slot < count[0]
        cells = cell[pl.ds(first, SUB), :]
        parts = halves_of(jnp.where(live, vol[pl.ds(first, SUB), :], 0.0)) + halves_of(
            jnp.where(live, drag[pl.ds(first, SUB), :], 0.0)
        )
        parts = [part.astype(F32) for part in parts]
        left = jnp.concatenate([jnp.where(even, part, 0.0) for part in parts], 0)
        right = jnp.concatenate([jnp.where(even, 0.0, part) for part in parts], 0)
        loads = jnp.concatenate([left, right], 1).astype(BF16)
        sums = [jnp.zeros((SUB, BLOCK), F32), jnp.zeros((SUB, BLOCK), F32)]
        for quad in range(SUB // 4):
            hot = [
                jnp.where(
                    rows_c == jnp.broadcast_to(cells[t : t + 1, :], (BLOCK, BLOCK)), 1.0, 0.0
                ).astype(BF16)
                for t in range(4 * quad, 4 * quad + 4)
            ]
            picked = jnp.concatenate(
                [jnp.concatenate(hot[:2], 1), jnp.concatenate(hot[2:], 1)], 0
            )
            placed = lax.dot_general(
                loads, picked, (((1,), (1,)), ((), ())), preferred_element_type=F32
            )
            for field in range(2):
                base = field * 2 * SUB
                total = placed[base : base + SUB] + placed[base + SUB : base + 2 * SUB]
                chosen = jnp.where(low_pair, total[:, :BLOCK], total[:, BLOCK:])
                sums[field] = jnp.where(sub // 4 == quad, chosen, sums[field])
        out[pl.ds(first, SUB), :BLOCK] = sums[0]
        out[pl.ds(first, SUB), BLOCK:] = sums[1]
        return carry

    lax.fori_loop(0, tiles // SUB, step, 0, unroll=4)
    out[tiles : tiles + SUB, :BLOCK] = jnp.broadcast_to(ids[...].astype(F32), (SUB, BLOCK))
    out[tiles : tiles + SUB, BLOCK:] = jnp.zeros((SUB, BLOCK), F32)


def halo_kernel(pos, vel, lists, _, state, near, far, dummy):
    dummy[...] = jnp.zeros(dummy.shape, F32)
    tiles = pos.shape[1] // BLOCK
    rows = lists.shape[1] // BLOCK
    for tile in range(tiles):
        lanes = slice(tile * BLOCK, (tile + 1) * BLOCK)
        mixed = SPRING * pos[:, lanes] - DAMPING * vel[:, lanes]
        for axis in range(3):
            state[axis * tiles + tile : axis * tiles + tile + 1, :] = mixed[axis : axis + 1]
    turned = [
        jnp.concatenate(halves_of(jnp.transpose(state[axis * tiles : (axis + 1) * tiles, :])), 1)
        for axis in range(3)
    ]
    turned = jnp.concatenate(turned, 0)
    span = 2 * BLOCK
    row = iota((BLOCK, span), 0)

    odd = lax.axis_index("reg") % 2
    for away, out in enumerate((near, far)):
        side = 1 - odd if away == 0 else odd

        def step(part, carry):
            named = lists[:, pl.ds(pl.multiple_of(part * span, span), span)]
            named = jnp.where(side == 0, named[:1], named[1:])
            block = lax.shift_right_logical(named, 7)
            lane = named & (BLOCK - 1)
            hot = jnp.where(row == jnp.broadcast_to(block, row.shape), 1.0, 0.0).astype(BF16)
            found = jnp.dot(
                turned, jnp.concatenate([hot, hot], 0), preferred_element_type=F32
            )
            here = row == jnp.broadcast_to(lane, row.shape)
            for axis in range(3):
                value = jnp.where(here, found[axis * BLOCK : (axis + 1) * BLOCK], 0.0)
                value = jnp.sum(value, axis=0, keepdims=True)
                for half in range(2):
                    out[pl.ds(axis * rows + 2 * part + half, 1), :] = value[
                        :, half * BLOCK : (half + 1) * BLOCK
                    ]
            return carry

        lax.fori_loop(0, rows // 2, step, 0, unroll=8)


def message_kernel(mine, second, third, halo_near, halo_far, _, near, far, dummy):
    dummy[...] = jnp.zeros(dummy.shape, F32)
    stride = mine.shape[0]
    half = halo_near.shape[0] // 2
    rows = near.shape[0] - half
    for halo, out in ((halo_near, near), (halo_far, far)):
        for index, group in enumerate((mine, second, third)):
            out[index * stride : (index + 1) * stride, :] = group[...]
        out[rows:, :BLOCK] = halo[:half, :]
        out[rows:, BLOCK:] = halo[half:, :]


def contact_kernel(
    partner, state, message_near, message_far, halo_near, halo_far, named, stiff, _, out, extended
):
    tiles = state.shape[0] // 3
    rows = halo_near.shape[0] // 3
    blocks = tiles + 2 * rows
    base = message_near.shape[0] - 3 * rows // 2
    odd = lax.axis_index("reg") % 2
    sweeps = lax.axis_index("grp") % CORES == 0
    for axis in range(3):
        extended[axis * blocks : axis * blocks + tiles, :] = state[
            axis * tiles : (axis + 1) * tiles, :
        ]
    for message, halo, upper in (
        (message_near, halo_near, 1 - odd), (message_far, halo_far, odd)
    ):
        carried = jnp.concatenate([message[base:, :BLOCK], message[base:, BLOCK:]], 0)
        carried = jnp.where(sweeps, carried, halo[...])
        for axis in range(3):
            first = pl.multiple_of(axis * blocks + tiles + upper * rows, SUB)
            extended[pl.ds(first, rows), :] = carried[axis * rows : (axis + 1) * rows]

    def step(tile, carry):
        lanes = pl.ds(pl.multiple_of(tile * BLOCK, BLOCK), BLOCK)
        entry = named[:, lanes]
        weight = jnp.where(entry >= 0, stiff[:, lanes], 0.0)
        own = entry < BLOCK
        lane = entry & (BLOCK - 1)
        other = partner[tile]
        for axis in range(3):
            mine = jnp.broadcast_to(extended[pl.ds(axis * blocks + tile, 1), :], entry.shape)
            theirs = jnp.broadcast_to(extended[pl.ds(axis * blocks + other, 1), :], entry.shape)
            met = jnp.where(own, lanes_of(mine, lane), lanes_of(theirs, lane))
            pull = jnp.sum(weight * (mine - met), axis=0, keepdims=True)
            out[pl.ds(axis * tiles + tile, 1), :] = pull
        return carry

    lax.fori_loop(0, tiles, step, 0, unroll=4)


def shifted(plane):
    height, width = plane.shape
    row = iota((SUB, width), 0)
    column = iota((height, BLOCK), 1)
    above, below = pltpu.roll(plane, 1, 0), pltpu.roll(plane, height - 1, 0)
    left, right = pltpu.roll(plane, 1, 1), pltpu.roll(plane, width - 1, 1)
    above = jnp.concatenate([jnp.where(row == 0, 0.0, above[:SUB]), above[SUB:]], 0)
    below = jnp.concatenate([below[:-SUB], jnp.where(row == SUB - 1, 0.0, below[-SUB:])], 0)
    left = jnp.concatenate([jnp.where(column == 0, 0.0, left[:, :BLOCK]), left[:, BLOCK:]], 1)
    right = jnp.concatenate(
        [right[:, :-BLOCK], jnp.where(column == BLOCK - 1, 0.0, right[:, -BLOCK:])], 1
    )
    return above, below, left, right


def inverse_of(value):
    near = pl.reciprocal(value, approx=True)
    return near * (2.0 - value * near)


def placed(groups, tiles):
    parts = [halves_of(group[:tiles, :]) for group in groups]
    loads = jnp.concatenate([part[i] for i in range(2) for part in parts], 0)
    ids = jnp.concatenate([group[tiles : tiles + 1, :BLOCK] for group in groups], 1)
    ids = ids.astype(jnp.int32)

    def gathered(wanted):
        hot = jnp.where(wanted == jnp.broadcast_to(ids, wanted.shape), 1.0, 0.0).astype(BF16)
        total = jnp.dot(
            jnp.concatenate([hot, hot], 1), loads, preferred_element_type=F32
        )
        return total[:, :BLOCK], total[:, BLOCK:]

    return ids, gathered


def driven_of(early, late, planes):
    return lambda x: early[planes + x] if x < HEAD else late[x - HEAD]


def coefficients(gathered, tiles, first, full, driven_at, constant, factor, turned, present):
    planes, height, width = constant.shape
    zones = width // BLOCK
    shape = (zones * height, 3 * tiles)
    line = iota(shape, 0)
    block = (line % height) * zones + line // height + first * zones

    for x in range(planes):
        solid, drag = gathered(block + x * (full * zones))
        at = x if turned is None else jnp.where(turned, planes - 1 - x, x)
        voids = 1.0 + solid
        scale = inverse_of(6.0 + (drag + 1.0) * voids)
        if present is not None:
            scale = jnp.where(present, scale, 0.0)
        inverse = voids * scale
        for zone in range(zones):
            lanes = slice(zone * BLOCK, (zone + 1) * BLOCK)
            rows = slice(zone * height, (zone + 1) * height)
            driving = driven_at(x)[:, lanes] + solid[rows]
            constant[at, :, lanes] = driving * inverse[rows]
            factor[at, :, lanes] = scale[rows]


def own_kernel(
    full, mine, second, third, early, late, _message, constant, factor, weight, picks
):
    tiles = weight.shape[0]
    planes, height, width = constant.shape
    place = Place(full, height)
    zones = width // BLOCK
    ids, gathered = placed((mine, second, third), tiles)
    coefficients(
        gathered, tiles, place.first, full, driven_of(early, late, planes), constant, factor,
        place.even, None,
    )
    turned = [
        jnp.transpose(
            jnp.broadcast_to(ids[:, i * tiles : (i + 1) * tiles], (BLOCK, tiles)).astype(F32)
        ).astype(jnp.int32)
        for i in range(3)
    ]
    solid, drag = gathered(jnp.concatenate([turned[0]] * 3, 1))
    weight[...] = 1.0 / (1.0 / (1.0 + solid) + drag)
    for i in range(3):
        block = turned[i]
        line, zone = block // zones, block % zones
        x, y = line // full, line % full
        row = (x * zones + zone) * height + y - place.first
        held = y // place.own_rows == jnp.where(place.sweeps, place.half, -1)
        row = jnp.concatenate([jnp.where(held, row, -1)] * (picks.shape[1] // BLOCK), 1)
        hot = jnp.where(row == iota(row.shape, 1), 1.0, 0.0).astype(BF16)
        picks[i * tiles : (i + 1) * tiles, :] = hot


def sweep(source, target, coefficient, start, stop):
    def plane(at, carry):
        above, below, left, right = shifted(source[at])
        around = source[at - 1] + source[at + 1] + above + below + left + right
        constant, factor = coefficient(at)
        target[at] = constant + factor * around
        return carry

    lax.fori_loop(start, stop, plane, 0, unroll=4)


def deposits_of(message, tiles):
    stride = tiles + SUB
    return placed([message.at[i * stride : (i + 1) * stride] for i in range(3)], tiles)[1]


def near_kernel(
    full, tiles, message, pressure, near, near_late, beyond, own_constant, own_factor, kept_even, kept_odd,
    constant, factor, old, new,
):
    planes, height, width = own_constant.shape
    place = Place(full, height)
    rim = planes + 1
    coefficients(
        deposits_of(message, tiles), tiles, place.first, full,
        driven_of(near, near_late, planes), constant, factor, place.even, jnp.where(place.odd, place.lower, place.upper),
    )
    old[0] = beyond[...]
    for x in range(planes):
        at = jnp.where(place.even, planes - 1 - x, x)
        old[1 + x] = near[at]
        old[rim + x] = pressure[at]
    buffers = (old, new)
    for index in range(planes):
        source, target = buffers[index % 2], buffers[(index + 1) % 2]
        sweep(source, target, lambda at: (constant[at - 1], factor[at - 1]), 1 + index, rim)
        sweep(
            source, target, lambda at: (own_constant[at - rim], own_factor[at - rim]),
            rim, 2 * planes - index,
        )
    kept_even[...] = old[planes : 2 * planes]
    kept_odd[...] = new[planes : 2 * planes]


def far_kernel(
    full, tiles, picks, message, pressure, far, far_late, own_constant, own_factor, kept_even, kept_odd,
    out_a, out_b, out_c, constant, factor, old, new, fields,
):
    planes, height, width = own_constant.shape
    zones = width // BLOCK
    place = Place(full, height)
    rim = planes + 1
    coefficients(
        deposits_of(message, tiles), tiles, place.first, full,
        driven_of(far, far_late, planes), constant, factor, place.even, jnp.where(place.odd, place.upper, place.lower),
    )
    old[planes : 2 * planes] = kept_even[...]
    new[planes : 2 * planes] = kept_odd[...]
    old[2 * planes] = pressure[jnp.where(place.even, 0, planes - 1)]
    for x in range(planes):
        at = jnp.where(place.even, planes - 1 - x, x)
        old[rim + planes + x] = far[at]
    old[rim + 2 * planes] = far[planes + HEAD]
    buffers = (old, new)
    edge = rim + planes
    for index in range(planes):
        source, target = buffers[index % 2], buffers[(index + 1) % 2]
        sweep(
            source, target, lambda at: (own_constant[at - rim], own_factor[at - rim]),
            2 * planes - index, edge,
        )
        sweep(
            source, target, lambda at: (constant[at - edge], factor[at - edge]),
            edge, edge + planes - index,
        )
    last = buffers[planes % 2]
    way = jnp.where(place.even, -0.5, 0.5)

    def gradient(x, carry):
        at = rim + x
        above, below, left, right = shifted(last[at])
        grads = (way * (last[at + 1] - last[at - 1]), 0.5 * (below - above), 0.5 * (right - left))
        line = jnp.where(place.even, planes - 1 - x, x) * zones
        for zone in range(zones):
            first = pl.multiple_of((line + zone) * height, SUB)
            for axis, grad in enumerate(grads):
                fields[pl.ds(first, height), axis * BLOCK : (axis + 1) * BLOCK] = (
                    grad[:, zone * BLOCK : (zone + 1) * BLOCK]
                )
        return carry

    lax.fori_loop(0, planes, gradient, 0, unroll=4)
    pieces = jnp.concatenate(halves_of(fields[...]), 1)
    total = jnp.dot(picks[...], pieces, preferred_element_type=F32)
    total = total[:, : 3 * BLOCK] + total[:, 3 * BLOCK :]
    for index, out in enumerate((out_a, out_b, out_c)):
        out[...] = total[index * tiles : (index + 1) * tiles]


def final_kernel(
    count, grads_a, grads_b, grads_c, weight, contact, vel, vol, drag, cell, out,
):
    tiles = cell.shape[0]
    cells = cell[...]
    heft = lanes_of(weight[...], cells)
    slot = iota(cells.shape, 0) * BLOCK + iota(cells.shape, 1)
    live = slot < count[0]
    volume = vol[...]
    push = TIME_STEP / volume
    for axis in range(3):
        lanes = slice(axis * BLOCK, (axis + 1) * BLOCK)
        gradient = lanes_of(grads_a[:, lanes] + grads_b[:, lanes] + grads_c[:, lanes], cells)
        own = jnp.concatenate(
            [vel[axis : axis + 1, t * BLOCK : (t + 1) * BLOCK] for t in range(tiles)], 0
        )
        fluid = -gradient * heft
        force = contact[axis * tiles : (axis + 1) * tiles, :] - volume * gradient
        force = force + drag[...] * (fluid - own)
        new = jnp.where(live, own + force * push, 0.0)
        for t in range(tiles):
            out[axis : axis + 1, t * BLOCK : (t + 1) * BLOCK] = new[t : t + 1, :]


def on_device(
    grain_pos,
    grain_vel,
    grain_vol,
    drag_coef,
    grain_count,
    contact_rows,
    contact_stiff,
    partner_block,
    halo_list,
    grain_cell,
    tile_cell_block,
    pressure_old,
    pressure_source,
    solid_old,
):
    groups, regions = lax.axis_size("grp"), lax.axis_size("reg")
    holding = groups - 1
    halves = groups // CORES
    slots = grain_pos.shape[1]
    tiles = slots // BLOCK
    planes, full, width = pressure_old.shape
    assert planes == ITERS
    own_rows = full // halves
    height = min(full, own_rows + SUB * min(2, halves - 1))
    owners = range(0, groups, CORES)
    holders = range(holding)

    def send(value, pairs):
        flat = [(a[0] * regions + a[1], b[0] * regions + b[1]) for a, b in pairs]
        return lax.ppermute(value, ("grp", "reg"), flat)

    def along_reg(value, members, goes, core=0):
        pairs = [
            ((g + core, r), (g, r + goes[r % 2]))
            for g in members
            for r in range(regions)
            if 0 <= r + goes[r % 2] < regions
        ]
        return send(value, pairs)

    def along_grp(value, step, members):
        pairs = [((g, r), ((g + step) % holding, r)) for g in members for r in range(regions)]
        return send(value, pairs)

    count = grain_count
    cell = grain_cell.reshape(tiles, BLOCK)
    vol = grain_vol.reshape(tiles, BLOCK)
    drag = drag_coef.reshape(tiles, BLOCK)
    ids = tile_cell_block.reshape(1, tiles)
    field_bytes = 4 * planes * height * width

    field = shaped(planes, height, width)
    plane = shaped(height, width)
    small = shaped(SUB, BLOCK)
    early, late, ends, inner = call(
        window_kernel,
        (
            shaped(planes + HEAD, height, width), shaped(planes - HEAD, height, width), plane,
            plane,
        ),
        [HBM] * 3, (pressure_old, pressure_source, solid_old),
        [pltpu.VMEM((planes, height, width), F32)] * 3
        + [pltpu.SemaphoreType.DMA((5 * planes + 2,))],
        flops=field_bytes, size=6 * field_bytes, limit=61_950_000, place=HBM,
    )
    near = along_reg(early, owners, (1, -1), core=1)
    near_late = along_reg(late, owners, (1, -1), core=1)
    beyond = along_reg(ends, owners, (-2, 2), core=1)
    mine, after_deposit = call(
        deposit_kernel, (shaped(tiles + SUB, 2 * BLOCK), small), [SMEM] + [VMEM] * 4,
        (count, cell, vol, drag, ids), flops=2 * 32 * 48 * 65536, size=5 * 4 * slots,
    )
    second = along_grp(mine, 1, holders)
    third = along_grp(mine, 2, holders)
    rows = halo_list.shape[1] // BLOCK
    halo = shaped(3 * rows, BLOCK)
    state, halo_near, halo_far, after_halo = call(
        halo_kernel, (shaped(3 * tiles, BLOCK), halo, halo, small),
        [VMEM] * 4, (grain_pos, grain_vel, halo_list, after_deposit), flops=2 * 3 * 8 * BLOCK * BLOCK * slots // 4,
        size=4 * 4 * 3 * slots,
    )
    others = [g for g in holders if g not in owners]
    came_near = along_reg(halo_near, others, (1, -1))
    came_far = along_reg(halo_far, others, (-1, 1))
    far, after_forward = call(
        forward_kernel, (shaped(planes + HEAD + 1, height, width), small), [VMEM] * 7,
        (near, inner, after_halo, second, third, came_near, came_far), size=5 * field_bytes,
    )
    far = along_reg(far, owners, (2, -2))
    far_late = along_reg(near_late, owners, (2, -2))
    message = shaped(holding * (tiles + SUB) + 3 * rows // 2, 2 * BLOCK)
    message_near, message_far, after_message = call(
        message_kernel, (message, message, small), [VMEM] * 6,
        (mine, second, third, halo_near, halo_far, after_forward), size=8 * 2 * BLOCK * 500,
    )
    message_near = along_reg(message_near, owners, (1, -1))
    message_far = along_reg(message_far, owners, (-1, 1))
    constant, factor, weight, picks = call(
        functools.partial(own_kernel, full),
        (
            field, field, shaped(tiles, BLOCK),
            jax.ShapeDtypeStruct((3 * tiles, planes * height * width // BLOCK), BF16),
        ),
        [VMEM] * 6, (mine, second, third, early, late, after_message),
        flops=planes * height * 4 * 384 * 256 * 6, size=9 * field_bytes,
    )
    window_of = lambda count: pltpu.VMEM((count, height, width), F32)
    kept_even, kept_odd = call(
        functools.partial(near_kernel, full, tiles), (field, field), [VMEM] * 7,
        (message_near, early, near, near_late, beyond, constant, factor),
        [window_of(planes)] * 2 + [window_of(2 * planes + 1)] * 2,
        flops=planes * height * 4 * 384 * 256 * 6, size=9 * field_bytes,
    )
    grads = shaped(tiles, 3 * BLOCK)
    grads_a, grads_b, grads_c = call(
        functools.partial(far_kernel, full, tiles), (grads,) * 3, [VMEM] * 9,
        (picks, message_far, early, far, far_late, constant, factor, kept_even, kept_odd),
        [window_of(planes)] * 2
        + [window_of(3 * planes + 2)] * 2
        + [pltpu.VMEM((planes * height * width // BLOCK, 3 * BLOCK), F32)],
        flops=planes * height * 4 * 384 * 256 * 6, size=9 * field_bytes,
    )
    grads_b = along_grp(grads_b, -1, owners)
    grads_c = along_grp(grads_c, -2, owners)

    contact = call(
        contact_kernel, shaped(3 * tiles, BLOCK), [SMEM] + [VMEM] * 7 + [ANY],
        (
            partner_block, state, message_near, message_far, came_near, came_far, contact_rows,
            contact_stiff, grads_a,
        ),
        [pltpu.VMEM((3 * (tiles + 2 * rows), BLOCK), F32)],
        flops=60 * 8 * slots, size=4 * 20 * slots,
    )
    return call(
        final_kernel, shaped(3, slots), [SMEM] + [VMEM] * 9,
        (count, grads_a, grads_b, grads_c, weight, contact, grain_vel, vol, drag, cell),
        flops=60 * slots, size=4 * 20 * slots,
    )


def solution(mesh):
    in_specs = (
        P(None, ("grp", "reg")),
        P(None, ("grp", "reg")),
        P(("grp", "reg")),
        P(("grp", "reg")),
        P(("grp", "reg")),
        P(None, ("grp", "reg")),
        P(None, ("grp", "reg")),
        P(("grp", "reg")),
        P(None, ("grp", "reg")),
        P(("grp", "reg")),
        P(("grp", "reg")),
        P("reg", None, None),
        P("reg", None, None),
        P("reg", None, None),
    )
    out_specs = P(None, ("grp", "reg"))
    return jax.shard_map(
        on_device, mesh=mesh, in_specs=in_specs, out_specs=out_specs, check_vma=False
    )
```

```python
import functools

import jax
import jax.numpy as jnp
from jax import lax
from jax.experimental import pallas as pl
from jax.experimental.pallas import tpu as pltpu
from jax.sharding import PartitionSpec as P

BLOCK = 128
SUB = 8
CORES = 2
ITERS = 4
HEAD = 1
SPRING = 1.0
DAMPING = 0.5
TIME_STEP = 0.5

VMEM = pl.BlockSpec(memory_space=pltpu.VMEM)
SMEM = pl.BlockSpec(memory_space=pltpu.SMEM)
ANY = pl.BlockSpec(memory_space=pl.ANY)
HBM = pl.BlockSpec(memory_space=pltpu.HBM)
F32 = jnp.float32
BF16 = jnp.bfloat16


def iota(shape, dim):
    return lax.broadcasted_iota(jnp.int32, shape, dim)


def shaped(*dims):
    return jax.ShapeDtypeStruct(dims, F32)


def call(kernel, outs, specs, args, scratch=(), flops=0, size=0, limit=40_000_000, place=VMEM):
    return pl.pallas_call(
        kernel,
        out_shape=outs,
        in_specs=specs,
        out_specs=jax.tree.map(lambda _: place, outs),
        scratch_shapes=list(scratch),
        compiler_params=pltpu.CompilerParams(vmem_limit_bytes=limit),
        cost_estimate=pl.CostEstimate(flops=flops, bytes_accessed=size, transcendentals=0),
    )(*args)


class Place:
    def __init__(self, full, height):
        groups, regions = lax.axis_size("grp"), lax.axis_size("reg")
        self.group, region = lax.axis_index("grp"), lax.axis_index("reg")
        self.half = self.group // CORES
        self.own_rows = full // (groups // CORES)
        first = jnp.clip(self.half * self.own_rows - SUB, 0, full - height)
        self.first = pl.multiple_of(first, SUB)
        self.sweeps = self.group % CORES == 0
        self.parity = region % 2
        self.odd, self.even = self.parity == 1, self.parity == 0
        self.lower, self.upper = region > 0, region < regions - 1


def lanes_of(source, index):
    return jnp.take_along_axis(source, index, axis=1, mode="promise_in_bounds")


def halves_of(value):
    high = value.astype(BF16)
    return high, (value - high.astype(F32)).astype(BF16)


def window_kernel(
    pressure_old, source, solid_before, early, late, ends, inner, pressure, driven, solid, sems
):
    planes, height, _ = solid.shape
    place = Place(pressure_old.shape[1], height)
    rows = pl.ds(place.first, height)
    used = []

    def copy(whole, part):
        used.append(None)
        return pltpu.make_async_copy(whole, part, sems.at[len(used) - 1])

    fetched = [
        [copy(whole.at[x, rows, :], part.at[x]) for x in range(planes)]
        for whole, part in ((pressure_old, pressure), (source, driven), (solid_before, solid))
    ]
    stored = [copy(pressure.at[x], early.at[x]) for x in range(planes)]
    for x in range(planes):
        stored.append(copy(driven.at[x], early.at[planes + x] if x < HEAD else late.at[x - HEAD]))
    sides = (
        copy(pressure.at[place.parity * (planes - 1)], ends),
        copy(pressure.at[(1 - place.parity) * (planes - 1)], inner),
    )
    for x in range(planes):
        for part in fetched:
            part[x].start()
    for x in range(planes):
        fetched[0][x].wait()
        stored[x].start()
        fetched[1][x].wait()
        fetched[2][x].wait()
        driven[x] = driven[x] - solid[x]
        stored[planes + x].start()
    for one in sides:
        one.start()
    for one in stored:
        one.wait()
    for one in sides:
        one.wait()


def forward_kernel(near, inner, _halo, _second, _third, _beyond, out, dummy):
    dummy[...] = jnp.zeros(dummy.shape, F32)
    count = near.shape[0]
    out[:count] = near[...]
    out[count] = inner[...]


def deposit_kernel(count, cell, vol, drag, ids, out, dummy):
    dummy[...] = jnp.zeros(dummy.shape, F32)
    tiles = cell.shape[0]
    sub = iota((SUB, BLOCK), 0)
    rows_c = iota((BLOCK, BLOCK), 0)
    even = sub % 2 == 0
    low_pair = sub % 4 < 2

    def step(group, carry):
        first = pl.multiple_of(group * SUB, SUB)
        slot = (first + sub) * BLOCK + iota((SUB, BLOCK), 1)
        live = slot < count[0]
        cells = cell[pl.ds(first, SUB), :]
        parts = halves_of(jnp.where(live, vol[pl.ds(first, SUB), :], 0.0)) + halves_of(
            jnp.where(live, drag[pl.ds(first, SUB), :], 0.0)
        )
        parts = [part.astype(F32) for part in parts]
        left = jnp.concatenate([jnp.where(even, part, 0.0) for part in parts], 0)
        right = jnp.concatenate([jnp.where(even, 0.0, part) for part in parts], 0)
        loads = jnp.concatenate([left, right], 1).astype(BF16)
        sums = [jnp.zeros((SUB, BLOCK), F32), jnp.zeros((SUB, BLOCK), F32)]
        for quad in range(SUB // 4):
            hot = [
                jnp.where(
                    rows_c == jnp.broadcast_to(cells[t : t + 1, :], (BLOCK, BLOCK)), 1.0, 0.0
                ).astype(BF16)
                for t in range(4 * quad, 4 * quad + 4)
            ]
            picked = jnp.concatenate(
                [jnp.concatenate(hot[:2], 1), jnp.concatenate(hot[2:], 1)], 0
            )
            placed = lax.dot_general(
                loads, picked, (((1,), (1,)), ((), ())), preferred_element_type=F32
            )
            for field in range(2):
                base = field * 2 * SUB
                total = placed[base : base + SUB] + placed[base + SUB : base + 2 * SUB]
                chosen = jnp.where(low_pair, total[:, :BLOCK], total[:, BLOCK:])
                sums[field] = jnp.where(sub // 4 == quad, chosen, sums[field])
        out[pl.ds(first, SUB), :BLOCK] = sums[0]
        out[pl.ds(first, SUB), BLOCK:] = sums[1]
        return carry

    lax.fori_loop(0, tiles // SUB, step, 0, unroll=4)
    out[tiles : tiles + SUB, :BLOCK] = jnp.broadcast_to(ids[...].astype(F32), (SUB, BLOCK))
    out[tiles : tiles + SUB, BLOCK:] = jnp.zeros((SUB, BLOCK), F32)


def halo_kernel(pos, vel, lists, _, state, near, far, dummy):
    dummy[...] = jnp.zeros(dummy.shape, F32)
    tiles = pos.shape[1] // BLOCK
    rows = lists.shape[1] // BLOCK
    for tile in range(tiles):
        lanes = slice(tile * BLOCK, (tile + 1) * BLOCK)
        mixed = SPRING * pos[:, lanes] - DAMPING * vel[:, lanes]
        for axis in range(3):
            state[axis * tiles + tile : axis * tiles + tile + 1, :] = mixed[axis : axis + 1]
    turned = [
        jnp.concatenate(halves_of(jnp.transpose(state[axis * tiles : (axis + 1) * tiles, :])), 1)
        for axis in range(3)
    ]
    turned = jnp.concatenate(turned, 0)
    span = 2 * BLOCK
    row = iota((BLOCK, span), 0)

    odd = lax.axis_index("reg") % 2
    for away, out in enumerate((near, far)):
        side = 1 - odd if away == 0 else odd

        def step(part, carry):
            named = lists[:, pl.ds(pl.multiple_of(part * span, span), span)]
            named = jnp.where(side == 0, named[:1], named[1:])
            block = lax.shift_right_logical(named, 7)
            lane = named & (BLOCK - 1)
            hot = jnp.where(row == jnp.broadcast_to(block, row.shape), 1.0, 0.0).astype(BF16)
            found = jnp.dot(
                turned, jnp.concatenate([hot, hot], 0), preferred_element_type=F32
            )
            here = row == jnp.broadcast_to(lane, row.shape)
            for axis in range(3):
                value = jnp.where(here, found[axis * BLOCK : (axis + 1) * BLOCK], 0.0)
                value = jnp.sum(value, axis=0, keepdims=True)
                for half in range(2):
                    out[pl.ds(axis * rows + 2 * part + half, 1), :] = value[
                        :, half * BLOCK : (half + 1) * BLOCK
                    ]
            return carry

        lax.fori_loop(0, rows // 2, step, 0, unroll=8)


def message_kernel(mine, second, third, halo_near, halo_far, _, near, far, dummy):
    dummy[...] = jnp.zeros(dummy.shape, F32)
    stride = mine.shape[0]
    half = halo_near.shape[0] // 2
    rows = near.shape[0] - half
    for halo, out in ((halo_near, near), (halo_far, far)):
        for index, group in enumerate((mine, second, third)):
            out[index * stride : (index + 1) * stride, :] = group[...]
        out[rows:, :BLOCK] = halo[:half, :]
        out[rows:, BLOCK:] = halo[half:, :]


def contact_kernel(
    partner, state, message_near, message_far, halo_near, halo_far, named, stiff, _, out, extended
):
    tiles = state.shape[0] // 3
    rows = halo_near.shape[0] // 3
    blocks = tiles + 2 * rows
    base = message_near.shape[0] - 3 * rows // 2
    odd = lax.axis_index("reg") % 2
    sweeps = lax.axis_index("grp") % CORES == 0
    for axis in range(3):
        extended[axis * blocks : axis * blocks + tiles, :] = state[
            axis * tiles : (axis + 1) * tiles, :
        ]
    for message, halo, upper in (
        (message_near, halo_near, 1 - odd), (message_far, halo_far, odd)
    ):
        carried = jnp.concatenate([message[base:, :BLOCK], message[base:, BLOCK:]], 0)
        carried = jnp.where(sweeps, carried, halo[...])
        for axis in range(3):
            first = pl.multiple_of(axis * blocks + tiles + upper * rows, SUB)
            extended[pl.ds(first, rows), :] = carried[axis * rows : (axis + 1) * rows]

    def step(tile, carry):
        lanes = pl.ds(pl.multiple_of(tile * BLOCK, BLOCK), BLOCK)
        entry = named[:, lanes]
        weight = jnp.where(entry >= 0, stiff[:, lanes], 0.0)
        own = entry < BLOCK
        lane = entry & (BLOCK - 1)
        other = partner[tile]
        for axis in range(3):
            mine = jnp.broadcast_to(extended[pl.ds(axis * blocks + tile, 1), :], entry.shape)
            theirs = jnp.broadcast_to(extended[pl.ds(axis * blocks + other, 1), :], entry.shape)
            met = jnp.where(own, lanes_of(mine, lane), lanes_of(theirs, lane))
            pull = jnp.sum(weight * (mine - met), axis=0, keepdims=True)
            out[pl.ds(axis * tiles + tile, 1), :] = pull
        return carry

    lax.fori_loop(0, tiles, step, 0, unroll=4)


def shifted(plane):
    height, width = plane.shape
    row = iota((SUB, width), 0)
    column = iota((height, BLOCK), 1)
    above, below = pltpu.roll(plane, 1, 0), pltpu.roll(plane, height - 1, 0)
    left, right = pltpu.roll(plane, 1, 1), pltpu.roll(plane, width - 1, 1)
    above = jnp.concatenate([jnp.where(row == 0, 0.0, above[:SUB]), above[SUB:]], 0)
    below = jnp.concatenate([below[:-SUB], jnp.where(row == SUB - 1, 0.0, below[-SUB:])], 0)
    left = jnp.concatenate([jnp.where(column == 0, 0.0, left[:, :BLOCK]), left[:, BLOCK:]], 1)
    right = jnp.concatenate(
        [right[:, :-BLOCK], jnp.where(column == BLOCK - 1, 0.0, right[:, -BLOCK:])], 1
    )
    return above, below, left, right


def inverse_of(value):
    near = pl.reciprocal(value, approx=True)
    return near * (2.0 - value * near)


def placed(groups, tiles):
    parts = [halves_of(group[:tiles, :]) for group in groups]
    loads = jnp.concatenate([part[i] for i in range(2) for part in parts], 0)
    ids = jnp.concatenate([group[tiles : tiles + 1, :BLOCK] for group in groups], 1)
    ids = ids.astype(jnp.int32)

    def gathered(wanted):
        hot = jnp.where(wanted == jnp.broadcast_to(ids, wanted.shape), 1.0, 0.0).astype(BF16)
        total = jnp.dot(
            jnp.concatenate([hot, hot], 1), loads, preferred_element_type=F32
        )
        return total[:, :BLOCK], total[:, BLOCK:]

    return ids, gathered


def driven_of(early, late, planes):
    return lambda x: early[planes + x] if x < HEAD else late[x - HEAD]


def coefficients(gathered, tiles, first, full, driven_at, constant, factor, turned, present):
    planes, height, width = constant.shape
    zones = width // BLOCK
    shape = (zones * height, 3 * tiles)
    line = iota(shape, 0)
    block = (line % height) * zones + line // height + first * zones

    for x in range(planes):
        solid, drag = gathered(block + x * (full * zones))
        at = x if turned is None else jnp.where(turned, planes - 1 - x, x)
        voids = 1.0 + solid
        scale = inverse_of(6.0 + (drag + 1.0) * voids)
        if present is not None:
            scale = jnp.where(present, scale, 0.0)
        inverse = voids * scale
        for zone in range(zones):
            lanes = slice(zone * BLOCK, (zone + 1) * BLOCK)
            rows = slice(zone * height, (zone + 1) * height)
            driving = driven_at(x)[:, lanes] + solid[rows]
            constant[at, :, lanes] = driving * inverse[rows]
            factor[at, :, lanes] = scale[rows]


def own_kernel(
    full, mine, second, third, early, late, _message, _near, _far, constant, factor, weight, picks
):
    tiles = weight.shape[0]
    planes, height, width = constant.shape
    place = Place(full, height)
    zones = width // BLOCK
    ids, gathered = placed((mine, second, third), tiles)
    coefficients(
        gathered, tiles, place.first, full, driven_of(early, late, planes), constant, factor,
        place.even, None,
    )
    turned = [
        jnp.transpose(
            jnp.broadcast_to(ids[:, i * tiles : (i + 1) * tiles], (BLOCK, tiles)).astype(F32)
        ).astype(jnp.int32)
        for i in range(3)
    ]
    solid, drag = gathered(jnp.concatenate([turned[0]] * 3, 1))
    weight[...] = 1.0 / (1.0 / (1.0 + solid) + drag)
    for i in range(3):
        block = turned[i]
        line, zone = block // zones, block % zones
        x, y = line // full, line % full
        row = (x * zones + zone) * height + y - place.first
        held = y // place.own_rows == jnp.where(place.sweeps, place.half, -1)
        row = jnp.concatenate([jnp.where(held, row, -1)] * (picks.shape[1] // BLOCK), 1)
        hot = jnp.where(row == iota(row.shape, 1), 1.0, 0.0).astype(BF16)
        picks[i * tiles : (i + 1) * tiles, :] = hot


def sweep(source, target, coefficient, start, stop):
    def plane(at, carry):
        above, below, left, right = shifted(source[at])
        around = source[at - 1] + source[at + 1] + above + below + left + right
        constant, factor = coefficient(at)
        target[at] = constant + factor * around
        return carry

    lax.fori_loop(start, stop, plane, 0, unroll=4)


def deposits_of(message, tiles):
    stride = tiles + SUB
    return placed([message.at[i * stride : (i + 1) * stride] for i in range(3)], tiles)[1]


def near_kernel(
    full, tiles, message, pressure, near, near_late, beyond, own_constant, own_factor, kept_even, kept_odd,
    constant, factor, old, new,
):
    planes, height, width = own_constant.shape
    place = Place(full, height)
    rim = planes + 1
    coefficients(
        deposits_of(message, tiles), tiles, place.first, full,
        driven_of(near, near_late, planes), constant, factor, place.even, jnp.where(place.odd, place.lower, place.upper),
    )
    old[0] = beyond[...]
    for x in range(planes):
        at = jnp.where(place.even, planes - 1 - x, x)
        old[1 + x] = near[at]
        old[rim + x] = pressure[at]
    buffers = (old, new)
    for index in range(planes):
        source, target = buffers[index % 2], buffers[(index + 1) % 2]
        sweep(source, target, lambda at: (constant[at - 1], factor[at - 1]), 1 + index, rim)
        sweep(
            source, target, lambda at: (own_constant[at - rim], own_factor[at - rim]),
            rim, 2 * planes - index,
        )
    kept_even[...] = old[planes : 2 * planes]
    kept_odd[...] = new[planes : 2 * planes]


def far_kernel(
    full, tiles, picks, message, pressure, far, far_late, own_constant, own_factor, kept_even, kept_odd,
    out_a, out_b, out_c, constant, factor, old, new, fields,
):
    planes, height, width = own_constant.shape
    zones = width // BLOCK
    place = Place(full, height)
    rim = planes + 1
    coefficients(
        deposits_of(message, tiles), tiles, place.first, full,
        driven_of(far, far_late, planes), constant, factor, place.even, jnp.where(place.odd, place.upper, place.lower),
    )
    old[planes : 2 * planes] = kept_even[...]
    new[planes : 2 * planes] = kept_odd[...]
    old[2 * planes] = pressure[jnp.where(place.even, 0, planes - 1)]
    for x in range(planes):
        at = jnp.where(place.even, planes - 1 - x, x)
        old[rim + planes + x] = far[at]
    old[rim + 2 * planes] = far[planes + HEAD]
    buffers = (old, new)
    edge = rim + planes
    for index in range(planes):
        source, target = buffers[index % 2], buffers[(index + 1) % 2]
        sweep(
            source, target, lambda at: (own_constant[at - rim], own_factor[at - rim]),
            2 * planes - index, edge,
        )
        sweep(
            source, target, lambda at: (constant[at - edge], factor[at - edge]),
            edge, edge + planes - index,
        )
    last = buffers[planes % 2]
    way = jnp.where(place.even, -0.5, 0.5)

    def gradient(x, carry):
        at = rim + x
        above, below, left, right = shifted(last[at])
        grads = (way * (last[at + 1] - last[at - 1]), 0.5 * (below - above), 0.5 * (right - left))
        line = jnp.where(place.even, planes - 1 - x, x) * zones
        for zone in range(zones):
            first = pl.multiple_of((line + zone) * height, SUB)
            for axis, grad in enumerate(grads):
                fields[pl.ds(first, height), axis * BLOCK : (axis + 1) * BLOCK] = (
                    grad[:, zone * BLOCK : (zone + 1) * BLOCK]
                )
        return carry

    lax.fori_loop(0, planes, gradient, 0, unroll=4)
    pieces = jnp.concatenate(halves_of(fields[...]), 1)
    total = jnp.dot(picks[...], pieces, preferred_element_type=F32)
    total = total[:, : 3 * BLOCK] + total[:, 3 * BLOCK :]
    for index, out in enumerate((out_a, out_b, out_c)):
        out[...] = total[index * tiles : (index + 1) * tiles]


def final_kernel(
    count, grads_a, grads_b, grads_c, weight, contact, vel, vol, drag, cell, out,
):
    tiles = cell.shape[0]
    cells = cell[...]
    heft = lanes_of(weight[...], cells)
    slot = iota(cells.shape, 0) * BLOCK + iota(cells.shape, 1)
    live = slot < count[0]
    volume = vol[...]
    push = TIME_STEP / volume
    for axis in range(3):
        lanes = slice(axis * BLOCK, (axis + 1) * BLOCK)
        gradient = lanes_of(grads_a[:, lanes] + grads_b[:, lanes] + grads_c[:, lanes], cells)
        own = jnp.concatenate(
            [vel[axis : axis + 1, t * BLOCK : (t + 1) * BLOCK] for t in range(tiles)], 0
        )
        fluid = -gradient * heft
        force = contact[axis * tiles : (axis + 1) * tiles, :] - volume * gradient
        force = force + drag[...] * (fluid - own)
        new = jnp.where(live, own + force * push, 0.0)
        for t in range(tiles):
            out[axis : axis + 1, t * BLOCK : (t + 1) * BLOCK] = new[t : t + 1, :]


def on_device(
    grain_pos,
    grain_vel,
    grain_vol,
    drag_coef,
    grain_count,
    contact_rows,
    contact_stiff,
    partner_block,
    halo_list,
    grain_cell,
    tile_cell_block,
    pressure_old,
    pressure_source,
    solid_old,
):
    groups, regions = lax.axis_size("grp"), lax.axis_size("reg")
    holding = groups - 1
    halves = groups // CORES
    slots = grain_pos.shape[1]
    tiles = slots // BLOCK
    planes, full, width = pressure_old.shape
    assert planes == ITERS
    own_rows = full // halves
    height = min(full, own_rows + SUB * min(2, halves - 1))
    owners = range(0, groups, CORES)
    holders = range(holding)

    def send(value, pairs):
        flat = [(a[0] * regions + a[1], b[0] * regions + b[1]) for a, b in pairs]
        return lax.ppermute(value, ("grp", "reg"), flat)

    def along_reg(value, members, goes, core=0):
        pairs = [
            ((g + core, r), (g, r + goes[r % 2]))
            for g in members
            for r in range(regions)
            if 0 <= r + goes[r % 2] < regions
        ]
        return send(value, pairs)

    def along_grp(value, step, members):
        pairs = [((g, r), ((g + step) % holding, r)) for g in members for r in range(regions)]
        return send(value, pairs)

    count = grain_count
    cell = grain_cell.reshape(tiles, BLOCK)
    vol = grain_vol.reshape(tiles, BLOCK)
    drag = drag_coef.reshape(tiles, BLOCK)
    ids = tile_cell_block.reshape(1, tiles)
    field_bytes = 4 * planes * height * width

    field = shaped(planes, height, width)
    plane = shaped(height, width)
    small = shaped(SUB, BLOCK)
    early, late, ends, inner = call(
        window_kernel,
        (
            shaped(planes + HEAD, height, width), shaped(planes - HEAD, height, width), plane,
            plane,
        ),
        [HBM] * 3, (pressure_old, pressure_source, solid_old),
        [pltpu.VMEM((planes, height, width), F32)] * 3
        + [pltpu.SemaphoreType.DMA((5 * planes + 2,))],
        flops=field_bytes, size=6 * field_bytes, limit=61_950_000, place=HBM,
    )
    near = along_reg(early, owners, (1, -1), core=1)
    near_late = along_reg(late, owners, (1, -1), core=1)
    beyond = along_reg(ends, owners, (-2, 2), core=1)
    mine, after_deposit = call(
        deposit_kernel, (shaped(tiles + SUB, 2 * BLOCK), small), [SMEM] + [VMEM] * 4,
        (count, cell, vol, drag, ids), flops=2 * 32 * 48 * 65536, size=5 * 4 * slots,
    )
    second = along_grp(mine, 1, holders)
    third = along_grp(mine, 2, holders)
    rows = halo_list.shape[1] // BLOCK
    halo = shaped(3 * rows, BLOCK)
    state, halo_near, halo_far, after_halo = call(
        halo_kernel, (shaped(3 * tiles, BLOCK), halo, halo, small),
        [VMEM] * 4, (grain_pos, grain_vel, halo_list, after_deposit), flops=slots,
        size=4 * 4 * 3 * slots,
    )
    others = [g for g in holders if g not in owners]
    came_near = along_reg(halo_near, others, (1, -1))
    came_far = along_reg(halo_far, others, (-1, 1))
    far, after_forward = call(
        forward_kernel, (shaped(planes + HEAD + 1, height, width), small), [VMEM] * 6,
        (near, inner, after_halo, second, third, beyond), size=5 * field_bytes,
    )
    far = along_reg(far, owners, (2, -2))
    far_late = along_reg(near_late, owners, (2, -2))
    message = shaped(holding * (tiles + SUB) + 3 * rows // 2, 2 * BLOCK)
    message_near, message_far, after_message = call(
        message_kernel, (message, message, small), [VMEM] * 6,
        (mine, second, third, halo_near, halo_far, after_forward), size=8 * 2 * BLOCK * 500,
    )
    message_near = along_reg(message_near, owners, (1, -1))
    message_far = along_reg(message_far, owners, (-1, 1))
    constant, factor, weight, picks = call(
        functools.partial(own_kernel, full),
        (
            field, field, shaped(tiles, BLOCK),
            jax.ShapeDtypeStruct((3 * tiles, planes * height * width // BLOCK), BF16),
        ),
        [VMEM] * 8,
        (mine, second, third, early, late, after_message, came_near, came_far),
        flops=planes * height * 4 * 384 * 256 * 6, size=9 * field_bytes,
    )
    window_of = lambda count: pltpu.VMEM((count, height, width), F32)
    kept_even, kept_odd = call(
        functools.partial(near_kernel, full, tiles), (field, field), [VMEM] * 7,
        (message_near, early, near, near_late, beyond, constant, factor),
        [window_of(planes)] * 2 + [window_of(2 * planes + 1)] * 2,
        flops=planes * height * 4 * 384 * 256 * 6, size=9 * field_bytes,
    )
    grads = shaped(tiles, 3 * BLOCK)
    grads_a, grads_b, grads_c = call(
        functools.partial(far_kernel, full, tiles), (grads,) * 3, [VMEM] * 9,
        (picks, message_far, early, far, far_late, constant, factor, kept_even, kept_odd),
        [window_of(planes)] * 2
        + [window_of(3 * planes + 2)] * 2
        + [pltpu.VMEM((planes * height * width // BLOCK, 3 * BLOCK), F32)],
        flops=planes * height * 4 * 384 * 256 * 6, size=9 * field_bytes,
    )
    grads_b = along_grp(grads_b, -1, owners)
    grads_c = along_grp(grads_c, -2, owners)

    contact = call(
        contact_kernel, shaped(3 * tiles, BLOCK), [SMEM] + [VMEM] * 7 + [ANY],
        (
            partner_block, state, message_near, message_far, came_near, came_far, contact_rows,
            contact_stiff, grads_a,
        ),
        [pltpu.VMEM((3 * (tiles + 2 * rows), BLOCK), F32)],
        flops=60 * 8 * slots, size=4 * 20 * slots,
    )
    return call(
        final_kernel, shaped(3, slots), [SMEM] + [VMEM] * 9,
        (count, grads_a, grads_b, grads_c, weight, contact, grain_vel, vol, drag, cell),
        flops=60 * slots, size=4 * 20 * slots,
    )


def solution(mesh):
    in_specs = (
        P(None, ("grp", "reg")),
        P(None, ("grp", "reg")),
        P(("grp", "reg")),
        P(("grp", "reg")),
        P(("grp", "reg")),
        P(None, ("grp", "reg")),
        P(None, ("grp", "reg")),
        P(("grp", "reg")),
        P(None, ("grp", "reg")),
        P(("grp", "reg")),
        P(("grp", "reg")),
        P("reg", None, None),
        P("reg", None, None),
        P("reg", None, None),
    )
    out_specs = P(None, ("grp", "reg"))
    return jax.shard_map(
        on_device, mesh=mesh, in_specs=in_specs, out_specs=out_specs, check_vma=False
    )
```

```python
import functools

import jax
import jax.numpy as jnp
from jax import lax
from jax.experimental import pallas as pl
from jax.experimental.pallas import tpu as pltpu
from jax.sharding import PartitionSpec as P

BLOCK = 128
SUB = 8
CORES = 2
ITERS = 4
HEAD = 1
SPRING = 1.0
DAMPING = 0.5
TIME_STEP = 0.5

VMEM = pl.BlockSpec(memory_space=pltpu.VMEM)
SMEM = pl.BlockSpec(memory_space=pltpu.SMEM)
ANY = pl.BlockSpec(memory_space=pl.ANY)
HBM = pl.BlockSpec(memory_space=pltpu.HBM)
F32 = jnp.float32
BF16 = jnp.bfloat16


def iota(shape, dim):
    return lax.broadcasted_iota(jnp.int32, shape, dim)


def shaped(*dims):
    return jax.ShapeDtypeStruct(dims, F32)


def call(kernel, outs, specs, args, scratch=(), flops=0, size=0, limit=40_000_000, place=VMEM):
    return pl.pallas_call(
        kernel,
        out_shape=outs,
        in_specs=specs,
        out_specs=jax.tree.map(lambda _: place, outs),
        scratch_shapes=list(scratch),
        compiler_params=pltpu.CompilerParams(vmem_limit_bytes=limit),
        cost_estimate=pl.CostEstimate(flops=flops, bytes_accessed=size, transcendentals=0),
    )(*args)


class Place:
    def __init__(self, full, height):
        groups, regions = lax.axis_size("grp"), lax.axis_size("reg")
        self.group, region = lax.axis_index("grp"), lax.axis_index("reg")
        self.half = self.group // CORES
        self.own_rows = full // (groups // CORES)
        first = jnp.clip(self.half * self.own_rows - SUB, 0, full - height)
        self.first = pl.multiple_of(first, SUB)
        self.sweeps = self.group % CORES == 0
        self.parity = region % 2
        self.odd, self.even = self.parity == 1, self.parity == 0
        self.lower, self.upper = region > 0, region < regions - 1


def lanes_of(source, index):
    return jnp.take_along_axis(source, index, axis=1, mode="promise_in_bounds")


def halves_of(value):
    high = value.astype(BF16)
    return high, (value - high.astype(F32)).astype(BF16)


def window_kernel(
    pressure_old, source, solid_before, ids, count, early, late, ends, inner, marks,
    pressure, driven, solid, held, counted, sems,
):
    planes, height, _ = solid.shape
    place = Place(pressure_old.shape[1], height)
    rows = pl.ds(place.first, height)
    used = []

    def copy(whole, part):
        used.append(None)
        return pltpu.make_async_copy(whole, part, sems.at[len(used) - 1])

    fetched = [
        [copy(whole.at[x, rows, :], part.at[x]) for x in range(planes)]
        for whole, part in ((pressure_old, pressure), (source, driven), (solid_before, solid))
    ]
    stored = [copy(pressure.at[x], early.at[x]) for x in range(planes)]
    for x in range(planes):
        stored.append(copy(driven.at[x], early.at[planes + x] if x < HEAD else late.at[x - HEAD]))
    sides = (
        copy(pressure.at[place.parity * (planes - 1)], ends),
        copy(pressure.at[(1 - place.parity) * (planes - 1)], inner),
    )
    given = (copy(ids, held.at[:1]), copy(count, counted))
    passed = copy(held, marks)
    for one in given:
        one.start()
    for x in range(planes):
        for part in fetched:
            part[x].start()
    for one in given:
        one.wait()
    held[1:2] = jnp.broadcast_to(counted[0], (1, BLOCK))
    passed.start()
    for x in range(planes):
        fetched[0][x].wait()
        stored[x].start()
        fetched[1][x].wait()
        fetched[2][x].wait()
        driven[x] = driven[x] - solid[x]
        stored[planes + x].start()
    for one in sides:
        one.start()
    for one in stored:
        one.wait()
    for one in sides:
        one.wait()
    passed.wait()


def forward_kernel(near, inner, _halo, _second, _third, _beyond, out, dummy):
    dummy[...] = jnp.zeros(dummy.shape, F32)
    count = near.shape[0]
    out[:count] = near[...]
    out[count] = inner[...]


def deposit_kernel(marks, cell, vol, drag, out, dummy):
    dummy[...] = jnp.zeros(dummy.shape, F32)
    tiles = cell.shape[0]
    sub = iota((SUB, BLOCK), 0)
    rows_c = iota((BLOCK, BLOCK), 0)
    even = sub % 2 == 0
    low_pair = sub % 4 < 2

    def step(group, carry):
        first = pl.multiple_of(group * SUB, SUB)
        slot = (first + sub) * BLOCK + iota((SUB, BLOCK), 1)
        live = slot < jnp.broadcast_to(marks[1:2, :], slot.shape)
        cells = cell[pl.ds(first, SUB), :]
        parts = halves_of(jnp.where(live, vol[pl.ds(first, SUB), :], 0.0)) + halves_of(
            jnp.where(live, drag[pl.ds(first, SUB), :], 0.0)
        )
        parts = [part.astype(F32) for part in parts]
        left = jnp.concatenate([jnp.where(even, part, 0.0) for part in parts], 0)
        right = jnp.concatenate([jnp.where(even, 0.0, part) for part in parts], 0)
        loads = jnp.concatenate([left, right], 1).astype(BF16)
        sums = [jnp.zeros((SUB, BLOCK), F32), jnp.zeros((SUB, BLOCK), F32)]
        for quad in range(SUB // 4):
            hot = [
                jnp.where(
                    rows_c == jnp.broadcast_to(cells[t : t + 1, :], (BLOCK, BLOCK)), 1.0, 0.0
                ).astype(BF16)
                for t in range(4 * quad, 4 * quad + 4)
            ]
            picked = jnp.concatenate(
                [jnp.concatenate(hot[:2], 1), jnp.concatenate(hot[2:], 1)], 0
            )
            placed = lax.dot_general(
                loads, picked, (((1,), (1,)), ((), ())), preferred_element_type=F32
            )
            for field in range(2):
                base = field * 2 * SUB
                total = placed[base : base + SUB] + placed[base + SUB : base + 2 * SUB]
                chosen = jnp.where(low_pair, total[:, :BLOCK], total[:, BLOCK:])
                sums[field] = jnp.where(sub // 4 == quad, chosen, sums[field])
        out[pl.ds(first, SUB), :BLOCK] = sums[0]
        out[pl.ds(first, SUB), BLOCK:] = sums[1]
        return carry

    lax.fori_loop(0, tiles // SUB, step, 0, unroll=4)
    out[tiles : tiles + SUB, :BLOCK] = jnp.broadcast_to(marks[:1, :].astype(F32), (SUB, BLOCK))
    out[tiles : tiles + SUB, BLOCK:] = jnp.zeros((SUB, BLOCK), F32)


def halo_kernel(pos, vel, lists, _, state, near, far, dummy):
    dummy[...] = jnp.zeros(dummy.shape, F32)
    tiles = pos.shape[1] // BLOCK
    rows = lists.shape[1] // BLOCK
    for tile in range(tiles):
        lanes = slice(tile * BLOCK, (tile + 1) * BLOCK)
        mixed = SPRING * pos[:, lanes] - DAMPING * vel[:, lanes]
        for axis in range(3):
            state[axis * tiles + tile : axis * tiles + tile + 1, :] = mixed[axis : axis + 1]
    turned = [
        jnp.concatenate(halves_of(jnp.transpose(state[axis * tiles : (axis + 1) * tiles, :])), 1)
        for axis in range(3)
    ]
    turned = jnp.concatenate(turned, 0)
    span = 2 * BLOCK
    row = iota((BLOCK, span), 0)

    odd = lax.axis_index("reg") % 2
    for away, out in enumerate((near, far)):
        side = 1 - odd if away == 0 else odd

        def step(part, carry):
            named = lists[:, pl.ds(pl.multiple_of(part * span, span), span)]
            named = jnp.where(side == 0, named[:1], named[1:])
            block = lax.shift_right_logical(named, 7)
            lane = named & (BLOCK - 1)
            hot = jnp.where(row == jnp.broadcast_to(block, row.shape), 1.0, 0.0).astype(BF16)
            found = jnp.dot(
                turned, jnp.concatenate([hot, hot], 0), preferred_element_type=F32
            )
            here = row == jnp.broadcast_to(lane, row.shape)
            for axis in range(3):
                value = jnp.where(here, found[axis * BLOCK : (axis + 1) * BLOCK], 0.0)
                value = jnp.sum(value, axis=0, keepdims=True)
                for half in range(2):
                    out[pl.ds(axis * rows + 2 * part + half, 1), :] = value[
                        :, half * BLOCK : (half + 1) * BLOCK
                    ]
            return carry

        lax.fori_loop(0, rows // 2, step, 0, unroll=8)


def message_kernel(mine, second, third, halo_near, halo_far, _, near, far, dummy):
    dummy[...] = jnp.zeros(dummy.shape, F32)
    stride = mine.shape[0]
    half = halo_near.shape[0] // 2
    rows = near.shape[0] - half
    for halo, out in ((halo_near, near), (halo_far, far)):
        for index, group in enumerate((mine, second, third)):
            out[index * stride : (index + 1) * stride, :] = group[...]
        out[rows:, :BLOCK] = halo[:half, :]
        out[rows:, BLOCK:] = halo[half:, :]


def contact_kernel(
    partner, state, message_near, message_far, halo_near, halo_far, named, stiff, vel, vol, drag,
    cell, weight, _, out, scale, extended
):
    tiles = state.shape[0] // 3
    rows = halo_near.shape[0] // 3
    blocks = tiles + 2 * rows
    base = message_near.shape[0] - 3 * rows // 2
    odd = lax.axis_index("reg") % 2
    sweeps = lax.axis_index("grp") % CORES == 0
    for axis in range(3):
        extended[axis * blocks : axis * blocks + tiles, :] = state[
            axis * tiles : (axis + 1) * tiles, :
        ]
    for message, halo, upper in (
        (message_near, halo_near, 1 - odd), (message_far, halo_far, odd)
    ):
        carried = jnp.concatenate([message[base:, :BLOCK], message[base:, BLOCK:]], 0)
        carried = jnp.where(sweeps, carried, halo[...])
        for axis in range(3):
            first = pl.multiple_of(axis * blocks + tiles + upper * rows, SUB)
            extended[pl.ds(first, rows), :] = carried[axis * rows : (axis + 1) * rows]

    def step(tile, carry):
        lanes = pl.ds(pl.multiple_of(tile * BLOCK, BLOCK), BLOCK)
        entry = named[:, lanes]
        weight = jnp.where(entry >= 0, stiff[:, lanes], 0.0)
        own = entry < BLOCK
        lane = entry & (BLOCK - 1)
        other = partner[tile]
        for axis in range(3):
            mine = jnp.broadcast_to(extended[pl.ds(axis * blocks + tile, 1), :], entry.shape)
            theirs = jnp.broadcast_to(extended[pl.ds(axis * blocks + other, 1), :], entry.shape)
            met = jnp.where(own, lanes_of(mine, lane), lanes_of(theirs, lane))
            pull = jnp.sum(weight * (mine - met), axis=0, keepdims=True)
            out[pl.ds(axis * tiles + tile, 1), :] = pull
        return carry

    lax.fori_loop(0, tiles, step, 0, unroll=4)
    volume = vol[...]
    push = TIME_STEP / volume
    scale[...] = push * (volume + drag[...] * lanes_of(weight[...], cell[...]))
    for axis in range(3):
        own = jnp.concatenate(
            [vel[axis : axis + 1, t * BLOCK : (t + 1) * BLOCK] for t in range(tiles)], 0
        )
        rows = slice(axis * tiles, (axis + 1) * tiles)
        out[rows, :] = own + push * (out[rows, :] - drag[...] * own)


def shifted(plane):
    height, width = plane.shape
    row = iota((SUB, width), 0)
    column = iota((height, BLOCK), 1)
    above, below = pltpu.roll(plane, 1, 0), pltpu.roll(plane, height - 1, 0)
    left, right = pltpu.roll(plane, 1, 1), pltpu.roll(plane, width - 1, 1)
    above = jnp.concatenate([jnp.where(row == 0, 0.0, above[:SUB]), above[SUB:]], 0)
    below = jnp.concatenate([below[:-SUB], jnp.where(row == SUB - 1, 0.0, below[-SUB:])], 0)
    left = jnp.concatenate([jnp.where(column == 0, 0.0, left[:, :BLOCK]), left[:, BLOCK:]], 1)
    right = jnp.concatenate(
        [right[:, :-BLOCK], jnp.where(column == BLOCK - 1, 0.0, right[:, -BLOCK:])], 1
    )
    return above, below, left, right


def inverse_of(value):
    near = pl.reciprocal(value, approx=True)
    return near * (2.0 - value * near)


def placed(groups, tiles):
    parts = [halves_of(group[:tiles, :]) for group in groups]
    loads = jnp.concatenate([part[i] for i in range(2) for part in parts], 0)
    ids = jnp.concatenate([group[tiles : tiles + 1, :BLOCK] for group in groups], 1)
    ids = ids.astype(jnp.int32)

    def gathered(wanted):
        hot = jnp.where(wanted == jnp.broadcast_to(ids, wanted.shape), 1.0, 0.0).astype(BF16)
        total = jnp.dot(
            jnp.concatenate([hot, hot], 1), loads, preferred_element_type=F32
        )
        return total[:, :BLOCK], total[:, BLOCK:]

    return ids, gathered


def driven_of(early, late, planes):
    return lambda x: early[planes + x] if x < HEAD else late[x - HEAD]


def coefficients(gathered, tiles, first, full, driven_at, constant, factor, turned, present):
    planes, height, width = constant.shape
    zones = width // BLOCK
    shape = (zones * height, 3 * tiles)
    line = iota(shape, 0)
    block = (line % height) * zones + line // height + first * zones

    for x in range(planes):
        solid, drag = gathered(block + x * (full * zones))
        at = x if turned is None else jnp.where(turned, planes - 1 - x, x)
        voids = 1.0 + solid
        scale = inverse_of(6.0 + (drag + 1.0) * voids)
        if present is not None:
            scale = jnp.where(present, scale, 0.0)
        inverse = voids * scale
        for zone in range(zones):
            lanes = slice(zone * BLOCK, (zone + 1) * BLOCK)
            rows = slice(zone * height, (zone + 1) * height)
            driving = driven_at(x)[:, lanes] + solid[rows]
            constant[at, :, lanes] = driving * inverse[rows]
            factor[at, :, lanes] = scale[rows]


def own_kernel(
    full, mine, second, third, early, late, _message, _near, _far, constant, factor, weight, picks
):
    tiles = weight.shape[0]
    planes, height, width = constant.shape
    place = Place(full, height)
    zones = width // BLOCK
    ids, gathered = placed((mine, second, third), tiles)
    coefficients(
        gathered, tiles, place.first, full, driven_of(early, late, planes), constant, factor,
        place.even, None,
    )
    turned = [
        jnp.transpose(
            jnp.broadcast_to(ids[:, i * tiles : (i + 1) * tiles], (BLOCK, tiles)).astype(F32)
        ).astype(jnp.int32)
        for i in range(3)
    ]
    solid, drag = gathered(jnp.concatenate([turned[0]] * 3, 1))
    weight[...] = 1.0 / (1.0 / (1.0 + solid) + drag)
    for i in range(3):
        block = turned[i]
        line, zone = block // zones, block % zones
        x, y = line // full, line % full
        row = (x * zones + zone) * height + y - place.first
        held = y // place.own_rows == jnp.where(place.sweeps, place.half, -1)
        row = jnp.concatenate([jnp.where(held, row, -1)] * (picks.shape[1] // BLOCK), 1)
        hot = jnp.where(row == iota(row.shape, 1), 1.0, 0.0).astype(BF16)
        picks[i * tiles : (i + 1) * tiles, :] = hot


def sweep(source, target, coefficient, start, stop):
    def plane(at, carry):
        above, below, left, right = shifted(source[at])
        around = source[at - 1] + source[at + 1] + above + below + left + right
        constant, factor = coefficient(at)
        target[at] = constant + factor * around
        return carry

    lax.fori_loop(start, stop, plane, 0, unroll=4)


def deposits_of(message, tiles):
    stride = tiles + SUB
    return placed([message.at[i * stride : (i + 1) * stride] for i in range(3)], tiles)[1]


def near_kernel(
    full, tiles, message, pressure, near, near_late, beyond, own_constant, own_factor, kept_even, kept_odd,
    constant, factor, old, new,
):
    planes, height, width = own_constant.shape
    place = Place(full, height)
    rim = planes + 1
    coefficients(
        deposits_of(message, tiles), tiles, place.first, full,
        driven_of(near, near_late, planes), constant, factor, place.even, jnp.where(place.odd, place.lower, place.upper),
    )
    old[0] = beyond[...]
    for x in range(planes):
        at = jnp.where(place.even, planes - 1 - x, x)
        old[1 + x] = near[at]
        old[rim + x] = pressure[at]
    buffers = (old, new)
    for index in range(planes):
        source, target = buffers[index % 2], buffers[(index + 1) % 2]
        sweep(source, target, lambda at: (constant[at - 1], factor[at - 1]), 1 + index, rim)
        sweep(
            source, target, lambda at: (own_constant[at - rim], own_factor[at - rim]),
            rim, 2 * planes - index,
        )
    kept_even[...] = old[planes : 2 * planes]
    kept_odd[...] = new[planes : 2 * planes]


def far_kernel(
    full, tiles, picks, message, pressure, far, far_late, own_constant, own_factor, kept_even, kept_odd,
    out_b, out_c, pieces, constant, factor, old, new, fields,
):
    planes, height, width = own_constant.shape
    zones = width // BLOCK
    place = Place(full, height)
    rim = planes + 1
    coefficients(
        deposits_of(message, tiles), tiles, place.first, full,
        driven_of(far, far_late, planes), constant, factor, place.even, jnp.where(place.odd, place.upper, place.lower),
    )
    old[planes : 2 * planes] = kept_even[...]
    new[planes : 2 * planes] = kept_odd[...]
    old[2 * planes] = pressure[jnp.where(place.even, 0, planes - 1)]
    for x in range(planes):
        at = jnp.where(place.even, planes - 1 - x, x)
        old[rim + planes + x] = far[at]
    old[rim + 2 * planes] = far[planes + HEAD]
    buffers = (old, new)
    edge = rim + planes
    for index in range(planes):
        source, target = buffers[index % 2], buffers[(index + 1) % 2]
        sweep(
            source, target, lambda at: (own_constant[at - rim], own_factor[at - rim]),
            2 * planes - index, edge,
        )
        sweep(
            source, target, lambda at: (constant[at - edge], factor[at - edge]),
            edge, edge + planes - index,
        )
    last = buffers[planes % 2]
    way = jnp.where(place.even, -0.5, 0.5)

    def gradient(x, carry):
        at = rim + x
        above, below, left, right = shifted(last[at])
        grads = (way * (last[at + 1] - last[at - 1]), 0.5 * (below - above), 0.5 * (right - left))
        line = jnp.where(place.even, planes - 1 - x, x) * zones
        for zone in range(zones):
            first = pl.multiple_of((line + zone) * height, SUB)
            for axis, grad in enumerate(grads):
                fields[pl.ds(first, height), axis * BLOCK : (axis + 1) * BLOCK] = (
                    grad[:, zone * BLOCK : (zone + 1) * BLOCK]
                )
        return carry

    lax.fori_loop(0, planes, gradient, 0, unroll=4)
    pieces[...] = jnp.concatenate(halves_of(fields[...]), 1)
    total = picked_rows(picks[tiles:, :], pieces)
    out_b[...] = total[:tiles]
    out_c[...] = total[tiles:]


def picked_rows(hot, pieces):
    total = jnp.dot(hot, pieces[...], preferred_element_type=F32)
    return total[:, : 3 * BLOCK] + total[:, 3 * BLOCK :]


def pick_kernel(picks, pieces, out):
    out[...] = picked_rows(picks[: out.shape[0], :], pieces)


def final_kernel(marks, grads_a, grads_b, grads_c, base, scale, cell, out):
    tiles = cell.shape[0]
    cells = cell[...]
    slot = iota(cells.shape, 0) * BLOCK + iota(cells.shape, 1)
    live = slot < jnp.broadcast_to(marks[1:2, :], slot.shape)
    for axis in range(3):
        lanes = slice(axis * BLOCK, (axis + 1) * BLOCK)
        gradient = lanes_of(grads_a[:, lanes] + grads_b[:, lanes] + grads_c[:, lanes], cells)
        new = base[axis * tiles : (axis + 1) * tiles, :] - gradient * scale[...]
        new = jnp.where(live, new, 0.0)
        for t in range(tiles):
            out[axis : axis + 1, t * BLOCK : (t + 1) * BLOCK] = new[t : t + 1, :]


def on_device(
    grain_pos,
    grain_vel,
    grain_vol,
    drag_coef,
    grain_count,
    contact_rows,
    contact_stiff,
    partner_block,
    halo_list,
    grain_cell,
    tile_cell_block,
    pressure_old,
    pressure_source,
    solid_old,
):
    groups, regions = lax.axis_size("grp"), lax.axis_size("reg")
    holding = groups - 1
    halves = groups // CORES
    slots = grain_pos.shape[1]
    tiles = slots // BLOCK
    planes, full, width = pressure_old.shape
    assert planes == ITERS
    own_rows = full // halves
    height = min(full, own_rows + SUB * min(2, halves - 1))
    owners = range(0, groups, CORES)
    holders = range(holding)

    def send(value, pairs):
        flat = [(a[0] * regions + a[1], b[0] * regions + b[1]) for a, b in pairs]
        return lax.ppermute(value, ("grp", "reg"), flat)

    def along_reg(value, members, goes, core=0):
        pairs = [
            ((g + core, r), (g, r + goes[r % 2]))
            for g in members
            for r in range(regions)
            if 0 <= r + goes[r % 2] < regions
        ]
        return send(value, pairs)

    def along_grp(value, step, members):
        pairs = [((g, r), ((g + step) % holding, r)) for g in members for r in range(regions)]
        return send(value, pairs)

    cell = grain_cell.reshape(tiles, BLOCK)
    vol = grain_vol.reshape(tiles, BLOCK)
    drag = drag_coef.reshape(tiles, BLOCK)
    ids = tile_cell_block.reshape(1, tiles)
    field_bytes = 4 * planes * height * width

    field = shaped(planes, height, width)
    plane = shaped(height, width)
    small = shaped(SUB, BLOCK)
    early, late, ends, inner, marks = call(
        window_kernel,
        (
            shaped(planes + HEAD, height, width), shaped(planes - HEAD, height, width), plane,
            plane, jax.ShapeDtypeStruct((2, BLOCK), jnp.int32),
        ),
        [HBM] * 5, (pressure_old, pressure_source, solid_old, ids, grain_count),
        [pltpu.VMEM((planes, height, width), F32)] * 3
        + [
            pltpu.VMEM((2, BLOCK), jnp.int32), pltpu.SMEM((1,), jnp.int32),
            pltpu.SemaphoreType.DMA((5 * planes + 5,)),
        ],
        flops=field_bytes, size=6 * field_bytes, limit=61_950_000, place=HBM,
    )
    near = along_reg(early, owners, (1, -1), core=1)
    near_late = along_reg(late, owners, (1, -1), core=1)
    beyond = along_reg(ends, owners, (-2, 2), core=1)
    mine, after_deposit = call(
        deposit_kernel, (shaped(tiles + SUB, 2 * BLOCK), small), [VMEM] * 4, (marks, cell, vol, drag), flops=2 * 32 * 48 * 65536, size=5 * 4 * slots,
    )
    second = along_grp(mine, 1, holders)
    third = along_grp(mine, 2, holders)
    rows = halo_list.shape[1] // BLOCK
    halo = shaped(3 * rows, BLOCK)
    state, halo_near, halo_far, after_halo = call(
        halo_kernel, (shaped(3 * tiles, BLOCK), halo, halo, small),
        [VMEM] * 4, (grain_pos, grain_vel, halo_list, after_deposit), flops=slots,
        size=4 * 4 * 3 * slots,
    )
    others = [g for g in holders if g not in owners]
    came_near = along_reg(halo_near, others, (1, -1))
    came_far = along_reg(halo_far, others, (-1, 1))
    far, after_forward = call(
        forward_kernel, (shaped(planes + HEAD + 1, height, width), small), [VMEM] * 6,
        (near, inner, after_halo, second, third, beyond), size=5 * field_bytes,
    )
    far = along_reg(far, owners, (2, -2))
    far_late = along_reg(near_late, owners, (2, -2))
    message = shaped(holding * (tiles + SUB) + 3 * rows // 2, 2 * BLOCK)
    message_near, message_far, after_message = call(
        message_kernel, (message, message, small), [VMEM] * 6,
        (mine, second, third, halo_near, halo_far, after_forward), size=8 * 2 * BLOCK * 500,
    )
    message_near = along_reg(message_near, owners, (1, -1))
    message_far = along_reg(message_far, owners, (-1, 1))
    constant, factor, weight, picks = call(
        functools.partial(own_kernel, full),
        (
            field, field, shaped(tiles, BLOCK),
            jax.ShapeDtypeStruct((3 * tiles, planes * height * width // BLOCK), BF16),
        ),
        [VMEM] * 8,
        (mine, second, third, early, late, after_message, came_near, came_far),
        flops=planes * height * 4 * 384 * 256 * 6, size=9 * field_bytes,
    )
    window_of = lambda count: pltpu.VMEM((count, height, width), F32)
    kept_even, kept_odd = call(
        functools.partial(near_kernel, full, tiles), (field, field), [VMEM] * 7,
        (message_near, early, near, near_late, beyond, constant, factor),
        [window_of(planes)] * 2 + [window_of(2 * planes + 1)] * 2,
        flops=planes * height * 4 * 384 * 256 * 6, size=9 * field_bytes,
    )
    grads = shaped(tiles, 3 * BLOCK)
    cells_held = planes * height * width // BLOCK
    grads_b, grads_c, pieces = call(
        functools.partial(far_kernel, full, tiles),
        (grads, grads, jax.ShapeDtypeStruct((cells_held, 6 * BLOCK), BF16)), [VMEM] * 9,
        (picks, message_far, early, far, far_late, constant, factor, kept_even, kept_odd),
        [window_of(planes)] * 2
        + [window_of(3 * planes + 2)] * 2
        + [pltpu.VMEM((planes * height * width // BLOCK, 3 * BLOCK), F32)],
        flops=planes * height * 4 * 384 * 256 * 6, size=9 * field_bytes,
    )
    grads_b = along_grp(grads_b, -1, owners)
    grads_c = along_grp(grads_c, -2, owners)
    grads_a = call(pick_kernel, grads, [VMEM] * 2, (picks, pieces), flops=slots, size=slots)

    base, scale = call(
        contact_kernel, (shaped(3 * tiles, BLOCK), shaped(tiles, BLOCK)),
        [SMEM] + [VMEM] * 12 + [ANY],
        (
            partner_block, state, message_near, message_far, came_near, came_far, contact_rows,
            contact_stiff, grain_vel, vol, drag, cell, weight, grads_a,
        ),
        [pltpu.VMEM((3 * (tiles + 2 * rows), BLOCK), F32)],
        flops=60 * 8 * slots, size=4 * 20 * slots,
    )
    return call(
        final_kernel, shaped(3, slots), [VMEM] * 7,
        (marks, grads_a, grads_b, grads_c, base, scale, cell),
        flops=60 * slots, size=4 * 20 * slots,
    )


def solution(mesh):
    in_specs = (
        P(None, ("grp", "reg")),
        P(None, ("grp", "reg")),
        P(("grp", "reg")),
        P(("grp", "reg")),
        P(("grp", "reg")),
        P(None, ("grp", "reg")),
        P(None, ("grp", "reg")),
        P(("grp", "reg")),
        P(None, ("grp", "reg")),
        P(("grp", "reg")),
        P(("grp", "reg")),
        P("reg", None, None),
        P("reg", None, None),
        P("reg", None, None),
    )
    out_specs = P(None, ("grp", "reg"))
    return jax.shard_map(
        on_device, mesh=mesh, in_specs=in_specs, out_specs=out_specs, check_vma=False
    )
```

```python
import functools

import jax
import jax.numpy as jnp
from jax import lax
from jax.experimental import pallas as pl
from jax.experimental.pallas import tpu as pltpu
from jax.sharding import PartitionSpec as P

BLOCK = 128
SUB = 8
CORES = 2
ITERS = 4
HEAD = 1
SPRING = 1.0
DAMPING = 0.5
TIME_STEP = 0.5

VMEM = pl.BlockSpec(memory_space=pltpu.VMEM)
SMEM = pl.BlockSpec(memory_space=pltpu.SMEM)
ANY = pl.BlockSpec(memory_space=pl.ANY)
HBM = pl.BlockSpec(memory_space=pltpu.HBM)
F32 = jnp.float32
BF16 = jnp.bfloat16


def iota(shape, dim):
    return lax.broadcasted_iota(jnp.int32, shape, dim)


def shaped(*dims):
    return jax.ShapeDtypeStruct(dims, F32)


def call(kernel, outs, specs, args, scratch=(), flops=0, size=0, limit=40_000_000, place=VMEM):
    return pl.pallas_call(
        kernel,
        out_shape=outs,
        in_specs=specs,
        out_specs=jax.tree.map(lambda _: place, outs),
        scratch_shapes=list(scratch),
        compiler_params=pltpu.CompilerParams(vmem_limit_bytes=limit),
        cost_estimate=pl.CostEstimate(flops=flops, bytes_accessed=size, transcendentals=0),
    )(*args)


class Place:
    def __init__(self, full, height):
        groups, regions = lax.axis_size("grp"), lax.axis_size("reg")
        self.group, region = lax.axis_index("grp"), lax.axis_index("reg")
        self.half = self.group // CORES
        self.own_rows = full // (groups // CORES)
        first = jnp.clip(self.half * self.own_rows - SUB, 0, full - height)
        self.first = pl.multiple_of(first, SUB)
        self.sweeps = self.group % CORES == 0
        self.parity = region % 2
        self.odd, self.even = self.parity == 1, self.parity == 0
        self.lower, self.upper = region > 0, region < regions - 1


def lanes_of(source, index):
    return jnp.take_along_axis(source, index, axis=1, mode="promise_in_bounds")


def halves_of(value):
    high = value.astype(BF16)
    return high, (value - high.astype(F32)).astype(BF16)


def window_kernel(
    pressure_old, source, solid_before, early, late, ends, inner, pressure, driven, solid, sems
):
    planes, height, _ = solid.shape
    place = Place(pressure_old.shape[1], height)
    rows = pl.ds(place.first, height)
    used = []

    def copy(whole, part):
        used.append(None)
        return pltpu.make_async_copy(whole, part, sems.at[len(used) - 1])

    fetched = [
        [copy(whole.at[x, rows, :], part.at[x]) for x in range(planes)]
        for whole, part in ((pressure_old, pressure), (source, driven), (solid_before, solid))
    ]
    stored = [copy(pressure.at[x], early.at[x]) for x in range(planes)]
    for x in range(planes):
        stored.append(copy(driven.at[x], early.at[planes + x] if x < HEAD else late.at[x - HEAD]))
    sides = (
        copy(pressure.at[place.parity * (planes - 1)], ends),
        copy(pressure.at[(1 - place.parity) * (planes - 1)], inner),
    )
    for x in range(planes):
        for part in fetched:
            part[x].start()
    for x in range(planes):
        fetched[0][x].wait()
        stored[x].start()
        fetched[1][x].wait()
        fetched[2][x].wait()
        driven[x] = driven[x] - solid[x]
        stored[planes + x].start()
    for one in sides:
        one.start()
    for one in stored:
        one.wait()
    for one in sides:
        one.wait()


def forward_kernel(near, inner, _halo, _second, _third, _beyond, out, dummy):
    dummy[...] = jnp.zeros(dummy.shape, F32)
    count = near.shape[0]
    out[:count] = near[...]
    out[count] = inner[...]


def deposit_kernel(count, cell, vol, drag, ids, out, dummy):
    dummy[...] = jnp.zeros(dummy.shape, F32)
    tiles = cell.shape[0]
    sub = iota((SUB, BLOCK), 0)
    rows_c = iota((BLOCK, BLOCK), 0)
    even = sub % 2 == 0
    low_pair = sub % 4 < 2

    def step(group, carry):
        first = pl.multiple_of(group * SUB, SUB)
        slot = (first + sub) * BLOCK + iota((SUB, BLOCK), 1)
        live = slot < count[0]
        cells = cell[pl.ds(first, SUB), :]
        parts = halves_of(jnp.where(live, vol[pl.ds(first, SUB), :], 0.0)) + halves_of(
            jnp.where(live, drag[pl.ds(first, SUB), :], 0.0)
        )
        parts = [part.astype(F32) for part in parts]
        left = jnp.concatenate([jnp.where(even, part, 0.0) for part in parts], 0)
        right = jnp.concatenate([jnp.where(even, 0.0, part) for part in parts], 0)
        loads = jnp.concatenate([left, right], 1).astype(BF16)
        sums = [jnp.zeros((SUB, BLOCK), F32), jnp.zeros((SUB, BLOCK), F32)]
        for quad in range(SUB // 4):
            hot = [
                jnp.where(
                    rows_c == jnp.broadcast_to(cells[t : t + 1, :], (BLOCK, BLOCK)), 1.0, 0.0
                ).astype(BF16)
                for t in range(4 * quad, 4 * quad + 4)
            ]
            picked = jnp.concatenate(
                [jnp.concatenate(hot[:2], 1), jnp.concatenate(hot[2:], 1)], 0
            )
            placed = lax.dot_general(
                loads, picked, (((1,), (1,)), ((), ())), preferred_element_type=F32
            )
            for field in range(2):
                base = field * 2 * SUB
                total = placed[base : base + SUB] + placed[base + SUB : base + 2 * SUB]
                chosen = jnp.where(low_pair, total[:, :BLOCK], total[:, BLOCK:])
                sums[field] = jnp.where(sub // 4 == quad, chosen, sums[field])
        out[pl.ds(first, SUB), :BLOCK] = sums[0]
        out[pl.ds(first, SUB), BLOCK:] = sums[1]
        return carry

    lax.fori_loop(0, tiles // SUB, step, 0, unroll=4)
    out[tiles : tiles + SUB, :BLOCK] = jnp.broadcast_to(ids[...].astype(F32), (SUB, BLOCK))
    out[tiles : tiles + SUB, BLOCK:] = jnp.zeros((SUB, BLOCK), F32)


def halo_kernel(pos, vel, lists, _, state, near, far, dummy):
    dummy[...] = jnp.zeros(dummy.shape, F32)
    tiles = pos.shape[1] // BLOCK
    rows = lists.shape[1] // BLOCK
    for tile in range(tiles):
        lanes = slice(tile * BLOCK, (tile + 1) * BLOCK)
        mixed = SPRING * pos[:, lanes] - DAMPING * vel[:, lanes]
        for axis in range(3):
            state[axis * tiles + tile : axis * tiles + tile + 1, :] = mixed[axis : axis + 1]
    turned = [
        jnp.concatenate(halves_of(jnp.transpose(state[axis * tiles : (axis + 1) * tiles, :])), 1)
        for axis in range(3)
    ]
    turned = jnp.concatenate(turned, 0)
    span = 2 * BLOCK
    row = iota((BLOCK, span), 0)

    odd = lax.axis_index("reg") % 2
    for away, out in enumerate((near, far)):
        side = 1 - odd if away == 0 else odd

        def step(part, carry):
            named = lists[:, pl.ds(pl.multiple_of(part * span, span), span)]
            named = jnp.where(side == 0, named[:1], named[1:])
            block = lax.shift_right_logical(named, 7)
            lane = named & (BLOCK - 1)
            hot = jnp.where(row == jnp.broadcast_to(block, row.shape), 1.0, 0.0).astype(BF16)
            found = jnp.dot(
                turned, jnp.concatenate([hot, hot], 0), preferred_element_type=F32
            )
            here = row == jnp.broadcast_to(lane, row.shape)
            for axis in range(3):
                value = jnp.where(here, found[axis * BLOCK : (axis + 1) * BLOCK], 0.0)
                value = jnp.sum(value, axis=0, keepdims=True)
                for half in range(2):
                    out[pl.ds(axis * rows + 2 * part + half, 1), :] = value[
                        :, half * BLOCK : (half + 1) * BLOCK
                    ]
            return carry

        lax.fori_loop(0, rows // 2, step, 0, unroll=8)


def message_kernel(mine, second, third, halo_near, halo_far, _, near, far, dummy):
    dummy[...] = jnp.zeros(dummy.shape, F32)
    stride = mine.shape[0]
    half = halo_near.shape[0] // 2
    rows = near.shape[0] - half
    for halo, out in ((halo_near, near), (halo_far, far)):
        for index, group in enumerate((mine, second, third)):
            out[index * stride : (index + 1) * stride, :] = group[...]
        out[rows:, :BLOCK] = halo[:half, :]
        out[rows:, BLOCK:] = halo[half:, :]


def inner_contact_kernel(state, named, stiff, _partner, _weight, out, dummy):
    dummy[...] = jnp.zeros(dummy.shape, F32)
    tiles = state.shape[0] // 3

    def step(tile, carry):
        lanes = pl.ds(pl.multiple_of(tile * BLOCK, BLOCK), BLOCK)
        entry = named[:, lanes]
        weight = jnp.where(entry >= 0, stiff[:, lanes], 0.0)
        own = entry < BLOCK
        lane = entry & (BLOCK - 1)
        for axis in range(3):
            row = pl.ds(axis * tiles + tile, 1)
            mine = jnp.broadcast_to(state[row, :], entry.shape)
            met = jnp.where(own, lanes_of(mine, lane), 0.0)
            out[row, :] = jnp.sum(weight * (mine - met), axis=0, keepdims=True)
        return carry

    lax.fori_loop(0, tiles, step, 0, unroll=4)


def contact_kernel(
    partner, state, message_near, message_far, halo_near, halo_far, named, stiff, inner, _, out,
    extended,
):
    tiles = state.shape[0] // 3
    rows = halo_near.shape[0] // 3
    blocks = tiles + 2 * rows
    base = message_near.shape[0] - 3 * rows // 2
    odd = lax.axis_index("reg") % 2
    sweeps = lax.axis_index("grp") % CORES == 0
    for axis in range(3):
        extended[axis * blocks : axis * blocks + tiles, :] = state[
            axis * tiles : (axis + 1) * tiles, :
        ]
    for message, halo, upper in (
        (message_near, halo_near, 1 - odd), (message_far, halo_far, odd)
    ):
        carried = jnp.concatenate([message[base:, :BLOCK], message[base:, BLOCK:]], 0)
        carried = jnp.where(sweeps, carried, halo[...])
        for axis in range(3):
            first = pl.multiple_of(axis * blocks + tiles + upper * rows, SUB)
            extended[pl.ds(first, rows), :] = carried[axis * rows : (axis + 1) * rows]

    def step(tile, carry):
        lanes = pl.ds(pl.multiple_of(tile * BLOCK, BLOCK), BLOCK)
        entry = named[:, lanes]
        weight = jnp.where(entry >= BLOCK, stiff[:, lanes], 0.0)
        lane = entry & (BLOCK - 1)
        other = partner[tile]
        for axis in range(3):
            theirs = jnp.broadcast_to(extended[pl.ds(axis * blocks + other, 1), :], entry.shape)
            pull = jnp.sum(weight * lanes_of(theirs, lane), axis=0, keepdims=True)
            row = pl.ds(axis * tiles + tile, 1)
            out[row, :] = inner[row, :] - pull
        return carry

    lax.fori_loop(0, tiles, step, 0, unroll=4)


def shifted(plane):
    height, width = plane.shape
    row = iota((SUB, width), 0)
    column = iota((height, BLOCK), 1)
    above, below = pltpu.roll(plane, 1, 0), pltpu.roll(plane, height - 1, 0)
    left, right = pltpu.roll(plane, 1, 1), pltpu.roll(plane, width - 1, 1)
    above = jnp.concatenate([jnp.where(row == 0, 0.0, above[:SUB]), above[SUB:]], 0)
    below = jnp.concatenate([below[:-SUB], jnp.where(row == SUB - 1, 0.0, below[-SUB:])], 0)
    left = jnp.concatenate([jnp.where(column == 0, 0.0, left[:, :BLOCK]), left[:, BLOCK:]], 1)
    right = jnp.concatenate(
        [right[:, :-BLOCK], jnp.where(column == BLOCK - 1, 0.0, right[:, -BLOCK:])], 1
    )
    return above, below, left, right


def inverse_of(value):
    near = pl.reciprocal(value, approx=True)
    return near * (2.0 - value * near)


def placed(groups, tiles):
    parts = [halves_of(group[:tiles, :]) for group in groups]
    loads = jnp.concatenate([part[i] for i in range(2) for part in parts], 0)
    ids = jnp.concatenate([group[tiles : tiles + 1, :BLOCK] for group in groups], 1)
    ids = ids.astype(jnp.int32)

    def gathered(wanted):
        hot = jnp.where(wanted == jnp.broadcast_to(ids, wanted.shape), 1.0, 0.0).astype(BF16)
        total = jnp.dot(
            jnp.concatenate([hot, hot], 1), loads, preferred_element_type=F32
        )
        return total[:, :BLOCK], total[:, BLOCK:]

    return ids, gathered


def driven_of(early, late, planes):
    return lambda x: early[planes + x] if x < HEAD else late[x - HEAD]


def coefficients(gathered, tiles, first, full, driven_at, constant, factor, turned, present):
    planes, height, width = constant.shape
    zones = width // BLOCK
    shape = (zones * height, 3 * tiles)
    line = iota(shape, 0)
    block = (line % height) * zones + line // height + first * zones

    for x in range(planes):
        solid, drag = gathered(block + x * (full * zones))
        at = x if turned is None else jnp.where(turned, planes - 1 - x, x)
        voids = 1.0 + solid
        scale = inverse_of(6.0 + (drag + 1.0) * voids)
        if present is not None:
            scale = jnp.where(present, scale, 0.0)
        inverse = voids * scale
        for zone in range(zones):
            lanes = slice(zone * BLOCK, (zone + 1) * BLOCK)
            rows = slice(zone * height, (zone + 1) * height)
            driving = driven_at(x)[:, lanes] + solid[rows]
            constant[at, :, lanes] = driving * inverse[rows]
            factor[at, :, lanes] = scale[rows]


def own_kernel(
    full, mine, second, third, early, late, _message, _near, _far, constant, factor, weight, picks
):
    tiles = weight.shape[0]
    planes, height, width = constant.shape
    place = Place(full, height)
    zones = width // BLOCK
    ids, gathered = placed((mine, second, third), tiles)
    coefficients(
        gathered, tiles, place.first, full, driven_of(early, late, planes), constant, factor,
        place.even, None,
    )
    turned = [
        jnp.transpose(
            jnp.broadcast_to(ids[:, i * tiles : (i + 1) * tiles], (BLOCK, tiles)).astype(F32)
        ).astype(jnp.int32)
        for i in range(3)
    ]
    solid, drag = gathered(jnp.concatenate([turned[0]] * 3, 1))
    weight[...] = 1.0 / (1.0 / (1.0 + solid) + drag)
    for i in range(3):
        block = turned[i]
        line, zone = block // zones, block % zones
        x, y = line // full, line % full
        row = (x * zones + zone) * height + y - place.first
        held = y // place.own_rows == jnp.where(place.sweeps, place.half, -1)
        row = jnp.concatenate([jnp.where(held, row, -1)] * (picks.shape[1] // BLOCK), 1)
        hot = jnp.where(row == iota(row.shape, 1), 1.0, 0.0).astype(BF16)
        picks[i * tiles : (i + 1) * tiles, :] = hot


def sweep(source, target, coefficient, start, stop):
    def plane(at, carry):
        above, below, left, right = shifted(source[at])
        around = source[at - 1] + source[at + 1] + above + below + left + right
        constant, factor = coefficient(at)
        target[at] = constant + factor * around
        return carry

    lax.fori_loop(start, stop, plane, 0, unroll=4)


def deposits_of(message, tiles):
    stride = tiles + SUB
    return placed([message.at[i * stride : (i + 1) * stride] for i in range(3)], tiles)[1]


def near_kernel(
    full, tiles, message, pressure, near, near_late, beyond, own_constant, own_factor, _inner,
    kept_even, kept_odd,
    constant, factor, old, new,
):
    planes, height, width = own_constant.shape
    place = Place(full, height)
    rim = planes + 1
    coefficients(
        deposits_of(message, tiles), tiles, place.first, full,
        driven_of(near, near_late, planes), constant, factor, place.even, jnp.where(place.odd, place.lower, place.upper),
    )
    old[0] = beyond[...]
    for x in range(planes):
        at = jnp.where(place.even, planes - 1 - x, x)
        old[1 + x] = near[at]
        old[rim + x] = pressure[at]
    buffers = (old, new)
    for index in range(planes):
        source, target = buffers[index % 2], buffers[(index + 1) % 2]
        sweep(source, target, lambda at: (constant[at - 1], factor[at - 1]), 1 + index, rim)
        sweep(
            source, target, lambda at: (own_constant[at - rim], own_factor[at - rim]),
            rim, 2 * planes - index,
        )
    kept_even[...] = old[planes : 2 * planes]
    kept_odd[...] = new[planes : 2 * planes]


def far_kernel(
    full, tiles, picks, message, pressure, far, far_late, own_constant, own_factor, kept_even, kept_odd,
    out, pieces, constant, factor, old, new, fields,
):
    planes, height, width = own_constant.shape
    zones = width // BLOCK
    place = Place(full, height)
    rim = planes + 1
    coefficients(
        deposits_of(message, tiles), tiles, place.first, full,
        driven_of(far, far_late, planes), constant, factor, place.even, jnp.where(place.odd, place.upper, place.lower),
    )
    old[planes : 2 * planes] = kept_even[...]
    new[planes : 2 * planes] = kept_odd[...]
    old[2 * planes] = pressure[jnp.where(place.even, 0, planes - 1)]
    for x in range(planes):
        at = jnp.where(place.even, planes - 1 - x, x)
        old[rim + planes + x] = far[at]
    old[rim + 2 * planes] = far[planes + HEAD]
    buffers = (old, new)
    edge = rim + planes
    for index in range(planes):
        source, target = buffers[index % 2], buffers[(index + 1) % 2]
        sweep(
            source, target, lambda at: (own_constant[at - rim], own_factor[at - rim]),
            2 * planes - index, edge,
        )
        sweep(
            source, target, lambda at: (constant[at - edge], factor[at - edge]),
            edge, edge + planes - index,
        )
    last = buffers[planes % 2]
    way = jnp.where(place.even, -0.5, 0.5)

    def gradient(x, carry):
        at = rim + x
        above, below, left, right = shifted(last[at])
        grads = (way * (last[at + 1] - last[at - 1]), 0.5 * (below - above), 0.5 * (right - left))
        line = jnp.where(place.even, planes - 1 - x, x) * zones
        for zone in range(zones):
            first = pl.multiple_of((line + zone) * height, SUB)
            for axis, grad in enumerate(grads):
                fields[pl.ds(first, height), axis * BLOCK : (axis + 1) * BLOCK] = (
                    grad[:, zone * BLOCK : (zone + 1) * BLOCK]
                )
        return carry

    lax.fori_loop(0, planes, gradient, 0, unroll=4)
    pieces[...] = jnp.concatenate(halves_of(fields[...]), 1)
    out[...] = picked_rows(picks[tiles : 2 * tiles, :], pieces)


def picked_rows(hot, pieces):
    total = jnp.dot(hot, pieces[...], preferred_element_type=F32)
    return total[:, : 3 * BLOCK] + total[:, 3 * BLOCK :]


def pick_kernel(place, picks, pieces, _, out):
    tiles = out.shape[0]
    out[...] = picked_rows(picks[place * tiles : (place + 1) * tiles, :], pieces)


def final_kernel(
    count, grads_a, grads_b, grads_c, weight, contact, vel, vol, drag, cell, out,
):
    tiles = cell.shape[0]
    cells = cell[...]
    heft = lanes_of(weight[...], cells)
    slot = iota(cells.shape, 0) * BLOCK + iota(cells.shape, 1)
    live = slot < count[0]
    volume = vol[...]
    push = TIME_STEP / volume
    for axis in range(3):
        lanes = slice(axis * BLOCK, (axis + 1) * BLOCK)
        gradient = lanes_of(grads_a[:, lanes] + grads_b[:, lanes] + grads_c[:, lanes], cells)
        own = jnp.concatenate(
            [vel[axis : axis + 1, t * BLOCK : (t + 1) * BLOCK] for t in range(tiles)], 0
        )
        fluid = -gradient * heft
        force = contact[axis * tiles : (axis + 1) * tiles, :] - volume * gradient
        force = force + drag[...] * (fluid - own)
        new = jnp.where(live, own + force * push, 0.0)
        for t in range(tiles):
            out[axis : axis + 1, t * BLOCK : (t + 1) * BLOCK] = new[t : t + 1, :]


def on_device(
    grain_pos,
    grain_vel,
    grain_vol,
    drag_coef,
    grain_count,
    contact_rows,
    contact_stiff,
    partner_block,
    halo_list,
    grain_cell,
    tile_cell_block,
    pressure_old,
    pressure_source,
    solid_old,
):
    groups, regions = lax.axis_size("grp"), lax.axis_size("reg")
    holding = groups - 1
    halves = groups // CORES
    slots = grain_pos.shape[1]
    tiles = slots // BLOCK
    planes, full, width = pressure_old.shape
    assert planes == ITERS
    own_rows = full // halves
    height = min(full, own_rows + SUB * min(2, halves - 1))
    owners = range(0, groups, CORES)
    holders = range(holding)

    def send(value, pairs):
        flat = [(a[0] * regions + a[1], b[0] * regions + b[1]) for a, b in pairs]
        return lax.ppermute(value, ("grp", "reg"), flat)

    def along_reg(value, members, goes, core=0):
        pairs = [
            ((g + core, r), (g, r + goes[r % 2]))
            for g in members
            for r in range(regions)
            if 0 <= r + goes[r % 2] < regions
        ]
        return send(value, pairs)

    def along_grp(value, step, members):
        pairs = [((g, r), ((g + step) % holding, r)) for g in members for r in range(regions)]
        return send(value, pairs)

    count = grain_count
    cell = grain_cell.reshape(tiles, BLOCK)
    vol = grain_vol.reshape(tiles, BLOCK)
    drag = drag_coef.reshape(tiles, BLOCK)
    ids = tile_cell_block.reshape(1, tiles)
    field_bytes = 4 * planes * height * width

    field = shaped(planes, height, width)
    plane = shaped(height, width)
    small = shaped(SUB, BLOCK)
    early, late, ends, inner = call(
        window_kernel,
        (
            shaped(planes + HEAD, height, width), shaped(planes - HEAD, height, width), plane,
            plane,
        ),
        [HBM] * 3, (pressure_old, pressure_source, solid_old),
        [pltpu.VMEM((planes, height, width), F32)] * 3
        + [pltpu.SemaphoreType.DMA((5 * planes + 2,))],
        flops=field_bytes, size=6 * field_bytes, limit=61_950_000, place=HBM,
    )
    near = along_reg(early, owners, (1, -1), core=1)
    near_late = along_reg(late, owners, (1, -1), core=1)
    beyond = along_reg(ends, owners, (-2, 2), core=1)
    mine, after_deposit = call(
        deposit_kernel, (shaped(tiles + SUB, 2 * BLOCK), small), [SMEM] + [VMEM] * 4,
        (count, cell, vol, drag, ids), flops=2 * 32 * 48 * 65536, size=5 * 4 * slots,
    )
    second = along_grp(mine, 1, holders)
    third = along_grp(mine, 2, holders)
    rows = halo_list.shape[1] // BLOCK
    halo = shaped(3 * rows, BLOCK)
    state, halo_near, halo_far, after_halo = call(
        halo_kernel, (shaped(3 * tiles, BLOCK), halo, halo, small),
        [VMEM] * 4, (grain_pos, grain_vel, halo_list, after_deposit), flops=slots,
        size=4 * 4 * 3 * slots,
    )
    others = [g for g in holders if g not in owners]
    came_near = along_reg(halo_near, others, (1, -1))
    came_far = along_reg(halo_far, others, (-1, 1))
    far, after_forward = call(
        forward_kernel, (shaped(planes + HEAD + 1, height, width), small), [VMEM] * 6,
        (near, inner, after_halo, second, third, beyond), size=5 * field_bytes,
    )
    far = along_reg(far, owners, (2, -2))
    far_late = along_reg(near_late, owners, (2, -2))
    message = shaped(holding * (tiles + SUB) + 3 * rows // 2, 2 * BLOCK)
    message_near, message_far, after_message = call(
        message_kernel, (message, message, small), [VMEM] * 6,
        (mine, second, third, halo_near, halo_far, after_forward), size=8 * 2 * BLOCK * 500,
    )
    message_near = along_reg(message_near, owners, (1, -1))
    message_far = along_reg(message_far, owners, (-1, 1))
    constant, factor, weight, picks = call(
        functools.partial(own_kernel, full),
        (
            field, field, shaped(tiles, BLOCK),
            jax.ShapeDtypeStruct((3 * tiles, planes * height * width // BLOCK), BF16),
        ),
        [VMEM] * 8,
        (mine, second, third, early, late, after_message, came_near, came_far),
        flops=planes * height * 4 * 384 * 256 * 6, size=9 * field_bytes,
    )
    inner_contact, after_inner = call(
        inner_contact_kernel, (shaped(3 * tiles, BLOCK), small), [VMEM] * 3 + [SMEM, VMEM],
        (state, contact_rows, contact_stiff, partner_block, weight),
        flops=60 * 8 * slots, size=4 * 20 * slots,
    )
    window_of = lambda count: pltpu.VMEM((count, height, width), F32)
    kept_even, kept_odd = call(
        functools.partial(near_kernel, full, tiles), (field, field), [VMEM] * 8,
        (message_near, early, near, near_late, beyond, constant, factor, after_inner),
        [window_of(planes)] * 2 + [window_of(2 * planes + 1)] * 2,
        flops=planes * height * 4 * 384 * 256 * 6, size=9 * field_bytes,
    )
    grads = shaped(tiles, 3 * BLOCK)
    cells_held = planes * height * width // BLOCK
    grads_b, pieces = call(
        functools.partial(far_kernel, full, tiles),
        (grads, jax.ShapeDtypeStruct((cells_held, 6 * BLOCK), BF16)), [VMEM] * 9,
        (picks, message_far, early, far, far_late, constant, factor, kept_even, kept_odd),
        [window_of(planes)] * 2
        + [window_of(3 * planes + 2)] * 2
        + [pltpu.VMEM((cells_held, 3 * BLOCK), F32)],
        flops=planes * height * 4 * 384 * 256 * 6, size=9 * field_bytes,
    )
    came_b = along_grp(grads_b, -1, owners)
    pick = lambda place, after: call(
        functools.partial(pick_kernel, place), grads, [VMEM] * 3, (picks, pieces, after),
        flops=slots, size=slots,
    )
    grads_c = pick(2, after_inner)
    grads_a = pick(0, after_inner)
    came_c = along_grp(grads_c, -2, owners)
    contact = call(
        contact_kernel, shaped(3 * tiles, BLOCK), [SMEM] + [VMEM] * 8 + [ANY],
        (
            partner_block, state, message_near, message_far, came_near, came_far, contact_rows,
            contact_stiff, inner_contact, grads_a,
        ),
        [pltpu.VMEM((3 * (tiles + 2 * rows), BLOCK), F32)],
        flops=60 * 8 * slots, size=4 * 20 * slots,
    )
    return call(
        final_kernel, shaped(3, slots), [SMEM] + [VMEM] * 9,
        (count, grads_a, came_c, came_b, weight, contact, grain_vel, vol, drag, cell),
        flops=60 * slots, size=4 * 20 * slots,
    )


def solution(mesh):
    in_specs = (
        P(None, ("grp", "reg")),
        P(None, ("grp", "reg")),
        P(("grp", "reg")),
        P(("grp", "reg")),
        P(("grp", "reg")),
        P(None, ("grp", "reg")),
        P(None, ("grp", "reg")),
        P(("grp", "reg")),
        P(None, ("grp", "reg")),
        P(("grp", "reg")),
        P(("grp", "reg")),
        P("reg", None, None),
        P("reg", None, None),
        P("reg", None, None),
    )
    out_specs = P(None, ("grp", "reg"))
    return jax.shard_map(
        on_device, mesh=mesh, in_specs=in_specs, out_specs=out_specs, check_vma=False
    )
```

```python
import functools

import jax
import jax.numpy as jnp
from jax import lax
from jax.experimental import pallas as pl
from jax.experimental.pallas import tpu as pltpu
from jax.sharding import PartitionSpec as P

BLOCK = 128
SUB = 8
CORES = 2
ITERS = 4
HEAD = 1
SPRING = 1.0
DAMPING = 0.5
TIME_STEP = 0.5

VMEM = pl.BlockSpec(memory_space=pltpu.VMEM)
SMEM = pl.BlockSpec(memory_space=pltpu.SMEM)
ANY = pl.BlockSpec(memory_space=pl.ANY)
HBM = pl.BlockSpec(memory_space=pltpu.HBM)
F32 = jnp.float32
BF16 = jnp.bfloat16


def iota(shape, dim):
    return lax.broadcasted_iota(jnp.int32, shape, dim)


def shaped(*dims):
    return jax.ShapeDtypeStruct(dims, F32)


def call(kernel, outs, specs, args, scratch=(), flops=0, size=0, limit=40_000_000, place=VMEM):
    return pl.pallas_call(
        kernel,
        out_shape=outs,
        in_specs=specs,
        out_specs=jax.tree.map(lambda _: place, outs),
        scratch_shapes=list(scratch),
        compiler_params=pltpu.CompilerParams(vmem_limit_bytes=limit),
        cost_estimate=pl.CostEstimate(flops=flops, bytes_accessed=size, transcendentals=0),
    )(*args)


class Place:
    def __init__(self, full, height):
        groups, regions = lax.axis_size("grp"), lax.axis_size("reg")
        self.group, region = lax.axis_index("grp"), lax.axis_index("reg")
        self.half = self.group // CORES
        self.own_rows = full // (groups // CORES)
        first = jnp.clip(self.half * self.own_rows - SUB, 0, full - height)
        self.first = pl.multiple_of(first, SUB)
        self.sweeps = self.group % CORES == 0
        self.parity = region % 2
        self.odd, self.even = self.parity == 1, self.parity == 0
        self.lower, self.upper = region > 0, region < regions - 1


def lanes_of(source, index):
    return jnp.take_along_axis(source, index, axis=1, mode="promise_in_bounds")


def halves_of(value):
    high = value.astype(BF16)
    return high, (value - high.astype(F32)).astype(BF16)


def window_kernel(
    pressure_old, source, solid_before, early, late, ends, inner, pressure, driven, solid, sems
):
    planes, height, _ = solid.shape
    place = Place(pressure_old.shape[1], height)
    rows = pl.ds(place.first, height)
    used = []

    def copy(whole, part):
        used.append(None)
        return pltpu.make_async_copy(whole, part, sems.at[len(used) - 1])

    fetched = [
        [copy(whole.at[x, rows, :], part.at[x]) for x in range(planes)]
        for whole, part in ((pressure_old, pressure), (source, driven), (solid_before, solid))
    ]
    stored = [copy(pressure.at[x], early.at[x]) for x in range(planes)]
    for x in range(planes):
        stored.append(copy(driven.at[x], early.at[planes + x] if x < HEAD else late.at[x - HEAD]))
    sides = (
        copy(pressure.at[place.parity * (planes - 1)], ends),
        copy(pressure.at[(1 - place.parity) * (planes - 1)], inner),
    )
    for x in range(planes):
        for part in fetched:
            part[x].start()
    for x in range(planes):
        fetched[0][x].wait()
        stored[x].start()
        fetched[1][x].wait()
        fetched[2][x].wait()
        driven[x] = driven[x] - solid[x]
        stored[planes + x].start()
    for one in sides:
        one.start()
    for one in stored:
        one.wait()
    for one in sides:
        one.wait()


def forward_kernel(near, inner, _halo, _second, _third, _beyond, out, dummy):
    dummy[...] = jnp.zeros(dummy.shape, F32)
    count = near.shape[0]
    out[:count] = near[...]
    out[count] = inner[...]


def deposit_kernel(count, cell, vol, drag, ids, out, dummy):
    dummy[...] = jnp.zeros(dummy.shape, F32)
    tiles = cell.shape[0]
    sub = iota((SUB, BLOCK), 0)
    rows_c = iota((BLOCK, BLOCK), 0)
    even = sub % 2 == 0
    low_pair = sub % 4 < 2

    def step(group, carry):
        first = pl.multiple_of(group * SUB, SUB)
        slot = (first + sub) * BLOCK + iota((SUB, BLOCK), 1)
        live = slot < count[0]
        cells = cell[pl.ds(first, SUB), :]
        parts = halves_of(jnp.where(live, vol[pl.ds(first, SUB), :], 0.0)) + halves_of(
            jnp.where(live, drag[pl.ds(first, SUB), :], 0.0)
        )
        parts = [part.astype(F32) for part in parts]
        left = jnp.concatenate([jnp.where(even, part, 0.0) for part in parts], 0)
        right = jnp.concatenate([jnp.where(even, 0.0, part) for part in parts], 0)
        loads = jnp.concatenate([left, right], 1).astype(BF16)
        sums = [jnp.zeros((SUB, BLOCK), F32), jnp.zeros((SUB, BLOCK), F32)]
        for quad in range(SUB // 4):
            hot = [
                jnp.where(
                    rows_c == jnp.broadcast_to(cells[t : t + 1, :], (BLOCK, BLOCK)), 1.0, 0.0
                ).astype(BF16)
                for t in range(4 * quad, 4 * quad + 4)
            ]
            picked = jnp.concatenate(
                [jnp.concatenate(hot[:2], 1), jnp.concatenate(hot[2:], 1)], 0
            )
            placed = lax.dot_general(
                loads, picked, (((1,), (1,)), ((), ())), preferred_element_type=F32
            )
            for field in range(2):
                base = field * 2 * SUB
                total = placed[base : base + SUB] + placed[base + SUB : base + 2 * SUB]
                chosen = jnp.where(low_pair, total[:, :BLOCK], total[:, BLOCK:])
                sums[field] = jnp.where(sub // 4 == quad, chosen, sums[field])
        out[pl.ds(first, SUB), :BLOCK] = sums[0]
        out[pl.ds(first, SUB), BLOCK:] = sums[1]
        return carry

    lax.fori_loop(0, tiles // SUB, step, 0, unroll=4)
    out[tiles : tiles + SUB, :BLOCK] = jnp.broadcast_to(ids[...].astype(F32), (SUB, BLOCK))
    out[tiles : tiles + SUB, BLOCK:] = jnp.zeros((SUB, BLOCK), F32)


def halo_kernel(pos, vel, lists, _, state, near, far, dummy):
    dummy[...] = jnp.zeros(dummy.shape, F32)
    tiles = pos.shape[1] // BLOCK
    rows = lists.shape[1] // BLOCK
    for tile in range(tiles):
        lanes = slice(tile * BLOCK, (tile + 1) * BLOCK)
        mixed = SPRING * pos[:, lanes] - DAMPING * vel[:, lanes]
        for axis in range(3):
            state[axis * tiles + tile : axis * tiles + tile + 1, :] = mixed[axis : axis + 1]
    turned = [
        jnp.concatenate(halves_of(jnp.transpose(state[axis * tiles : (axis + 1) * tiles, :])), 1)
        for axis in range(3)
    ]
    turned = jnp.concatenate(turned, 0)
    span = 2 * BLOCK
    row = iota((BLOCK, span), 0)

    odd = lax.axis_index("reg") % 2
    for away, out in enumerate((near, far)):
        side = 1 - odd if away == 0 else odd

        def step(part, carry):
            named = lists[:, pl.ds(pl.multiple_of(part * span, span), span)]
            named = jnp.where(side == 0, named[:1], named[1:])
            block = lax.shift_right_logical(named, 7)
            lane = named & (BLOCK - 1)
            hot = jnp.where(row == jnp.broadcast_to(block, row.shape), 1.0, 0.0).astype(BF16)
            found = jnp.dot(
                turned, jnp.concatenate([hot, hot], 0), preferred_element_type=F32
            )
            here = row == jnp.broadcast_to(lane, row.shape)
            for axis in range(3):
                value = jnp.where(here, found[axis * BLOCK : (axis + 1) * BLOCK], 0.0)
                value = jnp.sum(value, axis=0, keepdims=True)
                for half in range(2):
                    out[pl.ds(axis * rows + 2 * part + half, 1), :] = value[
                        :, half * BLOCK : (half + 1) * BLOCK
                    ]
            return carry

        lax.fori_loop(0, rows // 2, step, 0, unroll=8)


def message_kernel(mine, second, third, halo_near, halo_far, _, near, far, dummy):
    dummy[...] = jnp.zeros(dummy.shape, F32)
    stride = mine.shape[0]
    half = halo_near.shape[0] // 2
    rows = near.shape[0] - half
    for halo, out in ((halo_near, near), (halo_far, far)):
        for index, group in enumerate((mine, second, third)):
            out[index * stride : (index + 1) * stride, :] = group[...]
        out[rows:, :BLOCK] = halo[:half, :]
        out[rows:, BLOCK:] = halo[half:, :]


def merged(parts):
    sub = iota((SUB, BLOCK), 0)
    for step in (4, 2, 1):
        low = (sub & step) == 0
        paired = []
        for first, second in zip(parts[:step], parts[step:]):
            away = jnp.where(low, second, first)
            back = pltpu.roll(away, step, 0)
            if step < SUB // 2:
                back = jnp.where(low, pltpu.roll(away, SUB - step, 0), back)
            paired.append(jnp.where(low, first, second) + back)
        parts = paired
    return parts[0]


def contact_kernel(
    partner, state, message_near, message_far, halo_near, halo_far, named, stiff, _, out, extended,
):
    tiles = state.shape[0] // 3
    rows = halo_near.shape[0] // 3
    blocks = tiles + 2 * rows
    base = message_near.shape[0] - 3 * rows // 2
    odd = lax.axis_index("reg") % 2
    sweeps = lax.axis_index("grp") % CORES == 0
    for axis in range(3):
        extended[axis * blocks : axis * blocks + tiles, :] = state[
            axis * tiles : (axis + 1) * tiles, :
        ]
    for message, halo, upper in (
        (message_near, halo_near, 1 - odd), (message_far, halo_far, odd)
    ):
        carried = jnp.concatenate([message[base:, :BLOCK], message[base:, BLOCK:]], 0)
        carried = jnp.where(sweeps, carried, halo[...])
        for axis in range(3):
            first = pl.multiple_of(axis * blocks + tiles + upper * rows, SUB)
            extended[pl.ds(first, rows), :] = carried[axis * rows : (axis + 1) * rows]

    def step(group, carry):
        first = pl.multiple_of(group * SUB, SUB)
        held = [extended[pl.ds(axis * blocks + first, SUB), :] for axis in range(3)]
        pulls = [[], [], []]
        for t in range(SUB):
            lanes = pl.ds(pl.multiple_of((first + t) * BLOCK, BLOCK), BLOCK)
            entry = named[:, lanes]
            weight = jnp.where(entry >= 0, stiff[:, lanes], 0.0)
            own = entry < BLOCK
            lane = entry & (BLOCK - 1)
            other = partner[first + t]
            for axis in range(3):
                mine = jnp.broadcast_to(held[axis][t : t + 1], entry.shape)
                theirs = extended[pl.ds(axis * blocks + other, 1), :]
                theirs = jnp.broadcast_to(theirs, entry.shape)
                met = jnp.where(own, lanes_of(mine, lane), lanes_of(theirs, lane))
                pulls[axis].append(weight * (mine - met))
        for axis in range(3):
            out[pl.ds(axis * tiles + first, SUB), :] = merged(pulls[axis])
        return carry

    lax.fori_loop(0, tiles // SUB, step, 0)


def shifted(plane):
    height, width = plane.shape
    row = iota((SUB, width), 0)
    column = iota((height, BLOCK), 1)
    above, below = pltpu.roll(plane, 1, 0), pltpu.roll(plane, height - 1, 0)
    left, right = pltpu.roll(plane, 1, 1), pltpu.roll(plane, width - 1, 1)
    above = jnp.concatenate([jnp.where(row == 0, 0.0, above[:SUB]), above[SUB:]], 0)
    below = jnp.concatenate([below[:-SUB], jnp.where(row == SUB - 1, 0.0, below[-SUB:])], 0)
    left = jnp.concatenate([jnp.where(column == 0, 0.0, left[:, :BLOCK]), left[:, BLOCK:]], 1)
    right = jnp.concatenate(
        [right[:, :-BLOCK], jnp.where(column == BLOCK - 1, 0.0, right[:, -BLOCK:])], 1
    )
    return above, below, left, right


def inverse_of(value):
    near = pl.reciprocal(value, approx=True)
    return near * (2.0 - value * near)


def placed(groups, tiles):
    parts = [halves_of(group[:tiles, :]) for group in groups]
    loads = jnp.concatenate([part[i] for i in range(2) for part in parts], 0)
    ids = jnp.concatenate([group[tiles : tiles + 1, :BLOCK] for group in groups], 1)
    ids = ids.astype(jnp.int32)

    def gathered(wanted):
        hot = jnp.where(wanted == jnp.broadcast_to(ids, wanted.shape), 1.0, 0.0).astype(BF16)
        total = jnp.dot(
            jnp.concatenate([hot, hot], 1), loads, preferred_element_type=F32
        )
        return total[:, :BLOCK], total[:, BLOCK:]

    return ids, gathered


def driven_of(early, late, planes):
    return lambda x: early[planes + x] if x < HEAD else late[x - HEAD]


def coefficients(gathered, tiles, first, full, driven_at, constant, factor, turned, present):
    planes, height, width = constant.shape
    zones = width // BLOCK
    shape = (zones * height, 3 * tiles)
    line = iota(shape, 0)
    block = (line % height) * zones + line // height + first * zones

    for x in range(planes):
        solid, drag = gathered(block + x * (full * zones))
        at = x if turned is None else jnp.where(turned, planes - 1 - x, x)
        voids = 1.0 + solid
        scale = inverse_of(6.0 + (drag + 1.0) * voids)
        if present is not None:
            scale = jnp.where(present, scale, 0.0)
        inverse = voids * scale
        for zone in range(zones):
            lanes = slice(zone * BLOCK, (zone + 1) * BLOCK)
            rows = slice(zone * height, (zone + 1) * height)
            driving = driven_at(x)[:, lanes] + solid[rows]
            constant[at, :, lanes] = driving * inverse[rows]
            factor[at, :, lanes] = scale[rows]


def own_kernel(
    full, mine, second, third, early, late, _message, _near, _far, _partner, constant, factor, weight, picks
):
    tiles = weight.shape[0]
    planes, height, width = constant.shape
    place = Place(full, height)
    zones = width // BLOCK
    ids, gathered = placed((mine, second, third), tiles)
    coefficients(
        gathered, tiles, place.first, full, driven_of(early, late, planes), constant, factor,
        place.even, None,
    )
    turned = [
        jnp.transpose(
            jnp.broadcast_to(ids[:, i * tiles : (i + 1) * tiles], (BLOCK, tiles)).astype(F32)
        ).astype(jnp.int32)
        for i in range(3)
    ]
    solid, drag = gathered(jnp.concatenate([turned[0]] * 3, 1))
    weight[...] = 1.0 / (1.0 / (1.0 + solid) + drag)
    for i in range(3):
        block = turned[i]
        line, zone = block // zones, block % zones
        x, y = line // full, line % full
        row = (x * zones + zone) * height + y - place.first
        held = y // place.own_rows == jnp.where(place.sweeps, place.half, -1)
        row = jnp.concatenate([jnp.where(held, row, -1)] * (picks.shape[1] // BLOCK), 1)
        hot = jnp.where(row == iota(row.shape, 1), 1.0, 0.0).astype(BF16)
        picks[i * tiles : (i + 1) * tiles, :] = hot


def sweep(source, target, coefficient, start, stop):
    def plane(at, carry):
        above, below, left, right = shifted(source[at])
        around = source[at - 1] + source[at + 1] + above + below + left + right
        constant, factor = coefficient(at)
        target[at] = constant + factor * around
        return carry

    lax.fori_loop(start, stop, plane, 0, unroll=4)


def deposits_of(message, tiles):
    stride = tiles + SUB
    return placed([message.at[i * stride : (i + 1) * stride] for i in range(3)], tiles)[1]


def near_kernel(
    full, tiles, message, pressure, near, near_late, beyond, own_constant, own_factor, kept_even, kept_odd, constant, factor, old, new,
):
    planes, height, width = own_constant.shape
    place = Place(full, height)
    rim = planes + 1
    coefficients(
        deposits_of(message, tiles), tiles, place.first, full,
        driven_of(near, near_late, planes), constant, factor, place.even, jnp.where(place.odd, place.lower, place.upper),
    )
    old[0] = beyond[...]
    for x in range(planes):
        at = jnp.where(place.even, planes - 1 - x, x)
        old[1 + x] = near[at]
        old[rim + x] = pressure[at]
    buffers = (old, new)
    for index in range(planes):
        source, target = buffers[index % 2], buffers[(index + 1) % 2]
        sweep(source, target, lambda at: (constant[at - 1], factor[at - 1]), 1 + index, rim)
        sweep(
            source, target, lambda at: (own_constant[at - rim], own_factor[at - rim]),
            rim, 2 * planes - index,
        )
    kept_even[...] = old[planes : 2 * planes]
    kept_odd[...] = new[planes : 2 * planes]


def far_kernel(
    full, tiles, picks, message, pressure, far, far_late, own_constant, own_factor, kept_even, kept_odd,
    out, pieces, constant, factor, old, new, fields,
):
    planes, height, width = own_constant.shape
    zones = width // BLOCK
    place = Place(full, height)
    rim = planes + 1
    coefficients(
        deposits_of(message, tiles), tiles, place.first, full,
        driven_of(far, far_late, planes), constant, factor, place.even, jnp.where(place.odd, place.upper, place.lower),
    )
    old[planes : 2 * planes] = kept_even[...]
    new[planes : 2 * planes] = kept_odd[...]
    old[2 * planes] = pressure[jnp.where(place.even, 0, planes - 1)]
    for x in range(planes):
        at = jnp.where(place.even, planes - 1 - x, x)
        old[rim + planes + x] = far[at]
    old[rim + 2 * planes] = far[planes + HEAD]
    buffers = (old, new)
    edge = rim + planes
    for index in range(planes):
        source, target = buffers[index % 2], buffers[(index + 1) % 2]
        sweep(
            source, target, lambda at: (own_constant[at - rim], own_factor[at - rim]),
            2 * planes - index, edge,
        )
        sweep(
            source, target, lambda at: (constant[at - edge], factor[at - edge]),
            edge, edge + planes - index,
        )
    last = buffers[planes % 2]
    way = jnp.where(place.even, -0.5, 0.5)

    def gradient(x, carry):
        at = rim + x
        above, below, left, right = shifted(last[at])
        grads = (way * (last[at + 1] - last[at - 1]), 0.5 * (below - above), 0.5 * (right - left))
        line = jnp.where(place.even, planes - 1 - x, x) * zones
        for zone in range(zones):
            first = pl.multiple_of((line + zone) * height, SUB)
            for axis, grad in enumerate(grads):
                fields[pl.ds(first, height), axis * BLOCK : (axis + 1) * BLOCK] = (
                    grad[:, zone * BLOCK : (zone + 1) * BLOCK]
                )
        return carry

    lax.fori_loop(0, planes, gradient, 0, unroll=4)
    pieces[...] = jnp.concatenate(halves_of(fields[...]), 1)
    out[...] = picked_rows(picks[tiles : 2 * tiles, :], pieces)


def picked_rows(hot, pieces):
    total = jnp.dot(hot, pieces[...], preferred_element_type=F32)
    return total[:, : 3 * BLOCK] + total[:, 3 * BLOCK :]


def pick_kernel(place, picks, pieces, out):
    tiles = out.shape[0]
    out[...] = picked_rows(picks[place * tiles : (place + 1) * tiles, :], pieces)


def final_kernel(
    count, grads_a, grads_b, grads_c, weight, contact, vel, vol, drag, cell, out,
):
    tiles = cell.shape[0]
    cells = cell[...]
    heft = lanes_of(weight[...], cells)
    slot = iota(cells.shape, 0) * BLOCK + iota(cells.shape, 1)
    live = slot < count[0]
    volume = vol[...]
    push = TIME_STEP / volume
    for axis in range(3):
        lanes = slice(axis * BLOCK, (axis + 1) * BLOCK)
        gradient = lanes_of(grads_a[:, lanes] + grads_b[:, lanes] + grads_c[:, lanes], cells)
        own = jnp.concatenate(
            [vel[axis : axis + 1, t * BLOCK : (t + 1) * BLOCK] for t in range(tiles)], 0
        )
        fluid = -gradient * heft
        force = contact[axis * tiles : (axis + 1) * tiles, :] - volume * gradient
        force = force + drag[...] * (fluid - own)
        new = jnp.where(live, own + force * push, 0.0)
        for t in range(tiles):
            out[axis : axis + 1, t * BLOCK : (t + 1) * BLOCK] = new[t : t + 1, :]


def on_device(
    grain_pos,
    grain_vel,
    grain_vol,
    drag_coef,
    grain_count,
    contact_rows,
    contact_stiff,
    partner_block,
    halo_list,
    grain_cell,
    tile_cell_block,
    pressure_old,
    pressure_source,
    solid_old,
):
    groups, regions = lax.axis_size("grp"), lax.axis_size("reg")
    holding = groups - 1
    halves = groups // CORES
    slots = grain_pos.shape[1]
    tiles = slots // BLOCK
    planes, full, width = pressure_old.shape
    assert planes == ITERS
    own_rows = full // halves
    height = min(full, own_rows + SUB * min(2, halves - 1))
    owners = range(0, groups, CORES)
    holders = range(holding)

    def send(value, pairs):
        flat = [(a[0] * regions + a[1], b[0] * regions + b[1]) for a, b in pairs]
        return lax.ppermute(value, ("grp", "reg"), flat)

    def along_reg(value, members, goes, core=0):
        pairs = [
            ((g + core, r), (g, r + goes[r % 2]))
            for g in members
            for r in range(regions)
            if 0 <= r + goes[r % 2] < regions
        ]
        return send(value, pairs)

    def along_grp(value, step, members):
        pairs = [((g, r), ((g + step) % holding, r)) for g in members for r in range(regions)]
        return send(value, pairs)

    count = grain_count
    cell = grain_cell.reshape(tiles, BLOCK)
    vol = grain_vol.reshape(tiles, BLOCK)
    drag = drag_coef.reshape(tiles, BLOCK)
    ids = tile_cell_block.reshape(1, tiles)
    field_bytes = 4 * planes * height * width

    field = shaped(planes, height, width)
    plane = shaped(height, width)
    small = shaped(SUB, BLOCK)
    early, late, ends, inner = call(
        window_kernel,
        (
            shaped(planes + HEAD, height, width), shaped(planes - HEAD, height, width), plane,
            plane,
        ),
        [HBM] * 3, (pressure_old, pressure_source, solid_old),
        [pltpu.VMEM((planes, height, width), F32)] * 3
        + [pltpu.SemaphoreType.DMA((5 * planes + 2,))],
        flops=field_bytes, size=6 * field_bytes, limit=61_950_000, place=HBM,
    )
    near = along_reg(early, owners, (1, -1), core=1)
    near_late = along_reg(late, owners, (1, -1), core=1)
    beyond = along_reg(ends, owners, (-2, 2), core=1)
    mine, after_deposit = call(
        deposit_kernel, (shaped(tiles + SUB, 2 * BLOCK), small), [SMEM] + [VMEM] * 4,
        (count, cell, vol, drag, ids), flops=2 * 32 * 48 * 65536, size=5 * 4 * slots,
    )
    second = along_grp(mine, 1, holders)
    third = along_grp(mine, 2, holders)
    rows = halo_list.shape[1] // BLOCK
    halo = shaped(3 * rows, BLOCK)
    state, halo_near, halo_far, after_halo = call(
        halo_kernel, (shaped(3 * tiles, BLOCK), halo, halo, small),
        [VMEM] * 4, (grain_pos, grain_vel, halo_list, after_deposit), flops=slots,
        size=4 * 4 * 3 * slots,
    )
    others = [g for g in holders if g not in owners]
    came_near = along_reg(halo_near, others, (1, -1))
    came_far = along_reg(halo_far, others, (-1, 1))
    far, after_forward = call(
        forward_kernel, (shaped(planes + HEAD + 1, height, width), small), [VMEM] * 6,
        (near, inner, after_halo, second, third, beyond), size=5 * field_bytes,
    )
    far = along_reg(far, owners, (2, -2))
    far_late = along_reg(near_late, owners, (2, -2))
    message = shaped(holding * (tiles + SUB) + 3 * rows // 2, 2 * BLOCK)
    message_near, message_far, after_message = call(
        message_kernel, (message, message, small), [VMEM] * 6,
        (mine, second, third, halo_near, halo_far, after_forward), size=8 * 2 * BLOCK * 500,
    )
    message_near = along_reg(message_near, owners, (1, -1))
    message_far = along_reg(message_far, owners, (-1, 1))
    constant, factor, weight, picks = call(
        functools.partial(own_kernel, full),
        (
            field, field, shaped(tiles, BLOCK),
            jax.ShapeDtypeStruct((3 * tiles, planes * height * width // BLOCK), BF16),
        ),
        [VMEM] * 8 + [SMEM],
        (mine, second, third, early, late, after_message, came_near, came_far, partner_block),
        flops=planes * height * 4 * 384 * 256 * 6, size=9 * field_bytes,
    )
    window_of = lambda count: pltpu.VMEM((count, height, width), F32)
    kept_even, kept_odd = call(
        functools.partial(near_kernel, full, tiles), (field, field), [VMEM] * 7,
        (message_near, early, near, near_late, beyond, constant, factor),
        [window_of(planes)] * 2 + [window_of(2 * planes + 1)] * 2,
        flops=planes * height * 4 * 384 * 256 * 6, size=9 * field_bytes,
    )
    grads = shaped(tiles, 3 * BLOCK)
    cells_held = planes * height * width // BLOCK
    grads_b, pieces = call(
        functools.partial(far_kernel, full, tiles),
        (grads, jax.ShapeDtypeStruct((cells_held, 6 * BLOCK), BF16)), [VMEM] * 9,
        (picks, message_far, early, far, far_late, constant, factor, kept_even, kept_odd),
        [window_of(planes)] * 2
        + [window_of(3 * planes + 2)] * 2
        + [pltpu.VMEM((cells_held, 3 * BLOCK), F32)],
        flops=planes * height * 4 * 384 * 256 * 6, size=9 * field_bytes,
    )
    came_b = along_grp(grads_b, -1, owners)
    pick = lambda place: call(
        functools.partial(pick_kernel, place), grads, [VMEM] * 2, (picks, pieces),
        flops=slots, size=slots,
    )
    grads_c = pick(2)
    grads_a = pick(0)
    came_c = along_grp(grads_c, -2, owners)
    contact = call(
        contact_kernel, shaped(3 * tiles, BLOCK), [SMEM] + [VMEM] * 7 + [ANY],
        (
            partner_block, state, message_near, message_far, came_near, came_far, contact_rows,
            contact_stiff, grads_a,
        ),
        [pltpu.VMEM((3 * (tiles + 2 * rows), BLOCK), F32)],
        flops=60 * 8 * slots, size=4 * 20 * slots,
    )
    return call(
        final_kernel, shaped(3, slots), [SMEM] + [VMEM] * 9,
        (count, grads_a, came_c, came_b, weight, contact, grain_vel, vol, drag, cell),
        flops=60 * slots, size=4 * 20 * slots,
    )


def solution(mesh):
    in_specs = (
        P(None, ("grp", "reg")),
        P(None, ("grp", "reg")),
        P(("grp", "reg")),
        P(("grp", "reg")),
        P(("grp", "reg")),
        P(None, ("grp", "reg")),
        P(None, ("grp", "reg")),
        P(("grp", "reg")),
        P(None, ("grp", "reg")),
        P(("grp", "reg")),
        P(("grp", "reg")),
        P("reg", None, None),
        P("reg", None, None),
        P("reg", None, None),
    )
    out_specs = P(None, ("grp", "reg"))
    return jax.shard_map(
        on_device, mesh=mesh, in_specs=in_specs, out_specs=out_specs, check_vma=False
    )
```

```python
import functools

import jax
import jax.numpy as jnp
from jax import lax
from jax.experimental import pallas as pl
from jax.experimental.pallas import tpu as pltpu
from jax.sharding import PartitionSpec as P

BLOCK = 128
SUB = 8
CORES = 2
ITERS = 4
HEAD = 1
SPRING = 1.0
DAMPING = 0.5
TIME_STEP = 0.5

VMEM = pl.BlockSpec(memory_space=pltpu.VMEM)
SMEM = pl.BlockSpec(memory_space=pltpu.SMEM)
ANY = pl.BlockSpec(memory_space=pl.ANY)
HBM = pl.BlockSpec(memory_space=pltpu.HBM)
F32 = jnp.float32
BF16 = jnp.bfloat16


def iota(shape, dim):
    return lax.broadcasted_iota(jnp.int32, shape, dim)


def shaped(*dims):
    return jax.ShapeDtypeStruct(dims, F32)


def call(kernel, outs, specs, args, scratch=(), flops=0, size=0, limit=40_000_000, place=VMEM):
    return pl.pallas_call(
        kernel,
        out_shape=outs,
        in_specs=specs,
        out_specs=jax.tree.map(lambda _: place, outs),
        scratch_shapes=list(scratch),
        compiler_params=pltpu.CompilerParams(vmem_limit_bytes=limit),
        cost_estimate=pl.CostEstimate(flops=flops, bytes_accessed=size, transcendentals=0),
    )(*args)


class Place:
    def __init__(self, full, height):
        groups, regions = lax.axis_size("grp"), lax.axis_size("reg")
        self.group, region = lax.axis_index("grp"), lax.axis_index("reg")
        self.half = self.group // CORES
        self.own_rows = full // (groups // CORES)
        first = jnp.clip(self.half * self.own_rows - SUB, 0, full - height)
        self.first = pl.multiple_of(first, SUB)
        self.sweeps = self.group % CORES == 0
        self.parity = region % 2
        self.odd, self.even = self.parity == 1, self.parity == 0
        self.lower, self.upper = region > 0, region < regions - 1


def lanes_of(source, index):
    return jnp.take_along_axis(source, index, axis=1, mode="promise_in_bounds")


def halves_of(value):
    high = value.astype(BF16)
    return high, (value - high.astype(F32)).astype(BF16)


def window_kernel(
    pressure_old, source, solid_before, early, late, ends, inner, pressure, driven, solid, sems
):
    planes, height, _ = solid.shape
    place = Place(pressure_old.shape[1], height)
    rows = pl.ds(place.first, height)
    used = []

    def copy(whole, part):
        used.append(None)
        return pltpu.make_async_copy(whole, part, sems.at[len(used) - 1])

    fetched = [
        [copy(whole.at[x, rows, :], part.at[x]) for x in range(planes)]
        for whole, part in ((pressure_old, pressure), (source, driven), (solid_before, solid))
    ]
    stored = [copy(pressure.at[x], early.at[x]) for x in range(planes)]
    for x in range(planes):
        stored.append(copy(driven.at[x], early.at[planes + x] if x < HEAD else late.at[x - HEAD]))
    sides = (
        copy(pressure.at[place.parity * (planes - 1)], ends),
        copy(pressure.at[(1 - place.parity) * (planes - 1)], inner),
    )
    for x in range(planes):
        for part in fetched:
            part[x].start()
    for x in range(planes):
        fetched[0][x].wait()
        stored[x].start()
        fetched[1][x].wait()
        fetched[2][x].wait()
        driven[x] = driven[x] - solid[x]
        stored[planes + x].start()
    for one in sides:
        one.start()
    for one in stored:
        one.wait()
    for one in sides:
        one.wait()


def forward_kernel(near, inner, _halo, _second, _third, _beyond, out, dummy):
    dummy[...] = jnp.zeros(dummy.shape, F32)
    count = near.shape[0]
    out[:count] = near[...]
    out[count] = inner[...]


def deposit_kernel(count, cell, vol, drag, ids, out, dummy):
    dummy[...] = jnp.zeros(dummy.shape, F32)
    tiles = cell.shape[0]
    sub = iota((SUB, BLOCK), 0)
    rows_c = iota((BLOCK, BLOCK), 0)
    even = sub % 2 == 0
    low_pair = sub % 4 < 2

    def step(group, carry):
        first = pl.multiple_of(group * SUB, SUB)
        slot = (first + sub) * BLOCK + iota((SUB, BLOCK), 1)
        live = slot < count[0]
        cells = cell[pl.ds(first, SUB), :]
        parts = halves_of(jnp.where(live, vol[pl.ds(first, SUB), :], 0.0)) + halves_of(
            jnp.where(live, drag[pl.ds(first, SUB), :], 0.0)
        )
        parts = [part.astype(F32) for part in parts]
        left = jnp.concatenate([jnp.where(even, part, 0.0) for part in parts], 0)
        right = jnp.concatenate([jnp.where(even, 0.0, part) for part in parts], 0)
        loads = jnp.concatenate([left, right], 1).astype(BF16)
        sums = [jnp.zeros((SUB, BLOCK), F32), jnp.zeros((SUB, BLOCK), F32)]
        for quad in range(SUB // 4):
            hot = [
                jnp.where(
                    rows_c == jnp.broadcast_to(cells[t : t + 1, :], (BLOCK, BLOCK)), 1.0, 0.0
                ).astype(BF16)
                for t in range(4 * quad, 4 * quad + 4)
            ]
            picked = jnp.concatenate(
                [jnp.concatenate(hot[:2], 1), jnp.concatenate(hot[2:], 1)], 0
            )
            placed = lax.dot_general(
                loads, picked, (((1,), (1,)), ((), ())), preferred_element_type=F32
            )
            for field in range(2):
                base = field * 2 * SUB
                total = placed[base : base + SUB] + placed[base + SUB : base + 2 * SUB]
                chosen = jnp.where(low_pair, total[:, :BLOCK], total[:, BLOCK:])
                sums[field] = jnp.where(sub // 4 == quad, chosen, sums[field])
        out[pl.ds(first, SUB), :BLOCK] = sums[0]
        out[pl.ds(first, SUB), BLOCK:] = sums[1]
        return carry

    lax.fori_loop(0, tiles // SUB, step, 0, unroll=4)
    out[tiles : tiles + SUB, :BLOCK] = jnp.broadcast_to(ids[...].astype(F32), (SUB, BLOCK))
    out[tiles : tiles + SUB, BLOCK:] = jnp.zeros((SUB, BLOCK), F32)


def halo_kernel(pos, vel, lists, _, inner, state, near, far, dummy, held):
    held[...] = inner[...]
    dummy[...] = jnp.zeros(dummy.shape, F32)
    tiles = pos.shape[1] // BLOCK
    rows = lists.shape[1] // BLOCK
    for tile in range(tiles):
        lanes = slice(tile * BLOCK, (tile + 1) * BLOCK)
        mixed = SPRING * pos[:, lanes] - DAMPING * vel[:, lanes]
        for axis in range(3):
            state[axis * tiles + tile : axis * tiles + tile + 1, :] = mixed[axis : axis + 1]
    turned = [
        jnp.concatenate(halves_of(jnp.transpose(state[axis * tiles : (axis + 1) * tiles, :])), 1)
        for axis in range(3)
    ]
    turned = jnp.concatenate(turned, 0)
    span = 2 * BLOCK
    row = iota((BLOCK, span), 0)

    odd = lax.axis_index("reg") % 2
    for away, out in enumerate((near, far)):
        side = 1 - odd if away == 0 else odd

        def step(part, carry):
            named = lists[:, pl.ds(pl.multiple_of(part * span, span), span)]
            named = jnp.where(side == 0, named[:1], named[1:])
            block = lax.shift_right_logical(named, 7)
            lane = named & (BLOCK - 1)
            hot = jnp.where(row == jnp.broadcast_to(block, row.shape), 1.0, 0.0).astype(BF16)
            found = jnp.dot(
                turned, jnp.concatenate([hot, hot], 0), preferred_element_type=F32
            )
            here = row == jnp.broadcast_to(lane, row.shape)
            for axis in range(3):
                value = jnp.where(here, found[axis * BLOCK : (axis + 1) * BLOCK], 0.0)
                value = jnp.sum(value, axis=0, keepdims=True)
                for half in range(2):
                    out[pl.ds(axis * rows + 2 * part + half, 1), :] = value[
                        :, half * BLOCK : (half + 1) * BLOCK
                    ]
            return carry

        lax.fori_loop(0, rows // 2, step, 0, unroll=8)


def message_kernel(mine, second, third, halo_near, halo_far, _, near, far, dummy):
    dummy[...] = jnp.zeros(dummy.shape, F32)
    stride = mine.shape[0]
    half = halo_near.shape[0] // 2
    rows = near.shape[0] - half
    for halo, out in ((halo_near, near), (halo_far, far)):
        for index, group in enumerate((mine, second, third)):
            out[index * stride : (index + 1) * stride, :] = group[...]
        out[rows:, :BLOCK] = halo[:half, :]
        out[rows:, BLOCK:] = halo[half:, :]


def merged(parts):
    sub = iota((SUB, BLOCK), 0)
    for step in (4, 2, 1):
        low = (sub & step) == 0
        paired = []
        for first, second in zip(parts[:step], parts[step:]):
            away = jnp.where(low, second, first)
            back = pltpu.roll(away, step, 0)
            if step < SUB // 2:
                back = jnp.where(low, pltpu.roll(away, SUB - step, 0), back)
            paired.append(jnp.where(low, first, second) + back)
        parts = paired
    return parts[0]


def contact_kernel(
    partner, state, message_near, message_far, halo_near, halo_far, named, stiff, _, out, extended,
):
    tiles = state.shape[0] // 3
    rows = halo_near.shape[0] // 3
    blocks = tiles + 2 * rows
    base = message_near.shape[0] - 3 * rows // 2
    odd = lax.axis_index("reg") % 2
    sweeps = lax.axis_index("grp") % CORES == 0
    for axis in range(3):
        extended[axis * blocks : axis * blocks + tiles, :] = state[
            axis * tiles : (axis + 1) * tiles, :
        ]
    for message, halo, upper in (
        (message_near, halo_near, 1 - odd), (message_far, halo_far, odd)
    ):
        carried = jnp.concatenate([message[base:, :BLOCK], message[base:, BLOCK:]], 0)
        carried = jnp.where(sweeps, carried, halo[...])
        for axis in range(3):
            first = pl.multiple_of(axis * blocks + tiles + upper * rows, SUB)
            extended[pl.ds(first, rows), :] = carried[axis * rows : (axis + 1) * rows]

    def step(group, carry):
        first = pl.multiple_of(group * SUB, SUB)
        held = [extended[pl.ds(axis * blocks + first, SUB), :] for axis in range(3)]
        pulls = [[], [], []]
        for t in range(SUB):
            lanes = pl.ds(pl.multiple_of((first + t) * BLOCK, BLOCK), BLOCK)
            entry = named[:, lanes]
            weight = jnp.where(entry >= 0, stiff[:, lanes], 0.0)
            own = entry < BLOCK
            lane = entry & (BLOCK - 1)
            other = partner[first + t]
            for axis in range(3):
                mine = jnp.broadcast_to(held[axis][t : t + 1], entry.shape)
                theirs = extended[pl.ds(axis * blocks + other, 1), :]
                theirs = jnp.broadcast_to(theirs, entry.shape)
                met = jnp.where(own, lanes_of(mine, lane), lanes_of(theirs, lane))
                pulls[axis].append(weight * (mine - met))
        for axis in range(3):
            out[pl.ds(axis * tiles + first, SUB), :] = merged(pulls[axis])
        return carry

    lax.fori_loop(0, tiles // SUB, step, 0)


def shifted(plane):
    height, width = plane.shape
    row = iota((SUB, width), 0)
    column = iota((height, BLOCK), 1)
    above, below = pltpu.roll(plane, 1, 0), pltpu.roll(plane, height - 1, 0)
    left, right = pltpu.roll(plane, 1, 1), pltpu.roll(plane, width - 1, 1)
    above = jnp.concatenate([jnp.where(row == 0, 0.0, above[:SUB]), above[SUB:]], 0)
    below = jnp.concatenate([below[:-SUB], jnp.where(row == SUB - 1, 0.0, below[-SUB:])], 0)
    left = jnp.concatenate([jnp.where(column == 0, 0.0, left[:, :BLOCK]), left[:, BLOCK:]], 1)
    right = jnp.concatenate(
        [right[:, :-BLOCK], jnp.where(column == BLOCK - 1, 0.0, right[:, -BLOCK:])], 1
    )
    return above, below, left, right


def inverse_of(value):
    near = pl.reciprocal(value, approx=True)
    return near * (2.0 - value * near)


def placed(groups, tiles):
    parts = [halves_of(group[:tiles, :]) for group in groups]
    loads = jnp.concatenate([part[i] for i in range(2) for part in parts], 0)
    ids = jnp.concatenate([group[tiles : tiles + 1, :BLOCK] for group in groups], 1)
    ids = ids.astype(jnp.int32)

    def gathered(wanted):
        hot = jnp.where(wanted == jnp.broadcast_to(ids, wanted.shape), 1.0, 0.0).astype(BF16)
        total = jnp.dot(
            jnp.concatenate([hot, hot], 1), loads, preferred_element_type=F32
        )
        return total[:, :BLOCK], total[:, BLOCK:]

    return ids, gathered


def driven_of(early, late, planes):
    return lambda x: early[planes + x] if x < HEAD else late[x - HEAD]


def coefficients(gathered, tiles, first, full, driven_at, constant, factor, turned, present):
    planes, height, width = constant.shape
    zones = width // BLOCK
    shape = (zones * height, 3 * tiles)
    line = iota(shape, 0)
    block = (line % height) * zones + line // height + first * zones

    for x in range(planes):
        solid, drag = gathered(block + x * (full * zones))
        at = x if turned is None else jnp.where(turned, planes - 1 - x, x)
        voids = 1.0 + solid
        scale = inverse_of(6.0 + (drag + 1.0) * voids)
        if present is not None:
            scale = jnp.where(present, scale, 0.0)
        inverse = voids * scale
        for zone in range(zones):
            lanes = slice(zone * BLOCK, (zone + 1) * BLOCK)
            rows = slice(zone * height, (zone + 1) * height)
            driving = driven_at(x)[:, lanes] + solid[rows]
            constant[at, :, lanes] = driving * inverse[rows]
            factor[at, :, lanes] = scale[rows]


def own_kernel(
    full, mine, second, third, early, late, _message, _near, _far, _partner, constant, factor, weight, picks
):
    tiles = weight.shape[0]
    planes, height, width = constant.shape
    place = Place(full, height)
    zones = width // BLOCK
    ids, gathered = placed((mine, second, third), tiles)
    coefficients(
        gathered, tiles, place.first, full, driven_of(early, late, planes), constant, factor,
        place.even, None,
    )
    turned = [
        jnp.transpose(
            jnp.broadcast_to(ids[:, i * tiles : (i + 1) * tiles], (BLOCK, tiles)).astype(F32)
        ).astype(jnp.int32)
        for i in range(3)
    ]
    solid, drag = gathered(jnp.concatenate([turned[0]] * 3, 1))
    weight[...] = 1.0 / (1.0 / (1.0 + solid) + drag)
    for i in range(3):
        block = turned[i]
        line, zone = block // zones, block % zones
        x, y = line // full, line % full
        row = (x * zones + zone) * height + y - place.first
        held = y // place.own_rows == jnp.where(place.sweeps, place.half, -1)
        row = jnp.concatenate([jnp.where(held, row, -1)] * (picks.shape[1] // BLOCK), 1)
        hot = jnp.where(row == iota(row.shape, 1), 1.0, 0.0).astype(BF16)
        picks[i * tiles : (i + 1) * tiles, :] = hot


def sweep(source, target, coefficient, start, stop):
    def plane(at, carry):
        above, below, left, right = shifted(source[at])
        around = source[at - 1] + source[at + 1] + above + below + left + right
        constant, factor = coefficient(at)
        target[at] = constant + factor * around
        return carry

    lax.fori_loop(start, stop, plane, 0, unroll=4)


def deposits_of(message, tiles):
    stride = tiles + SUB
    return placed([message.at[i * stride : (i + 1) * stride] for i in range(3)], tiles)[1]


def near_kernel(
    full, tiles, message, pressure, near, near_late, beyond, own_constant, own_factor, kept_even, kept_odd, constant, factor, old, new,
):
    planes, height, width = own_constant.shape
    place = Place(full, height)
    rim = planes + 1
    coefficients(
        deposits_of(message, tiles), tiles, place.first, full,
        driven_of(near, near_late, planes), constant, factor, place.even, jnp.where(place.odd, place.lower, place.upper),
    )
    old[0] = beyond[...]
    for x in range(planes):
        at = jnp.where(place.even, planes - 1 - x, x)
        old[1 + x] = near[at]
        old[rim + x] = pressure[at]
    buffers = (old, new)
    for index in range(planes):
        source, target = buffers[index % 2], buffers[(index + 1) % 2]
        sweep(source, target, lambda at: (constant[at - 1], factor[at - 1]), 1 + index, rim)
        sweep(
            source, target, lambda at: (own_constant[at - rim], own_factor[at - rim]),
            rim, 2 * planes - index,
        )
    kept_even[...] = old[planes : 2 * planes]
    kept_odd[...] = new[planes : 2 * planes]


def far_kernel(
    full, tiles, picks, message, pressure, far, far_late, own_constant, own_factor, kept_even, kept_odd,
    out, pieces, constant, factor, old, new, fields,
):
    planes, height, width = own_constant.shape
    zones = width // BLOCK
    place = Place(full, height)
    rim = planes + 1
    coefficients(
        deposits_of(message, tiles), tiles, place.first, full,
        driven_of(far, far_late, planes), constant, factor, place.even, jnp.where(place.odd, place.upper, place.lower),
    )
    old[planes : 2 * planes] = kept_even[...]
    new[planes : 2 * planes] = kept_odd[...]
    old[2 * planes] = pressure[jnp.where(place.even, 0, planes - 1)]
    for x in range(planes):
        at = jnp.where(place.even, planes - 1 - x, x)
        old[rim + planes + x] = far[at]
    old[rim + 2 * planes] = far[planes + HEAD]
    buffers = (old, new)
    edge = rim + planes
    for index in range(planes):
        source, target = buffers[index % 2], buffers[(index + 1) % 2]
        sweep(
            source, target, lambda at: (own_constant[at - rim], own_factor[at - rim]),
            2 * planes - index, edge,
        )
        sweep(
            source, target, lambda at: (constant[at - edge], factor[at - edge]),
            edge, edge + planes - index,
        )
    last = buffers[planes % 2]
    way = jnp.where(place.even, -0.5, 0.5)

    def gradient(x, carry):
        at = rim + x
        above, below, left, right = shifted(last[at])
        grads = (way * (last[at + 1] - last[at - 1]), 0.5 * (below - above), 0.5 * (right - left))
        line = jnp.where(place.even, planes - 1 - x, x) * zones
        for zone in range(zones):
            first = pl.multiple_of((line + zone) * height, SUB)
            for axis, grad in enumerate(grads):
                fields[pl.ds(first, height), axis * BLOCK : (axis + 1) * BLOCK] = (
                    grad[:, zone * BLOCK : (zone + 1) * BLOCK]
                )
        return carry

    lax.fori_loop(0, planes, gradient, 0, unroll=4)
    pieces[...] = jnp.concatenate(halves_of(fields[...]), 1)
    out[...] = picked_rows(picks, 3 - across_set(), tiles, pieces)


def across_set():
    return jnp.where(lax.axis_index("grp") == 0, 1, 2)


def picked_rows(picks, chosen, tiles, pieces):
    hot = picks[pl.ds(pl.multiple_of(chosen * tiles, tiles), tiles), :]
    total = jnp.dot(hot, pieces[...], preferred_element_type=F32)
    return total[:, : 3 * BLOCK] + total[:, 3 * BLOCK :]


def pick_kernel(own, picks, pieces, out):
    chosen = 0 if own else across_set()
    out[...] = picked_rows(picks, chosen, out.shape[0], pieces)


def final_kernel(
    count, grads_a, grads_b, grads_c, grads_d, weight, contact, vel, vol, drag, cell, out,
):
    tiles = cell.shape[0]
    cells = cell[...]
    heft = lanes_of(weight[...], cells)
    slot = iota(cells.shape, 0) * BLOCK + iota(cells.shape, 1)
    live = slot < count[0]
    volume = vol[...]
    push = TIME_STEP / volume
    for axis in range(3):
        lanes = slice(axis * BLOCK, (axis + 1) * BLOCK)
        gradient = grads_a[:, lanes] + grads_b[:, lanes] + (grads_c[:, lanes] + grads_d[:, lanes])
        gradient = lanes_of(gradient, cells)
        own = jnp.concatenate(
            [vel[axis : axis + 1, t * BLOCK : (t + 1) * BLOCK] for t in range(tiles)], 0
        )
        fluid = -gradient * heft
        force = contact[axis * tiles : (axis + 1) * tiles, :] - volume * gradient
        force = force + drag[...] * (fluid - own)
        new = jnp.where(live, own + force * push, 0.0)
        for t in range(tiles):
            out[axis : axis + 1, t * BLOCK : (t + 1) * BLOCK] = new[t : t + 1, :]


def on_device(
    grain_pos,
    grain_vel,
    grain_vol,
    drag_coef,
    grain_count,
    contact_rows,
    contact_stiff,
    partner_block,
    halo_list,
    grain_cell,
    tile_cell_block,
    pressure_old,
    pressure_source,
    solid_old,
):
    groups, regions = lax.axis_size("grp"), lax.axis_size("reg")
    holding = groups - 1
    halves = groups // CORES
    slots = grain_pos.shape[1]
    tiles = slots // BLOCK
    planes, full, width = pressure_old.shape
    assert planes == ITERS
    own_rows = full // halves
    height = min(full, own_rows + SUB * min(2, halves - 1))
    owners = range(0, groups, CORES)
    holders = range(holding)

    def send(value, pairs):
        flat = [(a[0] * regions + a[1], b[0] * regions + b[1]) for a, b in pairs]
        return lax.ppermute(value, ("grp", "reg"), flat)

    def along_reg(value, members, goes, core=0):
        pairs = [
            ((g + core, r), (g, r + goes[r % 2]))
            for g in members
            for r in range(regions)
            if 0 <= r + goes[r % 2] < regions
        ]
        return send(value, pairs)

    def along_grp(value, step, members):
        pairs = [((g, r), ((g + step) % holding, r)) for g in members for r in range(regions)]
        return send(value, pairs)

    count = grain_count
    cell = grain_cell.reshape(tiles, BLOCK)
    vol = grain_vol.reshape(tiles, BLOCK)
    drag = drag_coef.reshape(tiles, BLOCK)
    ids = tile_cell_block.reshape(1, tiles)
    field_bytes = 4 * planes * height * width

    field = shaped(planes, height, width)
    plane = shaped(height, width)
    small = shaped(SUB, BLOCK)
    early, late, ends, inner = call(
        window_kernel,
        (
            shaped(planes + HEAD, height, width), shaped(planes - HEAD, height, width), plane,
            plane,
        ),
        [HBM] * 3, (pressure_old, pressure_source, solid_old),
        [pltpu.VMEM((planes, height, width), F32)] * 3
        + [pltpu.SemaphoreType.DMA((5 * planes + 2,))],
        flops=field_bytes, size=6 * field_bytes, limit=61_950_000, place=HBM,
    )
    near = along_reg(early, owners, (1, -1), core=1)
    near_late = along_reg(late, owners, (1, -1), core=1)
    beyond = along_reg(ends, owners, (-2, 2), core=1)
    mine, after_deposit = call(
        deposit_kernel, (shaped(tiles + SUB, 2 * BLOCK), small), [SMEM] + [VMEM] * 4,
        (count, cell, vol, drag, ids), flops=2 * 32 * 48 * 65536, size=5 * 4 * slots,
    )
    second = along_grp(mine, 1, holders)
    third = along_grp(mine, 2, holders)
    rows = halo_list.shape[1] // BLOCK
    halo = shaped(3 * rows, BLOCK)
    state, halo_near, halo_far, after_halo, inner = call(
        halo_kernel, (shaped(3 * tiles, BLOCK), halo, halo, small, plane),
        [VMEM] * 5, (grain_pos, grain_vel, halo_list, after_deposit, inner), flops=slots,
        size=4 * 4 * 3 * slots,
    )
    others = [g for g in holders if g not in owners]
    came_near = along_reg(halo_near, others, (1, -1))
    came_far = along_reg(halo_far, others, (-1, 1))
    far, after_forward = call(
        forward_kernel, (shaped(planes + HEAD + 1, height, width), small), [VMEM] * 6,
        (near, inner, after_halo, second, third, beyond), size=5 * field_bytes,
    )
    far = along_reg(far, owners, (2, -2))
    far_late = along_reg(near_late, owners, (2, -2))
    message = shaped(holding * (tiles + SUB) + 3 * rows // 2, 2 * BLOCK)
    message_near, message_far, after_message = call(
        message_kernel, (message, message, small), [VMEM] * 6,
        (mine, second, third, halo_near, halo_far, after_forward), size=8 * 2 * BLOCK * 500,
    )
    message_near = along_reg(message_near, owners, (1, -1))
    message_far = along_reg(message_far, owners, (-1, 1))
    constant, factor, weight, picks = call(
        functools.partial(own_kernel, full),
        (
            field, field, shaped(tiles, BLOCK),
            jax.ShapeDtypeStruct((3 * tiles, planes * height * width // BLOCK), BF16),
        ),
        [VMEM] * 8 + [SMEM],
        (mine, second, third, early, late, after_message, came_near, came_far, partner_block),
        flops=planes * height * 4 * 384 * 256 * 6, size=9 * field_bytes,
    )
    window_of = lambda count: pltpu.VMEM((count, height, width), F32)
    kept_even, kept_odd = call(
        functools.partial(near_kernel, full, tiles), (field, field), [VMEM] * 7,
        (message_near, early, near, near_late, beyond, constant, factor),
        [window_of(planes)] * 2 + [window_of(2 * planes + 1)] * 2,
        flops=planes * height * 4 * 384 * 256 * 6, size=9 * field_bytes,
    )
    grads = shaped(tiles, 3 * BLOCK)
    cells_held = planes * height * width // BLOCK
    grads_between, pieces = call(
        functools.partial(far_kernel, full, tiles),
        (grads, jax.ShapeDtypeStruct((cells_held, 6 * BLOCK), BF16)), [VMEM] * 9,
        (picks, message_far, early, far, far_late, constant, factor, kept_even, kept_odd),
        [window_of(planes)] * 2
        + [window_of(3 * planes + 2)] * 2
        + [pltpu.VMEM((cells_held, 3 * BLOCK), F32)],
        flops=planes * height * 4 * 384 * 256 * 6, size=9 * field_bytes,
    )
    ends_of = lambda source, target: [((source, r), (target, r)) for r in range(regions)]
    low, high, between = 0, CORES, 1
    came_low = send(grads_between, ends_of(low, between))
    came_high = send(grads_between, ends_of(high, between))
    pick = lambda own: call(
        functools.partial(pick_kernel, own), grads, [VMEM] * 2, (picks, pieces),
        flops=slots, size=slots,
    )
    came_across = send(pick(False), ends_of(low, high) + ends_of(high, low))
    grads_a = pick(True)
    contact = call(
        contact_kernel, shaped(3 * tiles, BLOCK), [SMEM] + [VMEM] * 7 + [ANY],
        (
            partner_block, state, message_near, message_far, came_near, came_far, contact_rows,
            contact_stiff, grads_a,
        ),
        [pltpu.VMEM((3 * (tiles + 2 * rows), BLOCK), F32)],
        flops=60 * 8 * slots, size=4 * 20 * slots,
    )
    return call(
        final_kernel, shaped(3, slots), [SMEM] + [VMEM] * 10,
        (
            count, grads_a, came_across, came_low, came_high, weight, contact, grain_vel, vol, drag,
            cell,
        ),
        flops=60 * slots, size=4 * 20 * slots,
    )


def solution(mesh):
    in_specs = (
        P(None, ("grp", "reg")),
        P(None, ("grp", "reg")),
        P(("grp", "reg")),
        P(("grp", "reg")),
        P(("grp", "reg")),
        P(None, ("grp", "reg")),
        P(None, ("grp", "reg")),
        P(("grp", "reg")),
        P(None, ("grp", "reg")),
        P(("grp", "reg")),
        P(("grp", "reg")),
        P("reg", None, None),
        P("reg", None, None),
        P("reg", None, None),
    )
    out_specs = P(None, ("grp", "reg"))
    return jax.shard_map(
        on_device, mesh=mesh, in_specs=in_specs, out_specs=out_specs, check_vma=False
    )
```

```python
import functools

import jax
import jax.numpy as jnp
from jax import lax
from jax.experimental import pallas as pl
from jax.experimental.pallas import tpu as pltpu
from jax.sharding import PartitionSpec as P

BLOCK = 128
SUB = 8
CORES = 2
ITERS = 4
HEAD = 1
SPRING = 1.0
DAMPING = 0.5
TIME_STEP = 0.5

VMEM = pl.BlockSpec(memory_space=pltpu.VMEM)
SMEM = pl.BlockSpec(memory_space=pltpu.SMEM)
ANY = pl.BlockSpec(memory_space=pl.ANY)
HBM = pl.BlockSpec(memory_space=pltpu.HBM)
F32 = jnp.float32
BF16 = jnp.bfloat16


def iota(shape, dim):
    return lax.broadcasted_iota(jnp.int32, shape, dim)


def shaped(*dims):
    return jax.ShapeDtypeStruct(dims, F32)


def call(kernel, outs, specs, args, scratch=(), flops=0, size=0, limit=40_000_000, place=VMEM):
    return pl.pallas_call(
        kernel,
        out_shape=outs,
        in_specs=specs,
        out_specs=jax.tree.map(lambda _: place, outs),
        scratch_shapes=list(scratch),
        compiler_params=pltpu.CompilerParams(vmem_limit_bytes=limit),
        cost_estimate=pl.CostEstimate(flops=flops, bytes_accessed=size, transcendentals=0),
    )(*args)


class Place:
    def __init__(self, full, height):
        groups, regions = lax.axis_size("grp"), lax.axis_size("reg")
        self.group, region = lax.axis_index("grp"), lax.axis_index("reg")
        self.half = self.group // CORES
        self.own_rows = full // (groups // CORES)
        first = jnp.clip(self.half * self.own_rows - SUB, 0, full - height)
        self.first = pl.multiple_of(first, SUB)
        self.sweeps = self.group % CORES == 0
        self.parity = region % 2
        self.odd, self.even = self.parity == 1, self.parity == 0
        self.lower, self.upper = region > 0, region < regions - 1


def lanes_of(source, index):
    return jnp.take_along_axis(source, index, axis=1, mode="promise_in_bounds")


def halves_of(value):
    high = value.astype(BF16)
    return high, (value - high.astype(F32)).astype(BF16)


def window_kernel(
    pressure_old, source, solid_before, early, late, ends, inner, pressure, driven, solid, sems
):
    planes, height, _ = solid.shape
    place = Place(pressure_old.shape[1], height)
    rows = pl.ds(place.first, height)
    used = []

    def copy(whole, part):
        used.append(None)
        return pltpu.make_async_copy(whole, part, sems.at[len(used) - 1])

    fetched = [
        [copy(whole.at[x, rows, :], part.at[x]) for x in range(planes)]
        for whole, part in ((pressure_old, pressure), (source, driven), (solid_before, solid))
    ]
    stored = [copy(pressure.at[x], early.at[x]) for x in range(planes)]
    for x in range(planes):
        stored.append(copy(driven.at[x], early.at[planes + x] if x < HEAD else late.at[x - HEAD]))
    sides = (
        copy(pressure.at[place.parity * (planes - 1)], ends),
        copy(pressure.at[(1 - place.parity) * (planes - 1)], inner),
    )
    for x in range(planes):
        for part in fetched:
            part[x].start()
    for x in range(planes):
        fetched[0][x].wait()
        stored[x].start()
        fetched[1][x].wait()
        fetched[2][x].wait()
        driven[x] = driven[x] - solid[x]
        stored[planes + x].start()
    for one in sides:
        one.start()
    for one in stored:
        one.wait()
    for one in sides:
        one.wait()


def forward_kernel(near, _halo, _second, _third, _beyond, out, dummy):
    dummy[...] = jnp.zeros(dummy.shape, F32)
    out[...] = near[...]


def deposit_kernel(count, cell, vol, drag, ids, out, dummy):
    dummy[...] = jnp.zeros(dummy.shape, F32)
    tiles = cell.shape[0]
    sub = iota((SUB, BLOCK), 0)
    rows_c = iota((BLOCK, BLOCK), 0)
    even = sub % 2 == 0
    low_pair = sub % 4 < 2

    def step(group, carry):
        first = pl.multiple_of(group * SUB, SUB)
        slot = (first + sub) * BLOCK + iota((SUB, BLOCK), 1)
        live = slot < count[0]
        cells = cell[pl.ds(first, SUB), :]
        parts = halves_of(jnp.where(live, vol[pl.ds(first, SUB), :], 0.0)) + halves_of(
            jnp.where(live, drag[pl.ds(first, SUB), :], 0.0)
        )
        parts = [part.astype(F32) for part in parts]
        left = jnp.concatenate([jnp.where(even, part, 0.0) for part in parts], 0)
        right = jnp.concatenate([jnp.where(even, 0.0, part) for part in parts], 0)
        loads = jnp.concatenate([left, right], 1).astype(BF16)
        sums = [jnp.zeros((SUB, BLOCK), F32), jnp.zeros((SUB, BLOCK), F32)]
        for quad in range(SUB // 4):
            hot = [
                jnp.where(
                    rows_c == jnp.broadcast_to(cells[t : t + 1, :], (BLOCK, BLOCK)), 1.0, 0.0
                ).astype(BF16)
                for t in range(4 * quad, 4 * quad + 4)
            ]
            picked = jnp.concatenate(
                [jnp.concatenate(hot[:2], 1), jnp.concatenate(hot[2:], 1)], 0
            )
            placed = lax.dot_general(
                loads, picked, (((1,), (1,)), ((), ())), preferred_element_type=F32
            )
            for field in range(2):
                base = field * 2 * SUB
                total = placed[base : base + SUB] + placed[base + SUB : base + 2 * SUB]
                chosen = jnp.where(low_pair, total[:, :BLOCK], total[:, BLOCK:])
                sums[field] = jnp.where(sub // 4 == quad, chosen, sums[field])
        out[pl.ds(first, SUB), :BLOCK] = sums[0]
        out[pl.ds(first, SUB), BLOCK:] = sums[1]
        return carry

    lax.fori_loop(0, tiles // SUB, step, 0, unroll=4)
    out[tiles : tiles + SUB, :BLOCK] = jnp.broadcast_to(ids[...].astype(F32), (SUB, BLOCK))
    out[tiles : tiles + SUB, BLOCK:] = jnp.zeros((SUB, BLOCK), F32)


def halo_kernel(pos, vel, lists, _, state, near, far, dummy):
    dummy[...] = jnp.zeros(dummy.shape, F32)
    tiles = pos.shape[1] // BLOCK
    rows = lists.shape[1] // BLOCK
    for tile in range(tiles):
        lanes = slice(tile * BLOCK, (tile + 1) * BLOCK)
        mixed = SPRING * pos[:, lanes] - DAMPING * vel[:, lanes]
        for axis in range(3):
            state[axis * tiles + tile : axis * tiles + tile + 1, :] = mixed[axis : axis + 1]
    turned = [
        jnp.concatenate(halves_of(jnp.transpose(state[axis * tiles : (axis + 1) * tiles, :])), 1)
        for axis in range(3)
    ]
    turned = jnp.concatenate(turned, 0)
    span = 2 * BLOCK
    row = iota((BLOCK, span), 0)

    odd = lax.axis_index("reg") % 2
    for away, out in enumerate((near, far)):
        side = 1 - odd if away == 0 else odd

        def step(part, carry):
            named = lists[:, pl.ds(pl.multiple_of(part * span, span), span)]
            named = jnp.where(side == 0, named[:1], named[1:])
            block = lax.shift_right_logical(named, 7)
            lane = named & (BLOCK - 1)
            hot = jnp.where(row == jnp.broadcast_to(block, row.shape), 1.0, 0.0).astype(BF16)
            found = jnp.dot(
                turned, jnp.concatenate([hot, hot], 0), preferred_element_type=F32
            )
            here = row == jnp.broadcast_to(lane, row.shape)
            for axis in range(3):
                value = jnp.where(here, found[axis * BLOCK : (axis + 1) * BLOCK], 0.0)
                value = jnp.sum(value, axis=0, keepdims=True)
                for half in range(2):
                    out[pl.ds(axis * rows + 2 * part + half, 1), :] = value[
                        :, half * BLOCK : (half + 1) * BLOCK
                    ]
            return carry

        lax.fori_loop(0, rows // 2, step, 0, unroll=8)


def message_kernel(mine, second, third, halo_near, halo_far, _, near, far, dummy):
    dummy[...] = jnp.zeros(dummy.shape, F32)
    stride = mine.shape[0]
    half = halo_near.shape[0] // 2
    rows = near.shape[0] - half
    for halo, out in ((halo_near, near), (halo_far, far)):
        for index, group in enumerate((mine, second, third)):
            out[index * stride : (index + 1) * stride, :] = group[...]
        out[rows:, :BLOCK] = halo[:half, :]
        out[rows:, BLOCK:] = halo[half:, :]


def merged(parts):
    sub = iota((SUB, BLOCK), 0)
    for step in (4, 2, 1):
        low = (sub & step) == 0
        paired = []
        for first, second in zip(parts[:step], parts[step:]):
            away = jnp.where(low, second, first)
            back = pltpu.roll(away, step, 0)
            if step < SUB // 2:
                back = jnp.where(low, pltpu.roll(away, SUB - step, 0), back)
            paired.append(jnp.where(low, first, second) + back)
        parts = paired
    return parts[0]


def contact_kernel(
    partner, state, message_near, message_far, halo_near, halo_far, named, stiff, _, out, extended,
):
    tiles = state.shape[0] // 3
    rows = halo_near.shape[0] // 3
    blocks = tiles + 2 * rows
    base = message_near.shape[0] - 3 * rows // 2
    odd = lax.axis_index("reg") % 2
    sweeps = lax.axis_index("grp") % CORES == 0
    for axis in range(3):
        extended[axis * blocks : axis * blocks + tiles, :] = state[
            axis * tiles : (axis + 1) * tiles, :
        ]
    for message, halo, upper in (
        (message_near, halo_near, 1 - odd), (message_far, halo_far, odd)
    ):
        carried = jnp.concatenate([message[base:, :BLOCK], message[base:, BLOCK:]], 0)
        carried = jnp.where(sweeps, carried, halo[...])
        for axis in range(3):
            first = pl.multiple_of(axis * blocks + tiles + upper * rows, SUB)
            extended[pl.ds(first, rows), :] = carried[axis * rows : (axis + 1) * rows]

    def step(group, carry):
        first = pl.multiple_of(group * SUB, SUB)
        held = [extended[pl.ds(axis * blocks + first, SUB), :] for axis in range(3)]
        pulls = [[], [], []]
        for t in range(SUB):
            lanes = pl.ds(pl.multiple_of((first + t) * BLOCK, BLOCK), BLOCK)
            entry = named[:, lanes]
            weight = jnp.where(entry >= 0, stiff[:, lanes], 0.0)
            own = entry < BLOCK
            lane = entry & (BLOCK - 1)
            other = partner[first + t]
            for axis in range(3):
                mine = jnp.broadcast_to(held[axis][t : t + 1], entry.shape)
                theirs = extended[pl.ds(axis * blocks + other, 1), :]
                theirs = jnp.broadcast_to(theirs, entry.shape)
                met = jnp.where(own, lanes_of(mine, lane), lanes_of(theirs, lane))
                pulls[axis].append(weight * (mine - met))
        for axis in range(3):
            out[pl.ds(axis * tiles + first, SUB), :] = merged(pulls[axis])
        return carry

    lax.fori_loop(0, tiles // SUB, step, 0)


def shifted(plane):
    height, width = plane.shape
    row = iota((SUB, width), 0)
    column = iota((height, BLOCK), 1)
    above, below = pltpu.roll(plane, 1, 0), pltpu.roll(plane, height - 1, 0)
    left, right = pltpu.roll(plane, 1, 1), pltpu.roll(plane, width - 1, 1)
    above = jnp.concatenate([jnp.where(row == 0, 0.0, above[:SUB]), above[SUB:]], 0)
    below = jnp.concatenate([below[:-SUB], jnp.where(row == SUB - 1, 0.0, below[-SUB:])], 0)
    left = jnp.concatenate([jnp.where(column == 0, 0.0, left[:, :BLOCK]), left[:, BLOCK:]], 1)
    right = jnp.concatenate(
        [right[:, :-BLOCK], jnp.where(column == BLOCK - 1, 0.0, right[:, -BLOCK:])], 1
    )
    return above, below, left, right


def inverse_of(value):
    near = pl.reciprocal(value, approx=True)
    return near * (2.0 - value * near)


def placed(groups, tiles):
    parts = [halves_of(group[:tiles, :]) for group in groups]
    loads = jnp.concatenate([part[i] for i in range(2) for part in parts], 0)
    ids = jnp.concatenate([group[tiles : tiles + 1, :BLOCK] for group in groups], 1)
    ids = ids.astype(jnp.int32)

    def gathered(wanted):
        hot = jnp.where(wanted == jnp.broadcast_to(ids, wanted.shape), 1.0, 0.0).astype(BF16)
        total = jnp.dot(
            jnp.concatenate([hot, hot], 1), loads, preferred_element_type=F32
        )
        return total[:, :BLOCK], total[:, BLOCK:]

    return ids, gathered


def driven_of(early, late, planes):
    return lambda x: early[planes + x] if x < HEAD else late[x - HEAD]


def coefficients(gathered, tiles, first, full, driven_at, constant, factor, turned, present):
    planes, height, width = constant.shape
    zones = width // BLOCK
    shape = (zones * height, 3 * tiles)
    line = iota(shape, 0)
    block = (line % height) * zones + line // height + first * zones

    for x in range(planes):
        solid, drag = gathered(block + x * (full * zones))
        at = x if turned is None else jnp.where(turned, planes - 1 - x, x)
        voids = 1.0 + solid
        scale = inverse_of(6.0 + (drag + 1.0) * voids)
        if present is not None:
            scale = jnp.where(present, scale, 0.0)
        inverse = voids * scale
        for zone in range(zones):
            lanes = slice(zone * BLOCK, (zone + 1) * BLOCK)
            rows = slice(zone * height, (zone + 1) * height)
            driving = driven_at(x)[:, lanes] + solid[rows]
            constant[at, :, lanes] = driving * inverse[rows]
            factor[at, :, lanes] = scale[rows]


def own_kernel(
    full, mine, second, third, early, late, _message, _near, _far, _partner, constant, factor, weight, picks
):
    tiles = weight.shape[0]
    planes, height, width = constant.shape
    place = Place(full, height)
    zones = width // BLOCK
    ids, gathered = placed((mine, second, third), tiles)
    coefficients(
        gathered, tiles, place.first, full, driven_of(early, late, planes), constant, factor,
        place.even, None,
    )
    turned = [
        jnp.transpose(
            jnp.broadcast_to(ids[:, i * tiles : (i + 1) * tiles], (BLOCK, tiles)).astype(F32)
        ).astype(jnp.int32)
        for i in range(3)
    ]
    solid, drag = gathered(jnp.concatenate([turned[0]] * 3, 1))
    weight[...] = 1.0 / (1.0 / (1.0 + solid) + drag)
    for i in range(3):
        block = turned[i]
        line, zone = block // zones, block % zones
        x, y = line // full, line % full
        row = (x * zones + zone) * height + y - place.first
        held = y // place.own_rows == jnp.where(place.sweeps, place.half, -1)
        row = jnp.concatenate([jnp.where(held, row, -1)] * (picks.shape[1] // BLOCK), 1)
        hot = jnp.where(row == iota(row.shape, 1), 1.0, 0.0).astype(BF16)
        picks[i * tiles : (i + 1) * tiles, :] = hot


def sweep(source, target, coefficient, start, stop):
    def plane(at, carry):
        above, below, left, right = shifted(source[at])
        around = source[at - 1] + source[at + 1] + above + below + left + right
        constant, factor = coefficient(at)
        target[at] = constant + factor * around
        return carry

    lax.fori_loop(start, stop, plane, 0, unroll=4)


def deposits_of(message, tiles):
    stride = tiles + SUB
    return placed([message.at[i * stride : (i + 1) * stride] for i in range(3)], tiles)[1]


def near_kernel(
    full, tiles, message, pressure, near, near_late, beyond, own_constant, own_factor, kept_even, kept_odd, constant, factor, old, new,
):
    planes, height, width = own_constant.shape
    place = Place(full, height)
    rim = planes + 1
    coefficients(
        deposits_of(message, tiles), tiles, place.first, full,
        driven_of(near, near_late, planes), constant, factor, place.even, jnp.where(place.odd, place.lower, place.upper),
    )
    old[0] = beyond[...]
    for x in range(planes):
        at = jnp.where(place.even, planes - 1 - x, x)
        old[1 + x] = near[at]
        old[rim + x] = pressure[at]
    buffers = (old, new)
    for index in range(planes):
        source, target = buffers[index % 2], buffers[(index + 1) % 2]
        sweep(source, target, lambda at: (constant[at - 1], factor[at - 1]), 1 + index, rim)
        sweep(
            source, target, lambda at: (own_constant[at - rim], own_factor[at - rim]),
            rim, 2 * planes - index,
        )
    kept_even[...] = old[planes : 2 * planes]
    kept_odd[...] = new[planes : 2 * planes]


def far_kernel(
    full, tiles, picks, message, pressure, far, far_late, outer, own_constant, own_factor, kept_even, kept_odd,
    out, pieces, constant, factor, old, new, fields,
):
    planes, height, width = own_constant.shape
    zones = width // BLOCK
    place = Place(full, height)
    rim = planes + 1
    coefficients(
        deposits_of(message, tiles), tiles, place.first, full,
        driven_of(far, far_late, planes), constant, factor, place.even, jnp.where(place.odd, place.upper, place.lower),
    )
    old[planes : 2 * planes] = kept_even[...]
    new[planes : 2 * planes] = kept_odd[...]
    old[2 * planes] = pressure[jnp.where(place.even, 0, planes - 1)]
    for x in range(planes):
        at = jnp.where(place.even, planes - 1 - x, x)
        old[rim + planes + x] = far[at]
    old[rim + 2 * planes] = outer[...]
    buffers = (old, new)
    edge = rim + planes
    for index in range(planes):
        source, target = buffers[index % 2], buffers[(index + 1) % 2]
        sweep(
            source, target, lambda at: (own_constant[at - rim], own_factor[at - rim]),
            2 * planes - index, edge,
        )
        sweep(
            source, target, lambda at: (constant[at - edge], factor[at - edge]),
            edge, edge + planes - index,
        )
    last = buffers[planes % 2]
    way = jnp.where(place.even, -0.5, 0.5)

    def gradient(x, carry):
        at = rim + x
        above, below, left, right = shifted(last[at])
        grads = (way * (last[at + 1] - last[at - 1]), 0.5 * (below - above), 0.5 * (right - left))
        line = jnp.where(place.even, planes - 1 - x, x) * zones
        for zone in range(zones):
            first = pl.multiple_of((line + zone) * height, SUB)
            for axis, grad in enumerate(grads):
                fields[pl.ds(first, height), axis * BLOCK : (axis + 1) * BLOCK] = (
                    grad[:, zone * BLOCK : (zone + 1) * BLOCK]
                )
        return carry

    lax.fori_loop(0, planes, gradient, 0, unroll=4)
    pieces[...] = jnp.concatenate(halves_of(fields[...]), 1)
    out[...] = picked_rows(picks, 3 - across_set(), tiles, pieces)


def across_set():
    return jnp.where(lax.axis_index("grp") == 0, 1, 2)


def picked_rows(picks, chosen, tiles, pieces):
    hot = picks[pl.ds(pl.multiple_of(chosen * tiles, tiles), tiles), :]
    total = jnp.dot(hot, pieces[...], preferred_element_type=F32)
    return total[:, : 3 * BLOCK] + total[:, 3 * BLOCK :]


def pick_kernel(own, picks, pieces, out):
    chosen = 0 if own else across_set()
    out[...] = picked_rows(picks, chosen, out.shape[0], pieces)


def final_kernel(
    count, grads_a, grads_b, grads_c, grads_d, weight, contact, vel, vol, drag, cell, out,
):
    tiles = cell.shape[0]
    cells = cell[...]
    heft = lanes_of(weight[...], cells)
    slot = iota(cells.shape, 0) * BLOCK + iota(cells.shape, 1)
    live = slot < count[0]
    volume = vol[...]
    push = TIME_STEP / volume
    for axis in range(3):
        lanes = slice(axis * BLOCK, (axis + 1) * BLOCK)
        gradient = grads_a[:, lanes] + grads_b[:, lanes] + (grads_c[:, lanes] + grads_d[:, lanes])
        gradient = lanes_of(gradient, cells)
        own = jnp.concatenate(
            [vel[axis : axis + 1, t * BLOCK : (t + 1) * BLOCK] for t in range(tiles)], 0
        )
        fluid = -gradient * heft
        force = contact[axis * tiles : (axis + 1) * tiles, :] - volume * gradient
        force = force + drag[...] * (fluid - own)
        new = jnp.where(live, own + force * push, 0.0)
        for t in range(tiles):
            out[axis : axis + 1, t * BLOCK : (t + 1) * BLOCK] = new[t : t + 1, :]


def on_device(
    grain_pos,
    grain_vel,
    grain_vol,
    drag_coef,
    grain_count,
    contact_rows,
    contact_stiff,
    partner_block,
    halo_list,
    grain_cell,
    tile_cell_block,
    pressure_old,
    pressure_source,
    solid_old,
):
    groups, regions = lax.axis_size("grp"), lax.axis_size("reg")
    holding = groups - 1
    halves = groups // CORES
    slots = grain_pos.shape[1]
    tiles = slots // BLOCK
    planes, full, width = pressure_old.shape
    assert planes == ITERS
    own_rows = full // halves
    height = min(full, own_rows + SUB * min(2, halves - 1))
    owners = range(0, groups, CORES)
    holders = range(holding)

    def send(value, pairs):
        flat = [(a[0] * regions + a[1], b[0] * regions + b[1]) for a, b in pairs]
        return lax.ppermute(value, ("grp", "reg"), flat)

    def along_reg(value, members, goes, core=0):
        pairs = [
            ((g + core, r), (g, r + goes[r % 2]))
            for g in members
            for r in range(regions)
            if 0 <= r + goes[r % 2] < regions
        ]
        return send(value, pairs)

    def along_grp(value, step, members):
        pairs = [((g, r), ((g + step) % holding, r)) for g in members for r in range(regions)]
        return send(value, pairs)

    count = grain_count
    cell = grain_cell.reshape(tiles, BLOCK)
    vol = grain_vol.reshape(tiles, BLOCK)
    drag = drag_coef.reshape(tiles, BLOCK)
    ids = tile_cell_block.reshape(1, tiles)
    field_bytes = 4 * planes * height * width

    field = shaped(planes, height, width)
    plane = shaped(height, width)
    small = shaped(SUB, BLOCK)
    early, late, ends, inner = call(
        window_kernel,
        (
            shaped(planes + HEAD, height, width), shaped(planes - HEAD, height, width), plane,
            plane,
        ),
        [HBM] * 3, (pressure_old, pressure_source, solid_old),
        [pltpu.VMEM((planes, height, width), F32)] * 3
        + [pltpu.SemaphoreType.DMA((5 * planes + 2,))],
        flops=field_bytes, size=6 * field_bytes, limit=61_950_000, place=HBM,
    )
    near = along_reg(early, owners, (1, -1), core=1)
    near_late = along_reg(late, owners, (1, -1), core=1)
    beyond = along_reg(ends, owners, (-2, 2), core=1)
    mine, after_deposit = call(
        deposit_kernel, (shaped(tiles + SUB, 2 * BLOCK), small), [SMEM] + [VMEM] * 4,
        (count, cell, vol, drag, ids), flops=2 * 32 * 48 * 65536, size=5 * 4 * slots,
    )
    second = along_grp(mine, 1, holders)
    third = along_grp(mine, 2, holders)
    rows = halo_list.shape[1] // BLOCK
    halo = shaped(3 * rows, BLOCK)
    state, halo_near, halo_far, after_halo = call(
        halo_kernel, (shaped(3 * tiles, BLOCK), halo, halo, small),
        [VMEM] * 4, (grain_pos, grain_vel, halo_list, after_deposit), flops=slots,
        size=4 * 4 * 3 * slots,
    )
    others = [g for g in holders if g not in owners]
    came_near = along_reg(halo_near, others, (1, -1))
    came_far = along_reg(halo_far, others, (-1, 1))
    far, after_forward = call(
        forward_kernel, (shaped(planes + HEAD, height, width), small), [VMEM] * 5,
        (near, after_halo, second, third, beyond), size=5 * field_bytes,
    )
    far = along_reg(far, owners, (2, -2))
    far_late = along_reg(near_late, owners, (2, -2))
    outer = along_reg(inner, owners, (2, -2), core=1)
    message = shaped(holding * (tiles + SUB) + 3 * rows // 2, 2 * BLOCK)
    message_near, message_far, after_message = call(
        message_kernel, (message, message, small), [VMEM] * 6,
        (mine, second, third, halo_near, halo_far, after_forward), size=8 * 2 * BLOCK * 500,
    )
    message_near = along_reg(message_near, owners, (1, -1))
    message_far = along_reg(message_far, owners, (-1, 1))
    constant, factor, weight, picks = call(
        functools.partial(own_kernel, full),
        (
            field, field, shaped(tiles, BLOCK),
            jax.ShapeDtypeStruct((3 * tiles, planes * height * width // BLOCK), BF16),
        ),
        [VMEM] * 8 + [SMEM],
        (mine, second, third, early, late, after_message, came_near, came_far, partner_block),
        flops=planes * height * 4 * 384 * 256 * 6, size=9 * field_bytes,
    )
    window_of = lambda count: pltpu.VMEM((count, height, width), F32)
    kept_even, kept_odd = call(
        functools.partial(near_kernel, full, tiles), (field, field), [VMEM] * 7,
        (message_near, early, near, near_late, beyond, constant, factor),
        [window_of(planes)] * 2 + [window_of(2 * planes + 1)] * 2,
        flops=planes * height * 4 * 384 * 256 * 6, size=9 * field_bytes,
    )
    grads = shaped(tiles, 3 * BLOCK)
    cells_held = planes * height * width // BLOCK
    grads_between, pieces = call(
        functools.partial(far_kernel, full, tiles),
        (grads, jax.ShapeDtypeStruct((cells_held, 6 * BLOCK), BF16)), [VMEM] * 10,
        (picks, message_far, early, far, far_late, outer, constant, factor, kept_even, kept_odd),
        [window_of(planes)] * 2
        + [window_of(3 * planes + 2)] * 2
        + [pltpu.VMEM((cells_held, 3 * BLOCK), F32)],
        flops=planes * height * 4 * 384 * 256 * 6, size=9 * field_bytes,
    )
    ends_of = lambda source, target: [((source, r), (target, r)) for r in range(regions)]
    low, high, between = 0, CORES, 1
    came_low = send(grads_between, ends_of(low, between))
    came_high = send(grads_between, ends_of(high, between))
    pick = lambda own: call(
        functools.partial(pick_kernel, own), grads, [VMEM] * 2, (picks, pieces),
        flops=slots, size=slots,
    )
    came_across = send(pick(False), ends_of(low, high) + ends_of(high, low))
    grads_a = pick(True)
    contact = call(
        contact_kernel, shaped(3 * tiles, BLOCK), [SMEM] + [VMEM] * 7 + [ANY],
        (
            partner_block, state, message_near, message_far, came_near, came_far, contact_rows,
            contact_stiff, grads_a,
        ),
        [pltpu.VMEM((3 * (tiles + 2 * rows), BLOCK), F32)],
        flops=60 * 8 * slots, size=4 * 20 * slots,
    )
    return call(
        final_kernel, shaped(3, slots), [SMEM] + [VMEM] * 10,
        (
            count, grads_a, came_across, came_low, came_high, weight, contact, grain_vel, vol, drag,
            cell,
        ),
        flops=60 * slots, size=4 * 20 * slots,
    )


def solution(mesh):
    in_specs = (
        P(None, ("grp", "reg")),
        P(None, ("grp", "reg")),
        P(("grp", "reg")),
        P(("grp", "reg")),
        P(("grp", "reg")),
        P(None, ("grp", "reg")),
        P(None, ("grp", "reg")),
        P(("grp", "reg")),
        P(None, ("grp", "reg")),
        P(("grp", "reg")),
        P(("grp", "reg")),
        P("reg", None, None),
        P("reg", None, None),
        P("reg", None, None),
    )
    out_specs = P(None, ("grp", "reg"))
    return jax.shard_map(
        on_device, mesh=mesh, in_specs=in_specs, out_specs=out_specs, check_vma=False
    )
```

```python
import functools

import jax
import jax.numpy as jnp
from jax import lax
from jax.experimental import pallas as pl
from jax.experimental.pallas import tpu as pltpu
from jax.sharding import PartitionSpec as P

BLOCK = 128
SUB = 8
CORES = 2
ITERS = 4
HEAD = 1
SPRING = 1.0
DAMPING = 0.5
TIME_STEP = 0.5

VMEM = pl.BlockSpec(memory_space=pltpu.VMEM)
SMEM = pl.BlockSpec(memory_space=pltpu.SMEM)
ANY = pl.BlockSpec(memory_space=pl.ANY)
HBM = pl.BlockSpec(memory_space=pltpu.HBM)
F32 = jnp.float32
BF16 = jnp.bfloat16


def iota(shape, dim):
    return lax.broadcasted_iota(jnp.int32, shape, dim)


def shaped(*dims):
    return jax.ShapeDtypeStruct(dims, F32)


def call(kernel, outs, specs, args, scratch=(), flops=0, size=0, limit=40_000_000, place=VMEM):
    return pl.pallas_call(
        kernel,
        out_shape=outs,
        in_specs=specs,
        out_specs=jax.tree.map(lambda _: place, outs),
        scratch_shapes=list(scratch),
        compiler_params=pltpu.CompilerParams(vmem_limit_bytes=limit),
        cost_estimate=pl.CostEstimate(flops=flops, bytes_accessed=size, transcendentals=0),
    )(*args)


class Place:
    def __init__(self, full, height):
        groups, regions = lax.axis_size("grp"), lax.axis_size("reg")
        self.group, region = lax.axis_index("grp"), lax.axis_index("reg")
        self.half = self.group // CORES
        self.own_rows = full // (groups // CORES)
        first = jnp.clip(self.half * self.own_rows - SUB, 0, full - height)
        self.first = pl.multiple_of(first, SUB)
        self.sweeps = self.group % CORES == 0
        self.parity = region % 2
        self.odd, self.even = self.parity == 1, self.parity == 0
        self.lower, self.upper = region > 0, region < regions - 1


def lanes_of(source, index):
    return jnp.take_along_axis(source, index, axis=1, mode="promise_in_bounds")


def halves_of(value):
    high = value.astype(BF16)
    return high, (value - high.astype(F32)).astype(BF16)


def window_kernel(
    pressure_old, source, solid_before, early, late, ends, pressure, driven, solid, sems
):
    planes, height, _ = solid.shape
    place = Place(pressure_old.shape[1], height)
    rows = pl.ds(place.first, height)
    used = []

    def copy(whole, part):
        used.append(None)
        return pltpu.make_async_copy(whole, part, sems.at[len(used) - 1])

    fetched = [
        [copy(whole.at[x, rows, :], part.at[x]) for x in range(planes)]
        for whole, part in ((pressure_old, pressure), (source, driven), (solid_before, solid))
    ]
    stored = [copy(pressure.at[x], early.at[x]) for x in range(planes)]
    for x in range(planes):
        stored.append(copy(driven.at[x], early.at[planes + x] if x < HEAD else late.at[x - HEAD]))
    stored.append(copy(pressure.at[place.parity * (planes - 1)], ends))
    for x in range(planes):
        for part in fetched:
            part[x].start()
    for x in range(planes):
        fetched[0][x].wait()
        stored[x].start()
        fetched[1][x].wait()
        fetched[2][x].wait()
        driven[x] = driven[x] - solid[x]
        stored[planes + x].start()
    stored[-1].start()
    for one in stored:
        one.wait()


def forward_kernel(near, early, _halo, _second, _third, _beyond, out, dummy):
    dummy[...] = jnp.zeros(dummy.shape, F32)
    count = near.shape[0]
    out[:count] = near[...]
    end = (1 - lax.axis_index("reg") % 2) * (count - HEAD - 1)
    out[count] = early[end]


def deposit_kernel(count, cell, vol, drag, ids, out, dummy):
    dummy[...] = jnp.zeros(dummy.shape, F32)
    tiles = cell.shape[0]
    sub = iota((SUB, BLOCK), 0)
    rows_c = iota((BLOCK, BLOCK), 0)
    even = sub % 2 == 0
    low_pair = sub % 4 < 2

    def step(group, carry):
        first = pl.multiple_of(group * SUB, SUB)
        slot = (first + sub) * BLOCK + iota((SUB, BLOCK), 1)
        live = slot < count[0]
        cells = cell[pl.ds(first, SUB), :]
        parts = halves_of(jnp.where(live, vol[pl.ds(first, SUB), :], 0.0)) + halves_of(
            jnp.where(live, drag[pl.ds(first, SUB), :], 0.0)
        )
        parts = [part.astype(F32) for part in parts]
        left = jnp.concatenate([jnp.where(even, part, 0.0) for part in parts], 0)
        right = jnp.concatenate([jnp.where(even, 0.0, part) for part in parts], 0)
        loads = jnp.concatenate([left, right], 1).astype(BF16)
        sums = [jnp.zeros((SUB, BLOCK), F32), jnp.zeros((SUB, BLOCK), F32)]
        for quad in range(SUB // 4):
            hot = [
                jnp.where(
                    rows_c == jnp.broadcast_to(cells[t : t + 1, :], (BLOCK, BLOCK)), 1.0, 0.0
                ).astype(BF16)
                for t in range(4 * quad, 4 * quad + 4)
            ]
            picked = jnp.concatenate(
                [jnp.concatenate(hot[:2], 1), jnp.concatenate(hot[2:], 1)], 0
            )
            placed = lax.dot_general(
                loads, picked, (((1,), (1,)), ((), ())), preferred_element_type=F32
            )
            for field in range(2):
                base = field * 2 * SUB
                total = placed[base : base + SUB] + placed[base + SUB : base + 2 * SUB]
                chosen = jnp.where(low_pair, total[:, :BLOCK], total[:, BLOCK:])
                sums[field] = jnp.where(sub // 4 == quad, chosen, sums[field])
        out[pl.ds(first, SUB), :BLOCK] = sums[0]
        out[pl.ds(first, SUB), BLOCK:] = sums[1]
        return carry

    lax.fori_loop(0, tiles // SUB, step, 0, unroll=4)
    out[tiles : tiles + SUB, :BLOCK] = jnp.broadcast_to(ids[...].astype(F32), (SUB, BLOCK))
    out[tiles : tiles + SUB, BLOCK:] = jnp.zeros((SUB, BLOCK), F32)


def halo_kernel(pos, vel, lists, _, state, near, far, dummy):
    dummy[...] = jnp.zeros(dummy.shape, F32)
    tiles = pos.shape[1] // BLOCK
    rows = lists.shape[1] // BLOCK
    for tile in range(tiles):
        lanes = slice(tile * BLOCK, (tile + 1) * BLOCK)
        mixed = SPRING * pos[:, lanes] - DAMPING * vel[:, lanes]
        for axis in range(3):
            state[axis * tiles + tile : axis * tiles + tile + 1, :] = mixed[axis : axis + 1]
    turned = [
        jnp.concatenate(halves_of(jnp.transpose(state[axis * tiles : (axis + 1) * tiles, :])), 1)
        for axis in range(3)
    ]
    turned = jnp.concatenate(turned, 0)
    span = 2 * BLOCK
    row = iota((BLOCK, span), 0)

    odd = lax.axis_index("reg") % 2
    for away, out in enumerate((near, far)):
        side = 1 - odd if away == 0 else odd

        def step(part, carry):
            named = lists[:, pl.ds(pl.multiple_of(part * span, span), span)]
            named = jnp.where(side == 0, named[:1], named[1:])
            block = lax.shift_right_logical(named, 7)
            lane = named & (BLOCK - 1)
            hot = jnp.where(row == jnp.broadcast_to(block, row.shape), 1.0, 0.0).astype(BF16)
            found = jnp.dot(
                turned, jnp.concatenate([hot, hot], 0), preferred_element_type=F32
            )
            here = row == jnp.broadcast_to(lane, row.shape)
            for axis in range(3):
                value = jnp.where(here, found[axis * BLOCK : (axis + 1) * BLOCK], 0.0)
                value = jnp.sum(value, axis=0, keepdims=True)
                for half in range(2):
                    out[pl.ds(axis * rows + 2 * part + half, 1), :] = value[
                        :, half * BLOCK : (half + 1) * BLOCK
                    ]
            return carry

        lax.fori_loop(0, rows // 2, step, 0, unroll=8)


def message_kernel(mine, second, third, halo_near, halo_far, _, near, far, dummy):
    dummy[...] = jnp.zeros(dummy.shape, F32)
    stride = mine.shape[0]
    half = halo_near.shape[0] // 2
    rows = near.shape[0] - half
    for halo, out in ((halo_near, near), (halo_far, far)):
        for index, group in enumerate((mine, second, third)):
            out[index * stride : (index + 1) * stride, :] = group[...]
        out[rows:, :BLOCK] = halo[:half, :]
        out[rows:, BLOCK:] = halo[half:, :]


def merged(parts):
    sub = iota((SUB, BLOCK), 0)
    for step in (4, 2, 1):
        low = (sub & step) == 0
        paired = []
        for first, second in zip(parts[:step], parts[step:]):
            away = jnp.where(low, second, first)
            back = pltpu.roll(away, step, 0)
            if step < SUB // 2:
                back = jnp.where(low, pltpu.roll(away, SUB - step, 0), back)
            paired.append(jnp.where(low, first, second) + back)
        parts = paired
    return parts[0]


def contact_kernel(
    partner, state, message_near, message_far, halo_near, halo_far, named, stiff, _, out, extended,
):
    tiles = state.shape[0] // 3
    rows = halo_near.shape[0] // 3
    blocks = tiles + 2 * rows
    base = message_near.shape[0] - 3 * rows // 2
    odd = lax.axis_index("reg") % 2
    sweeps = lax.axis_index("grp") % CORES == 0
    for axis in range(3):
        extended[axis * blocks : axis * blocks + tiles, :] = state[
            axis * tiles : (axis + 1) * tiles, :
        ]
    for message, halo, upper in (
        (message_near, halo_near, 1 - odd), (message_far, halo_far, odd)
    ):
        carried = jnp.concatenate([message[base:, :BLOCK], message[base:, BLOCK:]], 0)
        carried = jnp.where(sweeps, carried, halo[...])
        for axis in range(3):
            first = pl.multiple_of(axis * blocks + tiles + upper * rows, SUB)
            extended[pl.ds(first, rows), :] = carried[axis * rows : (axis + 1) * rows]

    def step(group, carry):
        first = pl.multiple_of(group * SUB, SUB)
        held = [extended[pl.ds(axis * blocks + first, SUB), :] for axis in range(3)]
        pulls = [[], [], []]
        for t in range(SUB):
            lanes = pl.ds(pl.multiple_of((first + t) * BLOCK, BLOCK), BLOCK)
            entry = named[:, lanes]
            weight = jnp.where(entry >= 0, stiff[:, lanes], 0.0)
            own = entry < BLOCK
            lane = entry & (BLOCK - 1)
            other = partner[first + t]
            for axis in range(3):
                mine = jnp.broadcast_to(held[axis][t : t + 1], entry.shape)
                theirs = extended[pl.ds(axis * blocks + other, 1), :]
                theirs = jnp.broadcast_to(theirs, entry.shape)
                met = jnp.where(own, lanes_of(mine, lane), lanes_of(theirs, lane))
                pulls[axis].append(weight * (mine - met))
        for axis in range(3):
            out[pl.ds(axis * tiles + first, SUB), :] = merged(pulls[axis])
        return carry

    lax.fori_loop(0, tiles // SUB, step, 0)


def shifted(plane):
    height, width = plane.shape
    row = iota((SUB, width), 0)
    column = iota((height, BLOCK), 1)
    above, below = pltpu.roll(plane, 1, 0), pltpu.roll(plane, height - 1, 0)
    left, right = pltpu.roll(plane, 1, 1), pltpu.roll(plane, width - 1, 1)
    above = jnp.concatenate([jnp.where(row == 0, 0.0, above[:SUB]), above[SUB:]], 0)
    below = jnp.concatenate([below[:-SUB], jnp.where(row == SUB - 1, 0.0, below[-SUB:])], 0)
    left = jnp.concatenate([jnp.where(column == 0, 0.0, left[:, :BLOCK]), left[:, BLOCK:]], 1)
    right = jnp.concatenate(
        [right[:, :-BLOCK], jnp.where(column == BLOCK - 1, 0.0, right[:, -BLOCK:])], 1
    )
    return above, below, left, right


def inverse_of(value):
    near = pl.reciprocal(value, approx=True)
    return near * (2.0 - value * near)


def placed(groups, tiles):
    parts = [halves_of(group[:tiles, :]) for group in groups]
    loads = jnp.concatenate([part[i] for i in range(2) for part in parts], 0)
    ids = jnp.concatenate([group[tiles : tiles + 1, :BLOCK] for group in groups], 1)
    ids = ids.astype(jnp.int32)

    def gathered(wanted):
        hot = jnp.where(wanted == jnp.broadcast_to(ids, wanted.shape), 1.0, 0.0).astype(BF16)
        total = jnp.dot(
            jnp.concatenate([hot, hot], 1), loads, preferred_element_type=F32
        )
        return total[:, :BLOCK], total[:, BLOCK:]

    return ids, gathered


def driven_of(early, late, planes):
    return lambda x: early[planes + x] if x < HEAD else late[x - HEAD]


def coefficients(gathered, tiles, first, full, driven_at, constant, factor, turned, present):
    planes, height, width = constant.shape
    zones = width // BLOCK
    shape = (zones * height, 3 * tiles)
    line = iota(shape, 0)
    block = (line % height) * zones + line // height + first * zones

    for x in range(planes):
        solid, drag = gathered(block + x * (full * zones))
        at = x if turned is None else jnp.where(turned, planes - 1 - x, x)
        voids = 1.0 + solid
        scale = inverse_of(6.0 + (drag + 1.0) * voids)
        if present is not None:
            scale = jnp.where(present, scale, 0.0)
        inverse = voids * scale
        for zone in range(zones):
            lanes = slice(zone * BLOCK, (zone + 1) * BLOCK)
            rows = slice(zone * height, (zone + 1) * height)
            driving = driven_at(x)[:, lanes] + solid[rows]
            constant[at, :, lanes] = driving * inverse[rows]
            factor[at, :, lanes] = scale[rows]


def own_kernel(
    full, mine, second, third, early, late, _message, _near, _far, _partner, constant, factor, weight, picks
):
    tiles = weight.shape[0]
    planes, height, width = constant.shape
    place = Place(full, height)
    zones = width // BLOCK
    ids, gathered = placed((mine, second, third), tiles)
    coefficients(
        gathered, tiles, place.first, full, driven_of(early, late, planes), constant, factor,
        place.even, None,
    )
    turned = [
        jnp.transpose(
            jnp.broadcast_to(ids[:, i * tiles : (i + 1) * tiles], (BLOCK, tiles)).astype(F32)
        ).astype(jnp.int32)
        for i in range(3)
    ]
    solid, drag = gathered(jnp.concatenate([turned[0]] * 3, 1))
    weight[...] = 1.0 / (1.0 / (1.0 + solid) + drag)
    for i in range(3):
        block = turned[i]
        line, zone = block // zones, block % zones
        x, y = line // full, line % full
        row = (x * zones + zone) * height + y - place.first
        held = y // place.own_rows == jnp.where(place.sweeps, place.half, -1)
        row = jnp.concatenate([jnp.where(held, row, -1)] * (picks.shape[1] // BLOCK), 1)
        hot = jnp.where(row == iota(row.shape, 1), 1.0, 0.0).astype(BF16)
        picks[i * tiles : (i + 1) * tiles, :] = hot


def sweep(source, target, coefficient, start, stop):
    def plane(at, carry):
        above, below, left, right = shifted(source[at])
        around = source[at - 1] + source[at + 1] + above + below + left + right
        constant, factor = coefficient(at)
        target[at] = constant + factor * around
        return carry

    lax.fori_loop(start, stop, plane, 0, unroll=4)


def deposits_of(message, tiles):
    stride = tiles + SUB
    return placed([message.at[i * stride : (i + 1) * stride] for i in range(3)], tiles)[1]


def near_kernel(
    full, tiles, message, pressure, near, near_late, beyond, own_constant, own_factor, kept_even, kept_odd, constant, factor, old, new,
):
    planes, height, width = own_constant.shape
    place = Place(full, height)
    rim = planes + 1
    coefficients(
        deposits_of(message, tiles), tiles, place.first, full,
        driven_of(near, near_late, planes), constant, factor, place.even, jnp.where(place.odd, place.lower, place.upper),
    )
    old[0] = beyond[...]
    for x in range(planes):
        at = jnp.where(place.even, planes - 1 - x, x)
        old[1 + x] = near[at]
        old[rim + x] = pressure[at]
    buffers = (old, new)
    for index in range(planes):
        source, target = buffers[index % 2], buffers[(index + 1) % 2]
        sweep(source, target, lambda at: (constant[at - 1], factor[at - 1]), 1 + index, rim)
        sweep(
            source, target, lambda at: (own_constant[at - rim], own_factor[at - rim]),
            rim, 2 * planes - index,
        )
    kept_even[...] = old[planes : 2 * planes]
    kept_odd[...] = new[planes : 2 * planes]


def far_kernel(
    full, tiles, picks, message, pressure, far, far_late, own_constant, own_factor, kept_even, kept_odd,
    out, pieces, constant, factor, old, new, fields,
):
    planes, height, width = own_constant.shape
    zones = width // BLOCK
    place = Place(full, height)
    rim = planes + 1
    coefficients(
        deposits_of(message, tiles), tiles, place.first, full,
        driven_of(far, far_late, planes), constant, factor, place.even, jnp.where(place.odd, place.upper, place.lower),
    )
    old[planes : 2 * planes] = kept_even[...]
    new[planes : 2 * planes] = kept_odd[...]
    old[2 * planes] = pressure[jnp.where(place.even, 0, planes - 1)]
    for x in range(planes):
        at = jnp.where(place.even, planes - 1 - x, x)
        old[rim + planes + x] = far[at]
    old[rim + 2 * planes] = far[planes + HEAD]
    buffers = (old, new)
    edge = rim + planes
    for index in range(planes):
        source, target = buffers[index % 2], buffers[(index + 1) % 2]
        sweep(
            source, target, lambda at: (own_constant[at - rim], own_factor[at - rim]),
            2 * planes - index, edge,
        )
        sweep(
            source, target, lambda at: (constant[at - edge], factor[at - edge]),
            edge, edge + planes - index,
        )
    last = buffers[planes % 2]
    way = jnp.where(place.even, -0.5, 0.5)

    def gradient(x, carry):
        at = rim + x
        above, below, left, right = shifted(last[at])
        grads = (way * (last[at + 1] - last[at - 1]), 0.5 * (below - above), 0.5 * (right - left))
        line = jnp.where(place.even, planes - 1 - x, x) * zones
        for zone in range(zones):
            first = pl.multiple_of((line + zone) * height, SUB)
            for axis, grad in enumerate(grads):
                fields[pl.ds(first, height), axis * BLOCK : (axis + 1) * BLOCK] = (
                    grad[:, zone * BLOCK : (zone + 1) * BLOCK]
                )
        return carry

    lax.fori_loop(0, planes, gradient, 0, unroll=4)
    pieces[...] = jnp.concatenate(halves_of(fields[...]), 1)
    out[...] = picked_rows(picks, 3 - across_set(), tiles, pieces)


def across_set():
    return jnp.where(lax.axis_index("grp") == 0, 1, 2)


def picked_rows(picks, chosen, tiles, pieces):
    hot = picks[pl.ds(pl.multiple_of(chosen * tiles, tiles), tiles), :]
    total = jnp.dot(hot, pieces[...], preferred_element_type=F32)
    return total[:, : 3 * BLOCK] + total[:, 3 * BLOCK :]


def pick_kernel(own, picks, pieces, out):
    chosen = 0 if own else across_set()
    out[...] = picked_rows(picks, chosen, out.shape[0], pieces)


def final_kernel(
    count, grads_a, grads_b, grads_c, grads_d, weight, contact, vel, vol, drag, cell, out,
):
    tiles = cell.shape[0]
    cells = cell[...]
    heft = lanes_of(weight[...], cells)
    slot = iota(cells.shape, 0) * BLOCK + iota(cells.shape, 1)
    live = slot < count[0]
    volume = vol[...]
    push = TIME_STEP / volume
    for axis in range(3):
        lanes = slice(axis * BLOCK, (axis + 1) * BLOCK)
        gradient = grads_a[:, lanes] + grads_b[:, lanes] + (grads_c[:, lanes] + grads_d[:, lanes])
        gradient = lanes_of(gradient, cells)
        own = jnp.concatenate(
            [vel[axis : axis + 1, t * BLOCK : (t + 1) * BLOCK] for t in range(tiles)], 0
        )
        fluid = -gradient * heft
        force = contact[axis * tiles : (axis + 1) * tiles, :] - volume * gradient
        force = force + drag[...] * (fluid - own)
        new = jnp.where(live, own + force * push, 0.0)
        for t in range(tiles):
            out[axis : axis + 1, t * BLOCK : (t + 1) * BLOCK] = new[t : t + 1, :]


def on_device(
    grain_pos,
    grain_vel,
    grain_vol,
    drag_coef,
    grain_count,
    contact_rows,
    contact_stiff,
    partner_block,
    halo_list,
    grain_cell,
    tile_cell_block,
    pressure_old,
    pressure_source,
    solid_old,
):
    groups, regions = lax.axis_size("grp"), lax.axis_size("reg")
    holding = groups - 1
    halves = groups // CORES
    slots = grain_pos.shape[1]
    tiles = slots // BLOCK
    planes, full, width = pressure_old.shape
    assert planes == ITERS
    own_rows = full // halves
    height = min(full, own_rows + SUB * min(2, halves - 1))
    owners = range(0, groups, CORES)
    holders = range(holding)

    def send(value, pairs):
        flat = [(a[0] * regions + a[1], b[0] * regions + b[1]) for a, b in pairs]
        return lax.ppermute(value, ("grp", "reg"), flat)

    def along_reg(value, members, goes, core=0):
        pairs = [
            ((g + core, r), (g, r + goes[r % 2]))
            for g in members
            for r in range(regions)
            if 0 <= r + goes[r % 2] < regions
        ]
        return send(value, pairs)

    def along_grp(value, step, members):
        pairs = [((g, r), ((g + step) % holding, r)) for g in members for r in range(regions)]
        return send(value, pairs)

    count = grain_count
    cell = grain_cell.reshape(tiles, BLOCK)
    vol = grain_vol.reshape(tiles, BLOCK)
    drag = drag_coef.reshape(tiles, BLOCK)
    ids = tile_cell_block.reshape(1, tiles)
    field_bytes = 4 * planes * height * width

    field = shaped(planes, height, width)
    plane = shaped(height, width)
    small = shaped(SUB, BLOCK)
    early, late, ends = call(
        window_kernel,
        (
            shaped(planes + HEAD, height, width), shaped(planes - HEAD, height, width), plane,
        ),
        [HBM] * 3, (pressure_old, pressure_source, solid_old),
        [pltpu.VMEM((planes, height, width), F32)] * 3
        + [pltpu.SemaphoreType.DMA((5 * planes + 1,))],
        flops=field_bytes, size=6 * field_bytes, limit=61_950_000, place=HBM,
    )
    near = along_reg(early, owners, (1, -1), core=1)
    near_late = along_reg(late, owners, (1, -1), core=1)
    beyond = along_reg(ends, owners, (-2, 2), core=1)
    mine, after_deposit = call(
        deposit_kernel, (shaped(tiles + SUB, 2 * BLOCK), small), [SMEM] + [VMEM] * 4,
        (count, cell, vol, drag, ids), flops=2 * 32 * 48 * 65536, size=5 * 4 * slots,
    )
    second = along_grp(mine, 1, holders)
    third = along_grp(mine, 2, holders)
    rows = halo_list.shape[1] // BLOCK
    halo = shaped(3 * rows, BLOCK)
    state, halo_near, halo_far, after_halo = call(
        halo_kernel, (shaped(3 * tiles, BLOCK), halo, halo, small),
        [VMEM] * 4, (grain_pos, grain_vel, halo_list, after_deposit), flops=slots,
        size=4 * 4 * 3 * slots,
    )
    others = [g for g in holders if g not in owners]
    came_near = along_reg(halo_near, others, (1, -1))
    came_far = along_reg(halo_far, others, (-1, 1))
    far, after_forward = call(
        forward_kernel, (shaped(planes + HEAD + 1, height, width), small), [VMEM] * 6,
        (near, early, after_halo, second, third, beyond), size=5 * field_bytes,
    )
    far = along_reg(far, owners, (2, -2))
    far_late = along_reg(near_late, owners, (2, -2))
    message = shaped(holding * (tiles + SUB) + 3 * rows // 2, 2 * BLOCK)
    message_near, message_far, after_message = call(
        message_kernel, (message, message, small), [VMEM] * 6,
        (mine, second, third, halo_near, halo_far, after_forward), size=8 * 2 * BLOCK * 500,
    )
    message_near = along_reg(message_near, owners, (1, -1))
    message_far = along_reg(message_far, owners, (-1, 1))
    constant, factor, weight, picks = call(
        functools.partial(own_kernel, full),
        (
            field, field, shaped(tiles, BLOCK),
            jax.ShapeDtypeStruct((3 * tiles, planes * height * width // BLOCK), BF16),
        ),
        [VMEM] * 8 + [SMEM],
        (mine, second, third, early, late, after_message, came_near, came_far, partner_block),
        flops=planes * height * 4 * 384 * 256 * 6, size=9 * field_bytes,
    )
    window_of = lambda count: pltpu.VMEM((count, height, width), F32)
    kept_even, kept_odd = call(
        functools.partial(near_kernel, full, tiles), (field, field), [VMEM] * 7,
        (message_near, early, near, near_late, beyond, constant, factor),
        [window_of(planes)] * 2 + [window_of(2 * planes + 1)] * 2,
        flops=planes * height * 4 * 384 * 256 * 6, size=9 * field_bytes,
    )
    grads = shaped(tiles, 3 * BLOCK)
    cells_held = planes * height * width // BLOCK
    grads_between, pieces = call(
        functools.partial(far_kernel, full, tiles),
        (grads, jax.ShapeDtypeStruct((cells_held, 6 * BLOCK), BF16)), [VMEM] * 9,
        (picks, message_far, early, far, far_late, constant, factor, kept_even, kept_odd),
        [window_of(planes)] * 2
        + [window_of(3 * planes + 2)] * 2
        + [pltpu.VMEM((cells_held, 3 * BLOCK), F32)],
        flops=planes * height * 4 * 384 * 256 * 6, size=9 * field_bytes,
    )
    ends_of = lambda source, target: [((source, r), (target, r)) for r in range(regions)]
    low, high, between = 0, CORES, 1
    came_low = send(grads_between, ends_of(low, between))
    came_high = send(grads_between, ends_of(high, between))
    pick = lambda own: call(
        functools.partial(pick_kernel, own), grads, [VMEM] * 2, (picks, pieces),
        flops=slots, size=slots,
    )
    came_across = send(pick(False), ends_of(low, high) + ends_of(high, low))
    grads_a = pick(True)
    contact = call(
        contact_kernel, shaped(3 * tiles, BLOCK), [SMEM] + [VMEM] * 7 + [ANY],
        (
            partner_block, state, message_near, message_far, came_near, came_far, contact_rows,
            contact_stiff, grads_a,
        ),
        [pltpu.VMEM((3 * (tiles + 2 * rows), BLOCK), F32)],
        flops=60 * 8 * slots, size=4 * 20 * slots,
    )
    return call(
        final_kernel, shaped(3, slots), [SMEM] + [VMEM] * 10,
        (
            count, grads_a, came_across, came_low, came_high, weight, contact, grain_vel, vol, drag,
            cell,
        ),
        flops=60 * slots, size=4 * 20 * slots,
    )


def solution(mesh):
    in_specs = (
        P(None, ("grp", "reg")),
        P(None, ("grp", "reg")),
        P(("grp", "reg")),
        P(("grp", "reg")),
        P(("grp", "reg")),
        P(None, ("grp", "reg")),
        P(None, ("grp", "reg")),
        P(("grp", "reg")),
        P(None, ("grp", "reg")),
        P(("grp", "reg")),
        P(("grp", "reg")),
        P("reg", None, None),
        P("reg", None, None),
        P("reg", None, None),
    )
    out_specs = P(None, ("grp", "reg"))
    return jax.shard_map(
        on_device, mesh=mesh, in_specs=in_specs, out_specs=out_specs, check_vma=False
    )
```

```python
import functools

import jax
import jax.numpy as jnp
from jax import lax
from jax.experimental import pallas as pl
from jax.experimental.pallas import tpu as pltpu
from jax.sharding import PartitionSpec as P

BLOCK = 128
SUB = 8
CORES = 2
ITERS = 4
HEAD = 1
SPRING = 1.0
DAMPING = 0.5
TIME_STEP = 0.5

VMEM = pl.BlockSpec(memory_space=pltpu.VMEM)
SMEM = pl.BlockSpec(memory_space=pltpu.SMEM)
ANY = pl.BlockSpec(memory_space=pl.ANY)
HBM = pl.BlockSpec(memory_space=pltpu.HBM)
F32 = jnp.float32
BF16 = jnp.bfloat16


def iota(shape, dim):
    return lax.broadcasted_iota(jnp.int32, shape, dim)


def shaped(*dims):
    return jax.ShapeDtypeStruct(dims, F32)


def call(kernel, outs, specs, args, scratch=(), flops=0, size=0, limit=40_000_000, place=VMEM):
    return pl.pallas_call(
        kernel,
        out_shape=outs,
        in_specs=specs,
        out_specs=jax.tree.map(lambda _: place, outs),
        scratch_shapes=list(scratch),
        compiler_params=pltpu.CompilerParams(vmem_limit_bytes=limit),
        cost_estimate=pl.CostEstimate(flops=flops, bytes_accessed=size, transcendentals=0),
    )(*args)


class Place:
    def __init__(self, full, height):
        groups, regions = lax.axis_size("grp"), lax.axis_size("reg")
        self.group, region = lax.axis_index("grp"), lax.axis_index("reg")
        self.half = self.group // CORES
        self.own_rows = full // (groups // CORES)
        first = jnp.clip(self.half * self.own_rows - SUB, 0, full - height)
        self.first = pl.multiple_of(first, SUB)
        self.sweeps = self.group % CORES == 0
        self.parity = region % 2
        self.odd, self.even = self.parity == 1, self.parity == 0
        self.lower, self.upper = region > 0, region < regions - 1


def lanes_of(source, index):
    return jnp.take_along_axis(source, index, axis=1, mode="promise_in_bounds")


def halves_of(value):
    high = value.astype(BF16)
    return high, (value - high.astype(F32)).astype(BF16)


def window_kernel(
    pressure_old, source, solid_before, early, late, ends, pressure, driven, solid, sems
):
    planes, height, _ = solid.shape
    place = Place(pressure_old.shape[1], height)
    rows = pl.ds(place.first, height)
    used = []

    def copy(whole, part):
        used.append(None)
        return pltpu.make_async_copy(whole, part, sems.at[len(used) - 1])

    fetched = [
        [copy(whole.at[x, rows, :], part.at[x]) for x in range(planes)]
        for whole, part in ((pressure_old, pressure), (source, driven), (solid_before, solid))
    ]
    stored = [copy(pressure.at[x], early.at[x]) for x in range(planes)]
    for x in range(planes):
        stored.append(copy(driven.at[x], early.at[planes + x] if x < HEAD else late.at[x - HEAD]))
    stored.append(copy(pressure.at[place.parity * (planes - 1)], ends))
    for x in range(planes):
        for part in fetched:
            part[x].start()
    for x in range(planes):
        fetched[0][x].wait()
        stored[x].start()
        fetched[1][x].wait()
        fetched[2][x].wait()
        driven[x] = driven[x] - solid[x]
        stored[planes + x].start()
    stored[-1].start()
    for one in stored:
        one.wait()


def forward_kernel(near, early, _halo, _second, _third, _beyond, out, dummy):
    dummy[...] = jnp.zeros(dummy.shape, F32)
    count = near.shape[0]
    out[:count] = near[...]
    end = (1 - lax.axis_index("reg") % 2) * (count - HEAD - 1)
    out[count] = early[end]


def deposit_kernel(count, cell, vol, drag, ids, out, dummy):
    dummy[...] = jnp.zeros(dummy.shape, F32)
    tiles = cell.shape[0]
    sub = iota((SUB, BLOCK), 0)
    rows_c = iota((BLOCK, BLOCK), 0)
    even = sub % 2 == 0
    low_pair = sub % 4 < 2

    def step(group, carry):
        first = pl.multiple_of(group * SUB, SUB)
        slot = (first + sub) * BLOCK + iota((SUB, BLOCK), 1)
        live = slot < count[0]
        cells = cell[pl.ds(first, SUB), :]
        parts = halves_of(jnp.where(live, vol[pl.ds(first, SUB), :], 0.0)) + halves_of(
            jnp.where(live, drag[pl.ds(first, SUB), :], 0.0)
        )
        parts = [part.astype(F32) for part in parts]
        left = jnp.concatenate([jnp.where(even, part, 0.0) for part in parts], 0)
        right = jnp.concatenate([jnp.where(even, 0.0, part) for part in parts], 0)
        loads = jnp.concatenate([left, right], 1).astype(BF16)
        sums = [jnp.zeros((SUB, BLOCK), F32), jnp.zeros((SUB, BLOCK), F32)]
        for quad in range(SUB // 4):
            hot = [
                jnp.where(
                    rows_c == jnp.broadcast_to(cells[t : t + 1, :], (BLOCK, BLOCK)), 1.0, 0.0
                ).astype(BF16)
                for t in range(4 * quad, 4 * quad + 4)
            ]
            picked = jnp.concatenate(
                [jnp.concatenate(hot[:2], 1), jnp.concatenate(hot[2:], 1)], 0
            )
            placed = lax.dot_general(
                loads, picked, (((1,), (1,)), ((), ())), preferred_element_type=F32
            )
            for field in range(2):
                base = field * 2 * SUB
                total = placed[base : base + SUB] + placed[base + SUB : base + 2 * SUB]
                chosen = jnp.where(low_pair, total[:, :BLOCK], total[:, BLOCK:])
                sums[field] = jnp.where(sub // 4 == quad, chosen, sums[field])
        out[pl.ds(first, SUB), :BLOCK] = sums[0]
        out[pl.ds(first, SUB), BLOCK:] = sums[1]
        return carry

    lax.fori_loop(0, tiles // SUB, step, 0, unroll=4)
    out[tiles : tiles + SUB, :BLOCK] = jnp.broadcast_to(ids[...].astype(F32), (SUB, BLOCK))
    out[tiles : tiles + SUB, BLOCK:] = jnp.zeros((SUB, BLOCK), F32)


def halo_kernel(pos, vel, lists, _, state, near, far, dummy):
    dummy[...] = jnp.zeros(dummy.shape, F32)
    tiles = pos.shape[1] // BLOCK
    rows = lists.shape[1] // BLOCK
    for tile in range(tiles):
        lanes = slice(tile * BLOCK, (tile + 1) * BLOCK)
        mixed = SPRING * pos[:, lanes] - DAMPING * vel[:, lanes]
        for axis in range(3):
            state[axis * tiles + tile : axis * tiles + tile + 1, :] = mixed[axis : axis + 1]
    turned = [
        jnp.concatenate(halves_of(jnp.transpose(state[axis * tiles : (axis + 1) * tiles, :])), 1)
        for axis in range(3)
    ]
    turned = jnp.concatenate(turned, 0)
    span = 2 * BLOCK
    row = iota((BLOCK, span), 0)

    odd = lax.axis_index("reg") % 2
    for away, out in enumerate((near, far)):
        side = 1 - odd if away == 0 else odd

        def step(part, carry):
            named = lists[:, pl.ds(pl.multiple_of(part * span, span), span)]
            named = jnp.where(side == 0, named[:1], named[1:])
            block = lax.shift_right_logical(named, 7)
            lane = named & (BLOCK - 1)
            hot = jnp.where(row == jnp.broadcast_to(block, row.shape), 1.0, 0.0).astype(BF16)
            found = jnp.dot(
                turned, jnp.concatenate([hot, hot], 0), preferred_element_type=F32
            )
            here = row == jnp.broadcast_to(lane, row.shape)
            for axis in range(3):
                value = jnp.where(here, found[axis * BLOCK : (axis + 1) * BLOCK], 0.0)
                value = jnp.sum(value, axis=0, keepdims=True)
                for half in range(2):
                    out[pl.ds(axis * rows + 2 * part + half, 1), :] = value[
                        :, half * BLOCK : (half + 1) * BLOCK
                    ]
            return carry

        lax.fori_loop(0, rows // 2, step, 0, unroll=8)


def message_kernel(mine, second, third, halo_near, halo_far, _, near, far, dummy):
    dummy[...] = jnp.zeros(dummy.shape, F32)
    tiles = mine.shape[0] - SUB
    half = halo_near.shape[0] // 2
    rows = near.shape[0] - half
    groups = (mine, second, third)
    sub = iota((SUB, 2 * BLOCK), 0)
    ids = groups[0][tiles:, :]
    for index in (1, 2):
        ids = jnp.where(sub == index, groups[index][tiles:, :], ids)
    for halo, out in ((halo_near, near), (halo_far, far)):
        for index, group in enumerate(groups):
            out[index * tiles : (index + 1) * tiles, :] = group[:tiles, :]
        out[rows - SUB : rows, :] = ids
        out[rows:, :BLOCK] = halo[:half, :]
        out[rows:, BLOCK:] = halo[half:, :]


def merged(parts):
    sub = iota((SUB, BLOCK), 0)
    for step in (4, 2, 1):
        low = (sub & step) == 0
        paired = []
        for first, second in zip(parts[:step], parts[step:]):
            away = jnp.where(low, second, first)
            back = pltpu.roll(away, step, 0)
            if step < SUB // 2:
                back = jnp.where(low, pltpu.roll(away, SUB - step, 0), back)
            paired.append(jnp.where(low, first, second) + back)
        parts = paired
    return parts[0]


def contact_kernel(
    partner, state, message_near, message_far, halo_near, halo_far, named, stiff, _, out, extended,
):
    tiles = state.shape[0] // 3
    rows = halo_near.shape[0] // 3
    blocks = tiles + 2 * rows
    base = message_near.shape[0] - 3 * rows // 2
    odd = lax.axis_index("reg") % 2
    sweeps = lax.axis_index("grp") % CORES == 0
    for axis in range(3):
        extended[axis * blocks : axis * blocks + tiles, :] = state[
            axis * tiles : (axis + 1) * tiles, :
        ]
    for message, halo, upper in (
        (message_near, halo_near, 1 - odd), (message_far, halo_far, odd)
    ):
        carried = jnp.concatenate([message[base:, :BLOCK], message[base:, BLOCK:]], 0)
        carried = jnp.where(sweeps, carried, halo[...])
        for axis in range(3):
            first = pl.multiple_of(axis * blocks + tiles + upper * rows, SUB)
            extended[pl.ds(first, rows), :] = carried[axis * rows : (axis + 1) * rows]

    def step(group, carry):
        first = pl.multiple_of(group * SUB, SUB)
        held = [extended[pl.ds(axis * blocks + first, SUB), :] for axis in range(3)]
        pulls = [[], [], []]
        for t in range(SUB):
            lanes = pl.ds(pl.multiple_of((first + t) * BLOCK, BLOCK), BLOCK)
            entry = named[:, lanes]
            weight = jnp.where(entry >= 0, stiff[:, lanes], 0.0)
            own = entry < BLOCK
            lane = entry & (BLOCK - 1)
            other = partner[first + t]
            for axis in range(3):
                mine = jnp.broadcast_to(held[axis][t : t + 1], entry.shape)
                theirs = extended[pl.ds(axis * blocks + other, 1), :]
                theirs = jnp.broadcast_to(theirs, entry.shape)
                met = jnp.where(own, lanes_of(mine, lane), lanes_of(theirs, lane))
                pulls[axis].append(weight * (mine - met))
        for axis in range(3):
            out[pl.ds(axis * tiles + first, SUB), :] = merged(pulls[axis])
        return carry

    lax.fori_loop(0, tiles // SUB, step, 0)


def shifted(plane):
    height, width = plane.shape
    row = iota((SUB, width), 0)
    column = iota((height, BLOCK), 1)
    above, below = pltpu.roll(plane, 1, 0), pltpu.roll(plane, height - 1, 0)
    left, right = pltpu.roll(plane, 1, 1), pltpu.roll(plane, width - 1, 1)
    above = jnp.concatenate([jnp.where(row == 0, 0.0, above[:SUB]), above[SUB:]], 0)
    below = jnp.concatenate([below[:-SUB], jnp.where(row == SUB - 1, 0.0, below[-SUB:])], 0)
    left = jnp.concatenate([jnp.where(column == 0, 0.0, left[:, :BLOCK]), left[:, BLOCK:]], 1)
    right = jnp.concatenate(
        [right[:, :-BLOCK], jnp.where(column == BLOCK - 1, 0.0, right[:, -BLOCK:])], 1
    )
    return above, below, left, right


def inverse_of(value):
    near = pl.reciprocal(value, approx=True)
    return near * (2.0 - value * near)


def placed(groups, ids, tiles):
    parts = [halves_of(group[:tiles, :]) for group in groups]
    loads = jnp.concatenate([part[i] for i in range(2) for part in parts], 0)
    ids = jnp.concatenate(ids, 1).astype(jnp.int32)

    def gathered(wanted):
        hot = jnp.where(wanted == jnp.broadcast_to(ids, wanted.shape), 1.0, 0.0).astype(BF16)
        total = jnp.dot(
            jnp.concatenate([hot, hot], 1), loads, preferred_element_type=F32
        )
        return total[:, :BLOCK], total[:, BLOCK:]

    return ids, gathered


def driven_of(early, late, planes):
    return lambda x: early[planes + x] if x < HEAD else late[x - HEAD]


def coefficients(gathered, tiles, first, full, driven_at, constant, factor, turned, present):
    planes, height, width = constant.shape
    zones = width // BLOCK
    shape = (zones * height, 3 * tiles)
    line = iota(shape, 0)
    block = (line % height) * zones + line // height + first * zones

    for x in range(planes):
        solid, drag = gathered(block + x * (full * zones))
        at = x if turned is None else jnp.where(turned, planes - 1 - x, x)
        voids = 1.0 + solid
        scale = inverse_of(6.0 + (drag + 1.0) * voids)
        if present is not None:
            scale = jnp.where(present, scale, 0.0)
        inverse = voids * scale
        for zone in range(zones):
            lanes = slice(zone * BLOCK, (zone + 1) * BLOCK)
            rows = slice(zone * height, (zone + 1) * height)
            driving = driven_at(x)[:, lanes] + solid[rows]
            constant[at, :, lanes] = driving * inverse[rows]
            factor[at, :, lanes] = scale[rows]


def own_kernel(
    full, mine, second, third, early, late, _message, _near, _far, _partner, constant, factor, weight, picks
):
    tiles = weight.shape[0]
    planes, height, width = constant.shape
    place = Place(full, height)
    zones = width // BLOCK
    groups = (mine, second, third)
    ids = [group[tiles : tiles + 1, :BLOCK] for group in groups]
    ids, gathered = placed(groups, ids, tiles)
    coefficients(
        gathered, tiles, place.first, full, driven_of(early, late, planes), constant, factor,
        place.even, None,
    )
    turned = [
        jnp.transpose(
            jnp.broadcast_to(ids[:, i * tiles : (i + 1) * tiles], (BLOCK, tiles)).astype(F32)
        ).astype(jnp.int32)
        for i in range(3)
    ]
    solid, drag = gathered(jnp.concatenate([turned[0]] * 3, 1))
    weight[...] = 1.0 / (1.0 / (1.0 + solid) + drag)
    for i in range(3):
        block = turned[i]
        line, zone = block // zones, block % zones
        x, y = line // full, line % full
        row = (x * zones + zone) * height + y - place.first
        held = y // place.own_rows == jnp.where(place.sweeps, place.half, -1)
        row = jnp.concatenate([jnp.where(held, row, -1)] * (picks.shape[1] // BLOCK), 1)
        hot = jnp.where(row == iota(row.shape, 1), 1.0, 0.0).astype(BF16)
        picks[i * tiles : (i + 1) * tiles, :] = hot


def sweep(source, target, coefficient, start, stop):
    def plane(at, carry):
        above, below, left, right = shifted(source[at])
        around = source[at - 1] + source[at + 1] + above + below + left + right
        constant, factor = coefficient(at)
        target[at] = constant + factor * around
        return carry

    lax.fori_loop(start, stop, plane, 0, unroll=4)


def deposits_of(message, tiles):
    groups = [message.at[i * tiles : (i + 1) * tiles] for i in range(3)]
    ids = [message[3 * tiles + i : 3 * tiles + i + 1, :BLOCK] for i in range(3)]
    return placed(groups, ids, tiles)[1]


def near_kernel(
    full, tiles, message, pressure, near, near_late, beyond, own_constant, own_factor, kept_even, kept_odd, constant, factor, old, new,
):
    planes, height, width = own_constant.shape
    place = Place(full, height)
    rim = planes + 1
    coefficients(
        deposits_of(message, tiles), tiles, place.first, full,
        driven_of(near, near_late, planes), constant, factor, place.even, jnp.where(place.odd, place.lower, place.upper),
    )
    old[0] = beyond[...]
    for x in range(planes):
        at = jnp.where(place.even, planes - 1 - x, x)
        old[1 + x] = near[at]
        old[rim + x] = pressure[at]
    buffers = (old, new)
    for index in range(planes):
        source, target = buffers[index % 2], buffers[(index + 1) % 2]
        sweep(source, target, lambda at: (constant[at - 1], factor[at - 1]), 1 + index, rim)
        sweep(
            source, target, lambda at: (own_constant[at - rim], own_factor[at - rim]),
            rim, 2 * planes - index,
        )
    kept_even[...] = old[planes : 2 * planes]
    kept_odd[...] = new[planes : 2 * planes]


def far_kernel(
    full, tiles, picks, message, pressure, far, far_late, own_constant, own_factor, kept_even, kept_odd,
    across, between, pieces, constant, factor, old, new, fields,
):
    planes, height, width = own_constant.shape
    zones = width // BLOCK
    place = Place(full, height)
    rim = planes + 1
    coefficients(
        deposits_of(message, tiles), tiles, place.first, full,
        driven_of(far, far_late, planes), constant, factor, place.even, jnp.where(place.odd, place.upper, place.lower),
    )
    old[planes : 2 * planes] = kept_even[...]
    new[planes : 2 * planes] = kept_odd[...]
    old[2 * planes] = pressure[jnp.where(place.even, 0, planes - 1)]
    for x in range(planes):
        at = jnp.where(place.even, planes - 1 - x, x)
        old[rim + planes + x] = far[at]
    old[rim + 2 * planes] = far[planes + HEAD]
    buffers = (old, new)
    edge = rim + planes
    for index in range(planes):
        source, target = buffers[index % 2], buffers[(index + 1) % 2]
        sweep(
            source, target, lambda at: (own_constant[at - rim], own_factor[at - rim]),
            2 * planes - index, edge,
        )
        sweep(
            source, target, lambda at: (constant[at - edge], factor[at - edge]),
            edge, edge + planes - index,
        )
    last = buffers[planes % 2]
    way = jnp.where(place.even, -0.5, 0.5)

    def gradient(x, carry):
        at = rim + x
        above, below, left, right = shifted(last[at])
        grads = (way * (last[at + 1] - last[at - 1]), 0.5 * (below - above), 0.5 * (right - left))
        line = jnp.where(place.even, planes - 1 - x, x) * zones
        for zone in range(zones):
            first = pl.multiple_of((line + zone) * height, SUB)
            for axis, grad in enumerate(grads):
                fields[pl.ds(first, height), axis * BLOCK : (axis + 1) * BLOCK] = (
                    grad[:, zone * BLOCK : (zone + 1) * BLOCK]
                )
        return carry

    lax.fori_loop(0, planes, gradient, 0, unroll=4)
    pieces[...] = jnp.concatenate(halves_of(fields[...]), 1)
    total = picked_rows(picks[tiles:, :], pieces)
    first, second = total[:tiles], total[tiles:]
    low = lax.axis_index("grp") == 0
    across[...] = jnp.where(low, first, second)
    between[...] = jnp.where(low, second, first)


def picked_rows(hot, pieces):
    total = jnp.dot(hot, pieces[...], preferred_element_type=F32)
    return total[:, : 3 * BLOCK] + total[:, 3 * BLOCK :]


def pick_kernel(picks, pieces, out):
    out[...] = picked_rows(picks[: out.shape[0], :], pieces)


def final_kernel(
    count, grads_a, grads_b, grads_c, grads_d, weight, contact, vel, vol, drag, cell, out,
):
    tiles = cell.shape[0]
    cells = cell[...]
    heft = lanes_of(weight[...], cells)
    slot = iota(cells.shape, 0) * BLOCK + iota(cells.shape, 1)
    live = slot < count[0]
    volume = vol[...]
    push = TIME_STEP / volume
    for axis in range(3):
        lanes = slice(axis * BLOCK, (axis + 1) * BLOCK)
        gradient = grads_a[:, lanes] + grads_b[:, lanes] + (grads_c[:, lanes] + grads_d[:, lanes])
        gradient = lanes_of(gradient, cells)
        own = jnp.concatenate(
            [vel[axis : axis + 1, t * BLOCK : (t + 1) * BLOCK] for t in range(tiles)], 0
        )
        fluid = -gradient * heft
        force = contact[axis * tiles : (axis + 1) * tiles, :] - volume * gradient
        force = force + drag[...] * (fluid - own)
        new = jnp.where(live, own + force * push, 0.0)
        for t in range(tiles):
            out[axis : axis + 1, t * BLOCK : (t + 1) * BLOCK] = new[t : t + 1, :]


def on_device(
    grain_pos,
    grain_vel,
    grain_vol,
    drag_coef,
    grain_count,
    contact_rows,
    contact_stiff,
    partner_block,
    halo_list,
    grain_cell,
    tile_cell_block,
    pressure_old,
    pressure_source,
    solid_old,
):
    groups, regions = lax.axis_size("grp"), lax.axis_size("reg")
    holding = groups - 1
    halves = groups // CORES
    slots = grain_pos.shape[1]
    tiles = slots // BLOCK
    planes, full, width = pressure_old.shape
    assert planes == ITERS
    own_rows = full // halves
    height = min(full, own_rows + SUB * min(2, halves - 1))
    owners = range(0, groups, CORES)
    holders = range(holding)

    def send(value, pairs):
        flat = [(a[0] * regions + a[1], b[0] * regions + b[1]) for a, b in pairs]
        return lax.ppermute(value, ("grp", "reg"), flat)

    def along_reg(value, members, goes, core=0):
        pairs = [
            ((g + core, r), (g, r + goes[r % 2]))
            for g in members
            for r in range(regions)
            if 0 <= r + goes[r % 2] < regions
        ]
        return send(value, pairs)

    def along_grp(value, step, members):
        pairs = [((g, r), ((g + step) % holding, r)) for g in members for r in range(regions)]
        return send(value, pairs)

    count = grain_count
    cell = grain_cell.reshape(tiles, BLOCK)
    vol = grain_vol.reshape(tiles, BLOCK)
    drag = drag_coef.reshape(tiles, BLOCK)
    ids = tile_cell_block.reshape(1, tiles)
    field_bytes = 4 * planes * height * width

    field = shaped(planes, height, width)
    plane = shaped(height, width)
    small = shaped(SUB, BLOCK)
    early, late, ends = call(
        window_kernel,
        (
            shaped(planes + HEAD, height, width), shaped(planes - HEAD, height, width), plane,
        ),
        [HBM] * 3, (pressure_old, pressure_source, solid_old),
        [pltpu.VMEM((planes, height, width), F32)] * 3
        + [pltpu.SemaphoreType.DMA((5 * planes + 1,))],
        flops=field_bytes, size=6 * field_bytes, limit=61_950_000, place=HBM,
    )
    near = along_reg(early, owners, (1, -1), core=1)
    near_late = along_reg(late, owners, (1, -1), core=1)
    beyond = along_reg(ends, owners, (-2, 2), core=1)
    mine, after_deposit = call(
        deposit_kernel, (shaped(tiles + SUB, 2 * BLOCK), small), [SMEM] + [VMEM] * 4,
        (count, cell, vol, drag, ids), flops=2 * 32 * 48 * 65536, size=5 * 4 * slots,
    )
    second = along_grp(mine, 1, holders)
    third = along_grp(mine, 2, holders)
    rows = halo_list.shape[1] // BLOCK
    halo = shaped(3 * rows, BLOCK)
    state, halo_near, halo_far, after_halo = call(
        halo_kernel, (shaped(3 * tiles, BLOCK), halo, halo, small),
        [VMEM] * 4, (grain_pos, grain_vel, halo_list, after_deposit), flops=slots,
        size=4 * 4 * 3 * slots,
    )
    others = [g for g in holders if g not in owners]
    came_near = along_reg(halo_near, others, (1, -1))
    came_far = along_reg(halo_far, others, (-1, 1))
    far, after_forward = call(
        forward_kernel, (shaped(planes + HEAD + 1, height, width), small), [VMEM] * 6,
        (near, early, after_halo, second, third, beyond), size=5 * field_bytes,
    )
    far = along_reg(far, owners, (2, -2))
    far_late = along_reg(near_late, owners, (2, -2))
    message = shaped(holding * tiles + SUB + 3 * rows // 2, 2 * BLOCK)
    message_near, message_far, after_message = call(
        message_kernel, (message, message, small), [VMEM] * 6,
        (mine, second, third, halo_near, halo_far, after_forward), size=8 * 2 * BLOCK * 500,
    )
    message_near = along_reg(message_near, owners, (1, -1))
    message_far = along_reg(message_far, owners, (-1, 1))
    constant, factor, weight, picks = call(
        functools.partial(own_kernel, full),
        (
            field, field, shaped(tiles, BLOCK),
            jax.ShapeDtypeStruct((3 * tiles, planes * height * width // BLOCK), BF16),
        ),
        [VMEM] * 8 + [SMEM],
        (mine, second, third, early, late, after_message, came_near, came_far, partner_block),
        flops=planes * height * 4 * 384 * 256 * 6, size=9 * field_bytes,
    )
    window_of = lambda count: pltpu.VMEM((count, height, width), F32)
    kept_even, kept_odd = call(
        functools.partial(near_kernel, full, tiles), (field, field), [VMEM] * 7,
        (message_near, early, near, near_late, beyond, constant, factor),
        [window_of(planes)] * 2 + [window_of(2 * planes + 1)] * 2,
        flops=planes * height * 4 * 384 * 256 * 6, size=9 * field_bytes,
    )
    grads = shaped(tiles, 3 * BLOCK)
    cells_held = planes * height * width // BLOCK
    grads_across, grads_between, pieces = call(
        functools.partial(far_kernel, full, tiles),
        (grads, grads, jax.ShapeDtypeStruct((cells_held, 6 * BLOCK), BF16)), [VMEM] * 9,
        (picks, message_far, early, far, far_late, constant, factor, kept_even, kept_odd),
        [window_of(planes)] * 2
        + [window_of(3 * planes + 2)] * 2
        + [pltpu.VMEM((cells_held, 3 * BLOCK), F32)],
        flops=planes * height * 4 * 384 * 256 * 6, size=9 * field_bytes,
    )
    ends_of = lambda source, target: [((source, r), (target, r)) for r in range(regions)]
    low, high, between = 0, CORES, 1
    came_low = send(grads_between, ends_of(low, between))
    came_high = send(grads_between, ends_of(high, between))
    came_across = send(grads_across, ends_of(low, high) + ends_of(high, low))
    grads_a = call(pick_kernel, grads, [VMEM] * 2, (picks, pieces), flops=slots, size=slots)
    contact = call(
        contact_kernel, shaped(3 * tiles, BLOCK), [SMEM] + [VMEM] * 7 + [ANY],
        (
            partner_block, state, message_near, message_far, came_near, came_far, contact_rows,
            contact_stiff, grads_a,
        ),
        [pltpu.VMEM((3 * (tiles + 2 * rows), BLOCK), F32)],
        flops=60 * 8 * slots, size=4 * 20 * slots,
    )
    return call(
        final_kernel, shaped(3, slots), [SMEM] + [VMEM] * 10,
        (
            count, grads_a, came_across, came_low, came_high, weight, contact, grain_vel, vol, drag,
            cell,
        ),
        flops=60 * slots, size=4 * 20 * slots,
    )


def solution(mesh):
    in_specs = (
        P(None, ("grp", "reg")),
        P(None, ("grp", "reg")),
        P(("grp", "reg")),
        P(("grp", "reg")),
        P(("grp", "reg")),
        P(None, ("grp", "reg")),
        P(None, ("grp", "reg")),
        P(("grp", "reg")),
        P(None, ("grp", "reg")),
        P(("grp", "reg")),
        P(("grp", "reg")),
        P("reg", None, None),
        P("reg", None, None),
        P("reg", None, None),
    )
    out_specs = P(None, ("grp", "reg"))
    return jax.shard_map(
        on_device, mesh=mesh, in_specs=in_specs, out_specs=out_specs, check_vma=False
    )
```

```python
import functools

import jax
import jax.numpy as jnp
from jax import lax
from jax.experimental import pallas as pl
from jax.experimental.pallas import tpu as pltpu
from jax.sharding import PartitionSpec as P

BLOCK = 128
SUB = 8
CORES = 2
ITERS = 4
HEAD = 1
SPRING = 1.0
DAMPING = 0.5
TIME_STEP = 0.5

VMEM = pl.BlockSpec(memory_space=pltpu.VMEM)
SMEM = pl.BlockSpec(memory_space=pltpu.SMEM)
ANY = pl.BlockSpec(memory_space=pl.ANY)
HBM = pl.BlockSpec(memory_space=pltpu.HBM)
F32 = jnp.float32
BF16 = jnp.bfloat16


def iota(shape, dim):
    return lax.broadcasted_iota(jnp.int32, shape, dim)


def shaped(*dims):
    return jax.ShapeDtypeStruct(dims, F32)


def call(kernel, outs, specs, args, scratch=(), flops=0, size=0, limit=40_000_000, place=VMEM):
    return pl.pallas_call(
        kernel,
        out_shape=outs,
        in_specs=specs,
        out_specs=jax.tree.map(lambda _: place, outs),
        scratch_shapes=list(scratch),
        compiler_params=pltpu.CompilerParams(vmem_limit_bytes=limit),
        cost_estimate=pl.CostEstimate(flops=flops, bytes_accessed=size, transcendentals=0),
    )(*args)


class Place:
    def __init__(self, full, height):
        groups, regions = lax.axis_size("grp"), lax.axis_size("reg")
        self.group, region = lax.axis_index("grp"), lax.axis_index("reg")
        self.half = self.group // CORES
        self.own_rows = full // (groups // CORES)
        first = jnp.clip(self.half * self.own_rows - SUB, 0, full - height)
        self.first = pl.multiple_of(first, SUB)
        self.sweeps = self.group % CORES == 0
        self.parity = region % 2
        self.odd, self.even = self.parity == 1, self.parity == 0
        self.lower, self.upper = region > 0, region < regions - 1


def lanes_of(source, index):
    return jnp.take_along_axis(source, index, axis=1, mode="promise_in_bounds")


def halves_of(value):
    high = value.astype(BF16)
    return high, (value - high.astype(F32)).astype(BF16)


def window_kernel(
    pressure_old, source, solid_before, early, late, ends, pressure, driven, solid, sems
):
    planes, height, _ = solid.shape
    place = Place(pressure_old.shape[1], height)
    rows = pl.ds(place.first, height)
    used = []

    def copy(whole, part):
        used.append(None)
        return pltpu.make_async_copy(whole, part, sems.at[len(used) - 1])

    fetched = [
        [copy(whole.at[x, rows, :], part.at[x]) for x in range(planes)]
        for whole, part in ((pressure_old, pressure), (source, driven), (solid_before, solid))
    ]
    stored = [copy(pressure.at[x], early.at[x]) for x in range(planes)]
    for x in range(planes):
        stored.append(copy(driven.at[x], early.at[planes + x] if x < HEAD else late.at[x - HEAD]))
    stored.append(copy(pressure.at[place.parity * (planes - 1)], ends))
    for x in range(planes):
        for part in fetched:
            part[x].start()
    for x in range(planes):
        fetched[0][x].wait()
        stored[x].start()
        fetched[1][x].wait()
        fetched[2][x].wait()
        driven[x] = driven[x] - solid[x]
        stored[planes + x].start()
    stored[-1].start()
    for one in stored:
        one.wait()


def forward_kernel(near, early, _halo, _second, _third, out, dummy):
    dummy[...] = jnp.zeros(dummy.shape, F32)
    count = near.shape[0]
    out[:count] = near[...]
    end = (1 - lax.axis_index("reg") % 2) * (count - HEAD - 1)
    out[count] = early[end]


def deposit_kernel(count, cell, vol, drag, ids, out, dummy):
    dummy[...] = jnp.zeros(dummy.shape, F32)
    tiles = cell.shape[0]
    sub = iota((SUB, BLOCK), 0)
    rows_c = iota((BLOCK, BLOCK), 0)
    even = sub % 2 == 0
    low_pair = sub % 4 < 2

    def step(group, carry):
        first = pl.multiple_of(group * SUB, SUB)
        slot = (first + sub) * BLOCK + iota((SUB, BLOCK), 1)
        live = slot < count[0]
        cells = cell[pl.ds(first, SUB), :]
        parts = halves_of(jnp.where(live, vol[pl.ds(first, SUB), :], 0.0)) + halves_of(
            jnp.where(live, drag[pl.ds(first, SUB), :], 0.0)
        )
        parts = [part.astype(F32) for part in parts]
        left = jnp.concatenate([jnp.where(even, part, 0.0) for part in parts], 0)
        right = jnp.concatenate([jnp.where(even, 0.0, part) for part in parts], 0)
        loads = jnp.concatenate([left, right], 1).astype(BF16)
        sums = [jnp.zeros((SUB, BLOCK), F32), jnp.zeros((SUB, BLOCK), F32)]
        for quad in range(SUB // 4):
            hot = [
                jnp.where(
                    rows_c == jnp.broadcast_to(cells[t : t + 1, :], (BLOCK, BLOCK)), 1.0, 0.0
                ).astype(BF16)
                for t in range(4 * quad, 4 * quad + 4)
            ]
            picked = jnp.concatenate(
                [jnp.concatenate(hot[:2], 1), jnp.concatenate(hot[2:], 1)], 0
            )
            placed = lax.dot_general(
                loads, picked, (((1,), (1,)), ((), ())), preferred_element_type=F32
            )
            for field in range(2):
                base = field * 2 * SUB
                total = placed[base : base + SUB] + placed[base + SUB : base + 2 * SUB]
                chosen = jnp.where(low_pair, total[:, :BLOCK], total[:, BLOCK:])
                sums[field] = jnp.where(sub // 4 == quad, chosen, sums[field])
        out[pl.ds(first, SUB), :BLOCK] = sums[0]
        out[pl.ds(first, SUB), BLOCK:] = sums[1]
        return carry

    lax.fori_loop(0, tiles // SUB, step, 0, unroll=4)
    out[tiles : tiles + SUB, :BLOCK] = jnp.broadcast_to(ids[...].astype(F32), (SUB, BLOCK))
    out[tiles : tiles + SUB, BLOCK:] = jnp.zeros((SUB, BLOCK), F32)


def halo_kernel(pos, vel, lists, _, state, near, far, dummy):
    dummy[...] = jnp.zeros(dummy.shape, F32)
    tiles = pos.shape[1] // BLOCK
    rows = lists.shape[1] // BLOCK
    for tile in range(tiles):
        lanes = slice(tile * BLOCK, (tile + 1) * BLOCK)
        mixed = SPRING * pos[:, lanes] - DAMPING * vel[:, lanes]
        for axis in range(3):
            state[axis * tiles + tile : axis * tiles + tile + 1, :] = mixed[axis : axis + 1]
    turned = [
        jnp.concatenate(halves_of(jnp.transpose(state[axis * tiles : (axis + 1) * tiles, :])), 1)
        for axis in range(3)
    ]
    turned = jnp.concatenate(turned, 0)
    span = 2 * BLOCK
    row = iota((BLOCK, span), 0)

    odd = lax.axis_index("reg") % 2
    for away, out in enumerate((near, far)):
        side = 1 - odd if away == 0 else odd

        def step(part, carry):
            named = lists[:, pl.ds(pl.multiple_of(part * span, span), span)]
            named = jnp.where(side == 0, named[:1], named[1:])
            block = lax.shift_right_logical(named, 7)
            lane = named & (BLOCK - 1)
            hot = jnp.where(row == jnp.broadcast_to(block, row.shape), 1.0, 0.0).astype(BF16)
            found = jnp.dot(
                turned, jnp.concatenate([hot, hot], 0), preferred_element_type=F32
            )
            here = row == jnp.broadcast_to(lane, row.shape)
            for axis in range(3):
                value = jnp.where(here, found[axis * BLOCK : (axis + 1) * BLOCK], 0.0)
                value = jnp.sum(value, axis=0, keepdims=True)
                for half in range(2):
                    out[pl.ds(axis * rows + 2 * part + half, 1), :] = value[
                        :, half * BLOCK : (half + 1) * BLOCK
                    ]
            return carry

        lax.fori_loop(0, rows // 2, step, 0, unroll=8)


def message_kernel(mine, second, third, halo_near, halo_far, _, near, far, dummy):
    dummy[...] = jnp.zeros(dummy.shape, F32)
    tiles = mine.shape[0] - SUB
    half = halo_near.shape[0] // 2
    rows = near.shape[0] - half
    groups = (mine, second, third)
    sub = iota((SUB, 2 * BLOCK), 0)
    ids = groups[0][tiles:, :]
    for index in (1, 2):
        ids = jnp.where(sub == index, groups[index][tiles:, :], ids)
    for halo, out in ((halo_near, near), (halo_far, far)):
        for index, group in enumerate(groups):
            out[index * tiles : (index + 1) * tiles, :] = group[:tiles, :]
        out[rows - SUB : rows, :] = ids
        out[rows:, :BLOCK] = halo[:half, :]
        out[rows:, BLOCK:] = halo[half:, :]


def merged(parts):
    sub = iota((SUB, BLOCK), 0)
    for step in (4, 2, 1):
        low = (sub & step) == 0
        paired = []
        for first, second in zip(parts[:step], parts[step:]):
            away = jnp.where(low, second, first)
            back = pltpu.roll(away, step, 0)
            if step < SUB // 2:
                back = jnp.where(low, pltpu.roll(away, SUB - step, 0), back)
            paired.append(jnp.where(low, first, second) + back)
        parts = paired
    return parts[0]


def contact_kernel(
    partner, state, message_near, message_far, halo_near, halo_far, named, stiff, _, out, extended,
):
    tiles = state.shape[0] // 3
    rows = halo_near.shape[0] // 3
    blocks = tiles + 2 * rows
    base = message_near.shape[0] - 3 * rows // 2
    odd = lax.axis_index("reg") % 2
    sweeps = lax.axis_index("grp") % CORES == 0
    for axis in range(3):
        extended[axis * blocks : axis * blocks + tiles, :] = state[
            axis * tiles : (axis + 1) * tiles, :
        ]
    for message, halo, upper in (
        (message_near, halo_near, 1 - odd), (message_far, halo_far, odd)
    ):
        carried = jnp.concatenate([message[base:, :BLOCK], message[base:, BLOCK:]], 0)
        carried = jnp.where(sweeps, carried, halo[...])
        for axis in range(3):
            first = pl.multiple_of(axis * blocks + tiles + upper * rows, SUB)
            extended[pl.ds(first, rows), :] = carried[axis * rows : (axis + 1) * rows]

    def step(group, carry):
        first = pl.multiple_of(group * SUB, SUB)
        held = [extended[pl.ds(axis * blocks + first, SUB), :] for axis in range(3)]
        pulls = [[], [], []]
        for t in range(SUB):
            lanes = pl.ds(pl.multiple_of((first + t) * BLOCK, BLOCK), BLOCK)
            entry = named[:, lanes]
            weight = jnp.where(entry >= 0, stiff[:, lanes], 0.0)
            own = entry < BLOCK
            lane = entry & (BLOCK - 1)
            other = partner[first + t]
            for axis in range(3):
                mine = jnp.broadcast_to(held[axis][t : t + 1], entry.shape)
                theirs = extended[pl.ds(axis * blocks + other, 1), :]
                theirs = jnp.broadcast_to(theirs, entry.shape)
                met = jnp.where(own, lanes_of(mine, lane), lanes_of(theirs, lane))
                pulls[axis].append(weight * (mine - met))
        for axis in range(3):
            out[pl.ds(axis * tiles + first, SUB), :] = merged(pulls[axis])
        return carry

    lax.fori_loop(0, tiles // SUB, step, 0)


def shifted(plane):
    height, width = plane.shape
    row = iota((SUB, width), 0)
    column = iota((height, BLOCK), 1)
    above, below = pltpu.roll(plane, 1, 0), pltpu.roll(plane, height - 1, 0)
    left, right = pltpu.roll(plane, 1, 1), pltpu.roll(plane, width - 1, 1)
    above = jnp.concatenate([jnp.where(row == 0, 0.0, above[:SUB]), above[SUB:]], 0)
    below = jnp.concatenate([below[:-SUB], jnp.where(row == SUB - 1, 0.0, below[-SUB:])], 0)
    left = jnp.concatenate([jnp.where(column == 0, 0.0, left[:, :BLOCK]), left[:, BLOCK:]], 1)
    right = jnp.concatenate(
        [right[:, :-BLOCK], jnp.where(column == BLOCK - 1, 0.0, right[:, -BLOCK:])], 1
    )
    return above, below, left, right


def inverse_of(value):
    near = pl.reciprocal(value, approx=True)
    return near * (2.0 - value * near)


def placed(groups, ids, tiles):
    parts = [halves_of(group[:tiles, :]) for group in groups]
    loads = jnp.concatenate([part[i] for i in range(2) for part in parts], 0)
    ids = jnp.concatenate(ids, 1).astype(jnp.int32)

    def gathered(wanted):
        hot = jnp.where(wanted == jnp.broadcast_to(ids, wanted.shape), 1.0, 0.0).astype(BF16)
        total = jnp.dot(
            jnp.concatenate([hot, hot], 1), loads, preferred_element_type=F32
        )
        return total[:, :BLOCK], total[:, BLOCK:]

    return ids, gathered


def driven_of(early, late, planes):
    return lambda x: early[planes + x] if x < HEAD else late[x - HEAD]


def coefficients(gathered, tiles, first, full, driven_at, constant, factor, turned, present):
    planes, height, width = constant.shape
    zones = width // BLOCK
    shape = (zones * height, 3 * tiles)
    line = iota(shape, 0)
    block = (line % height) * zones + line // height + first * zones

    for x in range(planes):
        solid, drag = gathered(block + x * (full * zones))
        at = x if turned is None else jnp.where(turned, planes - 1 - x, x)
        voids = 1.0 + solid
        scale = inverse_of(6.0 + (drag + 1.0) * voids)
        if present is not None:
            scale = jnp.where(present, scale, 0.0)
        inverse = voids * scale
        for zone in range(zones):
            lanes = slice(zone * BLOCK, (zone + 1) * BLOCK)
            rows = slice(zone * height, (zone + 1) * height)
            driving = driven_at(x)[:, lanes] + solid[rows]
            constant[at, :, lanes] = driving * inverse[rows]
            factor[at, :, lanes] = scale[rows]


def own_kernel(
    full, mine, second, third, early, late, _message, _near, _far, _partner, constant, factor, weight, picks
):
    tiles = weight.shape[0]
    planes, height, width = constant.shape
    place = Place(full, height)
    zones = width // BLOCK
    groups = (mine, second, third)
    ids = [group[tiles : tiles + 1, :BLOCK] for group in groups]
    ids, gathered = placed(groups, ids, tiles)
    coefficients(
        gathered, tiles, place.first, full, driven_of(early, late, planes), constant, factor,
        place.even, None,
    )
    turned = [
        jnp.transpose(
            jnp.broadcast_to(ids[:, i * tiles : (i + 1) * tiles], (BLOCK, tiles)).astype(F32)
        ).astype(jnp.int32)
        for i in range(3)
    ]
    solid, drag = gathered(jnp.concatenate([turned[0]] * 3, 1))
    weight[...] = 1.0 / (1.0 / (1.0 + solid) + drag)
    for i in range(3):
        block = turned[i]
        line, zone = block // zones, block % zones
        x, y = line // full, line % full
        row = (x * zones + zone) * height + y - place.first
        held = y // place.own_rows == jnp.where(place.sweeps, place.half, -1)
        row = jnp.concatenate([jnp.where(held, row, -1)] * (picks.shape[1] // BLOCK), 1)
        hot = jnp.where(row == iota(row.shape, 1), 1.0, 0.0).astype(BF16)
        picks[i * tiles : (i + 1) * tiles, :] = hot


def sweep(source, target, coefficient, start, stop):
    def plane(at, carry):
        above, below, left, right = shifted(source[at])
        around = source[at - 1] + source[at + 1] + above + below + left + right
        constant, factor = coefficient(at)
        target[at] = constant + factor * around
        return carry

    lax.fori_loop(start, stop, plane, 0, unroll=4)


def deposits_of(message, tiles):
    groups = [message.at[i * tiles : (i + 1) * tiles] for i in range(3)]
    ids = [message[3 * tiles + i : 3 * tiles + i + 1, :BLOCK] for i in range(3)]
    return placed(groups, ids, tiles)[1]


def near_kernel(
    full, tiles, message, pressure, near, near_late, beyond, own_constant, own_factor, kept_even, kept_odd, constant, factor, old, new,
):
    planes, height, width = own_constant.shape
    place = Place(full, height)
    rim = planes + 1
    coefficients(
        deposits_of(message, tiles), tiles, place.first, full,
        driven_of(near, near_late, planes), constant, factor, place.even, jnp.where(place.odd, place.lower, place.upper),
    )
    old[0] = beyond[...]
    for x in range(planes):
        at = jnp.where(place.even, planes - 1 - x, x)
        old[1 + x] = near[at]
        old[rim + x] = pressure[at]
    buffers = (old, new)
    for index in range(planes):
        source, target = buffers[index % 2], buffers[(index + 1) % 2]
        sweep(source, target, lambda at: (constant[at - 1], factor[at - 1]), 1 + index, rim)
        sweep(
            source, target, lambda at: (own_constant[at - rim], own_factor[at - rim]),
            rim, 2 * planes - index,
        )
    kept_even[...] = old[planes : 2 * planes]
    kept_odd[...] = new[planes : 2 * planes]


def far_kernel(
    full, tiles, picks, message, pressure, far, far_late, own_constant, own_factor, kept_even, kept_odd,
    across, between, pieces, constant, factor, old, new, fields,
):
    planes, height, width = own_constant.shape
    zones = width // BLOCK
    place = Place(full, height)
    rim = planes + 1
    coefficients(
        deposits_of(message, tiles), tiles, place.first, full,
        driven_of(far, far_late, planes), constant, factor, place.even, jnp.where(place.odd, place.upper, place.lower),
    )
    old[planes : 2 * planes] = kept_even[...]
    new[planes : 2 * planes] = kept_odd[...]
    old[2 * planes] = pressure[jnp.where(place.even, 0, planes - 1)]
    for x in range(planes):
        at = jnp.where(place.even, planes - 1 - x, x)
        old[rim + planes + x] = far[at]
    old[rim + 2 * planes] = far[planes + HEAD]
    buffers = (old, new)
    edge = rim + planes
    for index in range(planes):
        source, target = buffers[index % 2], buffers[(index + 1) % 2]
        sweep(
            source, target, lambda at: (own_constant[at - rim], own_factor[at - rim]),
            2 * planes - index, edge,
        )
        sweep(
            source, target, lambda at: (constant[at - edge], factor[at - edge]),
            edge, edge + planes - index,
        )
    last = buffers[planes % 2]
    way = jnp.where(place.even, -0.5, 0.5)

    def gradient(x, carry):
        at = rim + x
        above, below, left, right = shifted(last[at])
        grads = (way * (last[at + 1] - last[at - 1]), 0.5 * (below - above), 0.5 * (right - left))
        line = jnp.where(place.even, planes - 1 - x, x) * zones
        for zone in range(zones):
            first = pl.multiple_of((line + zone) * height, SUB)
            for axis, grad in enumerate(grads):
                fields[pl.ds(first, height), axis * BLOCK : (axis + 1) * BLOCK] = (
                    grad[:, zone * BLOCK : (zone + 1) * BLOCK]
                )
        return carry

    lax.fori_loop(0, planes, gradient, 0, unroll=4)
    pieces[...] = jnp.concatenate(halves_of(fields[...]), 1)
    total = picked_rows(picks[tiles:, :], pieces)
    first, second = total[:tiles], total[tiles:]
    low = lax.axis_index("grp") == 0
    across[...] = jnp.where(low, first, second)
    between[...] = jnp.where(low, second, first)


def picked_rows(hot, pieces):
    total = jnp.dot(hot, pieces[...], preferred_element_type=F32)
    return total[:, : 3 * BLOCK] + total[:, 3 * BLOCK :]


def pick_kernel(picks, pieces, out):
    out[...] = picked_rows(picks[: out.shape[0], :], pieces)


def final_kernel(
    count, grads_a, grads_b, grads_c, grads_d, weight, contact, vel, vol, drag, cell, out,
):
    tiles = cell.shape[0]
    cells = cell[...]
    heft = lanes_of(weight[...], cells)
    slot = iota(cells.shape, 0) * BLOCK + iota(cells.shape, 1)
    live = slot < count[0]
    volume = vol[...]
    push = TIME_STEP / volume
    for axis in range(3):
        lanes = slice(axis * BLOCK, (axis + 1) * BLOCK)
        gradient = grads_a[:, lanes] + grads_b[:, lanes] + (grads_c[:, lanes] + grads_d[:, lanes])
        gradient = lanes_of(gradient, cells)
        own = jnp.concatenate(
            [vel[axis : axis + 1, t * BLOCK : (t + 1) * BLOCK] for t in range(tiles)], 0
        )
        fluid = -gradient * heft
        force = contact[axis * tiles : (axis + 1) * tiles, :] - volume * gradient
        force = force + drag[...] * (fluid - own)
        new = jnp.where(live, own + force * push, 0.0)
        for t in range(tiles):
            out[axis : axis + 1, t * BLOCK : (t + 1) * BLOCK] = new[t : t + 1, :]


def on_device(
    grain_pos,
    grain_vel,
    grain_vol,
    drag_coef,
    grain_count,
    contact_rows,
    contact_stiff,
    partner_block,
    halo_list,
    grain_cell,
    tile_cell_block,
    pressure_old,
    pressure_source,
    solid_old,
):
    groups, regions = lax.axis_size("grp"), lax.axis_size("reg")
    holding = groups - 1
    halves = groups // CORES
    slots = grain_pos.shape[1]
    tiles = slots // BLOCK
    planes, full, width = pressure_old.shape
    assert planes == ITERS
    own_rows = full // halves
    height = min(full, own_rows + SUB * min(2, halves - 1))
    owners = range(0, groups, CORES)
    holders = range(holding)

    def send(value, pairs):
        flat = [(a[0] * regions + a[1], b[0] * regions + b[1]) for a, b in pairs]
        return lax.ppermute(value, ("grp", "reg"), flat)

    def along_reg(value, members, goes, core=0):
        pairs = [
            ((g + core, r), (g, r + goes[r % 2]))
            for g in members
            for r in range(regions)
            if 0 <= r + goes[r % 2] < regions
        ]
        return send(value, pairs)

    def along_grp(value, step, members):
        pairs = [((g, r), ((g + step) % holding, r)) for g in members for r in range(regions)]
        return send(value, pairs)

    count = grain_count
    cell = grain_cell.reshape(tiles, BLOCK)
    vol = grain_vol.reshape(tiles, BLOCK)
    drag = drag_coef.reshape(tiles, BLOCK)
    ids = tile_cell_block.reshape(1, tiles)
    field_bytes = 4 * planes * height * width

    field = shaped(planes, height, width)
    plane = shaped(height, width)
    small = shaped(SUB, BLOCK)
    early, late, ends = call(
        window_kernel,
        (
            shaped(planes + HEAD, height, width), shaped(planes - HEAD, height, width), plane,
        ),
        [HBM] * 3, (pressure_old, pressure_source, solid_old),
        [pltpu.VMEM((planes, height, width), F32)] * 3
        + [pltpu.SemaphoreType.DMA((5 * planes + 1,))],
        flops=field_bytes, size=6 * field_bytes, limit=61_950_000, place=HBM,
    )
    near = along_reg(early, owners, (1, -1), core=1)
    near_late = along_reg(late, owners, (1, -1), core=1)
    beyond = along_reg(ends, owners, (-2, 2), core=1)
    mine, after_deposit = call(
        deposit_kernel, (shaped(tiles + SUB, 2 * BLOCK), small), [SMEM] + [VMEM] * 4,
        (count, cell, vol, drag, ids), flops=2 * 32 * 48 * 65536, size=5 * 4 * slots,
    )
    second = along_grp(mine, 1, holders)
    third = along_grp(mine, 2, holders)
    rows = halo_list.shape[1] // BLOCK
    halo = shaped(3 * rows, BLOCK)
    state, halo_near, halo_far, after_halo = call(
        halo_kernel, (shaped(3 * tiles, BLOCK), halo, halo, small),
        [VMEM] * 4, (grain_pos, grain_vel, halo_list, after_deposit), flops=slots,
        size=4 * 4 * 3 * slots,
    )
    others = [g for g in holders if g not in owners]
    came_near = along_reg(halo_near, others, (1, -1))
    came_far = along_reg(halo_far, others, (-1, 1))
    far, after_forward = call(
        forward_kernel, (shaped(planes + HEAD + 1, height, width), small), [VMEM] * 5,
        (near, early, after_halo, second, third), size=5 * field_bytes,
    )
    far = along_reg(far, owners, (2, -2))
    far_late = along_reg(near_late, owners, (2, -2))
    message = shaped(holding * tiles + SUB + 3 * rows // 2, 2 * BLOCK)
    message_near, message_far, after_message = call(
        message_kernel, (message, message, small), [VMEM] * 6,
        (mine, second, third, halo_near, halo_far, after_forward), size=8 * 2 * BLOCK * 500,
    )
    message_near = along_reg(message_near, owners, (1, -1))
    message_far = along_reg(message_far, owners, (-1, 1))
    constant, factor, weight, picks = call(
        functools.partial(own_kernel, full),
        (
            field, field, shaped(tiles, BLOCK),
            jax.ShapeDtypeStruct((3 * tiles, planes * height * width // BLOCK), BF16),
        ),
        [VMEM] * 8 + [SMEM],
        (mine, second, third, early, late, after_message, came_near, came_far, partner_block),
        flops=planes * height * 4 * 384 * 256 * 6, size=9 * field_bytes,
    )
    window_of = lambda count: pltpu.VMEM((count, height, width), F32)
    kept_even, kept_odd = call(
        functools.partial(near_kernel, full, tiles), (field, field), [VMEM] * 7,
        (message_near, early, near, near_late, beyond, constant, factor),
        [window_of(planes)] * 2 + [window_of(2 * planes + 1)] * 2,
        flops=planes * height * 4 * 384 * 256 * 6, size=9 * field_bytes,
    )
    grads = shaped(tiles, 3 * BLOCK)
    cells_held = planes * height * width // BLOCK
    grads_across, grads_between, pieces = call(
        functools.partial(far_kernel, full, tiles),
        (grads, grads, jax.ShapeDtypeStruct((cells_held, 6 * BLOCK), BF16)), [VMEM] * 9,
        (picks, message_far, early, far, far_late, constant, factor, kept_even, kept_odd),
        [window_of(planes)] * 2
        + [window_of(3 * planes + 2)] * 2
        + [pltpu.VMEM((cells_held, 3 * BLOCK), F32)],
        flops=planes * height * 4 * 384 * 256 * 6, size=9 * field_bytes,
    )
    ends_of = lambda source, target: [((source, r), (target, r)) for r in range(regions)]
    low, high, between = 0, CORES, 1
    came_low = send(grads_between, ends_of(low, between))
    came_high = send(grads_between, ends_of(high, between))
    came_across = send(grads_across, ends_of(low, high) + ends_of(high, low))
    grads_a = call(pick_kernel, grads, [VMEM] * 2, (picks, pieces), flops=slots, size=slots)
    contact = call(
        contact_kernel, shaped(3 * tiles, BLOCK), [SMEM] + [VMEM] * 7 + [ANY],
        (
            partner_block, state, message_near, message_far, came_near, came_far, contact_rows,
            contact_stiff, grads_a,
        ),
        [pltpu.VMEM((3 * (tiles + 2 * rows), BLOCK), F32)],
        flops=60 * 8 * slots, size=4 * 20 * slots,
    )
    return call(
        final_kernel, shaped(3, slots), [SMEM] + [VMEM] * 10,
        (
            count, grads_a, came_across, came_low, came_high, weight, contact, grain_vel, vol, drag,
            cell,
        ),
        flops=60 * slots, size=4 * 20 * slots,
    )


def solution(mesh):
    in_specs = (
        P(None, ("grp", "reg")),
        P(None, ("grp", "reg")),
        P(("grp", "reg")),
        P(("grp", "reg")),
        P(("grp", "reg")),
        P(None, ("grp", "reg")),
        P(None, ("grp", "reg")),
        P(("grp", "reg")),
        P(None, ("grp", "reg")),
        P(("grp", "reg")),
        P(("grp", "reg")),
        P("reg", None, None),
        P("reg", None, None),
        P("reg", None, None),
    )
    out_specs = P(None, ("grp", "reg"))
    return jax.shard_map(
        on_device, mesh=mesh, in_specs=in_specs, out_specs=out_specs, check_vma=False
    )
```

```python
import functools

import jax
import jax.numpy as jnp
from jax import lax
from jax.experimental import pallas as pl
from jax.experimental.pallas import tpu as pltpu
from jax.sharding import PartitionSpec as P

BLOCK = 128
SUB = 8
CORES = 2
ITERS = 4
HEAD = 1
SPRING = 1.0
DAMPING = 0.5
TIME_STEP = 0.5

VMEM = pl.BlockSpec(memory_space=pltpu.VMEM)
SMEM = pl.BlockSpec(memory_space=pltpu.SMEM)
ANY = pl.BlockSpec(memory_space=pl.ANY)
HBM = pl.BlockSpec(memory_space=pltpu.HBM)
F32 = jnp.float32
BF16 = jnp.bfloat16


def iota(shape, dim):
    return lax.broadcasted_iota(jnp.int32, shape, dim)


def shaped(*dims):
    return jax.ShapeDtypeStruct(dims, F32)


def call(kernel, outs, specs, args, scratch=(), flops=0, size=0, limit=40_000_000, place=VMEM):
    return pl.pallas_call(
        kernel,
        out_shape=outs,
        in_specs=specs,
        out_specs=jax.tree.map(lambda _: place, outs),
        scratch_shapes=list(scratch),
        compiler_params=pltpu.CompilerParams(vmem_limit_bytes=limit),
        cost_estimate=pl.CostEstimate(flops=flops, bytes_accessed=size, transcendentals=0),
    )(*args)


class Place:
    def __init__(self, full, height):
        groups, regions = lax.axis_size("grp"), lax.axis_size("reg")
        self.group, region = lax.axis_index("grp"), lax.axis_index("reg")
        self.half = self.group // CORES
        self.own_rows = full // (groups // CORES)
        first = jnp.clip(self.half * self.own_rows - SUB, 0, full - height)
        self.first = pl.multiple_of(first, SUB)
        self.sweeps = self.group % CORES == 0
        self.parity = region % 2
        self.odd, self.even = self.parity == 1, self.parity == 0
        self.lower, self.upper = region > 0, region < regions - 1


def lanes_of(source, index):
    return jnp.take_along_axis(source, index, axis=1, mode="promise_in_bounds")


def halves_of(value):
    high = value.astype(BF16)
    return high, (value - high.astype(F32)).astype(BF16)


def window_kernel(
    pressure_old, source, solid_before, early, late, ends, pressure, driven, solid, sems
):
    planes, height, _ = solid.shape
    place = Place(pressure_old.shape[1], height)
    rows = pl.ds(place.first, height)
    used = []

    def copy(whole, part):
        used.append(None)
        return pltpu.make_async_copy(whole, part, sems.at[len(used) - 1])

    fetched = [
        [copy(whole.at[x, rows, :], part.at[x]) for x in range(planes)]
        for whole, part in ((pressure_old, pressure), (source, driven), (solid_before, solid))
    ]
    stored = [copy(pressure.at[x], early.at[x]) for x in range(planes)]
    for x in range(planes):
        stored.append(copy(driven.at[x], early.at[planes + x] if x < HEAD else late.at[x - HEAD]))
    stored.append(copy(pressure.at[place.parity * (planes - 1)], ends))
    for x in range(planes):
        for part in fetched:
            part[x].start()
    for x in range(planes):
        fetched[0][x].wait()
        stored[x].start()
        fetched[1][x].wait()
        fetched[2][x].wait()
        driven[x] = driven[x] - solid[x]
        stored[planes + x].start()
    stored[-1].start()
    for one in stored:
        one.wait()


def forward_kernel(near, early, _halo, _second, _third, _beyond, out, dummy):
    dummy[...] = jnp.zeros(dummy.shape, F32)
    count = near.shape[0]
    out[:count] = near[...]
    end = (1 - lax.axis_index("reg") % 2) * (count - HEAD - 1)
    out[count] = early[end]


def deposit_kernel(count, cell, vol, drag, ids, out, dummy):
    dummy[...] = jnp.zeros(dummy.shape, F32)
    tiles = cell.shape[0]
    sub = iota((SUB, BLOCK), 0)
    rows_c = iota((BLOCK, BLOCK), 0)
    even = sub % 2 == 0
    low_pair = sub % 4 < 2

    def step(group, carry):
        first = pl.multiple_of(group * SUB, SUB)
        slot = (first + sub) * BLOCK + iota((SUB, BLOCK), 1)
        live = slot < count[0]
        cells = cell[pl.ds(first, SUB), :]
        parts = halves_of(jnp.where(live, vol[pl.ds(first, SUB), :], 0.0)) + halves_of(
            jnp.where(live, drag[pl.ds(first, SUB), :], 0.0)
        )
        parts = [part.astype(F32) for part in parts]
        left = jnp.concatenate([jnp.where(even, part, 0.0) for part in parts], 0)
        right = jnp.concatenate([jnp.where(even, 0.0, part) for part in parts], 0)
        loads = jnp.concatenate([left, right], 1).astype(BF16)
        sums = [jnp.zeros((SUB, BLOCK), F32), jnp.zeros((SUB, BLOCK), F32)]
        for quad in range(SUB // 4):
            hot = [
                jnp.where(
                    rows_c == jnp.broadcast_to(cells[t : t + 1, :], (BLOCK, BLOCK)), 1.0, 0.0
                ).astype(BF16)
                for t in range(4 * quad, 4 * quad + 4)
            ]
            picked = jnp.concatenate(
                [jnp.concatenate(hot[:2], 1), jnp.concatenate(hot[2:], 1)], 0
            )
            placed = lax.dot_general(
                loads, picked, (((1,), (1,)), ((), ())), preferred_element_type=F32
            )
            for field in range(2):
                base = field * 2 * SUB
                total = placed[base : base + SUB] + placed[base + SUB : base + 2 * SUB]
                chosen = jnp.where(low_pair, total[:, :BLOCK], total[:, BLOCK:])
                sums[field] = jnp.where(sub // 4 == quad, chosen, sums[field])
        out[pl.ds(first, SUB), :BLOCK] = sums[0]
        out[pl.ds(first, SUB), BLOCK:] = sums[1]
        return carry

    lax.fori_loop(0, tiles // SUB, step, 0, unroll=4)
    out[tiles : tiles + SUB, :BLOCK] = jnp.broadcast_to(ids[...].astype(F32), (SUB, BLOCK))
    out[tiles : tiles + SUB, BLOCK:] = jnp.zeros((SUB, BLOCK), F32)


def halo_kernel(pos, vel, lists, _, state, near, far, dummy):
    dummy[...] = jnp.zeros(dummy.shape, F32)
    tiles = pos.shape[1] // BLOCK
    rows = lists.shape[1] // BLOCK
    for tile in range(tiles):
        lanes = slice(tile * BLOCK, (tile + 1) * BLOCK)
        mixed = SPRING * pos[:, lanes] - DAMPING * vel[:, lanes]
        for axis in range(3):
            state[axis * tiles + tile : axis * tiles + tile + 1, :] = mixed[axis : axis + 1]
    turned = [
        jnp.concatenate(halves_of(jnp.transpose(state[axis * tiles : (axis + 1) * tiles, :])), 1)
        for axis in range(3)
    ]
    turned = jnp.concatenate(turned, 0)
    span = 2 * BLOCK
    row = iota((BLOCK, span), 0)

    odd = lax.axis_index("reg") % 2
    for away, out in enumerate((near, far)):
        side = 1 - odd if away == 0 else odd

        def step(part, carry):
            named = lists[:, pl.ds(pl.multiple_of(part * span, span), span)]
            named = jnp.where(side == 0, named[:1], named[1:])
            block = lax.shift_right_logical(named, 7)
            lane = named & (BLOCK - 1)
            hot = jnp.where(row == jnp.broadcast_to(block, row.shape), 1.0, 0.0).astype(BF16)
            found = jnp.dot(
                turned, jnp.concatenate([hot, hot], 0), preferred_element_type=F32
            )
            here = row == jnp.broadcast_to(lane, row.shape)
            for axis in range(3):
                value = jnp.where(here, found[axis * BLOCK : (axis + 1) * BLOCK], 0.0)
                value = jnp.sum(value, axis=0, keepdims=True)
                for half in range(2):
                    out[pl.ds(axis * rows + 2 * part + half, 1), :] = value[
                        :, half * BLOCK : (half + 1) * BLOCK
                    ]
            return carry

        lax.fori_loop(0, rows // 2, step, 0, unroll=8)


def message_kernel(mine, second, third, halo_near, halo_far, _, near, far, dummy):
    dummy[...] = jnp.zeros(dummy.shape, F32)
    tiles = mine.shape[0] - SUB
    half = halo_near.shape[0] // 2
    rows = near.shape[0] - half
    groups = (mine, second, third)
    sub = iota((SUB, 2 * BLOCK), 0)
    ids = groups[0][tiles:, :]
    for index in (1, 2):
        ids = jnp.where(sub == index, groups[index][tiles:, :], ids)
    for halo, out in ((halo_near, near), (halo_far, far)):
        for index, group in enumerate(groups):
            out[index * tiles : (index + 1) * tiles, :] = group[:tiles, :]
        out[rows - SUB : rows, :] = ids
        out[rows:, :BLOCK] = halo[:half, :]
        out[rows:, BLOCK:] = halo[half:, :]


def merged(parts):
    sub = iota((SUB, BLOCK), 0)
    for step in (4, 2, 1):
        low = (sub & step) == 0
        paired = []
        for first, second in zip(parts[:step], parts[step:]):
            away = jnp.where(low, second, first)
            back = pltpu.roll(away, step, 0)
            if step < SUB // 2:
                back = jnp.where(low, pltpu.roll(away, SUB - step, 0), back)
            paired.append(jnp.where(low, first, second) + back)
        parts = paired
    return parts[0]


def contact_kernel(
    partner, state, message_near, message_far, halo_near, halo_far, named, stiff, _, out, extended,
):
    tiles = state.shape[0] // 3
    rows = halo_near.shape[0] // 3
    blocks = tiles + 2 * rows
    base = message_near.shape[0] - 3 * rows // 2
    odd = lax.axis_index("reg") % 2
    sweeps = lax.axis_index("grp") % CORES == 0
    for axis in range(3):
        extended[axis * blocks : axis * blocks + tiles, :] = state[
            axis * tiles : (axis + 1) * tiles, :
        ]
    for message, halo, upper in (
        (message_near, halo_near, 1 - odd), (message_far, halo_far, odd)
    ):
        carried = jnp.concatenate([message[base:, :BLOCK], message[base:, BLOCK:]], 0)
        carried = jnp.where(sweeps, carried, halo[...])
        for axis in range(3):
            first = pl.multiple_of(axis * blocks + tiles + upper * rows, SUB)
            extended[pl.ds(first, rows), :] = carried[axis * rows : (axis + 1) * rows]

    def step(group, carry):
        first = pl.multiple_of(group * SUB, SUB)
        held = [extended[pl.ds(axis * blocks + first, SUB), :] for axis in range(3)]
        pulls = [[], [], []]
        for t in range(SUB):
            lanes = pl.ds(pl.multiple_of((first + t) * BLOCK, BLOCK), BLOCK)
            entry = named[:, lanes]
            weight = jnp.where(entry >= 0, stiff[:, lanes], 0.0)
            own = entry < BLOCK
            lane = entry & (BLOCK - 1)
            other = partner[first + t]
            for axis in range(3):
                mine = jnp.broadcast_to(held[axis][t : t + 1], entry.shape)
                theirs = extended[pl.ds(axis * blocks + other, 1), :]
                theirs = jnp.broadcast_to(theirs, entry.shape)
                met = jnp.where(own, lanes_of(mine, lane), lanes_of(theirs, lane))
                pulls[axis].append(weight * (mine - met))
        for axis in range(3):
            out[pl.ds(axis * tiles + first, SUB), :] = merged(pulls[axis])
        return carry

    lax.fori_loop(0, tiles // SUB, step, 0, unroll=2)


def shifted(plane):
    height, width = plane.shape
    row = iota((SUB, width), 0)
    column = iota((height, BLOCK), 1)
    above, below = pltpu.roll(plane, 1, 0), pltpu.roll(plane, height - 1, 0)
    left, right = pltpu.roll(plane, 1, 1), pltpu.roll(plane, width - 1, 1)
    above = jnp.concatenate([jnp.where(row == 0, 0.0, above[:SUB]), above[SUB:]], 0)
    below = jnp.concatenate([below[:-SUB], jnp.where(row == SUB - 1, 0.0, below[-SUB:])], 0)
    left = jnp.concatenate([jnp.where(column == 0, 0.0, left[:, :BLOCK]), left[:, BLOCK:]], 1)
    right = jnp.concatenate(
        [right[:, :-BLOCK], jnp.where(column == BLOCK - 1, 0.0, right[:, -BLOCK:])], 1
    )
    return above, below, left, right


def inverse_of(value):
    near = pl.reciprocal(value, approx=True)
    return near * (2.0 - value * near)


def placed(groups, ids, tiles):
    parts = [halves_of(group[:tiles, :]) for group in groups]
    loads = jnp.concatenate([part[i] for i in range(2) for part in parts], 0)
    ids = jnp.concatenate(ids, 1).astype(jnp.int32)

    def gathered(wanted):
        hot = jnp.where(wanted == jnp.broadcast_to(ids, wanted.shape), 1.0, 0.0).astype(BF16)
        total = jnp.dot(
            jnp.concatenate([hot, hot], 1), loads, preferred_element_type=F32
        )
        return total[:, :BLOCK], total[:, BLOCK:]

    return ids, gathered


def driven_of(early, late, planes):
    return lambda x: early[planes + x] if x < HEAD else late[x - HEAD]


def coefficients(gathered, tiles, first, full, driven_at, constant, factor, turned, present):
    planes, height, width = constant.shape
    zones = width // BLOCK
    shape = (zones * height, 3 * tiles)
    line = iota(shape, 0)
    block = (line % height) * zones + line // height + first * zones

    for x in range(planes):
        solid, drag = gathered(block + x * (full * zones))
        at = x if turned is None else jnp.where(turned, planes - 1 - x, x)
        voids = 1.0 + solid
        scale = inverse_of(6.0 + (drag + 1.0) * voids)
        if present is not None:
            scale = jnp.where(present, scale, 0.0)
        inverse = voids * scale
        for zone in range(zones):
            lanes = slice(zone * BLOCK, (zone + 1) * BLOCK)
            rows = slice(zone * height, (zone + 1) * height)
            driving = driven_at(x)[:, lanes] + solid[rows]
            constant[at, :, lanes] = driving * inverse[rows]
            factor[at, :, lanes] = scale[rows]


def own_kernel(
    full, mine, second, third, early, late, _message, _near, _far, _partner, constant, factor, weight, picks
):
    tiles = weight.shape[0]
    planes, height, width = constant.shape
    place = Place(full, height)
    zones = width // BLOCK
    groups = (mine, second, third)
    ids = [group[tiles : tiles + 1, :BLOCK] for group in groups]
    ids, gathered = placed(groups, ids, tiles)
    coefficients(
        gathered, tiles, place.first, full, driven_of(early, late, planes), constant, factor,
        place.even, None,
    )
    turned = [
        jnp.transpose(
            jnp.broadcast_to(ids[:, i * tiles : (i + 1) * tiles], (BLOCK, tiles)).astype(F32)
        ).astype(jnp.int32)
        for i in range(3)
    ]
    solid, drag = gathered(jnp.concatenate([turned[0]] * 3, 1))
    weight[...] = 1.0 / (1.0 / (1.0 + solid) + drag)
    for i in range(3):
        block = turned[i]
        line, zone = block // zones, block % zones
        x, y = line // full, line % full
        row = (x * zones + zone) * height + y - place.first
        held = y // place.own_rows == jnp.where(place.sweeps, place.half, -1)
        row = jnp.concatenate([jnp.where(held, row, -1)] * (picks.shape[1] // BLOCK), 1)
        hot = jnp.where(row == iota(row.shape, 1), 1.0, 0.0).astype(BF16)
        picks[i * tiles : (i + 1) * tiles, :] = hot


def sweep(source, target, coefficient, start, stop):
    def plane(at, carry):
        above, below, left, right = shifted(source[at])
        around = source[at - 1] + source[at + 1] + above + below + left + right
        constant, factor = coefficient(at)
        target[at] = constant + factor * around
        return carry

    lax.fori_loop(start, stop, plane, 0, unroll=4)


def deposits_of(message, tiles):
    groups = [message.at[i * tiles : (i + 1) * tiles] for i in range(3)]
    ids = [message[3 * tiles + i : 3 * tiles + i + 1, :BLOCK] for i in range(3)]
    return placed(groups, ids, tiles)[1]


def near_kernel(
    full, tiles, message, pressure, near, near_late, beyond, own_constant, own_factor, kept_even, kept_odd, constant, factor, old, new,
):
    planes, height, width = own_constant.shape
    place = Place(full, height)
    rim = planes + 1
    coefficients(
        deposits_of(message, tiles), tiles, place.first, full,
        driven_of(near, near_late, planes), constant, factor, place.even, jnp.where(place.odd, place.lower, place.upper),
    )
    old[0] = beyond[...]
    for x in range(planes):
        at = jnp.where(place.even, planes - 1 - x, x)
        old[1 + x] = near[at]
        old[rim + x] = pressure[at]
    buffers = (old, new)
    for index in range(planes):
        source, target = buffers[index % 2], buffers[(index + 1) % 2]
        sweep(source, target, lambda at: (constant[at - 1], factor[at - 1]), 1 + index, rim)
        sweep(
            source, target, lambda at: (own_constant[at - rim], own_factor[at - rim]),
            rim, 2 * planes - index,
        )
    kept_even[...] = old[planes : 2 * planes]
    kept_odd[...] = new[planes : 2 * planes]


def far_kernel(
    full, tiles, picks, message, pressure, far, far_late, own_constant, own_factor, kept_even, kept_odd,
    across, between, pieces, constant, factor, old, new, fields,
):
    planes, height, width = own_constant.shape
    zones = width // BLOCK
    place = Place(full, height)
    rim = planes + 1
    coefficients(
        deposits_of(message, tiles), tiles, place.first, full,
        driven_of(far, far_late, planes), constant, factor, place.even, jnp.where(place.odd, place.upper, place.lower),
    )
    old[planes : 2 * planes] = kept_even[...]
    new[planes : 2 * planes] = kept_odd[...]
    old[2 * planes] = pressure[jnp.where(place.even, 0, planes - 1)]
    for x in range(planes):
        at = jnp.where(place.even, planes - 1 - x, x)
        old[rim + planes + x] = far[at]
    old[rim + 2 * planes] = far[planes + HEAD]
    buffers = (old, new)
    edge = rim + planes
    for index in range(planes):
        source, target = buffers[index % 2], buffers[(index + 1) % 2]
        sweep(
            source, target, lambda at: (own_constant[at - rim], own_factor[at - rim]),
            2 * planes - index, edge,
        )
        sweep(
            source, target, lambda at: (constant[at - edge], factor[at - edge]),
            edge, edge + planes - index,
        )
    last = buffers[planes % 2]
    way = jnp.where(place.even, -0.5, 0.5)

    def gradient(x, carry):
        at = rim + x
        above, below, left, right = shifted(last[at])
        grads = (way * (last[at + 1] - last[at - 1]), 0.5 * (below - above), 0.5 * (right - left))
        line = jnp.where(place.even, planes - 1 - x, x) * zones
        for zone in range(zones):
            first = pl.multiple_of((line + zone) * height, SUB)
            for axis, grad in enumerate(grads):
                fields[pl.ds(first, height), axis * BLOCK : (axis + 1) * BLOCK] = (
                    grad[:, zone * BLOCK : (zone + 1) * BLOCK]
                )
        return carry

    lax.fori_loop(0, planes, gradient, 0, unroll=4)
    pieces[...] = jnp.concatenate(halves_of(fields[...]), 1)
    total = picked_rows(picks[tiles:, :], pieces)
    first, second = total[:tiles], total[tiles:]
    low = lax.axis_index("grp") == 0
    across[...] = jnp.where(low, first, second)
    between[...] = jnp.where(low, second, first)


def picked_rows(hot, pieces):
    total = jnp.dot(hot, pieces[...], preferred_element_type=F32)
    return total[:, : 3 * BLOCK] + total[:, 3 * BLOCK :]


def pick_kernel(picks, pieces, out):
    out[...] = picked_rows(picks[: out.shape[0], :], pieces)


def final_kernel(
    count, grads_a, grads_b, grads_c, grads_d, weight, contact, vel, vol, drag, cell, out,
):
    tiles = cell.shape[0]
    cells = cell[...]
    heft = lanes_of(weight[...], cells)
    slot = iota(cells.shape, 0) * BLOCK + iota(cells.shape, 1)
    live = slot < count[0]
    volume = vol[...]
    push = TIME_STEP / volume
    for axis in range(3):
        lanes = slice(axis * BLOCK, (axis + 1) * BLOCK)
        gradient = grads_a[:, lanes] + grads_b[:, lanes] + (grads_c[:, lanes] + grads_d[:, lanes])
        gradient = lanes_of(gradient, cells)
        own = jnp.concatenate(
            [vel[axis : axis + 1, t * BLOCK : (t + 1) * BLOCK] for t in range(tiles)], 0
        )
        fluid = -gradient * heft
        force = contact[axis * tiles : (axis + 1) * tiles, :] - volume * gradient
        force = force + drag[...] * (fluid - own)
        new = jnp.where(live, own + force * push, 0.0)
        for t in range(tiles):
            out[axis : axis + 1, t * BLOCK : (t + 1) * BLOCK] = new[t : t + 1, :]


def on_device(
    grain_pos,
    grain_vel,
    grain_vol,
    drag_coef,
    grain_count,
    contact_rows,
    contact_stiff,
    partner_block,
    halo_list,
    grain_cell,
    tile_cell_block,
    pressure_old,
    pressure_source,
    solid_old,
):
    groups, regions = lax.axis_size("grp"), lax.axis_size("reg")
    holding = groups - 1
    halves = groups // CORES
    slots = grain_pos.shape[1]
    tiles = slots // BLOCK
    planes, full, width = pressure_old.shape
    assert planes == ITERS
    own_rows = full // halves
    height = min(full, own_rows + SUB * min(2, halves - 1))
    owners = range(0, groups, CORES)
    holders = range(holding)

    def send(value, pairs):
        flat = [(a[0] * regions + a[1], b[0] * regions + b[1]) for a, b in pairs]
        return lax.ppermute(value, ("grp", "reg"), flat)

    def along_reg(value, members, goes, core=0):
        pairs = [
            ((g + core, r), (g, r + goes[r % 2]))
            for g in members
            for r in range(regions)
            if 0 <= r + goes[r % 2] < regions
        ]
        return send(value, pairs)

    def along_grp(value, step, members):
        pairs = [((g, r), ((g + step) % holding, r)) for g in members for r in range(regions)]
        return send(value, pairs)

    count = grain_count
    cell = grain_cell.reshape(tiles, BLOCK)
    vol = grain_vol.reshape(tiles, BLOCK)
    drag = drag_coef.reshape(tiles, BLOCK)
    ids = tile_cell_block.reshape(1, tiles)
    field_bytes = 4 * planes * height * width

    field = shaped(planes, height, width)
    plane = shaped(height, width)
    small = shaped(SUB, BLOCK)
    early, late, ends = call(
        window_kernel,
        (
            shaped(planes + HEAD, height, width), shaped(planes - HEAD, height, width), plane,
        ),
        [HBM] * 3, (pressure_old, pressure_source, solid_old),
        [pltpu.VMEM((planes, height, width), F32)] * 3
        + [pltpu.SemaphoreType.DMA((5 * planes + 1,))],
        flops=field_bytes, size=6 * field_bytes, limit=61_950_000, place=HBM,
    )
    near = along_reg(early, owners, (1, -1), core=1)
    near_late = along_reg(late, owners, (1, -1), core=1)
    beyond = along_reg(ends, owners, (-2, 2), core=1)
    mine, after_deposit = call(
        deposit_kernel, (shaped(tiles + SUB, 2 * BLOCK), small), [SMEM] + [VMEM] * 4,
        (count, cell, vol, drag, ids), flops=2 * 32 * 48 * 65536, size=5 * 4 * slots,
    )
    second = along_grp(mine, 1, holders)
    third = along_grp(mine, 2, holders)
    rows = halo_list.shape[1] // BLOCK
    halo = shaped(3 * rows, BLOCK)
    state, halo_near, halo_far, after_halo = call(
        halo_kernel, (shaped(3 * tiles, BLOCK), halo, halo, small),
        [VMEM] * 4, (grain_pos, grain_vel, halo_list, after_deposit), flops=slots,
        size=4 * 4 * 3 * slots,
    )
    others = [g for g in holders if g not in owners]
    came_near = along_reg(halo_near, others, (1, -1))
    came_far = along_reg(halo_far, others, (-1, 1))
    far, after_forward = call(
        forward_kernel, (shaped(planes + HEAD + 1, height, width), small), [VMEM] * 6,
        (near, early, after_halo, second, third, beyond), size=5 * field_bytes,
    )
    far = along_reg(far, owners, (2, -2))
    far_late = along_reg(near_late, owners, (2, -2))
    message = shaped(holding * tiles + SUB + 3 * rows // 2, 2 * BLOCK)
    message_near, message_far, after_message = call(
        message_kernel, (message, message, small), [VMEM] * 6,
        (mine, second, third, halo_near, halo_far, after_forward), size=8 * 2 * BLOCK * 500,
    )
    message_near = along_reg(message_near, owners, (1, -1))
    message_far = along_reg(message_far, owners, (-1, 1))
    constant, factor, weight, picks = call(
        functools.partial(own_kernel, full),
        (
            field, field, shaped(tiles, BLOCK),
            jax.ShapeDtypeStruct((3 * tiles, planes * height * width // BLOCK), BF16),
        ),
        [VMEM] * 8 + [SMEM],
        (mine, second, third, early, late, after_message, came_near, came_far, partner_block),
        flops=planes * height * 4 * 384 * 256 * 6, size=9 * field_bytes,
    )
    window_of = lambda count: pltpu.VMEM((count, height, width), F32)
    kept_even, kept_odd = call(
        functools.partial(near_kernel, full, tiles), (field, field), [VMEM] * 7,
        (message_near, early, near, near_late, beyond, constant, factor),
        [window_of(planes)] * 2 + [window_of(2 * planes + 1)] * 2,
        flops=planes * height * 4 * 384 * 256 * 6, size=9 * field_bytes,
    )
    grads = shaped(tiles, 3 * BLOCK)
    cells_held = planes * height * width // BLOCK
    grads_across, grads_between, pieces = call(
        functools.partial(far_kernel, full, tiles),
        (grads, grads, jax.ShapeDtypeStruct((cells_held, 6 * BLOCK), BF16)), [VMEM] * 9,
        (picks, message_far, early, far, far_late, constant, factor, kept_even, kept_odd),
        [window_of(planes)] * 2
        + [window_of(3 * planes + 2)] * 2
        + [pltpu.VMEM((cells_held, 3 * BLOCK), F32)],
        flops=planes * height * 4 * 384 * 256 * 6, size=9 * field_bytes,
    )
    ends_of = lambda source, target: [((source, r), (target, r)) for r in range(regions)]
    low, high, between = 0, CORES, 1
    came_low = send(grads_between, ends_of(low, between))
    came_high = send(grads_between, ends_of(high, between))
    came_across = send(grads_across, ends_of(low, high) + ends_of(high, low))
    grads_a = call(pick_kernel, grads, [VMEM] * 2, (picks, pieces), flops=slots, size=slots)
    contact = call(
        contact_kernel, shaped(3 * tiles, BLOCK), [SMEM] + [VMEM] * 7 + [ANY],
        (
            partner_block, state, message_near, message_far, came_near, came_far, contact_rows,
            contact_stiff, grads_a,
        ),
        [pltpu.VMEM((3 * (tiles + 2 * rows), BLOCK), F32)],
        flops=60 * 8 * slots, size=4 * 20 * slots,
    )
    return call(
        final_kernel, shaped(3, slots), [SMEM] + [VMEM] * 10,
        (
            count, grads_a, came_across, came_low, came_high, weight, contact, grain_vel, vol, drag,
            cell,
        ),
        flops=60 * slots, size=4 * 20 * slots,
    )


def solution(mesh):
    in_specs = (
        P(None, ("grp", "reg")),
        P(None, ("grp", "reg")),
        P(("grp", "reg")),
        P(("grp", "reg")),
        P(("grp", "reg")),
        P(None, ("grp", "reg")),
        P(None, ("grp", "reg")),
        P(("grp", "reg")),
        P(None, ("grp", "reg")),
        P(("grp", "reg")),
        P(("grp", "reg")),
        P("reg", None, None),
        P("reg", None, None),
        P("reg", None, None),
    )
    out_specs = P(None, ("grp", "reg"))
    return jax.shard_map(
        on_device, mesh=mesh, in_specs=in_specs, out_specs=out_specs, check_vma=False
    )
```
